32 devices in a mesh: zone: 8 (over z, y), ja: 4 (over x, core).
Axes of the slice: x: 2, y: 2, z: 4, core: 2. Of those that a mesh axis runs over, the one named last changes fastest.
Arguments:
- flow_state: float32 [8, 32, 5, 16, 128], P('zone', 'ja'), may hold values from -3 to 3
- forcing: float32 [8, 32, 5, 16, 128], P('zone', 'ja'), may hold values from -6 to 6
- diag_block: float32 [8, 32, 5, 5, 16, 128], P('zone', 'ja'), may hold values from -0.4 to 7.2
- lower_jac: float32 [8, 32, 5, 5, 16, 128], P('zone', 'ja'), may hold values from -4.9 to 0.2
- upper_jac: float32 [8, 32, 5, 5, 16, 128], P('zone', 'ja'), may hold values from -4.9 to 0.2
- block_inv: float32 [8, 32, 5, 5, 16, 128], P('zone', 'ja'), may hold values from -0.03 to 0.21
- east_zone: int32 [8], replicated, may hold values from 0 to 7, each once
- zone_depth: int32 [8], replicated, may hold values from 4 to 16, as said below
Outputs:
- new_state: float32 [8, 32, 5, 16, 128], P('zone', 'ja')
- last_residual: float32 [8, 32, 5, 16, 128], P('zone', 'ja')
The draws below stay inside these ranges and needn't reach their ends.
Inputs may be any that keep to these rules, and one draw needn't show every extreme that they name: `east_zone`: a permutation of the zones. `zone_depth`: some zone has all 16 planes live.
All inputs are finite; a program needn't handle non-finite values.
Results may differ from the reference program's by a relative error of at most 0.0003.
Values sent between devices are 32-bit elements; how exact they have to be, the bound alone decides.
No kernel may reach another device: no remote copies, remote signals or barrier semaphores. Data moves between devices by JAX's collectives and lax.ppermute only.
A program may use at most 64 MiB of HBM per device.

```python
import math
import jax
import jax.numpy as jnp
from jax import lax

NVAR = 5
KC = 16
IC = 128
ITERS = 2
ZONES = 8
JZ = 32


def block_field(key, diag_lo, diag_hi, rough, off_scale):
    shape = (ZONES, JZ, 5, 5, KC, IC)
    key_base, key_rough, key_off = jax.random.split(key, 3)
    base = jnp.exp(jax.random.uniform(key_base, (ZONES, 1, 5, 1, 1, 1), jnp.float32, math.log(diag_lo), math.log(diag_hi)))
    roughness = jax.random.uniform(key_rough, shape, jnp.float32, 1.0 - rough, 1.0 + rough)
    noise = off_scale * jax.random.uniform(key_off, shape, jnp.float32, -1.0, 1.0)
    identity = jnp.eye(5, dtype=jnp.float32).reshape(1, 1, 5, 5, 1, 1)
    return identity * base * roughness + (1.0 - identity) * noise


def draw_diag_block(key, part):
    return block_field(jax.random.fold_in(key, 11), 5.0, 6.5, 0.1, 0.4)


def draw_lower_jac(key, part):
    return -block_field(jax.random.fold_in(key, 12), 4.0, 4.4, 0.1, 0.2)


def draw_upper_jac(key, part):
    return -block_field(jax.random.fold_in(key, 13), 4.0, 4.4, 0.1, 0.2)


def draw_block_inv(key, part):
    return block_field(jax.random.fold_in(key, 14), 0.15, 0.19, 0.1, 0.03)


def draw_zone_depth(key, part):
    key_depth, key_full = jax.random.split(jax.random.fold_in(key, 7))
    lowest = max(1, KC // 4)
    depths = jax.random.randint(key_depth, (ZONES,), lowest, KC + 1, dtype=jnp.int32)
    full_zone = jax.random.randint(key_full, (), 0, ZONES, dtype=jnp.int32)
    return jnp.where(jnp.arange(ZONES, dtype=jnp.int32) == full_zone, KC, depths).astype(jnp.int32)


def block_scale(rng, extent, cuts, smallest, high):
    level, own = 1.0, jax.random.fold_in(rng, 6)
    for position, shards_of in cuts:
        draws = jnp.exp(jax.random.uniform(jax.random.fold_in(own, position), (shards_of,), jnp.float32, smallest / len(cuts), high / len(cuts)))
        level = level * jnp.repeat(draws, extent[position] // shards_of).reshape([-1 if axis == position else 1 for axis in range(len(extent))])
    return level


def bell_draw(rng, dims, deviation, limit, pieces=(), kind=jnp.bfloat16):
    result = jax.random.normal(rng, dims, jnp.float32) * deviation
    if len(pieces) > 0:
        result = block_scale(rng, dims, pieces, -0.22, 0.18) * result
    return jnp.clip(result, min=-limit, max=limit).astype(kind)


def setup_inputs(seed: int = 0) -> dict:
    keys = jax.random.split(jax.random.key(seed), 9)
    return {
        "flow_state": bell_draw(keys[0], (ZONES, JZ, NVAR, KC, IC), 0.3, 3.0, ((0, 8), (1, 4)), jnp.float32),
        "forcing": bell_draw(keys[1], (ZONES, JZ, NVAR, KC, IC), 1.0, 6.0, ((0, 8), (1, 4)), jnp.float32),
        "diag_block": draw_diag_block(jax.random.fold_in(keys[8], 71), 0),
        "lower_jac": draw_lower_jac(jax.random.fold_in(keys[8], 71), 0),
        "upper_jac": draw_upper_jac(jax.random.fold_in(keys[8], 71), 0),
        "block_inv": draw_block_inv(jax.random.fold_in(keys[8], 71), 0),
        "east_zone": jax.random.permutation(keys[6], ZONES).astype(jnp.int32),
        "zone_depth": draw_zone_depth(jax.random.fold_in(keys[8], 71), 0),
    }


OMEGA = 1.2
COUPLE = 0.25


def matvec(matrix, vector):
    return jnp.sum(matrix * vector[..., None, :, :, :], axis=-3)


def zone_update(inputs):
    current, forcing, diag_block, lower_jac, upper_jac, block_inv, ghost_low, ghost_high, live_count = inputs
    k_index = jnp.arange(current.shape[2], dtype=jnp.int32)
    live_mask = (k_index < live_count).astype(jnp.float32)[None, None, :, None]
    zero_j = jnp.zeros_like(current[:1])
    below_j = jnp.concatenate([zero_j, current[:-1]], axis=0)
    above_j = jnp.concatenate([current[1:], zero_j], axis=0)
    left_i = jnp.concatenate([ghost_low[..., None], current[..., :-1]], axis=3)
    right_i = jnp.concatenate([current[..., 1:], ghost_high[..., None]], axis=3)
    zero_k = jnp.zeros_like(current[:, :, :1])
    down_k = jnp.concatenate([zero_k, current[:, :, :-1]], axis=2)
    up_k = jnp.concatenate([current[:, :, 1:], zero_k], axis=2)
    applied = matvec(diag_block, current) - matvec(lower_jac, below_j) - matvec(upper_jac, above_j) - COUPLE * (left_i + right_i + down_k + up_k)
    residual = live_mask * (forcing - applied)

    def lower_step(previous, planes):
        res_plane, inv_plane, jac_plane = planes
        value = matvec(inv_plane, res_plane + OMEGA * matvec(jac_plane, previous))
        return value, value

    no_inflow = jnp.zeros_like(residual[0])
    _, lowered = lax.scan(lower_step, no_inflow, (residual, block_inv, lower_jac))

    def upper_step(following, planes):
        low_plane, inv_plane, jac_plane = planes
        value = low_plane + OMEGA * matvec(inv_plane, matvec(jac_plane, following))
        return value, value

    _, raised = lax.scan(upper_step, no_inflow, (lowered, block_inv, upper_jac), reverse=True)
    return current + raised, residual


def reference(flow_state, forcing, diag_block, lower_jac, upper_jac, block_inv, east_zone, zone_depth):
    k_index = jnp.arange(KC, dtype=jnp.int32)
    live_mask = (k_index[None, :] < zone_depth[:, None]).astype(jnp.float32)
    current = flow_state * live_mask[:, None, None, :, None]
    west_zone = jnp.zeros((ZONES,), jnp.int32).at[east_zone].set(jnp.arange(ZONES, dtype=jnp.int32))
    residual = jnp.zeros_like(current)
    for iteration in range(ITERS):
        low_faces = current[..., 0]
        high_faces = current[..., -1]
        ghost_high = low_faces[east_zone]
        ghost_low = high_faces[west_zone]
        current, residual = lax.map(zone_update, (current, forcing, diag_block, lower_jac, upper_jac, block_inv, ghost_low, ghost_high, zone_depth))
    return current, residual
```

```python
import functools

import jax
import jax.numpy as jnp
from jax import lax
from jax.experimental import pallas as pl
from jax.experimental.pallas import tpu as pltpu
from jax.sharding import PartitionSpec as P

ITERS = 2
OMEGA = 1.2
COUPLE = 0.25

VMEM = pl.BlockSpec(memory_space=pltpu.VMEM)
SMEM = pl.BlockSpec(memory_space=pltpu.SMEM)


def call(kernel, shapes, scratch=(), flops=10**6):
    moved = sum(4 * functools.reduce(lambda a, b: a * b, s, 1) for s in shapes)

    def run(*arrays):
        total = moved + sum(a.size * 4 for a in arrays)
        return pl.pallas_call(
            kernel,
            out_shape=[jax.ShapeDtypeStruct(s, jnp.float32) for s in shapes],
            in_specs=[VMEM if a.dtype == jnp.float32 else SMEM for a in arrays],
            out_specs=[VMEM] * len(shapes),
            scratch_shapes=list(scratch),
            compiler_params=pltpu.CompilerParams(vmem_limit_bytes=10 * 2**20),
            cost_estimate=pl.CostEstimate(flops=flops, bytes_accessed=total, transcendentals=0),
        )(*arrays)

    return run


def iota(dim):
    return lax.broadcasted_iota(jnp.int32, (16, 128), dim)


def matvec(matrix, vector):
    n = len(vector)
    out = []
    for r in range(n):
        acc = matrix[r][0] * vector[0]
        for c in range(1, n):
            acc = acc + matrix[r][c] * vector[c]
        out.append(acc)
    return out


def block(ref, *lead):
    return [[ref[(*lead, r, c)] for c in range(5)] for r in range(5)]


def cell(ref, *lead):
    return [ref[(*lead, v)] for v in range(5)]


def put(ref, values, *lead):
    for v, value in enumerate(values):
        ref[(*lead, v)] = value


def add(a, b):
    return [x + y for x, y in zip(a, b)]


def pack_faces(load, planes, tile_ref):
    lane = iota(1)
    tile = jnp.zeros((16, 128), jnp.float32)
    for j in range(planes):
        for v in range(5):
            q = 2 * (j * 5 + v)
            here = (lane == q) | (lane == (q - 1) % 128)
            x = load(j, v)
            tile = jnp.where(here, pltpu.roll(x, q, 1) if q else x, tile)
    for w in range(tile_ref.shape[0]):
        tile_ref[w] = tile


def live_rows(depth_ref):
    return iota(0) < depth_ref[lax.axis_index("zone")]


def pack_kernel(depth_ref, flow_ref, tile_ref):
    live = live_rows(depth_ref)
    pack_faces(lambda j, v: jnp.where(live, flow_ref[j, v], 0.0), flow_ref.shape[0], tile_ref)


def matrix_kernel(inv_ref, low_ref, up_ref, e_ref, f_ref, mats_ref, y_ref):
    planes = inv_ref.shape[0]
    for h in range(2):
        rows = pl.ds(8 * h, 8)

        def col(ref, q, j):
            return [ref[j, r, q, rows] for r in range(5)]

        def put_col(ref, values, q, j):
            for r in range(5):
                ref[j, r, q, rows] = values[r]

        def mat(ref, j):
            return [[ref[j, r, c, rows] for c in range(5)] for r in range(5)]

        def product(ref_out, j, jac_ref):
            inv = mat(inv_ref, j)
            for q in range(5):
                put_col(ref_out, [OMEGA * x for x in matvec(inv, col(jac_ref, q, j))], q, j)

        def forward(j, carry):
            product(e_ref, j, low_ref)
            e = mat(e_ref, j)
            for q in range(5):
                put_col(y_ref, matvec(e, col(y_ref, q, j - 1)), q, j)
            return carry

        product(e_ref, 0, low_ref)
        for q in range(5):
            put_col(y_ref, col(e_ref, q, 0), q, 0)
        lax.fori_loop(1, planes, forward, 0)

        def backward(step, carry):
            j = planes - 2 - step
            product(f_ref, j, up_ref)
            f = mat(f_ref, j)
            for q in range(5):
                put_col(mats_ref, add(col(y_ref, q, j), matvec(f, col(mats_ref, q, 1))), q, 1)
                put_col(mats_ref, matvec(f, col(mats_ref, q, 2)), q, 2)
            return carry

        last = planes - 1
        product(f_ref, last, up_ref)
        for q in range(5):
            put_col(mats_ref, col(y_ref, q, last), q, 0)
            put_col(mats_ref, col(y_ref, q, last), q, 1)
            put_col(mats_ref, col(f_ref, q, last), q, 2)
        lax.fori_loop(0, planes - 1, backward, 0)


def by_place(mine_refs, other_refs, run):
    odd = lax.axis_index("ja") % 2

    @pl.when(odd == 0)
    def _():
        run(*mine_refs, *other_refs)

    @pl.when(odd == 1)
    def _():
        run(*other_refs, *mine_refs)


def beta_kernel(mine_ref, other_ref, beta_ref):
    def run(lo, hi):
        d_hi, n_lo = block(hi, 1), block(lo, 2)
        for q in range(5):
            m_col = [lo[0, r, q] for r in range(5)]
            d_col = [lo[1, r, q] for r in range(5)]
            out = add(d_col, matvec(n_lo, matvec(d_hi, m_col)))
            for r in range(5):
                beta_ref[r, q] = out[r]

    by_place([mine_ref], [other_ref], run)


def local_kernel(
    depth_ref, east_ref, cur_ref, force_ref, diag_ref, low_ref, up_ref, inv_ref, e_ref, f_ref,
    below_ref, above_ref, tiles_ref, res_ref, s_ref, ends_ref, y_ref,
):
    planes = cur_ref.shape[0]
    zone = lax.axis_index("zone")
    live = live_rows(depth_ref)
    lane, row = iota(1), iota(0)
    east = east_ref[zone]
    west = jnp.int32(0)
    for w in range(tiles_ref.shape[0]):
        west = west + jnp.where(east_ref[w] == zone, w, 0)
    ghosts = jnp.where(
        lane % 2 == 0, pltpu.roll(tiles_ref[west], 1, 1), pltpu.roll(tiles_ref[east], 127, 1)
    )

    def state(j):
        source = below_ref if j < 0 else above_ref if j >= planes else cur_ref.at[j]
        return [jnp.where(live, source[v], 0.0) for v in range(5)]

    value = None
    for j in range(planes):
        here = state(j)
        own = matvec(block(diag_ref, j), here)
        lower = matvec(block(low_ref, j), state(j - 1))
        upper = matvec(block(up_ref, j), state(j + 1))
        res = []
        for v in range(5):
            x = here[v]
            q = 2 * (j * 5 + v)
            ghost = pltpu.roll(ghosts, 128 - q, 1) if q else ghosts
            sides = jnp.where(lane == 0, ghost, pltpu.roll(x, 1, 1))
            sides = sides + jnp.where(lane == 127, ghost, pltpu.roll(x, 127, 1))
            sides = sides + jnp.where(row == 0, 0.0, pltpu.roll(x, 1, 0))
            sides = sides + jnp.where(row == 15, 0.0, pltpu.roll(x, 15, 0))
            applied = own[v] - lower[v] - upper[v] - COUPLE * sides
            res.append(jnp.where(live, force_ref[j, v] - applied, 0.0))
        put(res_ref, res, j)
        s = matvec(block(inv_ref, j), res)
        put(s_ref, s, j)
        value = s if j == 0 else add(s, matvec(block(e_ref, j), value))
        put(y_ref, value, j)
    put(ends_ref, value, 0)
    for j in range(planes - 2, -1, -1):
        value = add(cell(y_ref, j), matvec(block(f_ref, j), value))
    put(ends_ref, value, 1)


def mid_kernel(ends_ref, ends_other_ref, mats_ref, mats_other_ref, out_ref):
    def run(ends_lo, mats_lo, ends_hi, mats_hi):
        c_lo = cell(ends_lo, 0)

        @pl.when(lax.axis_index("ja") < 2)
        def _():
            put(out_ref, add(cell(ends_hi, 0), matvec(block(mats_hi, 0), c_lo)))

        @pl.when(lax.axis_index("ja") >= 2)
        def _():
            turned = add(cell(ends_hi, 1), matvec(block(mats_hi, 1), c_lo))
            put(out_ref, add(cell(ends_lo, 1), matvec(block(mats_lo, 2), turned)))

    by_place([ends_ref, mats_ref], [ends_other_ref, mats_other_ref], run)


def final_kernel(
    depth_ref, cur_ref, s_ref, e_ref, f_ref, below_ref, above_ref, f_below_ref,
    ends_ref, ends_other_ref, mats_ref, mats_other_ref, pair_ref, pair_other_ref, beta_ref,
    new_ref, *more,
):
    y_ref, inflow_ref = more[-2:]
    planes = cur_ref.shape[0]
    ja = lax.axis_index("ja")
    live = live_rows(depth_ref)

    def far(a, alpha):
        return add(cell(alpha), matvec(block(beta_ref), cell(a)))

    @pl.when(ja == 0)
    def _():
        put(inflow_ref, [jnp.zeros((16, 128), jnp.float32)] * 5, 0)
        b = add(cell(ends_other_ref, 1), matvec(block(mats_other_ref, 1), cell(ends_ref, 0)))
        b = add(b, matvec(block(mats_other_ref, 2), far(pair_ref, pair_other_ref)))
        put(inflow_ref, b, 1)

    @pl.when(ja == 1)
    def _():
        put(inflow_ref, cell(ends_other_ref, 0), 0)
        put(inflow_ref, far(pair_ref, pair_other_ref), 1)

    @pl.when(ja == 2)
    def _():
        a = cell(pair_other_ref)
        put(inflow_ref, a, 0)
        a = add(cell(ends_ref, 0), matvec(block(mats_ref, 0), a))
        b = add(cell(ends_other_ref, 1), matvec(block(mats_other_ref, 1), a))
        put(inflow_ref, b, 1)

    @pl.when(ja == 3)
    def _():
        a = add(cell(ends_other_ref, 0), matvec(block(mats_other_ref, 0), cell(pair_other_ref)))
        put(inflow_ref, a, 0)
        put(inflow_ref, [jnp.zeros((16, 128), jnp.float32)] * 5, 1)

    value = cell(inflow_ref, 0)
    for j in range(planes):
        value = add(cell(s_ref, j), matvec(block(e_ref, j), value))
        put(y_ref, value, j)
    value = cell(inflow_ref, 1)
    for j in range(planes - 1, -1, -1):
        value = add(cell(y_ref, j), matvec(block(f_ref, j), value))
        put(new_ref, [jnp.where(live, cur_ref[j, v], 0.0) + value[v] for v in range(5)], j)
    if len(more) > 2:
        below_new_ref, above_new_ref, tile_ref = more[:3]
        before = add(cell(inflow_ref, 0), matvec(block(f_below_ref), value))
        put(below_new_ref, add([jnp.where(live, below_ref[v], 0.0) for v in range(5)], before))
        after = cell(inflow_ref, 1)
        put(above_new_ref, add([jnp.where(live, above_ref[v], 0.0) for v in range(5)], after))
        pack_faces(lambda j, v: new_ref[j, v], planes, tile_ref)


def per_device(
    flow_state, forcing, diag_block, lower_jac, upper_jac, block_inv, east_zone, zone_depth
):
    zones, parts = lax.axis_size("zone"), lax.axis_size("ja")
    assert parts == 4
    current, force, diag, low, up, inv = (
        x[0] for x in (flow_state, forcing, diag_block, lower_jac, upper_jac, block_inv)
    )
    state = current.shape
    plane, blocks, tiles = state[1:], diag.shape, (zones, *state[2:])
    matrix = blocks[1:]

    def swap(x, bit):
        return lax.ppermute(x, "ja", [(p, p ^ bit) for p in range(parts)])

    def faces(x):
        return lax.all_to_all(x, "zone", 0, 0, tiled=True)

    got = faces(call(pack_kernel, [tiles])(zone_depth, current)[0])
    above = lax.ppermute(current[0], "ja", [(p + 1, p) for p in range(parts - 1)])
    e, f, mats = call(
        matrix_kernel, [blocks, blocks, (3, *matrix)], [pltpu.VMEM(blocks, jnp.float32)]
    )(inv, low, up)
    edge = jnp.concatenate([current[-1].reshape(1, *plane), f[-1]], axis=0)
    edge = lax.ppermute(edge, "ja", [(p, p + 1) for p in range(parts - 1)])
    below, f_below = edge[0], edge[1:]
    mats_other = swap(mats, 1)
    beta = call(beta_kernel, [matrix])(mats, mats_other)[0]
    beta = lax.ppermute(beta, "ja", [(2, 0), (3, 1)])

    for iteration in range(ITERS):
        last = iteration == ITERS - 1
        residual, s, ends = call(
            local_kernel, [state, state, (2, *plane)], [pltpu.VMEM(state, jnp.float32)]
        )(zone_depth, east_zone, current, force, diag, low, up, inv, e, f, below, above, got)
        ends_other = swap(ends, 1)
        pair = call(mid_kernel, [plane])(ends, ends_other, mats, mats_other)[0]
        pair_other = swap(pair, 2)
        current, *more = call(
            final_kernel,
            [state] if last else [state, plane, plane, tiles],
            [pltpu.VMEM(state, jnp.float32), pltpu.VMEM((2, *plane), jnp.float32)],
        )(
            zone_depth, current, s, e, f, below, above, f_below,
            ends, ends_other, mats, mats_other, pair, pair_other, beta,
        )
        if not last:
            below, above, got = more[0], more[1], faces(more[2])
    return (current[None], residual[None])


def solution(mesh):
    state = P("zone", "ja", None, None, None)
    blocks = P("zone", "ja", None, None, None, None)
    return jax.shard_map(
        per_device,
        mesh=mesh,
        in_specs=(state, state, blocks, blocks, blocks, blocks, P(), P()),
        out_specs=(state, state),
        check_vma=False,
    )
```

```python
import functools

import jax
import jax.numpy as jnp
from jax import lax
from jax.experimental import pallas as pl
from jax.experimental.pallas import tpu as pltpu
from jax.sharding import PartitionSpec as P

ITERS = 2
OMEGA = 1.2
COUPLE = 0.25

VMEM = pl.BlockSpec(memory_space=pltpu.VMEM)
SMEM = pl.BlockSpec(memory_space=pltpu.SMEM)
HBM = pl.BlockSpec(memory_space=pltpu.HBM)


def call(kernel, shapes, scratch=(), flops=10**9, far=(), far_out=()):
    moved = sum(4 * functools.reduce(lambda a, b: a * b, s, 1) for s in shapes)

    def spec(i, a):
        return HBM if i in far else VMEM if a.dtype == jnp.float32 else SMEM

    def run(*arrays):
        total = moved + sum(a.size * 4 for a in arrays)
        return pl.pallas_call(
            kernel,
            out_shape=[jax.ShapeDtypeStruct(s, jnp.float32) for s in shapes],
            in_specs=[spec(i, a) for i, a in enumerate(arrays)],
            out_specs=[HBM if i in far_out else VMEM for i in range(len(shapes))],
            scratch_shapes=list(scratch),
            compiler_params=pltpu.CompilerParams(vmem_limit_bytes=12 * 2**20),
            cost_estimate=pl.CostEstimate(flops=flops, bytes_accessed=total, transcendentals=0),
        )(*arrays)

    return run


def buffer(*shape):
    return pltpu.VMEM(shape, jnp.float32)


def iota(dim):
    return lax.broadcasted_iota(jnp.int32, (16, 128), dim)


def matvec(matrix, vector):
    n = len(vector)
    out = []
    for r in range(n):
        acc = matrix[r][0] * vector[0]
        for c in range(1, n):
            acc = acc + matrix[r][c] * vector[c]
        out.append(acc)
    return out


def block(ref, *lead):
    return [[ref[(*lead, r, c)] for c in range(5)] for r in range(5)]


def cell(ref, *lead):
    return [ref[(*lead, v)] for v in range(5)]


def put(ref, values, *lead):
    for v, value in enumerate(values):
        ref[(*lead, v)] = value


def add(a, b):
    return [x + y for x, y in zip(a, b)]


def pack_faces(load, planes, tile_ref):
    lane = iota(1)
    tile = jnp.zeros((16, 128), jnp.float32)
    for j in range(planes):
        for v in range(5):
            q = 2 * (j * 5 + v)
            here = (lane == q) | (lane == (q - 1) % 128)
            x = load(j, v)
            tile = jnp.where(here, pltpu.roll(x, q, 1) if q else x, tile)
    for w in range(tile_ref.shape[0]):
        tile_ref[w] = tile


def live_rows(depth_ref):
    return iota(0) < depth_ref[lax.axis_index("zone")]


def pack_kernel(depth_ref, flow_hbm, tile_ref, cur_ref, first_ref, flow_ref, sem):
    copy = pltpu.make_async_copy(flow_hbm, flow_ref, sem)
    copy.start()
    live = live_rows(depth_ref)
    copy.wait()
    planes = flow_ref.shape[0]
    for j in range(planes):
        for v in range(5):
            cur_ref[j, v] = jnp.where(live, flow_ref[j, v], 0.0)
    for v in range(5):
        first_ref[v] = jnp.where(live, flow_ref[0, v], 0.0)
    pack_faces(lambda j, v: cur_ref[j, v], planes, tile_ref)


def neighbours(x):
    lane, row = iota(1), iota(0)
    total = jnp.where(lane == 0, 0.0, pltpu.roll(x, 1, 1))
    total = total + jnp.where(lane == 127, 0.0, pltpu.roll(x, 127, 1))
    total = total + jnp.where(row == 0, 0.0, pltpu.roll(x, 1, 0))
    return total + jnp.where(row == 15, 0.0, pltpu.roll(x, 15, 0))


def ghosts_of(east_ref, tiles_ref):
    zone = lax.axis_index("zone")
    east = east_ref[zone]
    west = jnp.int32(0)
    for w in range(tiles_ref.shape[0]):
        west = west + jnp.where(east_ref[w] == zone, w, 0)
    return jnp.where(
        iota(1) % 2 == 0, pltpu.roll(tiles_ref[west], 1, 1), pltpu.roll(tiles_ref[east], 127, 1)
    )


def ghost_at(ghosts, j, v, ends):
    q = 2 * (j * 5 + v)
    turned = pltpu.roll(ghosts, 128 - q, 1) if q else ghosts
    return jnp.where(ends, turned, 0.0)


def first_kernel(
    depth_ref, cur_ref, above_ref, force_hbm, diag_hbm, low_hbm, up_hbm, inv_hbm,
    e_ref, f_ref, inv_ref, s_ref, mats_ref,
    force_ref, diag_ref, low_ref, up_ref, y_ref, wide_ref, sems,
):
    planes = cur_ref.shape[0]
    pairs = [
        (inv_hbm, inv_ref), (low_hbm, low_ref), (up_hbm, up_ref),
        (diag_hbm, diag_ref), (force_hbm, force_ref),
    ]

    def copies(j):
        return [
            pltpu.make_async_copy(src.at[j], dst.at[j], sems.at[i, j])
            for i, (src, dst) in enumerate(pairs)
        ]

    for j in range(planes):
        for copy in copies(j):
            copy.start()
    live = live_rows(depth_ref)
    zero = jnp.zeros((16, 128), jnp.float32)
    for v in range(5):
        wide_ref[0, v] = zero
        wide_ref[planes + 1, v] = above_ref[v]
        for j in range(planes):
            wide_ref[j + 1, v] = cur_ref[j, v]

    halves = [pl.ds(0, 8), pl.ds(8, 8)]

    def col(ref, q, j, rows):
        return [ref[j, r, q, rows] for r in range(5)]

    def put_col(ref, values, q, j, rows):
        for r in range(5):
            ref[j, r, q, rows] = values[r]

    def mat(ref, j, rows):
        return [[ref[j, r, c, rows] for c in range(5)] for r in range(5)]

    def forward(j, carry):
        for copy in copies(j):
            copy.wait()
        for rows in halves:
            inv = mat(inv_ref, j, rows)
            for jac_ref, out_ref in ((low_ref, e_ref), (up_ref, f_ref)):
                for q in range(5):
                    product = matvec(inv, col(jac_ref, q, j, rows))
                    put_col(out_ref, [OMEGA * x for x in product], q, j, rows)
        here = cell(wide_ref, j + 1)
        own = matvec(block(diag_ref, j), here)
        lower = matvec(block(low_ref, j), cell(wide_ref, j))
        upper = matvec(block(up_ref, j), cell(wide_ref, j + 2))
        res = []
        for v in range(5):
            applied = own[v] - lower[v] - upper[v] - COUPLE * neighbours(here[v])
            res.append(jnp.where(live, force_ref[j, v] - applied, 0.0))
        put(s_ref, matvec(block(inv_ref, j), res), j)
        return carry

    def chain(j, carry):
        for rows in halves:
            e = mat(e_ref, j, rows)
            for q in range(5):
                put_col(y_ref, matvec(e, col(y_ref, q, j - 1, rows)), q, j, rows)
        return carry

    forward(0, 0)
    for rows in halves:
        for q in range(5):
            put_col(y_ref, col(e_ref, q, 0, rows), q, 0, rows)

    def both(j, carry):
        return chain(j, forward(j, carry))

    lax.fori_loop(1, planes, both, 0)
    last = planes - 1
    for rows in halves:
        for q in range(5):
            put_col(mats_ref, col(y_ref, q, last, rows), q, 0, rows)
            put_col(mats_ref, col(y_ref, q, last, rows), q, 1, rows)
            put_col(mats_ref, col(f_ref, q, last, rows), q, 2, rows)

    def backward(step, carry):
        j = planes - 2 - step
        for rows in halves:
            f = mat(f_ref, j, rows)
            for q in range(5):
                turned = matvec(f, col(mats_ref, q, 1, rows))
                put_col(mats_ref, add(col(y_ref, q, j, rows), turned), q, 1, rows)
                put_col(mats_ref, matvec(f, col(mats_ref, q, 2, rows)), q, 2, rows)
        return carry

    lax.fori_loop(0, planes - 1, backward, 0)


def by_place(mine_refs, other_refs, run):
    odd = lax.axis_index("ja") % 2

    @pl.when(odd == 0)
    def _():
        run(*mine_refs, *other_refs)

    @pl.when(odd == 1)
    def _():
        run(*other_refs, *mine_refs)


def beta_kernel(mine_ref, other_ref, beta_ref):
    def run(lo, hi):
        d_hi, n_lo = block(hi, 1), block(lo, 2)
        for q in range(5):
            m_col = [lo[0, r, q] for r in range(5)]
            d_col = [lo[1, r, q] for r in range(5)]
            out = add(d_col, matvec(n_lo, matvec(d_hi, m_col)))
            for r in range(5):
                beta_ref[r, q] = out[r]

    by_place([mine_ref], [other_ref], run)


def sweeps(s_ref, e_ref, f_ref, y_ref, ends_ref, last):
    planes = s_ref.shape[0]
    value = cell(s_ref, 0)
    put(y_ref, value, 0)
    for j in range(1, planes):
        value = add(cell(s_ref, j), matvec(block(e_ref, j), value))
        put(y_ref, value, j)
    put(ends_ref, [x + z * (1.0 / OMEGA) for x, z in zip(value, last)], 0)
    for j in range(planes - 2, -1, -1):
        value = add(cell(y_ref, j), matvec(block(f_ref, j), value))
    put(ends_ref, value, 1)


def ghost_kernel(
    depth_ref, east_ref, tiles_ref, cur_ref, s0_ref, inv_ref, e_ref, f_ref,
    s_ref, ends_ref, y_ref,
):
    planes = cur_ref.shape[0]
    ghosts = ghosts_of(east_ref, tiles_ref)
    ghosts = jnp.where(live_rows(depth_ref), COUPLE * ghosts, 0.0)
    lane = iota(1)
    ends = (lane == 0) | (lane == 127)
    for j in range(planes):
        extra = [ghost_at(ghosts, j, v, ends) for v in range(5)]
        put(s_ref, add(cell(s0_ref, j), matvec(block(inv_ref, j), extra)), j)
    sweeps(s_ref, e_ref, f_ref, y_ref, ends_ref, cell(cur_ref, planes - 1))


def local_kernel(
    depth_ref, east_ref, tiles_ref, cur_ref, above_ref, force_ref, diag_ref, low_ref, up_ref,
    inv_ref, e_ref, f_ref,
    res_ref, s_ref, ends_ref, y_ref,
):
    planes = cur_ref.shape[0]
    live = live_rows(depth_ref)
    ghosts = ghosts_of(east_ref, tiles_ref)
    lane = iota(1)
    ends = (lane == 0) | (lane == 127)
    for j in range(planes):
        here = cell(cur_ref, j)
        applied = matvec(block(diag_ref, j), here)
        if j > 0:
            lower = matvec(block(low_ref, j), cell(cur_ref, j - 1))
            applied = [x - z for x, z in zip(applied, lower)]
        above = cell(cur_ref, j + 1) if j < planes - 1 else cell(above_ref)
        upper = matvec(block(up_ref, j), above)
        res = []
        for v in range(5):
            sides = neighbours(here[v]) + ghost_at(ghosts, j, v, ends)
            all_of = applied[v] - upper[v] - COUPLE * sides
            res.append(jnp.where(live, force_ref[j, v] - all_of, 0.0))
        put(res_ref, res, j)
        put(s_ref, matvec(block(inv_ref, j), res), j)
    last = cell(cur_ref, planes - 1)
    sweeps(s_ref, e_ref, f_ref, y_ref, ends_ref, last)
    put(ends_ref, last, 2)


def mid_kernel(ends_ref, ends_other_ref, mats_ref, mats_other_ref, out_ref):
    def run(ends_lo, mats_lo, ends_hi, mats_hi):
        c_lo = cell(ends_lo, 0)

        @pl.when(lax.axis_index("ja") < 2)
        def _():
            put(out_ref, add(cell(ends_hi, 0), matvec(block(mats_hi, 0), c_lo)), 0)

        @pl.when(lax.axis_index("ja") >= 2)
        def _():
            turned = add(cell(ends_hi, 1), matvec(block(mats_hi, 1), c_lo))
            put(out_ref, add(cell(ends_lo, 1), matvec(block(mats_lo, 2), turned)), 0)

        if out_ref.shape[0] > 1:
            put(out_ref, cell(ends_hi, 2), 1)

    by_place([ends_ref, mats_ref], [ends_other_ref, mats_other_ref], run)


def inflows(
    ends_ref, ends_other_ref, mats_ref, mats_other_ref, pair_ref, pair_other_ref, beta_ref,
    inflow_ref,
):
    ja = lax.axis_index("ja")
    zeros = [jnp.zeros((16, 128), jnp.float32)] * 5

    def far(a, alpha):
        return add(cell(alpha, 0), matvec(block(beta_ref), cell(a, 0)))

    @pl.when(ja == 0)
    def _():
        put(inflow_ref, zeros, 0)
        b = add(cell(ends_other_ref, 1), matvec(block(mats_other_ref, 1), cell(ends_ref, 0)))
        b = add(b, matvec(block(mats_other_ref, 2), far(pair_ref, pair_other_ref)))
        put(inflow_ref, b, 1)

    @pl.when(ja == 1)
    def _():
        put(inflow_ref, cell(ends_other_ref, 0), 0)
        put(inflow_ref, far(pair_ref, pair_other_ref), 1)

    @pl.when(ja == 2)
    def _():
        a = cell(pair_other_ref, 0)
        put(inflow_ref, a, 0)
        a = add(cell(ends_ref, 0), matvec(block(mats_ref, 0), a))
        b = add(cell(ends_other_ref, 1), matvec(block(mats_other_ref, 1), a))
        put(inflow_ref, b, 1)

    @pl.when(ja == 3)
    def _():
        a = add(cell(ends_other_ref, 0), matvec(block(mats_other_ref, 0), cell(pair_other_ref, 0)))
        put(inflow_ref, a, 0)
        put(inflow_ref, zeros, 1)


def final_kernel(
    cur_ref, above_ref, s_ref, e_ref, f_ref,
    ends_ref, ends_other_ref, mats_ref, mats_other_ref, pair_ref, pair_other_ref, beta_ref,
    new_ref, above_new_ref, tile_ref, y_ref, inflow_ref,
):
    planes = cur_ref.shape[0]
    inflows(
        ends_ref, ends_other_ref, mats_ref, mats_other_ref, pair_ref, pair_other_ref, beta_ref,
        inflow_ref,
    )
    value = cell(inflow_ref, 0)
    for j in range(planes):
        value = add(cell(s_ref, j), matvec(block(e_ref, j), value))
        put(y_ref, value, j)
    value = cell(inflow_ref, 1)
    put(above_new_ref, add(cell(above_ref), value))
    for j in range(planes - 1, -1, -1):
        value = add(cell(y_ref, j), matvec(block(f_ref, j), value))
        put(new_ref, add(cell(cur_ref, j), value), j)
    pack_faces(lambda j, v: new_ref[j, v], planes, tile_ref)


def last_kernel(
    depth_ref, low_hbm, cur_ref, res_ref, s_ref, e_ref, f_ref,
    ends_ref, ends_other_ref, mats_ref, mats_other_ref, pair_ref, pair_other_ref, beta_ref,
    new_hbm, res_hbm, y_ref, inflow_ref, new_ref, low_ref, edge_ref, sems,
):
    planes = cur_ref.shape[0]
    low_copy = pltpu.make_async_copy(low_hbm.at[0], low_ref, sems.at[0, 0])
    low_copy.start()
    copies = []
    for j in range(1, planes):
        copies.append(pltpu.make_async_copy(res_ref.at[j], res_hbm.at[j], sems.at[0, j]))
        copies[-1].start()
    inflows(
        ends_ref, ends_other_ref, mats_ref, mats_other_ref, pair_ref, pair_other_ref, beta_ref,
        inflow_ref,
    )
    value = cell(inflow_ref, 0)
    for j in range(planes):
        value = add(cell(s_ref, j), matvec(block(e_ref, j), value))
        put(y_ref, value, j)
    ja = lax.axis_index("ja")
    live = live_rows(depth_ref)
    before = [
        jnp.where(ja == 0, 0.0, jnp.where(ja == 2, pair_other_ref[1, v], ends_other_ref[2, v]))
        for v in range(5)
    ]
    low_copy.wait()
    extra = matvec(block(low_ref), before)
    put(edge_ref, [res_ref[0, v] + jnp.where(live, extra[v], 0.0) for v in range(5)])
    copies.append(pltpu.make_async_copy(edge_ref, res_hbm.at[0], sems.at[1, planes]))
    copies[-1].start()
    value = cell(inflow_ref, 1)
    for j in range(planes - 1, -1, -1):
        value = add(cell(y_ref, j), matvec(block(f_ref, j), value))
        put(new_ref, add(cell(cur_ref, j), value), j)
        copies.append(pltpu.make_async_copy(new_ref.at[j], new_hbm.at[j], sems.at[1, j]))
        copies[-1].start()
    for copy in copies:
        copy.wait()


def per_device(
    flow_state, forcing, diag_block, lower_jac, upper_jac, block_inv, east_zone, zone_depth
):
    zones, parts = lax.axis_size("zone"), lax.axis_size("ja")
    assert parts == 4 and ITERS == 2
    current, force, diag, low, up, inv = (
        x[0] for x in (flow_state, forcing, diag_block, lower_jac, upper_jac, block_inv)
    )
    state = current.shape
    planes, plane, blocks, tiles = state[0], state[1:], diag.shape, (zones, *state[2:])
    matrix = blocks[1:]
    wide = buffer(planes + 2, *plane)

    def swap(x, bit):
        return lax.ppermute(x, "ja", [(p, p ^ bit) for p in range(parts)])

    def faces(x):
        return lax.all_to_all(x, "zone", 0, 0, tiled=True)

    tile, current, first = call(
        pack_kernel,
        [tiles, state, plane],
        [buffer(*state), pltpu.SemaphoreType.DMA],
        far=(1,),
    )(zone_depth, current)
    above = lax.ppermute(first, "ja", [(p + 1, p) for p in range(parts - 1)])
    got = faces(tile)
    e, f, inv, s0, mats = call(
        first_kernel,
        [blocks, blocks, blocks, state, (3, *matrix)],
        [buffer(*state)] + [buffer(*blocks)] * 4 + [wide, pltpu.SemaphoreType.DMA((5, planes))],
        flops=5 * 10**9,
        far=(3, 4, 5, 6, 7),
    )(zone_depth, current, above, force, diag, low, up, inv)
    mats_other = swap(mats, 1)
    s, ends = call(ghost_kernel, [state, (2, *plane)], [buffer(*state)])(
        zone_depth, east_zone, got, current, s0, inv, e, f
    )
    ends_other = swap(ends, 1)
    pair = call(mid_kernel, [(1, *plane)])(ends, ends_other, mats, mats_other)[0]
    beta = call(beta_kernel, [matrix])(mats, mats_other)[0]
    beta = lax.ppermute(beta, "ja", [(2, 0), (3, 1)])
    pair_other = swap(pair, 2)
    current, above, tile = call(
        final_kernel,
        [state, plane, tiles],
        [buffer(*state), buffer(2, *plane)],
    )(current, above, s, e, f, ends, ends_other, mats, mats_other, pair, pair_other, beta)

    got = faces(tile)
    residual, s, ends = call(local_kernel, [state, state, (3, *plane)], [buffer(*state)])(
        zone_depth, east_zone, got, current, above, force, diag, low, up, inv, e, f
    )
    ends_other = swap(ends, 1)
    pair = call(mid_kernel, [(2, *plane)])(ends, ends_other, mats, mats_other)[0]
    pair_other = swap(pair, 2)
    current, residual = call(
        last_kernel,
        [state, state],
        [
            buffer(*state), buffer(2, *plane), buffer(*state), buffer(*matrix), buffer(*plane),
            pltpu.SemaphoreType.DMA((2, planes + 1)),
        ],
        far=(1,),
        far_out=(0, 1),
    )(
        zone_depth, low, current, residual, s, e, f,
        ends, ends_other, mats, mats_other, pair, pair_other, beta,
    )
    return (current[None], residual[None])


def solution(mesh):
    state = P("zone", "ja", None, None, None)
    blocks = P("zone", "ja", None, None, None, None)
    return jax.shard_map(
        per_device,
        mesh=mesh,
        in_specs=(state, state, blocks, blocks, blocks, blocks, P(), P()),
        out_specs=(state, state),
        check_vma=False,
    )
```

```python
import functools

import jax
import jax.numpy as jnp
from jax import lax
from jax.experimental import pallas as pl
from jax.experimental.pallas import tpu as pltpu
from jax.sharding import PartitionSpec as P

ITERS = 2
OMEGA = 1.2
COUPLE = 0.25

VMEM = pl.BlockSpec(memory_space=pltpu.VMEM)
SMEM = pl.BlockSpec(memory_space=pltpu.SMEM)
ANY = pl.BlockSpec(memory_space=pl.ANY)
HBM = pl.BlockSpec(memory_space=pltpu.HBM)


def call(kernel, shapes, scratch=(), flops=10**9, out_specs=None, alias=None):
    moved = sum(4 * functools.reduce(lambda a, b: a * b, s, 1) for s in shapes)
    alias = alias or {}

    def spec(i, a):
        return ANY if i in alias else VMEM if a.dtype == jnp.float32 else SMEM

    def run(*arrays):
        total = moved + sum(a.size * 4 for a in arrays)
        return pl.pallas_call(
            kernel,
            out_shape=[jax.ShapeDtypeStruct(s, jnp.float32) for s in shapes],
            in_specs=[spec(i, a) for i, a in enumerate(arrays)],
            out_specs=out_specs or [VMEM] * len(shapes),
            scratch_shapes=list(scratch),
            input_output_aliases=alias,
            compiler_params=pltpu.CompilerParams(vmem_limit_bytes=12 * 2**20),
            cost_estimate=pl.CostEstimate(flops=flops, bytes_accessed=total, transcendentals=0),
        )(*arrays)

    return run


def buffer(*shape):
    return pltpu.VMEM(shape, jnp.float32)


def iota(dim):
    return lax.broadcasted_iota(jnp.int32, (16, 128), dim)


def matvec(matrix, vector):
    n = len(vector)
    out = []
    for r in range(n):
        acc = matrix[r][0] * vector[0]
        for c in range(1, n):
            acc = acc + matrix[r][c] * vector[c]
        out.append(acc)
    return out


def block(ref, *lead):
    return [[ref[(*lead, r, c)] for c in range(5)] for r in range(5)]


def cell(ref, *lead):
    return [ref[(*lead, v)] for v in range(5)]


def put(ref, values, *lead):
    for v, value in enumerate(values):
        ref[(*lead, v)] = value


def add(a, b):
    return [x + y for x, y in zip(a, b)]


def pack_faces(load, planes, tile_ref):
    lane = iota(1)
    tile = jnp.zeros((16, 128), jnp.float32)
    for j in range(planes):
        for v in range(5):
            q = 2 * (j * 5 + v)
            here = (lane == q) | (lane == (q - 1) % 128)
            x = load(j, v)
            tile = jnp.where(here, pltpu.roll(x, q, 1) if q else x, tile)
    for w in range(tile_ref.shape[0]):
        tile_ref[w] = tile


def live_rows(depth_ref):
    return iota(0) < depth_ref[lax.axis_index("zone")]


def masked(live, values):
    return [jnp.where(live, x, 0.0) for x in values]


def pack_kernel(flow_ref, tile_ref, first_ref):
    put(first_ref, cell(flow_ref, 0))
    pack_faces(lambda j, v: flow_ref[j, v], flow_ref.shape[0], tile_ref)


def neighbours(x):
    lane, row = iota(1), iota(0)
    total = jnp.where(lane == 0, 0.0, pltpu.roll(x, 1, 1))
    total = total + jnp.where(lane == 127, 0.0, pltpu.roll(x, 127, 1))
    total = total + jnp.where(row == 0, 0.0, pltpu.roll(x, 1, 0))
    return total + jnp.where(row == 15, 0.0, pltpu.roll(x, 15, 0))


def ghosts_of(depth_ref, east_ref, tiles_ref):
    zone = lax.axis_index("zone")
    east = east_ref[zone]
    west = jnp.int32(0)
    for w in range(tiles_ref.shape[0]):
        west = west + jnp.where(east_ref[w] == zone, w, 0)
    row = iota(0)
    low = jnp.where(row < depth_ref[west], tiles_ref[west], 0.0)
    high = jnp.where(row < depth_ref[east], tiles_ref[east], 0.0)
    return jnp.where(iota(1) % 2 == 0, pltpu.roll(low, 1, 1), pltpu.roll(high, 127, 1))


def ghost_at(ghosts, j, v):
    lane = iota(1)
    q = 2 * (j * 5 + v)
    turned = pltpu.roll(ghosts, 128 - q, 1) if q else ghosts
    return jnp.where((lane == 0) | (lane == 127), turned, 0.0)


def matrix_kernel(inv_ref, low_ref, up_ref, e_ref, f_ref, mats_ref, y_ref):
    planes = inv_ref.shape[0]
    last = planes - 1
    halves = [pl.ds(0, 8), pl.ds(8, 8)]

    def col(ref, q, j, rows):
        return [ref[j, r, q, rows] for r in range(5)]

    def put_col(ref, values, q, j, rows):
        for r in range(5):
            ref[j, r, q, rows] = values[r]

    def mat(ref, j, rows):
        return [[ref[j, r, c, rows] for c in range(5)] for r in range(5)]

    def products(j, rows):
        inv = mat(inv_ref, j, rows)
        for jac_ref, out_ref in ((low_ref, e_ref), (up_ref, f_ref)):
            for q in range(5):
                product = matvec(inv, col(jac_ref, q, j, rows))
                put_col(out_ref, [OMEGA * x for x in product], q, j, rows)

    def forward(j, carry):
        for rows in halves:
            products(j, rows)
            e = mat(e_ref, j, rows)
            for q in range(5):
                put_col(y_ref, matvec(e, col(y_ref, q, j - 1, rows)), q, j, rows)
        return carry

    for rows in halves:
        products(0, rows)
        for q in range(5):
            put_col(y_ref, col(e_ref, q, 0, rows), q, 0, rows)
    lax.fori_loop(1, planes, forward, 0)
    for rows in halves:
        for q in range(5):
            put_col(mats_ref, col(y_ref, q, last, rows), q, 0, rows)
            put_col(mats_ref, col(y_ref, q, last, rows), q, 1, rows)
            put_col(mats_ref, col(f_ref, q, last, rows), q, 2, rows)

    def backward(step, carry):
        j = planes - 2 - step
        for rows in halves:
            f = mat(f_ref, j, rows)
            for q in range(5):
                turned = matvec(f, col(mats_ref, q, 1, rows))
                put_col(mats_ref, add(col(y_ref, q, j, rows), turned), q, 1, rows)
                put_col(mats_ref, matvec(f, col(mats_ref, q, 2, rows)), q, 2, rows)
        return carry

    lax.fori_loop(0, planes - 1, backward, 0)


def by_place(mine_refs, other_refs, run):
    odd = lax.axis_index("ja") % 2

    @pl.when(odd == 0)
    def _():
        run(*mine_refs, *other_refs)

    @pl.when(odd == 1)
    def _():
        run(*other_refs, *mine_refs)


def beta_kernel(mine_ref, other_ref, beta_ref):
    def run(lo, hi):
        d_hi, n_lo = block(hi, 1), block(lo, 2)
        for q in range(5):
            m_col = [lo[0, r, q] for r in range(5)]
            d_col = [lo[1, r, q] for r in range(5)]
            out = add(d_col, matvec(n_lo, matvec(d_hi, m_col)))
            for r in range(5):
                beta_ref[r, q] = out[r]

    by_place([mine_ref], [other_ref], run)


def sweeps(s_ref, e_ref, f_ref, y_ref, ends_ref, last):
    planes = s_ref.shape[0]
    value = cell(s_ref, 0)
    put(y_ref, value, 0)
    for j in range(1, planes):
        value = add(cell(s_ref, j), matvec(block(e_ref, j), value))
        put(y_ref, value, j)
    put(ends_ref, [x + z * (1.0 / OMEGA) for x, z in zip(value, last)], 0)
    for j in range(planes - 2, -1, -1):
        value = add(cell(y_ref, j), matvec(block(f_ref, j), value))
    put(ends_ref, value, 1)


def local_kernel(
    depth_ref, east_ref, tiles_ref, cur_ref, above_ref, force_ref, diag_ref, inv_ref,
    e_ref, f_ref, mats_ref,
    s_ref, ends_ref, mats_out_ref, y_ref,
):
    del mats_ref, mats_out_ref
    planes = cur_ref.shape[0]
    live = live_rows(depth_ref)
    ghosts = ghosts_of(depth_ref, east_ref, tiles_ref)
    before, here = None, masked(live, cell(cur_ref, 0))
    for j in range(planes):
        after = masked(live, cell(cur_ref, j + 1) if j < planes - 1 else cell(above_ref))
        own = matvec(block(diag_ref, j), here)
        res = []
        for v in range(5):
            sides = neighbours(here[v]) + ghost_at(ghosts, j, v)
            res.append(force_ref[j, v] - own[v] + COUPLE * sides)
        linked = matvec(block(f_ref, j), after)
        if before is not None:
            linked = add(linked, matvec(block(e_ref, j), before))
        linked = [x * (1.0 / OMEGA) for x in linked]
        put(s_ref, add(matvec(block(inv_ref, j), masked(live, res)), linked), j)
        before, here = here, after
    sweeps(s_ref, e_ref, f_ref, y_ref, ends_ref, before)


def residual_kernel(
    depth_ref, cur_ref, above_ref, force_ref, diag_ref, low_ref, up_ref, inv_ref,
    res_ref, s_ref, low0_ref,
):
    planes = cur_ref.shape[0]
    live = live_rows(depth_ref)
    for r in range(5):
        put(low0_ref, cell(low_ref, 0, r), r)
    for j in range(planes):
        here = cell(cur_ref, j)
        applied = matvec(block(diag_ref, j), here)
        if j > 0:
            lower = matvec(block(low_ref, j), cell(cur_ref, j - 1))
            applied = [x - z for x, z in zip(applied, lower)]
        above = cell(cur_ref, j + 1) if j < planes - 1 else cell(above_ref)
        upper = matvec(block(up_ref, j), above)
        res = []
        for v in range(5):
            all_of = applied[v] - upper[v] - COUPLE * neighbours(here[v])
            res.append(jnp.where(live, force_ref[j, v] - all_of, 0.0))
        put(res_ref, res, j)
        put(s_ref, matvec(block(inv_ref, j), res), j)


def ghost_kernel(
    depth_ref, east_ref, tiles_ref, cur_ref, res0_ref, s0_ref, inv_ref, e_ref, f_ref,
    res_ref, s_ref, ends_ref, y_ref,
):
    planes = cur_ref.shape[0]
    live = live_rows(depth_ref)
    ghosts = jnp.where(live, COUPLE * ghosts_of(depth_ref, east_ref, tiles_ref), 0.0)
    for j in range(planes):
        extra = [ghost_at(ghosts, j, v) for v in range(5)]
        put(res_ref, add(cell(res0_ref, j), extra), j)
        put(s_ref, add(cell(s0_ref, j), matvec(block(inv_ref, j), extra)), j)
    last = cell(cur_ref, planes - 1)
    sweeps(s_ref, e_ref, f_ref, y_ref, ends_ref, last)
    put(ends_ref, last, 2)


def write_kernel(res_ref, edge_ref, res_hbm, edge_out_ref, sem):
    copy = pltpu.make_async_copy(res_ref, res_hbm, sem)
    copy.start()
    put(edge_out_ref, cell(edge_ref))
    copy.wait()


def mid_kernel(ends_ref, ends_other_ref, mats_ref, mats_other_ref, out_ref, *more):
    def run(ends_lo, mats_lo, ends_hi, mats_hi):
        c_lo = cell(ends_lo, 0)

        @pl.when(lax.axis_index("ja") < 2)
        def _():
            put(out_ref, add(cell(ends_hi, 0), matvec(block(mats_hi, 0), c_lo)))

        @pl.when(lax.axis_index("ja") >= 2)
        def _():
            turned = add(cell(ends_hi, 1), matvec(block(mats_hi, 1), c_lo))
            put(out_ref, add(cell(ends_lo, 1), matvec(block(mats_lo, 2), turned)))

        if more:
            put(more[0], cell(ends_hi, 2))

    by_place([ends_ref, mats_ref], [ends_other_ref, mats_other_ref], run)


def inflows(
    ends_ref, ends_other_ref, mats_ref, mats_other_ref, pair_ref, pair_other_ref, beta_ref,
    inflow_ref,
):
    ja = lax.axis_index("ja")
    zeros = [jnp.zeros((16, 128), jnp.float32)] * 5

    def far(a, alpha):
        return add(cell(alpha), matvec(block(beta_ref), cell(a)))

    @pl.when(ja == 0)
    def _():
        put(inflow_ref, zeros, 0)
        b = add(cell(ends_other_ref, 1), matvec(block(mats_other_ref, 1), cell(ends_ref, 0)))
        b = add(b, matvec(block(mats_other_ref, 2), far(pair_ref, pair_other_ref)))
        put(inflow_ref, b, 1)

    @pl.when(ja == 1)
    def _():
        put(inflow_ref, cell(ends_other_ref, 0), 0)
        put(inflow_ref, far(pair_ref, pair_other_ref), 1)

    @pl.when(ja == 2)
    def _():
        a = cell(pair_other_ref)
        put(inflow_ref, a, 0)
        a = add(cell(ends_ref, 0), matvec(block(mats_ref, 0), a))
        b = add(cell(ends_other_ref, 1), matvec(block(mats_other_ref, 1), a))
        put(inflow_ref, b, 1)

    @pl.when(ja == 3)
    def _():
        a = add(cell(ends_other_ref, 0), matvec(block(mats_other_ref, 0), cell(pair_other_ref)))
        put(inflow_ref, a, 0)
        put(inflow_ref, zeros, 1)


def final_kernel(
    depth_ref, cur_ref, above_ref, s_ref, e_ref, f_ref,
    ends_ref, ends_other_ref, mats_ref, mats_other_ref, pair_ref, pair_other_ref, beta_ref,
    new_ref, above_new_ref, tile_ref, y_ref, inflow_ref,
):
    planes = cur_ref.shape[0]
    inflows(
        ends_ref, ends_other_ref, mats_ref, mats_other_ref, pair_ref, pair_other_ref, beta_ref,
        inflow_ref,
    )
    value = cell(inflow_ref, 0)
    for j in range(planes):
        value = add(cell(s_ref, j), matvec(block(e_ref, j), value))
        put(y_ref, value, j)
    value = cell(inflow_ref, 1)
    live = live_rows(depth_ref)
    put(above_new_ref, add(masked(live, cell(above_ref)), value))
    for j in range(planes - 1, -1, -1):
        value = add(cell(y_ref, j), matvec(block(f_ref, j), value))
        put(new_ref, add(masked(live, cell(cur_ref, j)), value), j)
    pack_faces(lambda j, v: new_ref[j, v], planes, tile_ref)


def last_kernel(
    depth_ref, low0_ref, edge_ref, cur_ref, res_ref, s_ref, e_ref, f_ref,
    ends_ref, ends_other_ref, mats_ref, mats_other_ref, pair_ref, pair_other_ref, beta_ref,
    res_in_hbm,
    new_hbm, res_hbm, y_ref, inflow_ref, new_ref, res0_ref, sems,
):
    del res_in_hbm
    planes = cur_ref.shape[0]
    ja = lax.axis_index("ja")
    live = live_rows(depth_ref)
    before = [
        jnp.where(ja == 0, 0.0, jnp.where(ja == 2, edge_ref[v], ends_other_ref[2, v]))
        for v in range(5)
    ]
    put(res0_ref, add(cell(res_ref, 0), masked(live, matvec(block(low0_ref), before))))
    copies = [pltpu.make_async_copy(res0_ref, res_hbm.at[0], sems.at[planes])]
    copies[0].start()
    inflows(
        ends_ref, ends_other_ref, mats_ref, mats_other_ref, pair_ref, pair_other_ref, beta_ref,
        inflow_ref,
    )
    value = cell(inflow_ref, 0)
    for j in range(planes):
        value = add(cell(s_ref, j), matvec(block(e_ref, j), value))
        put(y_ref, value, j)
    value = cell(inflow_ref, 1)
    for j in range(planes - 1, -1, -1):
        value = add(cell(y_ref, j), matvec(block(f_ref, j), value))
        put(new_ref, add(cell(cur_ref, j), value), j)
        copies.append(pltpu.make_async_copy(new_ref.at[j], new_hbm.at[j], sems.at[j]))
        copies[-1].start()
    for copy in copies:
        copy.wait()


def per_device(
    flow_state, forcing, diag_block, lower_jac, upper_jac, block_inv, east_zone, zone_depth
):
    zones, parts = lax.axis_size("zone"), lax.axis_size("ja")
    assert parts == 4 and ITERS == 2
    current, force, diag, low, up, inv = (
        x[0] for x in (flow_state, forcing, diag_block, lower_jac, upper_jac, block_inv)
    )
    state = current.shape
    planes, plane, blocks, tiles = state[0], state[1:], diag.shape, (zones, *state[2:])
    matrix = blocks[1:]
    work = [buffer(*state)]

    def swap(x, bit):
        return lax.ppermute(x, "ja", [(p, p ^ bit) for p in range(parts)])

    def faces(x):
        return lax.all_to_all(x, "zone", 0, 0, tiled=True)

    tile, first = call(pack_kernel, [tiles, plane], flops=2 * 10**10)(current)
    got = faces(tile)
    above = lax.ppermute(first, "ja", [(p + 1, p) for p in range(parts - 1)])
    e, f, mats = call(
        matrix_kernel, [blocks, blocks, (3, *matrix)], [buffer(*blocks)], flops=5 * 10**9
    )(inv, low, up)
    s, ends, mats = call(
        local_kernel,
        [state, (2, *plane), (3, *matrix)],
        work,
        out_specs=[VMEM, VMEM, ANY],
        alias={10: 2},
    )(zone_depth, east_zone, got, current, above, force, diag, inv, e, f, mats)
    ends_other = swap(ends, 1)
    mats_other = swap(mats, 1)
    beta = call(beta_kernel, [matrix])(mats, mats_other)[0]
    beta = lax.ppermute(beta, "ja", [(2, 0), (3, 1)])
    pair = call(mid_kernel, [plane])(ends, ends_other, mats, mats_other)[0]
    pair_other = swap(pair, 2)
    flows = [buffer(2, *plane)]
    current, above, tile = call(final_kernel, [state, plane, tiles], work + flows)(
        zone_depth, current, above, s, e, f,
        ends, ends_other, mats, mats_other, pair, pair_other, beta,
    )

    got = faces(tile)
    residual, s, low0 = call(residual_kernel, [state, state, matrix], flops=2 * 10**9)(
        zone_depth, current, above, force, diag, low, up, inv
    )
    residual, s, ends = call(ghost_kernel, [state, state, (3, *plane)], work)(
        zone_depth, east_zone, got, current, residual, s, inv, e, f
    )
    ends_other = swap(ends, 1)
    pair, edge = call(mid_kernel, [plane, plane])(ends, ends_other, mats, mats_other)
    pair_other = swap(pair, 2)
    written, edge = call(
        write_kernel, [state, plane], [pltpu.SemaphoreType.DMA], out_specs=[HBM, VMEM]
    )(residual, edge)
    edge = lax.ppermute(edge, "ja", [(1, 2)])
    current, residual = call(
        last_kernel,
        [state, state],
        work + flows + work + [buffer(*plane), pltpu.SemaphoreType.DMA((planes + 1,))],
        out_specs=[HBM, HBM],
        alias={15: 1},
    )(
        zone_depth, low0, edge, current, residual, s, e, f,
        ends, ends_other, mats, mats_other, pair, pair_other, beta, written,
    )
    return (current[None], residual[None])


def solution(mesh):
    state = P("zone", "ja", None, None, None)
    blocks = P("zone", "ja", None, None, None, None)
    return jax.shard_map(
        per_device,
        mesh=mesh,
        in_specs=(state, state, blocks, blocks, blocks, blocks, P(), P()),
        out_specs=(state, state),
        check_vma=False,
    )
```

```python
import functools

import jax
import jax.numpy as jnp
from jax import lax
from jax.experimental import pallas as pl
from jax.experimental.pallas import tpu as pltpu
from jax.sharding import PartitionSpec as P

ITERS = 2
OMEGA = 1.2
COUPLE = 0.25

VMEM = pl.BlockSpec(memory_space=pltpu.VMEM)
SMEM = pl.BlockSpec(memory_space=pltpu.SMEM)
ANY = pl.BlockSpec(memory_space=pl.ANY)
HBM = pl.BlockSpec(memory_space=pltpu.HBM)


def call(kernel, shapes, scratch=(), flops=10**9, out_specs=None, alias=None):
    moved = sum(4 * functools.reduce(lambda a, b: a * b, s, 1) for s in shapes)
    alias = alias or {}

    def spec(i, a):
        return ANY if i in alias else VMEM if a.dtype == jnp.float32 else SMEM

    def run(*arrays):
        total = moved + sum(a.size * 4 for a in arrays)
        return pl.pallas_call(
            kernel,
            out_shape=[jax.ShapeDtypeStruct(s, jnp.float32) for s in shapes],
            in_specs=[spec(i, a) for i, a in enumerate(arrays)],
            out_specs=out_specs or [VMEM] * len(shapes),
            scratch_shapes=list(scratch),
            input_output_aliases=alias,
            compiler_params=pltpu.CompilerParams(vmem_limit_bytes=12 * 2**20),
            cost_estimate=pl.CostEstimate(flops=flops, bytes_accessed=total, transcendentals=0),
        )(*arrays)

    return run


def buffer(*shape):
    return pltpu.VMEM(shape, jnp.float32)


def iota(dim):
    return lax.broadcasted_iota(jnp.int32, (16, 128), dim)


def matvec(matrix, vector):
    n = len(vector)
    out = []
    for r in range(n):
        acc = matrix[r][0] * vector[0]
        for c in range(1, n):
            acc = acc + matrix[r][c] * vector[c]
        out.append(acc)
    return out


def block(ref, *lead):
    return [[ref[(*lead, r, c)] for c in range(5)] for r in range(5)]


def cell(ref, *lead):
    return [ref[(*lead, v)] for v in range(5)]


def put(ref, values, *lead):
    for v, value in enumerate(values):
        ref[(*lead, v)] = value


def add(a, b):
    return [x + y for x, y in zip(a, b)]


def pack_faces(load, planes, tile_ref):
    lane = iota(1)
    tile = jnp.zeros((16, 128), jnp.float32)
    for j in range(planes):
        for v in range(5):
            q = 2 * (j * 5 + v)
            here = (lane == q) | (lane == (q - 1) % 128)
            x = load(j, v)
            tile = jnp.where(here, pltpu.roll(x, q, 1) if q else x, tile)
    for w in range(tile_ref.shape[0]):
        tile_ref[w] = tile


def live_rows(depth_ref):
    return iota(0) < depth_ref[lax.axis_index("zone")]


def masked(live, values):
    return [jnp.where(live, x, 0.0) for x in values]


def pack_kernel(flow_ref, tile_ref, first_ref):
    put(first_ref, cell(flow_ref, 0))
    pack_faces(lambda j, v: flow_ref[j, v], flow_ref.shape[0], tile_ref)


def neighbours(x):
    lane, row = iota(1), iota(0)
    total = jnp.where(lane == 0, 0.0, pltpu.roll(x, 1, 1))
    total = total + jnp.where(lane == 127, 0.0, pltpu.roll(x, 127, 1))
    total = total + jnp.where(row == 0, 0.0, pltpu.roll(x, 1, 0))
    return total + jnp.where(row == 15, 0.0, pltpu.roll(x, 15, 0))


def ghosts_of(depth_ref, east_ref, tiles_ref):
    zone = lax.axis_index("zone")
    east = east_ref[zone]
    west = jnp.int32(0)
    for w in range(tiles_ref.shape[0]):
        west = west + jnp.where(east_ref[w] == zone, w, 0)
    row = iota(0)
    low = jnp.where(row < depth_ref[west], tiles_ref[west], 0.0)
    high = jnp.where(row < depth_ref[east], tiles_ref[east], 0.0)
    return jnp.where(iota(1) % 2 == 0, pltpu.roll(low, 1, 1), pltpu.roll(high, 127, 1))


def ghost_at(ghosts, j, v):
    lane = iota(1)
    q = 2 * (j * 5 + v)
    turned = pltpu.roll(ghosts, 128 - q, 1) if q else ghosts
    return jnp.where((lane == 0) | (lane == 127), turned, 0.0)


def matrix_kernel(tiles_ref, inv_ref, low_ref, up_ref, e_ref, f_ref, mats_ref, y_ref):
    del tiles_ref
    planes = inv_ref.shape[0]
    last = planes - 1
    halves = [pl.ds(0, 8), pl.ds(8, 8)]

    def col(ref, q, j, rows):
        return [ref[j, r, q, rows] for r in range(5)]

    def put_col(ref, values, q, j, rows):
        for r in range(5):
            ref[j, r, q, rows] = values[r]

    def mat(ref, j, rows):
        return [[ref[j, r, c, rows] for c in range(5)] for r in range(5)]

    def products(j, rows):
        inv = mat(inv_ref, j, rows)
        for jac_ref, out_ref in ((low_ref, e_ref), (up_ref, f_ref)):
            for q in range(5):
                product = matvec(inv, col(jac_ref, q, j, rows))
                put_col(out_ref, [OMEGA * x for x in product], q, j, rows)

    def forward(j, carry):
        for rows in halves:
            products(j, rows)
            e = mat(e_ref, j, rows)
            for q in range(5):
                put_col(y_ref, matvec(e, col(y_ref, q, j - 1, rows)), q, j, rows)
        return carry

    for rows in halves:
        products(0, rows)
        for q in range(5):
            put_col(y_ref, col(e_ref, q, 0, rows), q, 0, rows)
    lax.fori_loop(1, planes, forward, 0)
    for rows in halves:
        for q in range(5):
            put_col(mats_ref, col(y_ref, q, last, rows), q, 0, rows)
            put_col(mats_ref, col(y_ref, q, last, rows), q, 1, rows)
            put_col(mats_ref, col(f_ref, q, last, rows), q, 2, rows)

    def backward(step, carry):
        j = planes - 2 - step
        for rows in halves:
            f = mat(f_ref, j, rows)
            for q in range(5):
                turned = matvec(f, col(mats_ref, q, 1, rows))
                put_col(mats_ref, add(col(y_ref, q, j, rows), turned), q, 1, rows)
                put_col(mats_ref, matvec(f, col(mats_ref, q, 2, rows)), q, 2, rows)
        return carry

    lax.fori_loop(0, planes - 1, backward, 0)


def by_place(mine_refs, other_refs, run):
    odd = lax.axis_index("ja") % 2

    @pl.when(odd == 0)
    def _():
        run(*mine_refs, *other_refs)

    @pl.when(odd == 1)
    def _():
        run(*other_refs, *mine_refs)


def beta_kernel(mine_ref, other_ref, half_ref):
    def run(lo, hi):
        def part(ref, *at):
            return ref[at][rows]

        d_hi = [[part(hi, 1, r, c) for c in range(5)] for r in range(5)]
        n_lo = [[part(lo, 2, r, c) for c in range(5)] for r in range(5)]
        for q in range(5):
            m_col = [part(lo, 0, r, q) for r in range(5)]
            d_col = [part(lo, 1, r, q) for r in range(5)]
            out = add(d_col, matvec(n_lo, matvec(d_hi, m_col)))
            for r in range(5):
                half_ref[r, q] = out[r]

    odd = lax.axis_index("ja") % 2
    for side in range(2):
        rows = slice(8 * side, 8 * side + 8)
        pair = (mine_ref, other_ref) if side == 0 else (other_ref, mine_ref)
        pl.when(odd == side)(functools.partial(run, *pair))


def relay_kernel(half_ref, pair_ref, out_ref):
    del pair_ref
    for r in range(5):
        put(out_ref, cell(half_ref, r), r)


def sweeps(s_ref, e_ref, f_ref, y_ref, ends_ref, last):
    planes = s_ref.shape[0]
    value = cell(s_ref, 0)
    put(y_ref, value, 0)
    for j in range(1, planes):
        value = add(cell(s_ref, j), matvec(block(e_ref, j), value))
        put(y_ref, value, j)
    put(ends_ref, [x + z * (1.0 / OMEGA) for x, z in zip(value, last)], 0)
    for j in range(planes - 2, -1, -1):
        value = add(cell(y_ref, j), matvec(block(f_ref, j), value))
    put(ends_ref, value, 1)


def local_kernel(
    depth_ref, east_ref, tiles_ref, cur_ref, above_ref, force_ref, diag_ref, inv_ref,
    e_ref, f_ref,
    s_ref, ends_ref, y_ref,
):
    planes = cur_ref.shape[0]
    live = live_rows(depth_ref)
    ghosts = ghosts_of(depth_ref, east_ref, tiles_ref)
    before, here = None, masked(live, cell(cur_ref, 0))
    for j in range(planes):
        after = masked(live, cell(cur_ref, j + 1) if j < planes - 1 else cell(above_ref))
        own = matvec(block(diag_ref, j), here)
        res = []
        for v in range(5):
            sides = neighbours(here[v]) + ghost_at(ghosts, j, v)
            res.append(force_ref[j, v] - own[v] + COUPLE * sides)
        linked = matvec(block(f_ref, j), after)
        if before is not None:
            linked = add(linked, matvec(block(e_ref, j), before))
        linked = [x * (1.0 / OMEGA) for x in linked]
        put(s_ref, add(matvec(block(inv_ref, j), masked(live, res)), linked), j)
        before, here = here, after
    sweeps(s_ref, e_ref, f_ref, y_ref, ends_ref, before)


def second_kernel(
    depth_ref, east_ref, tiles_ref, cur_ref, above_ref, force_ref, diag_ref, low_ref, up_ref,
    inv_ref, e_ref, f_ref,
    res_ref, s_ref, ends_ref, low0_ref, y_ref,
):
    planes = cur_ref.shape[0]
    live = live_rows(depth_ref)
    ghosts = ghosts_of(depth_ref, east_ref, tiles_ref)
    for r in range(5):
        put(low0_ref, cell(low_ref, 0, r), r)
    for j in range(planes):
        here = cell(cur_ref, j)
        applied = matvec(block(diag_ref, j), here)
        if j > 0:
            lower = matvec(block(low_ref, j), cell(cur_ref, j - 1))
            applied = [x - z for x, z in zip(applied, lower)]
        above = cell(cur_ref, j + 1) if j < planes - 1 else cell(above_ref)
        upper = matvec(block(up_ref, j), above)
        res = []
        for v in range(5):
            sides = neighbours(here[v]) + ghost_at(ghosts, j, v)
            all_of = applied[v] - upper[v] - COUPLE * sides
            res.append(jnp.where(live, force_ref[j, v] - all_of, 0.0))
        put(res_ref, res, j)
        put(s_ref, matvec(block(inv_ref, j), res), j)
    last = cell(cur_ref, planes - 1)
    sweeps(s_ref, e_ref, f_ref, y_ref, ends_ref, last)
    put(ends_ref, last, 2)


def write_kernel(res_ref, res_hbm, sem):
    copy = pltpu.make_async_copy(res_ref, res_hbm, sem)
    copy.start()
    copy.wait()


def mid_kernel(ends_ref, ends_other_ref, mats_ref, mats_other_ref, out_ref):
    def run(ends_lo, mats_lo, ends_hi, mats_hi):
        c_lo = cell(ends_lo, 0)

        @pl.when(lax.axis_index("ja") < 2)
        def _():
            put(out_ref, add(cell(ends_hi, 0), matvec(block(mats_hi, 0), c_lo)), 0)

        @pl.when(lax.axis_index("ja") >= 2)
        def _():
            turned = add(cell(ends_hi, 1), matvec(block(mats_hi, 1), c_lo))
            put(out_ref, add(cell(ends_lo, 1), matvec(block(mats_lo, 2), turned)), 0)

        if out_ref.shape[0] > 1:
            put(out_ref, cell(ends_hi, 2), 1)

    by_place([ends_ref, mats_ref], [ends_other_ref, mats_other_ref], run)


def inflows(
    ends_ref, ends_other_ref, mats_ref, mats_other_ref, pair_ref, pair_other_ref,
    half_ref, half_other_ref, inflow_ref,
):
    ja = lax.axis_index("ja")
    zeros = [jnp.zeros((16, 128), jnp.float32)] * 5

    def far(top_ref, bottom_ref):
        beta = [
            [jnp.concatenate([top_ref[r, c], bottom_ref[r, c]], axis=0) for c in range(5)]
            for r in range(5)
        ]
        return add(cell(pair_other_ref, 0), matvec(beta, cell(pair_ref, 0)))

    @pl.when(ja == 0)
    def _():
        put(inflow_ref, zeros, 0)
        b = add(cell(ends_other_ref, 1), matvec(block(mats_other_ref, 1), cell(ends_ref, 0)))
        b = add(b, matvec(block(mats_other_ref, 2), far(half_ref, half_other_ref)))
        put(inflow_ref, b, 1)

    @pl.when(ja == 1)
    def _():
        put(inflow_ref, cell(ends_other_ref, 0), 0)
        put(inflow_ref, far(half_other_ref, half_ref), 1)

    @pl.when(ja == 2)
    def _():
        a = cell(pair_other_ref, 0)
        put(inflow_ref, a, 0)
        a = add(cell(ends_ref, 0), matvec(block(mats_ref, 0), a))
        b = add(cell(ends_other_ref, 1), matvec(block(mats_other_ref, 1), a))
        put(inflow_ref, b, 1)

    @pl.when(ja == 3)
    def _():
        a = add(cell(ends_other_ref, 0), matvec(block(mats_other_ref, 0), cell(pair_other_ref, 0)))
        put(inflow_ref, a, 0)
        put(inflow_ref, zeros, 1)


def final_kernel(
    depth_ref, cur_ref, above_ref, s_ref, e_ref, f_ref,
    ends_ref, ends_other_ref, mats_ref, mats_other_ref, pair_ref, pair_other_ref,
    half_ref, half_other_ref,
    new_ref, above_new_ref, tile_ref, y_ref, inflow_ref,
):
    planes = cur_ref.shape[0]
    inflows(
        ends_ref, ends_other_ref, mats_ref, mats_other_ref, pair_ref, pair_other_ref,
        half_ref, half_other_ref, inflow_ref,
    )
    value = cell(inflow_ref, 0)
    for j in range(planes):
        value = add(cell(s_ref, j), matvec(block(e_ref, j), value))
        put(y_ref, value, j)
    value = cell(inflow_ref, 1)
    live = live_rows(depth_ref)
    put(above_new_ref, add(masked(live, cell(above_ref)), value))
    for j in range(planes - 1, -1, -1):
        value = add(cell(y_ref, j), matvec(block(f_ref, j), value))
        put(new_ref, add(masked(live, cell(cur_ref, j)), value), j)
    pack_faces(lambda j, v: new_ref[j, v], planes, tile_ref)


def last_kernel(
    depth_ref, low0_ref, cur_ref, res_ref, s_ref, e_ref, f_ref,
    ends_ref, ends_other_ref, mats_ref, mats_other_ref, pair_ref, pair_other_ref,
    half_ref, half_other_ref,
    res_in_hbm,
    new_hbm, res_hbm, y_ref, inflow_ref, new_ref, res0_ref, sems,
):
    del res_in_hbm
    planes = cur_ref.shape[0]
    ja = lax.axis_index("ja")
    live = live_rows(depth_ref)
    before = [
        jnp.where(ja == 0, 0.0, jnp.where(ja == 2, pair_other_ref[1, v], ends_other_ref[2, v]))
        for v in range(5)
    ]
    put(res0_ref, add(cell(res_ref, 0), masked(live, matvec(block(low0_ref), before))))
    copies = [pltpu.make_async_copy(res0_ref, res_hbm.at[0], sems.at[planes])]
    copies[0].start()
    inflows(
        ends_ref, ends_other_ref, mats_ref, mats_other_ref, pair_ref, pair_other_ref,
        half_ref, half_other_ref, inflow_ref,
    )
    value = cell(inflow_ref, 0)
    for j in range(planes):
        value = add(cell(s_ref, j), matvec(block(e_ref, j), value))
        put(y_ref, value, j)
    value = cell(inflow_ref, 1)
    for j in range(planes - 1, -1, -1):
        value = add(cell(y_ref, j), matvec(block(f_ref, j), value))
        put(new_ref, add(cell(cur_ref, j), value), j)
        copies.append(pltpu.make_async_copy(new_ref.at[j], new_hbm.at[j], sems.at[j]))
        copies[-1].start()
    for copy in copies:
        copy.wait()


def per_device(
    flow_state, forcing, diag_block, lower_jac, upper_jac, block_inv, east_zone, zone_depth
):
    zones, parts = lax.axis_size("zone"), lax.axis_size("ja")
    assert parts == 4 and ITERS == 2
    current, force, diag, low, up, inv = (
        x[0] for x in (flow_state, forcing, diag_block, lower_jac, upper_jac, block_inv)
    )
    state = current.shape
    planes, plane, blocks, tiles = state[0], state[1:], diag.shape, (zones, *state[2:])
    matrix = blocks[1:]
    work = [buffer(*state)]

    def swap(x, bit):
        return lax.ppermute(x, "ja", [(p, p ^ bit) for p in range(parts)])

    def faces(x):
        return lax.all_to_all(x, "zone", 0, 0, tiled=True)

    tile, first = call(pack_kernel, [tiles, plane], flops=2 * 10**10)(current)
    above = lax.ppermute(first, "ja", [(p + 1, p) for p in range(parts - 1)])
    got = faces(tile)
    e, f, mats = call(
        matrix_kernel, [blocks, blocks, (3, *matrix)], [buffer(*blocks)], flops=5 * 10**9
    )(got, inv, low, up)
    mats_other = swap(mats, 1)
    s, ends = call(local_kernel, [state, (2, *plane)], work)(
        zone_depth, east_zone, got, current, above, force, diag, inv, e, f
    )
    ends_other = swap(ends, 1)
    half = call(beta_kernel, [(*matrix[:2], 8, matrix[3])])(mats, mats_other)[0]
    half = lax.ppermute(half, "ja", [(2, 0), (3, 1)])
    pair = call(mid_kernel, [(1, *plane)])(ends, ends_other, mats, mats_other)[0]
    pair_other = swap(pair, 2)
    half_sent = call(relay_kernel, [half.shape])(half, pair)[0]
    half_other = lax.ppermute(half_sent, "ja", [(0, 1), (1, 0)])
    flows = [buffer(2, *plane)]
    current, above, tile = call(final_kernel, [state, plane, tiles], work + flows)(
        zone_depth, current, above, s, e, f,
        ends, ends_other, mats, mats_other, pair, pair_other, half, half_other,
    )

    got = faces(tile)
    residual, s, ends, low0 = call(
        second_kernel, [state, state, (3, *plane), matrix], work
    )(
        zone_depth, east_zone, got, current, above, force, diag, low, up, inv, e, f
    )
    ends_other = swap(ends, 1)
    pair = call(mid_kernel, [(2, *plane)])(ends, ends_other, mats, mats_other)[0]
    pair_other = swap(pair, 2)
    written = call(write_kernel, [state], [pltpu.SemaphoreType.DMA], out_specs=[HBM])(residual)[0]
    current, residual = call(
        last_kernel,
        [state, state],
        work + flows + work + [buffer(*plane), pltpu.SemaphoreType.DMA((planes + 1,))],
        out_specs=[HBM, HBM],
        alias={15: 1},
    )(
        zone_depth, low0, current, residual, s, e, f,
        ends, ends_other, mats, mats_other, pair, pair_other, half, half_other, written,
    )
    return (current[None], residual[None])


def solution(mesh):
    state = P("zone", "ja", None, None, None)
    blocks = P("zone", "ja", None, None, None, None)
    return jax.shard_map(
        per_device,
        mesh=mesh,
        in_specs=(state, state, blocks, blocks, blocks, blocks, P(), P()),
        out_specs=(state, state),
        check_vma=False,
    )
```

```python
import jax
import jax.numpy as jnp
from jax import lax
from jax.experimental import pallas as pl
from jax.experimental.pallas import tpu as pltpu
from jax.sharding import PartitionSpec as P

ITERS = 2
OMEGA = 1.2
COUPLE = 0.25

VMEM = pl.BlockSpec(memory_space=pltpu.VMEM)
ANY = pl.BlockSpec(memory_space=pl.ANY)
HBM = pl.BlockSpec(memory_space=pltpu.HBM)


def call(kernel, shapes, scratch=(), flops=10**9, far=(), out_specs=None, alias=None):
    alias = alias or {}

    def run(*arrays):
        arrays = [
            pltpu.with_memory_space_constraint(a, pltpu.HBM) if i in far else a
            for i, a in enumerate(arrays)
        ]
        return pl.pallas_call(
            kernel,
            out_shape=[jax.ShapeDtypeStruct(s, jnp.float32) for s in shapes],
            in_specs=[
                HBM if i in far else ANY if i in alias else VMEM for i in range(len(arrays))
            ],
            out_specs=out_specs or [VMEM] * len(shapes),
            scratch_shapes=list(scratch),
            input_output_aliases=alias,
            compiler_params=pltpu.CompilerParams(vmem_limit_bytes=12 * 2**20),
            cost_estimate=pl.CostEstimate(flops=flops, bytes_accessed=flops // 10**3, transcendentals=0),
        )(*arrays)

    return run


def buffer(*shape):
    return pltpu.VMEM(shape, jnp.float32)


def iota(dim):
    return lax.broadcasted_iota(jnp.int32, (16, 128), dim)


def matvec(matrix, vector):
    n = len(vector)
    out = []
    for r in range(n):
        acc = matrix[r][0] * vector[0]
        for c in range(1, n):
            acc = acc + matrix[r][c] * vector[c]
        out.append(acc)
    return out


def block(ref, *lead):
    return [[ref[(*lead, r, c)] for c in range(5)] for r in range(5)]


def cell(ref, *lead):
    return [ref[(*lead, v)] for v in range(5)]


def put(ref, values, *lead):
    for v, value in enumerate(values):
        ref[(*lead, v)] = value


def add(a, b):
    return [x + y for x, y in zip(a, b)]


def pack_faces(load, planes, tile_ref):
    lane = iota(1)
    tile = jnp.zeros((16, 128), jnp.float32)
    for j in range(planes):
        for v in range(5):
            q = 2 * (j * 5 + v)
            here = (lane == q) | (lane == (q - 1) % 128)
            x = load(j, v)
            tile = jnp.where(here, pltpu.roll(x, q, 1) if q else x, tile)
    for w in range(tile_ref.shape[0]):
        tile_ref[w] = tile


def masked(live_ref, values):
    live = live_ref[...] > 0.0
    return [jnp.where(live, x, 0.0) for x in values]


def has_above(values):
    inner = lax.axis_index("ja") < lax.axis_size("ja") - 1
    return [jnp.where(inner, x, 0.0) for x in values]


def pack_kernel(mats_ref, flow_ref, tile_ref, first_ref):
    del mats_ref
    put(first_ref, cell(flow_ref, 0))
    pack_faces(lambda j, v: flow_ref[j, v], flow_ref.shape[0], tile_ref)


def neighbours(x):
    lane, row = iota(1), iota(0)
    total = jnp.where(lane == 0, 0.0, pltpu.roll(x, 1, 1))
    total = total + jnp.where(lane == 127, 0.0, pltpu.roll(x, 127, 1))
    total = total + jnp.where(row == 0, 0.0, pltpu.roll(x, 1, 0))
    return total + jnp.where(row == 15, 0.0, pltpu.roll(x, 15, 0))


def ghosts_of(pick_ref, tiles_ref):
    low = high = jnp.zeros((16, 128), jnp.float32)
    for w in range(tiles_ref.shape[0]):
        low = jnp.where(pick_ref[0, w] > 0.0, tiles_ref[w], low)
        high = jnp.where(pick_ref[1, w] > 0.0, tiles_ref[w], high)
    return jnp.where(iota(1) % 2 == 0, pltpu.roll(low, 1, 1), pltpu.roll(high, 127, 1))


def ghost_at(ghosts, j, v):
    lane = iota(1)
    q = 2 * (j * 5 + v)
    turned = pltpu.roll(ghosts, 128 - q, 1) if q else ghosts
    return jnp.where((lane == 0) | (lane == 127), turned, 0.0)


def matrix_kernel(
    depth_hbm, east_hbm, inv_hbm, low_hbm, up_hbm,
    e_ref, f_ref, mats_ref, live_ref, pick_ref,
    inv_ref, low_ref, up_ref, y_ref, depth_ref, east_ref, sems, small_sems,
):
    planes = inv_ref.shape[0]

    def copies(j):
        return [
            pltpu.make_async_copy(src.at[j], dst.at[j], sems.at[i, j])
            for i, (src, dst) in enumerate(
                [(inv_hbm, inv_ref), (low_hbm, low_ref), (up_hbm, up_ref)]
            )
        ]

    for j in range(planes):
        for copy in copies(j):
            copy.start()
    scalars = [
        pltpu.make_async_copy(depth_hbm, depth_ref, small_sems.at[0]),
        pltpu.make_async_copy(east_hbm, east_ref, small_sems.at[1]),
    ]
    for copy in scalars:
        copy.start()
    last = planes - 1
    halves = [pl.ds(0, 8), pl.ds(8, 8)]

    def col(ref, q, j, rows):
        return [ref[j, r, q, rows] for r in range(5)]

    def put_col(ref, values, q, j, rows):
        for r in range(5):
            ref[j, r, q, rows] = values[r]

    def mat(ref, j, rows):
        return [[ref[j, r, c, rows] for c in range(5)] for r in range(5)]

    def products(j, rows):
        inv = mat(inv_ref, j, rows)
        for jac_ref, out_ref in ((low_ref, e_ref), (up_ref, f_ref)):
            for q in range(5):
                product = matvec(inv, col(jac_ref, q, j, rows))
                put_col(out_ref, [OMEGA * x for x in product], q, j, rows)

    def forward(j, carry):
        for copy in copies(j):
            copy.wait()
        for rows in halves:
            products(j, rows)
            e = mat(e_ref, j, rows)
            for q in range(5):
                put_col(y_ref, matvec(e, col(y_ref, q, j - 1, rows)), q, j, rows)
        return carry

    for copy in copies(0):
        copy.wait()
    for rows in halves:
        products(0, rows)
        for q in range(5):
            put_col(y_ref, col(e_ref, q, 0, rows), q, 0, rows)
    lax.fori_loop(1, planes, forward, 0)
    for rows in halves:
        for q in range(5):
            put_col(mats_ref, col(y_ref, q, last, rows), q, 0, rows)
            put_col(mats_ref, col(y_ref, q, last, rows), q, 1, rows)
            put_col(mats_ref, col(f_ref, q, last, rows), q, 2, rows)

    def backward(step, carry):
        j = planes - 2 - step
        for rows in halves:
            f = mat(f_ref, j, rows)
            for q in range(5):
                turned = matvec(f, col(mats_ref, q, 1, rows))
                put_col(mats_ref, add(col(y_ref, q, j, rows), turned), q, 1, rows)
                put_col(mats_ref, matvec(f, col(mats_ref, q, 2, rows)), q, 2, rows)
        return carry

    lax.fori_loop(0, planes - 1, backward, 0)
    for copy in scalars:
        copy.wait()
    zone = lax.axis_index("zone")
    row = iota(0)
    live_ref[...] = jnp.where(row < depth_ref[zone], 1.0, 0.0)
    for w in range(pick_ref.shape[1]):
        rows = row < depth_ref[w]
        pick_ref[0, w] = jnp.where(rows & (east_ref[w] == zone), 1.0, 0.0)
        pick_ref[1, w] = jnp.where(rows & (east_ref[zone] == w), 1.0, 0.0)


def by_place(mine_refs, other_refs, run):
    odd = lax.axis_index("ja") % 2

    @pl.when(odd == 0)
    def _():
        run(*mine_refs, *other_refs)

    @pl.when(odd == 1)
    def _():
        run(*other_refs, *mine_refs)


def beta_kernel(mine_ref, other_ref, beta_ref):
    def run(lo, hi):
        d_hi, n_lo = block(hi, 1), block(lo, 2)
        for q in range(5):
            m_col = [lo[0, r, q] for r in range(5)]
            d_col = [lo[1, r, q] for r in range(5)]
            out = add(d_col, matvec(n_lo, matvec(d_hi, m_col)))
            for r in range(5):
                beta_ref[r, q] = out[r]

    by_place([mine_ref], [other_ref], run)


def sweeps(s_ref, e_ref, f_ref, y_ref, ends_ref, last):
    planes = s_ref.shape[0]
    value = cell(s_ref, 0)
    put(y_ref, value, 0)
    for j in range(1, planes):
        value = add(cell(s_ref, j), matvec(block(e_ref, j), value))
        put(y_ref, value, j)
    put(ends_ref, [x + z * (1.0 / OMEGA) for x, z in zip(value, last)], 0)
    for j in range(planes - 2, -1, -1):
        value = add(cell(y_ref, j), matvec(block(f_ref, j), value))
    put(ends_ref, value, 1)


def local_kernel(
    beta_ref, live_ref, pick_ref, tiles_ref, cur_ref, above_ref, force_ref, diag_ref, inv_ref,
    e_ref, f_ref,
    s_ref, ends_ref, y_ref,
):
    del beta_ref
    planes = cur_ref.shape[0]
    ghosts = ghosts_of(pick_ref, tiles_ref)
    before, here = None, masked(live_ref, cell(cur_ref, 0))
    for j in range(planes):
        after = cell(cur_ref, j + 1) if j < planes - 1 else has_above(cell(above_ref))
        after = masked(live_ref, after)
        own = matvec(block(diag_ref, j), here)
        res = []
        for v in range(5):
            sides = neighbours(here[v]) + ghost_at(ghosts, j, v)
            res.append(force_ref[j, v] - own[v] + COUPLE * sides)
        linked = matvec(block(f_ref, j), after)
        if before is not None:
            linked = add(linked, matvec(block(e_ref, j), before))
        linked = [x * (1.0 / OMEGA) for x in linked]
        put(s_ref, add(matvec(block(inv_ref, j), masked(live_ref, res)), linked), j)
        before, here = here, after
    sweeps(s_ref, e_ref, f_ref, y_ref, ends_ref, masked(live_ref, cell(cur_ref, planes - 1)))


def second_kernel(
    live_ref, pick_ref, tiles_ref, cur_ref, above_ref, force_ref, diag_ref, low_ref, up_ref,
    inv_ref, e_ref, f_ref,
    res_ref, s_ref, ends_ref, low0_ref, y_ref,
):
    planes = cur_ref.shape[0]
    ghosts = ghosts_of(pick_ref, tiles_ref)
    for r in range(5):
        put(low0_ref, cell(low_ref, 0, r), r)
    for j in range(planes):
        here = cell(cur_ref, j)
        applied = matvec(block(diag_ref, j), here)
        if j > 0:
            lower = matvec(block(low_ref, j), cell(cur_ref, j - 1))
            applied = [x - z for x, z in zip(applied, lower)]
        above = cell(cur_ref, j + 1) if j < planes - 1 else cell(above_ref)
        upper = matvec(block(up_ref, j), above)
        res = []
        for v in range(5):
            sides = neighbours(here[v]) + ghost_at(ghosts, j, v)
            all_of = applied[v] - upper[v] - COUPLE * sides
            res.append(force_ref[j, v] - all_of)
        res = masked(live_ref, res)
        put(res_ref, res, j)
        put(s_ref, matvec(block(inv_ref, j), res), j)
    last = cell(cur_ref, planes - 1)
    sweeps(s_ref, e_ref, f_ref, y_ref, ends_ref, last)
    put(ends_ref, last, 2)


def write_kernel(res_ref, res_hbm, sem):
    copy = pltpu.make_async_copy(res_ref, res_hbm, sem)
    copy.start()
    copy.wait()


def mid_kernel(ends_ref, ends_other_ref, mats_ref, mats_other_ref, out_ref):
    def run(ends_lo, mats_lo, ends_hi, mats_hi):
        c_lo = cell(ends_lo, 0)

        @pl.when(lax.axis_index("ja") < 2)
        def _():
            put(out_ref, add(cell(ends_hi, 0), matvec(block(mats_hi, 0), c_lo)), 0)

        @pl.when(lax.axis_index("ja") >= 2)
        def _():
            turned = add(cell(ends_hi, 1), matvec(block(mats_hi, 1), c_lo))
            put(out_ref, add(cell(ends_lo, 1), matvec(block(mats_lo, 2), turned)), 0)

        if out_ref.shape[0] > 1:
            put(out_ref, cell(ends_hi, 2), 1)

    by_place([ends_ref, mats_ref], [ends_other_ref, mats_other_ref], run)


def inflows(
    ends_ref, ends_other_ref, mats_ref, mats_other_ref, pair_ref, pair_other_ref,
    beta_ref, inflow_ref,
):
    ja = lax.axis_index("ja")
    zeros = [jnp.zeros((16, 128), jnp.float32)] * 5

    def far():
        return add(cell(pair_other_ref, 0), matvec(block(beta_ref), cell(pair_ref, 0)))

    @pl.when(ja == 0)
    def _():
        put(inflow_ref, zeros, 0)
        b = add(cell(ends_other_ref, 1), matvec(block(mats_other_ref, 1), cell(ends_ref, 0)))
        b = add(b, matvec(block(mats_other_ref, 2), far()))
        put(inflow_ref, b, 1)

    @pl.when(ja == 1)
    def _():
        put(inflow_ref, cell(ends_other_ref, 0), 0)
        put(inflow_ref, far(), 1)

    @pl.when(ja == 2)
    def _():
        a = cell(pair_other_ref, 0)
        put(inflow_ref, a, 0)
        a = add(cell(ends_ref, 0), matvec(block(mats_ref, 0), a))
        b = add(cell(ends_other_ref, 1), matvec(block(mats_other_ref, 1), a))
        put(inflow_ref, b, 1)

    @pl.when(ja == 3)
    def _():
        a = add(cell(ends_other_ref, 0), matvec(block(mats_other_ref, 0), cell(pair_other_ref, 0)))
        put(inflow_ref, a, 0)
        put(inflow_ref, zeros, 1)


def final_kernel(
    live_ref, cur_ref, above_ref, s_ref, e_ref, f_ref,
    ends_ref, ends_other_ref, mats_ref, mats_other_ref, pair_ref, pair_other_ref,
    beta_ref,
    new_ref, above_new_ref, tile_ref, y_ref, inflow_ref,
):
    planes = cur_ref.shape[0]
    inflows(
        ends_ref, ends_other_ref, mats_ref, mats_other_ref, pair_ref, pair_other_ref,
        beta_ref, inflow_ref,
    )
    value = cell(inflow_ref, 0)
    for j in range(planes):
        value = add(cell(s_ref, j), matvec(block(e_ref, j), value))
        put(y_ref, value, j)
    value = cell(inflow_ref, 1)
    put(above_new_ref, add(masked(live_ref, has_above(cell(above_ref))), value))
    for j in range(planes - 1, -1, -1):
        value = add(cell(y_ref, j), matvec(block(f_ref, j), value))
        put(new_ref, add(masked(live_ref, cell(cur_ref, j)), value), j)
    pack_faces(lambda j, v: new_ref[j, v], planes, tile_ref)


def last_kernel(
    live_ref, low0_ref, cur_ref, res_ref, s_ref, e_ref, f_ref,
    ends_ref, ends_other_ref, mats_ref, mats_other_ref, pair_ref, pair_other_ref,
    beta_ref,
    res_in_hbm,
    new_hbm, res_hbm, y_ref, inflow_ref, new_ref, res0_ref, sems,
):
    del res_in_hbm
    planes = cur_ref.shape[0]
    ja = lax.axis_index("ja")
    before = [
        jnp.where(ja == 0, 0.0, jnp.where(ja == 2, pair_other_ref[1, v], ends_other_ref[2, v]))
        for v in range(5)
    ]
    put(res0_ref, add(cell(res_ref, 0), masked(live_ref, matvec(block(low0_ref), before))))
    copies = [pltpu.make_async_copy(res0_ref, res_hbm.at[0], sems.at[planes])]
    copies[0].start()
    inflows(
        ends_ref, ends_other_ref, mats_ref, mats_other_ref, pair_ref, pair_other_ref,
        beta_ref, inflow_ref,
    )
    value = cell(inflow_ref, 0)
    for j in range(planes):
        value = add(cell(s_ref, j), matvec(block(e_ref, j), value))
        put(y_ref, value, j)
    value = cell(inflow_ref, 1)
    for j in range(planes - 1, -1, -1):
        value = add(cell(y_ref, j), matvec(block(f_ref, j), value))
        put(new_ref, add(cell(cur_ref, j), value), j)
        copies.append(pltpu.make_async_copy(new_ref.at[j], new_hbm.at[j], sems.at[j]))
        copies[-1].start()
    for copy in copies:
        copy.wait()


def per_device(
    flow_state, forcing, diag_block, lower_jac, upper_jac, block_inv, east_zone, zone_depth
):
    zones, parts = lax.axis_size("zone"), lax.axis_size("ja")
    assert parts == 4 and ITERS == 2
    current, force, diag, low, up, inv = (
        x[0] for x in (flow_state, forcing, diag_block, lower_jac, upper_jac, block_inv)
    )
    state = current.shape
    planes, plane, blocks, tiles = state[0], state[1:], diag.shape, (zones, *state[2:])
    matrix = blocks[1:]
    work = [buffer(*state)]

    def swap(x, bit):
        return lax.ppermute(x, "ja", [(p, p ^ bit) for p in range(parts)])

    def faces(x):
        return lax.all_to_all(x, "zone", 0, 0, tiled=True)

    e, f, mats, live, pick = call(
        matrix_kernel,
        [blocks, blocks, (3, *matrix), state[2:], (2, *tiles)],
        [buffer(*blocks)] * 4
        + [pltpu.SMEM((zones,), jnp.int32)] * 2
        + [pltpu.SemaphoreType.DMA((3, planes)), pltpu.SemaphoreType.DMA((2,))],
        flops=5 * 10**9,
        far=(0, 1, 2, 3, 4),
    )(zone_depth, east_zone, inv, low, up)
    tile, first = call(pack_kernel, [tiles, plane], flops=2 * 10**10)(mats, current)
    above = lax.ppermute(first, "ja", [((p + 1) % parts, p) for p in range(parts)])
    mats_other = swap(mats, 1)
    got = faces(tile)
    beta = call(beta_kernel, [matrix], flops=10**5)(mats, mats_other)[0]
    s, ends = call(local_kernel, [state, (2, *plane)], work)(
        beta, live, pick, got, current, above, force, diag, inv, e, f
    )
    beta = swap(beta, 2)
    ends_other = swap(ends, 1)
    pair = call(mid_kernel, [(1, *plane)])(ends, ends_other, mats, mats_other)[0]
    pair_other = swap(pair, 2)
    flows = [buffer(2, *plane)]
    current, above, tile = call(final_kernel, [state, plane, tiles], work + flows)(
        live, current, above, s, e, f,
        ends, ends_other, mats, mats_other, pair, pair_other, beta,
    )

    got = faces(tile)
    residual, s, ends, low0 = call(
        second_kernel, [state, state, (3, *plane), matrix], work
    )(
        live, pick, got, current, above, force, diag, low, up, inv, e, f
    )
    ends_other = swap(ends, 1)
    pair = call(mid_kernel, [(2, *plane)])(ends, ends_other, mats, mats_other)[0]
    pair_other = swap(pair, 2)
    written = call(write_kernel, [state], [pltpu.SemaphoreType.DMA], out_specs=[HBM])(residual)[0]
    current, residual = call(
        last_kernel,
        [state, state],
        work + flows + work + [buffer(*plane), pltpu.SemaphoreType.DMA((planes + 1,))],
        out_specs=[HBM, HBM],
        alias={14: 1},
    )(
        live, low0, current, residual, s, e, f,
        ends, ends_other, mats, mats_other, pair, pair_other, beta, written,
    )
    return (current[None], residual[None])


def solution(mesh):
    state = P("zone", "ja", None, None, None)
    blocks = P("zone", "ja", None, None, None, None)
    return jax.shard_map(
        per_device,
        mesh=mesh,
        in_specs=(state, state, blocks, blocks, blocks, blocks, P(), P()),
        out_specs=(state, state),
        check_vma=False,
    )
```

```python
import jax
import jax.numpy as jnp
from jax import lax
from jax.experimental import pallas as pl
from jax.experimental.pallas import tpu as pltpu
from jax.sharding import PartitionSpec as P

ITERS = 2
OMEGA = 1.2
COUPLE = 0.25

VMEM = pl.BlockSpec(memory_space=pltpu.VMEM)
HBM = pl.BlockSpec(memory_space=pltpu.HBM)


def call(kernel, shapes, scratch=(), flops=10**9, far=(), out_specs=None, alias=None):
    alias = alias or {}

    def run(*arrays):
        arrays = [
            pltpu.with_memory_space_constraint(a, pltpu.HBM if i in far else pltpu.VMEM)
            for i, a in enumerate(arrays)
        ]
        specs = out_specs or [VMEM] * len(shapes)
        return pl.pallas_call(
            kernel,
            out_shape=[
                pltpu.VMEM(s, jnp.float32) if spec is VMEM else jax.ShapeDtypeStruct(s, jnp.float32)
                for s, spec in zip(shapes, specs)
            ],
            in_specs=[HBM if i in far else VMEM for i in range(len(arrays))],
            out_specs=specs,
            scratch_shapes=list(scratch),
            input_output_aliases=alias,
            compiler_params=pltpu.CompilerParams(vmem_limit_bytes=8 * 2**20),
            cost_estimate=pl.CostEstimate(
                flops=flops, bytes_accessed=flops // 10**3, transcendentals=0
            ),
        )(*arrays)

    return run


def buffer(*shape):
    return pltpu.VMEM(shape, jnp.float32)


def iota(dim):
    return lax.broadcasted_iota(jnp.int32, (16, 128), dim)


def matvec(matrix, vector):
    n = len(vector)
    out = []
    for r in range(n):
        acc = matrix[r][0] * vector[0]
        for c in range(1, n):
            acc = acc + matrix[r][c] * vector[c]
        out.append(acc)
    return out


def block(ref, *lead):
    return [[ref[(*lead, r, c)] for c in range(5)] for r in range(5)]


def cell(ref, *lead):
    return [ref[(*lead, v)] for v in range(5)]


def put(ref, values, *lead):
    for v, value in enumerate(values):
        ref[(*lead, v)] = value


def add(a, b):
    return [x + y for x, y in zip(a, b)]


def pack_faces(load, planes, tile_ref):
    lane = iota(1)
    tile = jnp.zeros((16, 128), jnp.float32)
    for j in range(planes):
        for v in range(5):
            q = 2 * (j * 5 + v)
            here = (lane == q) | (lane == (q - 1) % 128)
            x = load(j, v)
            tile = jnp.where(here, pltpu.roll(x, q, 1) if q else x, tile)
    for w in range(tile_ref.shape[0]):
        tile_ref[w] = tile


def masked(live_ref, values):
    live = live_ref[...] > 0.0
    return [jnp.where(live, x, 0.0) for x in values]


def has_above(values):
    inner = lax.axis_index("ja") < lax.axis_size("ja") - 1
    return [jnp.where(inner, x, 0.0) for x in values]


def pack_kernel(live_ref, flow_ref, tile_ref, cur_ref, first_ref):
    planes = flow_ref.shape[0]
    for j in range(planes):
        put(cur_ref, masked(live_ref, cell(flow_ref, j)), j)
    put(first_ref, masked(live_ref, cell(flow_ref, 0)))
    pack_faces(lambda j, v: cur_ref[j, v], planes, tile_ref)


def load_kernel(diag_hbm, force_hbm, diag_ref, force_ref, sems):
    copies = [
        pltpu.make_async_copy(diag_hbm, diag_ref, sems.at[0]),
        pltpu.make_async_copy(force_hbm, force_ref, sems.at[1]),
    ]
    for copy in copies:
        copy.start()
    for copy in copies:
        copy.wait()


def neighbours(x):
    lane, row = iota(1), iota(0)
    total = jnp.where(lane == 0, 0.0, pltpu.roll(x, 1, 1))
    total = total + jnp.where(lane == 127, 0.0, pltpu.roll(x, 127, 1))
    total = total + jnp.where(row == 0, 0.0, pltpu.roll(x, 1, 0))
    return total + jnp.where(row == 15, 0.0, pltpu.roll(x, 15, 0))


def ghosts_of(pick_ref, tiles_ref):
    low = high = jnp.zeros((16, 128), jnp.float32)
    for w in range(tiles_ref.shape[0]):
        low = jnp.where(pick_ref[0, w] > 0.0, tiles_ref[w], low)
        high = jnp.where(pick_ref[1, w] > 0.0, tiles_ref[w], high)
    return jnp.where(iota(1) % 2 == 0, pltpu.roll(low, 1, 1), pltpu.roll(high, 127, 1))


def ghost_at(ghosts, j, v):
    lane = iota(1)
    q = 2 * (j * 5 + v)
    turned = pltpu.roll(ghosts, 128 - q, 1) if q else ghosts
    return jnp.where((lane == 0) | (lane == 127), turned, 0.0)


def matrix_kernel(
    depth_hbm, east_hbm, inv_hbm, low_hbm, up_hbm,
    inv_ref, low_ref, up_ref, e_ref, f_ref, mats_ref, live_ref, pick_ref,
    y_ref, depth_ref, east_ref, sems, small_sems,
):
    planes = inv_ref.shape[0]

    def copies(j):
        return [
            pltpu.make_async_copy(src.at[j], dst.at[j], sems.at[i, j])
            for i, (src, dst) in enumerate(
                [(inv_hbm, inv_ref), (low_hbm, low_ref), (up_hbm, up_ref)]
            )
        ]

    for j in range(planes):
        for copy in copies(j):
            copy.start()
    scalars = [
        pltpu.make_async_copy(depth_hbm, depth_ref, small_sems.at[0]),
        pltpu.make_async_copy(east_hbm, east_ref, small_sems.at[1]),
    ]
    for copy in scalars:
        copy.start()
    last = planes - 1
    halves = [pl.ds(0, 8), pl.ds(8, 8)]

    def col(ref, q, j, rows):
        return [ref[j, r, q, rows] for r in range(5)]

    def put_col(ref, values, q, j, rows):
        for r in range(5):
            ref[j, r, q, rows] = values[r]

    def mat(ref, j, rows):
        return [[ref[j, r, c, rows] for c in range(5)] for r in range(5)]

    def products(j, rows):
        inv = mat(inv_ref, j, rows)
        for jac_ref, out_ref in ((low_ref, e_ref), (up_ref, f_ref)):
            for q in range(5):
                product = matvec(inv, col(jac_ref, q, j, rows))
                put_col(out_ref, [OMEGA * x for x in product], q, j, rows)

    def forward(j, carry):
        for copy in copies(j):
            copy.wait()
        for rows in halves:
            products(j, rows)
            e = mat(e_ref, j, rows)
            for q in range(5):
                put_col(y_ref, matvec(e, col(y_ref, q, j - 1, rows)), q, j, rows)
        return carry

    for copy in copies(0):
        copy.wait()
    for rows in halves:
        products(0, rows)
        for q in range(5):
            put_col(y_ref, col(e_ref, q, 0, rows), q, 0, rows)
    lax.fori_loop(1, planes, forward, 0)
    for rows in halves:
        for q in range(5):
            put_col(mats_ref, col(y_ref, q, last, rows), q, 0, rows)
            put_col(mats_ref, col(y_ref, q, last, rows), q, 1, rows)
            put_col(mats_ref, col(f_ref, q, last, rows), q, 2, rows)

    def backward(step, carry):
        j = planes - 2 - step
        for rows in halves:
            f = mat(f_ref, j, rows)
            for q in range(5):
                turned = matvec(f, col(mats_ref, q, 1, rows))
                put_col(mats_ref, add(col(y_ref, q, j, rows), turned), q, 1, rows)
                put_col(mats_ref, matvec(f, col(mats_ref, q, 2, rows)), q, 2, rows)
        return carry

    lax.fori_loop(0, planes - 1, backward, 0)
    for copy in scalars:
        copy.wait()
    zone = lax.axis_index("zone")
    row = iota(0)
    live_ref[...] = jnp.where(row < depth_ref[zone], 1.0, 0.0)
    for w in range(pick_ref.shape[1]):
        pick_ref[0, w] = jnp.where((row >= 0) & (east_ref[w] == zone), 1.0, 0.0)
        pick_ref[1, w] = jnp.where((row >= 0) & (east_ref[zone] == w), 1.0, 0.0)


def by_place(mine_refs, other_refs, run):
    odd = lax.axis_index("ja") % 2

    @pl.when(odd == 0)
    def _():
        run(*mine_refs, *other_refs)

    @pl.when(odd == 1)
    def _():
        run(*other_refs, *mine_refs)


def beta_kernel(mine_ref, other_ref, half_ref):
    odd = lax.axis_index("ja") % 2
    for side in range(2):
        lo, hi = (mine_ref, other_ref) if side == 0 else (other_ref, mine_ref)
        rows = pl.ds(8 * side, 8)

        @pl.when(odd == side)
        def _():
            d_hi = [[hi[1, r, c, rows] for c in range(5)] for r in range(5)]
            n_lo = [[lo[2, r, c, rows] for c in range(5)] for r in range(5)]
            for q in range(5):
                m_col = [lo[0, r, q, rows] for r in range(5)]
                d_col = [lo[1, r, q, rows] for r in range(5)]
                out = add(d_col, matvec(n_lo, matvec(d_hi, m_col)))
                for r in range(5):
                    half_ref[r, q] = out[r]


def sweeps(s_ref, e_ref, f_ref, y_ref, ends_ref, last):
    planes = s_ref.shape[0]
    value = cell(s_ref, 0)
    put(y_ref, value, 0)
    for j in range(1, planes):
        value = add(cell(s_ref, j), matvec(block(e_ref, j), value))
        put(y_ref, value, j)
    put(ends_ref, [x + z * (1.0 / OMEGA) for x, z in zip(value, last)], 0)
    for j in range(planes - 2, -1, -1):
        value = add(cell(y_ref, j), matvec(block(f_ref, j), value))
    put(ends_ref, value, 1)


def local_kernel(
    half_ref, live_ref, pick_ref, tiles_ref, cur_ref, above_ref, force_ref, diag_ref, inv_ref,
    e_ref, f_ref,
    s_ref, ends_ref, half_out_ref, y_ref,
):
    for r in range(5):
        put(half_out_ref, cell(half_ref, r), r)
    planes = cur_ref.shape[0]
    ghosts = ghosts_of(pick_ref, tiles_ref)
    before, here = None, cell(cur_ref, 0)
    for j in range(planes):
        after = cell(cur_ref, j + 1) if j < planes - 1 else has_above(cell(above_ref))
        own = matvec(block(diag_ref, j), here)
        res = []
        for v in range(5):
            sides = neighbours(here[v]) + ghost_at(ghosts, j, v)
            res.append(force_ref[j, v] - own[v] + COUPLE * sides)
        linked = matvec(block(f_ref, j), after)
        if before is not None:
            linked = add(linked, matvec(block(e_ref, j), before))
        linked = [x * (1.0 / OMEGA) for x in linked]
        put(s_ref, add(matvec(block(inv_ref, j), masked(live_ref, res)), linked), j)
        before, here = here, after
    sweeps(s_ref, e_ref, f_ref, y_ref, ends_ref, cell(cur_ref, planes - 1))


def residual_kernel(
    live_ref, cur_ref, above_ref, force_ref, diag_ref, low_ref, up_ref, inv_ref,
    res_ref, s_ref,
):
    planes = cur_ref.shape[0]
    for j in range(planes):
        here = cell(cur_ref, j)
        applied = matvec(block(diag_ref, j), here)
        if j > 0:
            lower = matvec(block(low_ref, j), cell(cur_ref, j - 1))
            applied = [x - z for x, z in zip(applied, lower)]
        above = cell(cur_ref, j + 1) if j < planes - 1 else cell(above_ref)
        upper = matvec(block(up_ref, j), above)
        res = []
        for v in range(5):
            all_of = applied[v] - upper[v] - COUPLE * neighbours(here[v])
            res.append(force_ref[j, v] - all_of)
        res = masked(live_ref, res)
        put(res_ref, res, j)
        put(s_ref, matvec(block(inv_ref, j), res), j)


def ghost_kernel(
    live_ref, pick_ref, tiles_ref, cur_ref, res0_ref, s0_ref, inv_ref, e_ref, f_ref,
    res_ref, s_ref, ends_ref, y_ref,
):
    planes = cur_ref.shape[0]
    ghosts = jnp.where(live_ref[...] > 0.0, COUPLE * ghosts_of(pick_ref, tiles_ref), 0.0)
    for j in range(planes):
        extra = [ghost_at(ghosts, j, v) for v in range(5)]
        put(res_ref, add(cell(res0_ref, j), extra), j)
        put(s_ref, add(cell(s0_ref, j), matvec(block(inv_ref, j), extra)), j)
    last = cell(cur_ref, planes - 1)
    sweeps(s_ref, e_ref, f_ref, y_ref, ends_ref, last)
    put(ends_ref, last, 2)


def write_kernel(res_ref, res_hbm, sem):
    copy = pltpu.make_async_copy(res_ref, res_hbm, sem)
    copy.start()
    copy.wait()


def mid_kernel(ends_ref, ends_other_ref, mats_ref, mats_other_ref, out_ref):
    def run(ends_lo, mats_lo, ends_hi, mats_hi):
        c_lo = cell(ends_lo, 0)

        @pl.when(lax.axis_index("ja") < 2)
        def _():
            put(out_ref, add(cell(ends_hi, 0), matvec(block(mats_hi, 0), c_lo)), 0)

        @pl.when(lax.axis_index("ja") >= 2)
        def _():
            turned = add(cell(ends_hi, 1), matvec(block(mats_hi, 1), c_lo))
            put(out_ref, add(cell(ends_lo, 1), matvec(block(mats_lo, 2), turned)), 0)

        if out_ref.shape[0] > 1:
            put(out_ref, cell(ends_hi, 2), 1)

    by_place([ends_ref, mats_ref], [ends_other_ref, mats_other_ref], run)


def inflows(
    ends_ref, ends_other_ref, mats_ref, mats_other_ref, pair_ref, pair_other_ref,
    half_ref, half_other_ref, inflow_ref,
):
    ja = lax.axis_index("ja")
    zeros = [jnp.zeros((16, 128), jnp.float32)] * 5

    def far(top_ref, bottom_ref):
        beta = [
            [jnp.concatenate([top_ref[r, c], bottom_ref[r, c]], axis=0) for c in range(5)]
            for r in range(5)
        ]
        return add(cell(pair_other_ref, 0), matvec(beta, cell(pair_ref, 0)))

    @pl.when(ja == 0)
    def _():
        put(inflow_ref, zeros, 0)
        b = add(cell(ends_other_ref, 1), matvec(block(mats_other_ref, 1), cell(ends_ref, 0)))
        b = add(b, matvec(block(mats_other_ref, 2), far(half_ref, half_other_ref)))
        put(inflow_ref, b, 1)

    @pl.when(ja == 1)
    def _():
        put(inflow_ref, cell(ends_other_ref, 0), 0)
        put(inflow_ref, far(half_other_ref, half_ref), 1)

    @pl.when(ja == 2)
    def _():
        a = cell(pair_other_ref, 0)
        put(inflow_ref, a, 0)
        a = add(cell(ends_ref, 0), matvec(block(mats_ref, 0), a))
        b = add(cell(ends_other_ref, 1), matvec(block(mats_other_ref, 1), a))
        put(inflow_ref, b, 1)

    @pl.when(ja == 3)
    def _():
        a = add(cell(ends_other_ref, 0), matvec(block(mats_other_ref, 0), cell(pair_other_ref, 0)))
        put(inflow_ref, a, 0)
        put(inflow_ref, zeros, 1)


def final_kernel(
    cur_ref, above_ref, s_ref, e_ref, f_ref,
    ends_ref, ends_other_ref, mats_ref, mats_other_ref, pair_ref, pair_other_ref,
    half_ref, half_other_ref,
    new_ref, above_new_ref, tile_ref, y_ref, inflow_ref,
):
    planes = cur_ref.shape[0]
    inflows(
        ends_ref, ends_other_ref, mats_ref, mats_other_ref, pair_ref, pair_other_ref,
        half_ref, half_other_ref, inflow_ref,
    )
    value = cell(inflow_ref, 0)
    for j in range(planes):
        value = add(cell(s_ref, j), matvec(block(e_ref, j), value))
        put(y_ref, value, j)
    value = cell(inflow_ref, 1)
    put(above_new_ref, add(has_above(cell(above_ref)), value))
    for j in range(planes - 1, -1, -1):
        value = add(cell(y_ref, j), matvec(block(f_ref, j), value))
        put(new_ref, add(cell(cur_ref, j), value), j)
    pack_faces(lambda j, v: new_ref[j, v], planes, tile_ref)


def last_kernel(
    live_ref, low_ref, cur_ref, res_ref, s_ref, e_ref, f_ref,
    ends_ref, ends_other_ref, mats_ref, mats_other_ref, pair_ref, pair_other_ref,
    half_ref, half_other_ref,
    res_in_hbm,
    new_hbm, res_hbm, y_ref, inflow_ref, new_ref, res0_ref, sems,
):
    del res_in_hbm
    planes = cur_ref.shape[0]
    ja = lax.axis_index("ja")
    before = [
        jnp.where(ja == 0, 0.0, jnp.where(ja == 2, pair_other_ref[1, v], ends_other_ref[2, v]))
        for v in range(5)
    ]
    put(res0_ref, add(cell(res_ref, 0), masked(live_ref, matvec(block(low_ref, 0), before))))
    copies = [pltpu.make_async_copy(res0_ref, res_hbm.at[0], sems.at[planes])]
    copies[0].start()
    inflows(
        ends_ref, ends_other_ref, mats_ref, mats_other_ref, pair_ref, pair_other_ref,
        half_ref, half_other_ref, inflow_ref,
    )
    value = cell(inflow_ref, 0)
    for j in range(planes):
        value = add(cell(s_ref, j), matvec(block(e_ref, j), value))
        put(y_ref, value, j)
    value = cell(inflow_ref, 1)
    for j in range(planes - 1, -1, -1):
        value = add(cell(y_ref, j), matvec(block(f_ref, j), value))
        put(new_ref, add(cell(cur_ref, j), value), j)
        copies.append(pltpu.make_async_copy(new_ref.at[j], new_hbm.at[j], sems.at[j]))
        copies[-1].start()
    for copy in copies:
        copy.wait()


def per_device(
    flow_state, forcing, diag_block, lower_jac, upper_jac, block_inv, east_zone, zone_depth
):
    zones, parts = lax.axis_size("zone"), lax.axis_size("ja")
    assert parts == 4 and ITERS == 2
    current, force, diag, low, up, inv = (
        x[0] for x in (flow_state, forcing, diag_block, lower_jac, upper_jac, block_inv)
    )
    state = current.shape
    planes, plane, blocks, tiles = state[0], state[1:], diag.shape, (zones, *state[2:])
    matrix = blocks[1:]
    work = [buffer(*state)]

    def swap(x, bit):
        return lax.ppermute(x, "ja", [(p, p ^ bit) for p in range(parts)])

    def faces(x):
        return lax.all_to_all(x, "zone", 0, 0, tiled=True)

    inv, low, up, e, f, mats, live, pick = call(
        matrix_kernel,
        [blocks] * 5 + [(3, *matrix), state[2:], (2, *tiles)],
        [buffer(*blocks)]
        + [pltpu.SMEM((zones,), jnp.int32)] * 2
        + [pltpu.SemaphoreType.DMA((3, planes)), pltpu.SemaphoreType.DMA((2,))],
        flops=5 * 10**9,
        far=(0, 1, 2, 3, 4),
    )(zone_depth, east_zone, inv, low, up)
    tile, current, first = call(pack_kernel, [tiles, state, plane])(live, current)
    above = lax.ppermute(first, "ja", [((p + 1) % parts, p) for p in range(parts)])
    mats_other = swap(mats, 1)
    got = faces(tile)
    diag, force = call(
        load_kernel, [blocks, state], [pltpu.SemaphoreType.DMA((2,))], far=(0, 1)
    )(diag, force)
    half = call(beta_kernel, [(*matrix[:2], 8, matrix[3])], flops=10**5)(mats, mats_other)[0]
    half = swap(half, 2)
    s, ends, half = call(local_kernel, [state, (2, *plane), half.shape], work)(
        half, live, pick, got, current, above, force, diag, inv, e, f
    )
    ends_other = swap(ends, 1)
    half_other = swap(half, 1)
    pair = call(mid_kernel, [(1, *plane)])(ends, ends_other, mats, mats_other)[0]
    pair_other = swap(pair, 2)
    flows = [buffer(2, *plane)]
    current, above, tile = call(final_kernel, [state, plane, tiles], work + flows)(
        current, above, s, e, f,
        ends, ends_other, mats, mats_other, pair, pair_other, half, half_other,
    )

    got = faces(tile)
    residual, s = call(residual_kernel, [state, state])(
        live, current, above, force, diag, low, up, inv
    )
    residual, s, ends = call(ghost_kernel, [state, state, (3, *plane)], work)(
        live, pick, got, current, residual, s, inv, e, f
    )
    ends_other = swap(ends, 1)
    pair = call(mid_kernel, [(2, *plane)])(ends, ends_other, mats, mats_other)[0]
    pair_other = swap(pair, 2)
    written = call(write_kernel, [state], [pltpu.SemaphoreType.DMA], out_specs=[HBM])(residual)[0]
    current, residual = call(
        last_kernel,
        [state, state],
        work + flows + work + [buffer(*plane), pltpu.SemaphoreType.DMA((planes + 1,))],
        out_specs=[HBM, HBM],
        far=(15,),
        alias={15: 1},
    )(
        live, low, current, residual, s, e, f,
        ends, ends_other, mats, mats_other, pair, pair_other, half, half_other, written,
    )
    return (current[None], residual[None])


def solution(mesh):
    state = P("zone", "ja", None, None, None)
    blocks = P("zone", "ja", None, None, None, None)
    return jax.shard_map(
        per_device,
        mesh=mesh,
        in_specs=(state, state, blocks, blocks, blocks, blocks, P(), P()),
        out_specs=(state, state),
        check_vma=False,
    )
```

```python
import jax
import jax.numpy as jnp
from jax import lax
from jax.experimental import pallas as pl
from jax.experimental.pallas import tpu as pltpu
from jax.sharding import PartitionSpec as P

ITERS = 2
OMEGA = 1.2
COUPLE = 0.25

VMEM = pl.BlockSpec(memory_space=pltpu.VMEM)
ANY = pl.BlockSpec(memory_space=pl.ANY)
HBM = pl.BlockSpec(memory_space=pltpu.HBM)


def call(kernel, shapes, scratch=(), flops=10**9, far=(), out_specs=None, alias=None):
    alias = alias or {}

    def run(*arrays):
        arrays = [
            pltpu.with_memory_space_constraint(a, pltpu.HBM) if i in far else a
            for i, a in enumerate(arrays)
        ]
        return pl.pallas_call(
            kernel,
            out_shape=[jax.ShapeDtypeStruct(s, jnp.float32) for s in shapes],
            in_specs=[
                HBM if i in far else ANY if i in alias else VMEM for i in range(len(arrays))
            ],
            out_specs=out_specs or [VMEM] * len(shapes),
            scratch_shapes=list(scratch),
            input_output_aliases=alias,
            compiler_params=pltpu.CompilerParams(vmem_limit_bytes=8 * 2**20),
            cost_estimate=pl.CostEstimate(flops=flops, bytes_accessed=flops // 10**3, transcendentals=0),
        )(*arrays)

    return run


def buffer(*shape):
    return pltpu.VMEM(shape, jnp.float32)


def iota(dim):
    return lax.broadcasted_iota(jnp.int32, (16, 128), dim)


def matvec(matrix, vector):
    n = len(vector)
    out = []
    for r in range(n):
        acc = matrix[r][0] * vector[0]
        for c in range(1, n):
            acc = acc + matrix[r][c] * vector[c]
        out.append(acc)
    return out


def block(ref, *lead):
    return [[ref[(*lead, r, c)] for c in range(5)] for r in range(5)]


def cell(ref, *lead):
    return [ref[(*lead, v)] for v in range(5)]


def put(ref, values, *lead):
    for v, value in enumerate(values):
        ref[(*lead, v)] = value


def add(a, b):
    return [x + y for x, y in zip(a, b)]


def pack_faces(load, planes, tile_ref):
    lane = iota(1)
    tile = jnp.zeros((16, 128), jnp.float32)
    for j in range(planes):
        for v in range(5):
            q = 2 * (j * 5 + v)
            here = (lane == q) | (lane == (q - 1) % 128)
            x = load(j, v)
            tile = jnp.where(here, pltpu.roll(x, q, 1) if q else x, tile)
    for w in range(tile_ref.shape[0]):
        tile_ref[w] = tile


def masked(live_ref, values):
    live = live_ref[...] > 0.0
    return [jnp.where(live, x, 0.0) for x in values]


def has_above(values):
    inner = lax.axis_index("ja") < lax.axis_size("ja") - 1
    return [jnp.where(inner, x, 0.0) for x in values]


def pack_kernel(flow_ref, tile_ref, first_ref):
    put(first_ref, cell(flow_ref, 0))
    pack_faces(lambda j, v: flow_ref[j, v], flow_ref.shape[0], tile_ref)


def neighbours(x):
    lane, row = iota(1), iota(0)
    total = jnp.where(lane == 0, 0.0, pltpu.roll(x, 1, 1))
    total = total + jnp.where(lane == 127, 0.0, pltpu.roll(x, 127, 1))
    total = total + jnp.where(row == 0, 0.0, pltpu.roll(x, 1, 0))
    return total + jnp.where(row == 15, 0.0, pltpu.roll(x, 15, 0))


def ghosts_of(pick_ref, tiles_ref):
    low = high = jnp.zeros((16, 128), jnp.float32)
    for w in range(tiles_ref.shape[0]):
        low = jnp.where(pick_ref[0, w] > 0.0, tiles_ref[w], low)
        high = jnp.where(pick_ref[1, w] > 0.0, tiles_ref[w], high)
    return jnp.where(iota(1) % 2 == 0, pltpu.roll(low, 1, 1), pltpu.roll(high, 127, 1))


def ghost_at(ghosts, j, v):
    lane = iota(1)
    q = 2 * (j * 5 + v)
    turned = pltpu.roll(ghosts, 128 - q, 1) if q else ghosts
    return jnp.where((lane == 0) | (lane == 127), turned, 0.0)


def matrix_kernel(
    depth_hbm, east_hbm, tiles_ref, inv_ref, low_ref, up_ref,
    e_ref, f_ref, mats_ref, live_ref, pick_ref,
    y_ref, depth_ref, east_ref, sems,
):
    del tiles_ref
    planes = inv_ref.shape[0]
    scalars = [
        pltpu.make_async_copy(depth_hbm, depth_ref, sems.at[0]),
        pltpu.make_async_copy(east_hbm, east_ref, sems.at[1]),
    ]
    for copy in scalars:
        copy.start()
    last = planes - 1
    halves = [pl.ds(0, 8), pl.ds(8, 8)]

    def col(ref, q, j, rows):
        return [ref[j, r, q, rows] for r in range(5)]

    def put_col(ref, values, q, j, rows):
        for r in range(5):
            ref[j, r, q, rows] = values[r]

    def mat(ref, j, rows):
        return [[ref[j, r, c, rows] for c in range(5)] for r in range(5)]

    def products(j, rows):
        inv = mat(inv_ref, j, rows)
        for jac_ref, out_ref in ((low_ref, e_ref), (up_ref, f_ref)):
            for q in range(5):
                product = matvec(inv, col(jac_ref, q, j, rows))
                put_col(out_ref, [OMEGA * x for x in product], q, j, rows)

    def forward(j, carry):
        for rows in halves:
            products(j, rows)
            e = mat(e_ref, j, rows)
            for q in range(5):
                put_col(y_ref, matvec(e, col(y_ref, q, j - 1, rows)), q, j, rows)
        return carry

    for rows in halves:
        products(0, rows)
        for q in range(5):
            put_col(y_ref, col(e_ref, q, 0, rows), q, 0, rows)
    lax.fori_loop(1, planes, forward, 0)
    for rows in halves:
        for q in range(5):
            put_col(mats_ref, col(y_ref, q, last, rows), q, 0, rows)
            put_col(mats_ref, col(y_ref, q, last, rows), q, 1, rows)
            put_col(mats_ref, col(f_ref, q, last, rows), q, 2, rows)

    def backward(step, carry):
        j = planes - 2 - step
        for rows in halves:
            f = mat(f_ref, j, rows)
            for q in range(5):
                turned = matvec(f, col(mats_ref, q, 1, rows))
                put_col(mats_ref, add(col(y_ref, q, j, rows), turned), q, 1, rows)
                put_col(mats_ref, matvec(f, col(mats_ref, q, 2, rows)), q, 2, rows)
        return carry

    lax.fori_loop(0, planes - 1, backward, 0)
    for copy in scalars:
        copy.wait()
    zone = lax.axis_index("zone")
    row = iota(0)
    live_ref[...] = jnp.where(row < depth_ref[zone], 1.0, 0.0)
    for w in range(pick_ref.shape[1]):
        rows = row < depth_ref[w]
        pick_ref[0, w] = jnp.where(rows & (east_ref[w] == zone), 1.0, 0.0)
        pick_ref[1, w] = jnp.where(rows & (east_ref[zone] == w), 1.0, 0.0)


def by_place(mine_refs, other_refs, run):
    odd = lax.axis_index("ja") % 2

    @pl.when(odd == 0)
    def _():
        run(*mine_refs, *other_refs)

    @pl.when(odd == 1)
    def _():
        run(*other_refs, *mine_refs)


def beta_kernel(mine_ref, other_ref, beta_ref):
    def run(lo, hi):
        d_hi, n_lo = block(hi, 1), block(lo, 2)
        for q in range(5):
            m_col = [lo[0, r, q] for r in range(5)]
            d_col = [lo[1, r, q] for r in range(5)]
            out = add(d_col, matvec(n_lo, matvec(d_hi, m_col)))
            for r in range(5):
                beta_ref[r, q] = out[r]

    by_place([mine_ref], [other_ref], run)


def sweeps(s_ref, e_ref, f_ref, y_ref, ends_ref, last):
    planes = s_ref.shape[0]
    value = cell(s_ref, 0)
    put(y_ref, value, 0)
    for j in range(1, planes):
        value = add(cell(s_ref, j), matvec(block(e_ref, j), value))
        put(y_ref, value, j)
    put(ends_ref, [x + z * (1.0 / OMEGA) for x, z in zip(value, last)], 0)
    for j in range(planes - 2, -1, -1):
        value = add(cell(y_ref, j), matvec(block(f_ref, j), value))
    put(ends_ref, value, 1)


def local_kernel(
    mats_ref, live_ref, pick_ref, tiles_ref, cur_ref, above_ref, force_ref, diag_ref, inv_ref,
    e_ref, f_ref,
    s_ref, ends_ref, mats_out_ref, y_ref,
):
    for i in range(3):
        for r in range(5):
            put(mats_out_ref, cell(mats_ref, i, r), i, r)
    planes = cur_ref.shape[0]
    ghosts = ghosts_of(pick_ref, tiles_ref)
    before, here = None, masked(live_ref, cell(cur_ref, 0))
    for j in range(planes):
        after = cell(cur_ref, j + 1) if j < planes - 1 else has_above(cell(above_ref))
        after = masked(live_ref, after)
        own = matvec(block(diag_ref, j), here)
        res = []
        for v in range(5):
            sides = neighbours(here[v]) + ghost_at(ghosts, j, v)
            res.append(force_ref[j, v] - own[v] + COUPLE * sides)
        linked = matvec(block(f_ref, j), after)
        if before is not None:
            linked = add(linked, matvec(block(e_ref, j), before))
        linked = [x * (1.0 / OMEGA) for x in linked]
        put(s_ref, add(matvec(block(inv_ref, j), masked(live_ref, res)), linked), j)
        before, here = here, after
    sweeps(s_ref, e_ref, f_ref, y_ref, ends_ref, masked(live_ref, cell(cur_ref, planes - 1)))


def second_kernel(
    beta_ref, live_ref, pick_ref, tiles_ref, cur_ref, above_ref, force_ref, diag_ref, low_ref, up_ref,
    inv_ref, e_ref, f_ref,
    res_ref, s_ref, ends_ref, low0_ref, y_ref,
):
    del beta_ref
    planes = cur_ref.shape[0]
    ghosts = ghosts_of(pick_ref, tiles_ref)
    for r in range(5):
        put(low0_ref, cell(low_ref, 0, r), r)
    for j in range(planes):
        here = cell(cur_ref, j)
        applied = matvec(block(diag_ref, j), here)
        if j > 0:
            lower = matvec(block(low_ref, j), cell(cur_ref, j - 1))
            applied = [x - z for x, z in zip(applied, lower)]
        above = cell(cur_ref, j + 1) if j < planes - 1 else cell(above_ref)
        upper = matvec(block(up_ref, j), above)
        res = []
        for v in range(5):
            sides = neighbours(here[v]) + ghost_at(ghosts, j, v)
            all_of = applied[v] - upper[v] - COUPLE * sides
            res.append(force_ref[j, v] - all_of)
        res = masked(live_ref, res)
        put(res_ref, res, j)
        put(s_ref, matvec(block(inv_ref, j), res), j)
    last = cell(cur_ref, planes - 1)
    sweeps(s_ref, e_ref, f_ref, y_ref, ends_ref, last)
    put(ends_ref, last, 2)


def write_kernel(res_ref, res_hbm, sem):
    copy = pltpu.make_async_copy(res_ref, res_hbm, sem)
    copy.start()
    copy.wait()


def mid_kernel(ends_ref, ends_other_ref, mats_ref, mats_other_ref, out_ref):
    def run(ends_lo, mats_lo, ends_hi, mats_hi):
        c_lo = cell(ends_lo, 0)

        @pl.when(lax.axis_index("ja") < 2)
        def _():
            put(out_ref, add(cell(ends_hi, 0), matvec(block(mats_hi, 0), c_lo)), 0)

        @pl.when(lax.axis_index("ja") >= 2)
        def _():
            turned = add(cell(ends_hi, 1), matvec(block(mats_hi, 1), c_lo))
            put(out_ref, add(cell(ends_lo, 1), matvec(block(mats_lo, 2), turned)), 0)

        if out_ref.shape[0] > 1:
            put(out_ref, cell(ends_hi, 2), 1)

    by_place([ends_ref, mats_ref], [ends_other_ref, mats_other_ref], run)


def raise_kernel(pair_ref, pair_other_ref, beta_ref, raised_ref):
    beyond = add(cell(pair_ref, 0), matvec(block(beta_ref), cell(pair_other_ref, 0)))
    put(raised_ref, beyond, 0)


def inflows(
    ends_ref, ends_other_ref, mats_ref, mats_other_ref, pair_ref, pair_other_ref, far, inflow_ref
):
    ja = lax.axis_index("ja")
    zeros = [jnp.zeros((16, 128), jnp.float32)] * 5

    @pl.when(ja == 0)
    def _():
        put(inflow_ref, zeros, 0)
        b = add(cell(ends_other_ref, 1), matvec(block(mats_other_ref, 1), cell(ends_ref, 0)))
        b = add(b, matvec(block(mats_other_ref, 2), far()))
        put(inflow_ref, b, 1)

    @pl.when(ja == 1)
    def _():
        put(inflow_ref, cell(ends_other_ref, 0), 0)
        put(inflow_ref, far(), 1)

    @pl.when(ja == 2)
    def _():
        a = cell(pair_other_ref, 0)
        put(inflow_ref, a, 0)
        a = add(cell(ends_ref, 0), matvec(block(mats_ref, 0), a))
        b = add(cell(ends_other_ref, 1), matvec(block(mats_other_ref, 1), a))
        put(inflow_ref, b, 1)

    @pl.when(ja == 3)
    def _():
        a = add(cell(ends_other_ref, 0), matvec(block(mats_other_ref, 0), cell(pair_other_ref, 0)))
        put(inflow_ref, a, 0)
        put(inflow_ref, zeros, 1)


def final_kernel(
    live_ref, cur_ref, above_ref, s_ref, e_ref, f_ref,
    ends_ref, ends_other_ref, mats_ref, mats_other_ref, pair_ref, pair_other_ref, raised_ref,
    new_ref, above_new_ref, tile_ref, y_ref, inflow_ref,
):
    planes = cur_ref.shape[0]
    inflows(
        ends_ref, ends_other_ref, mats_ref, mats_other_ref, pair_ref, pair_other_ref,
        lambda: cell(raised_ref, 0), inflow_ref,
    )
    value = cell(inflow_ref, 0)
    for j in range(planes):
        value = add(cell(s_ref, j), matvec(block(e_ref, j), value))
        put(y_ref, value, j)
    value = cell(inflow_ref, 1)
    put(above_new_ref, add(masked(live_ref, has_above(cell(above_ref))), value))
    for j in range(planes - 1, -1, -1):
        value = add(cell(y_ref, j), matvec(block(f_ref, j), value))
        put(new_ref, add(masked(live_ref, cell(cur_ref, j)), value), j)
    pack_faces(lambda j, v: new_ref[j, v], planes, tile_ref)


def last_kernel(
    live_ref, low0_ref, cur_ref, res_ref, s_ref, e_ref, f_ref,
    ends_ref, ends_other_ref, mats_ref, mats_other_ref, pair_ref, pair_other_ref,
    beta_ref,
    res_in_hbm,
    new_hbm, res_hbm, y_ref, inflow_ref, new_ref, res0_ref, sems,
):
    del res_in_hbm
    planes = cur_ref.shape[0]
    ja = lax.axis_index("ja")
    before = [
        jnp.where(ja == 0, 0.0, jnp.where(ja == 2, pair_other_ref[1, v], ends_other_ref[2, v]))
        for v in range(5)
    ]
    put(res0_ref, add(cell(res_ref, 0), masked(live_ref, matvec(block(low0_ref), before))))
    copies = [pltpu.make_async_copy(res0_ref, res_hbm.at[0], sems.at[planes])]
    copies[0].start()

    def far():
        return add(cell(pair_other_ref, 0), matvec(block(beta_ref), cell(pair_ref, 0)))

    inflows(
        ends_ref, ends_other_ref, mats_ref, mats_other_ref, pair_ref, pair_other_ref,
        far, inflow_ref,
    )
    value = cell(inflow_ref, 0)
    for j in range(planes):
        value = add(cell(s_ref, j), matvec(block(e_ref, j), value))
        put(y_ref, value, j)
    value = cell(inflow_ref, 1)
    for j in range(planes - 1, -1, -1):
        value = add(cell(y_ref, j), matvec(block(f_ref, j), value))
        put(new_ref, add(cell(cur_ref, j), value), j)
        copies.append(pltpu.make_async_copy(new_ref.at[j], new_hbm.at[j], sems.at[j]))
        copies[-1].start()
    for copy in copies:
        copy.wait()


def per_device(
    flow_state, forcing, diag_block, lower_jac, upper_jac, block_inv, east_zone, zone_depth
):
    zones, parts = lax.axis_size("zone"), lax.axis_size("ja")
    assert parts == 4 and ITERS == 2
    current, force, diag, low, up, inv = (
        x[0] for x in (flow_state, forcing, diag_block, lower_jac, upper_jac, block_inv)
    )
    state = current.shape
    planes, plane, blocks, tiles = state[0], state[1:], diag.shape, (zones, *state[2:])
    matrix = blocks[1:]
    work = [buffer(*state)]

    def swap(x, bit):
        return lax.ppermute(x, "ja", [(p, p ^ bit) for p in range(parts)])

    def faces(x):
        return lax.all_to_all(x, "zone", 0, 0, tiled=True)

    tile, first = call(pack_kernel, [tiles, plane], flops=2 * 10**10)(current)
    above = lax.ppermute(first, "ja", [((p + 1) % parts, p) for p in range(parts)])
    got = faces(tile)
    e, f, mats, live, pick = call(
        matrix_kernel,
        [blocks, blocks, (3, *matrix), state[2:], (2, *tiles)],
        [buffer(*blocks)]
        + [pltpu.SMEM((zones,), jnp.int32)] * 2
        + [pltpu.SemaphoreType.DMA((2,))],
        flops=5 * 10**9,
        far=(0, 1),
    )(zone_depth, east_zone, got, inv, low, up)
    s, ends, mats = call(local_kernel, [state, (2, *plane), mats.shape], work)(
        mats, live, pick, got, current, above, force, diag, inv, e, f
    )
    ends_other = swap(ends, 1)
    mats_other = swap(mats, 1)
    pair = call(mid_kernel, [(1, *plane)], flops=10**5)(ends, ends_other, mats, mats_other)[0]
    beta = call(beta_kernel, [matrix], flops=10**5)(mats, mats_other)[0]
    pair_other = swap(pair, 2)
    raised = call(raise_kernel, [(1, *plane)], flops=10**5)(pair, pair_other, beta)[0]
    raised = swap(raised, 2)
    beta = swap(beta, 2)
    flows = [buffer(2, *plane)]
    current, above, tile = call(final_kernel, [state, plane, tiles], work + flows)(
        live, current, above, s, e, f,
        ends, ends_other, mats, mats_other, pair, pair_other, raised,
    )

    got = faces(tile)
    residual, s, ends, low0 = call(
        second_kernel, [state, state, (3, *plane), matrix], work
    )(
        beta, live, pick, got, current, above, force, diag, low, up, inv, e, f
    )
    ends_other = swap(ends, 1)
    pair = call(mid_kernel, [(2, *plane)])(ends, ends_other, mats, mats_other)[0]
    pair_other = swap(pair, 2)
    written = call(write_kernel, [state], [pltpu.SemaphoreType.DMA], out_specs=[HBM])(residual)[0]
    current, residual = call(
        last_kernel,
        [state, state],
        work + flows + work + [buffer(*plane), pltpu.SemaphoreType.DMA((planes + 1,))],
        out_specs=[HBM, HBM],
        alias={14: 1},
    )(
        live, low0, current, residual, s, e, f,
        ends, ends_other, mats, mats_other, pair, pair_other, beta, written,
    )
    return (current[None], residual[None])


def solution(mesh):
    state = P("zone", "ja", None, None, None)
    blocks = P("zone", "ja", None, None, None, None)
    return jax.shard_map(
        per_device,
        mesh=mesh,
        in_specs=(state, state, blocks, blocks, blocks, blocks, P(), P()),
        out_specs=(state, state),
        check_vma=False,
    )
```

```python
import jax
import jax.numpy as jnp
from jax import lax
from jax.experimental import pallas as pl
from jax.experimental.pallas import tpu as pltpu
from jax.sharding import PartitionSpec as P

ITERS = 2
OMEGA = 1.2
COUPLE = 0.25

VMEM = pl.BlockSpec(memory_space=pltpu.VMEM)
ANY = pl.BlockSpec(memory_space=pl.ANY)
HBM = pl.BlockSpec(memory_space=pltpu.HBM)


def call(kernel, shapes, scratch=(), flops=10**9, far=(), out_specs=None, alias=None):
    alias = alias or {}

    def run(*arrays):
        arrays = [
            pltpu.with_memory_space_constraint(a, pltpu.HBM) if i in far else a
            for i, a in enumerate(arrays)
        ]
        return pl.pallas_call(
            kernel,
            out_shape=[jax.ShapeDtypeStruct(s, jnp.float32) for s in shapes],
            in_specs=[
                HBM if i in far else ANY if i in alias else VMEM for i in range(len(arrays))
            ],
            out_specs=out_specs or [VMEM] * len(shapes),
            scratch_shapes=list(scratch),
            input_output_aliases=alias,
            compiler_params=pltpu.CompilerParams(vmem_limit_bytes=8 * 2**20),
            cost_estimate=pl.CostEstimate(flops=flops, bytes_accessed=flops // 10**3, transcendentals=0),
        )(*arrays)

    return run


def buffer(*shape):
    return pltpu.VMEM(shape, jnp.float32)


def iota(dim):
    return lax.broadcasted_iota(jnp.int32, (16, 128), dim)


def matvec(matrix, vector):
    n = len(vector)
    out = []
    for r in range(n):
        acc = matrix[r][0] * vector[0]
        for c in range(1, n):
            acc = acc + matrix[r][c] * vector[c]
        out.append(acc)
    return out


def block(ref, *lead):
    return [[ref[(*lead, r, c)] for c in range(5)] for r in range(5)]


def cell(ref, *lead):
    return [ref[(*lead, v)] for v in range(5)]


def put(ref, values, *lead):
    for v, value in enumerate(values):
        ref[(*lead, v)] = value


def add(a, b):
    return [x + y for x, y in zip(a, b)]


def pack_faces(load, planes, tile_ref):
    lane = iota(1)
    tile = jnp.zeros((16, 128), jnp.float32)
    for j in range(planes):
        for v in range(5):
            q = 2 * (j * 5 + v)
            here = (lane == q) | (lane == (q - 1) % 128)
            x = load(j, v)
            tile = jnp.where(here, pltpu.roll(x, q, 1) if q else x, tile)
    for w in range(tile_ref.shape[0]):
        tile_ref[w] = tile


def masked(live_ref, values):
    live = live_ref[...] > 0.0
    return [jnp.where(live, x, 0.0) for x in values]


def has_above(values):
    inner = lax.axis_index("ja") < lax.axis_size("ja") - 1
    return [jnp.where(inner, x, 0.0) for x in values]


def first_kernel(tiles_ref, flow_ref, first_ref):
    del tiles_ref
    put(first_ref, cell(flow_ref, 0))


def pack_kernel(flow_ref, tile_ref):
    pack_faces(lambda j, v: flow_ref[j, v], flow_ref.shape[0], tile_ref)


def neighbours(x):
    lane, row = iota(1), iota(0)
    total = jnp.where(lane == 0, 0.0, pltpu.roll(x, 1, 1))
    total = total + jnp.where(lane == 127, 0.0, pltpu.roll(x, 127, 1))
    total = total + jnp.where(row == 0, 0.0, pltpu.roll(x, 1, 0))
    return total + jnp.where(row == 15, 0.0, pltpu.roll(x, 15, 0))


def ghosts_of(pick_ref, tiles_ref):
    low = high = jnp.zeros((16, 128), jnp.float32)
    for w in range(tiles_ref.shape[0]):
        low = jnp.where(pick_ref[0, w] > 0.0, tiles_ref[w], low)
        high = jnp.where(pick_ref[1, w] > 0.0, tiles_ref[w], high)
    return jnp.where(iota(1) % 2 == 0, pltpu.roll(low, 1, 1), pltpu.roll(high, 127, 1))


def ghost_at(ghosts, j, v):
    lane = iota(1)
    q = 2 * (j * 5 + v)
    turned = pltpu.roll(ghosts, 128 - q, 1) if q else ghosts
    return jnp.where((lane == 0) | (lane == 127), turned, 0.0)


def matrix_kernel(
    depth_hbm, east_hbm, tiles_ref, inv_ref, low_ref, up_ref,
    e_ref, f_ref, mats_ref, live_ref, pick_ref,
    y_ref, depth_ref, east_ref, sems,
):
    del tiles_ref
    planes = inv_ref.shape[0]
    scalars = [
        pltpu.make_async_copy(depth_hbm, depth_ref, sems.at[0]),
        pltpu.make_async_copy(east_hbm, east_ref, sems.at[1]),
    ]
    for copy in scalars:
        copy.start()
    last = planes - 1
    halves = [pl.ds(0, 8), pl.ds(8, 8)]

    def col(ref, q, j, rows):
        return [ref[j, r, q, rows] for r in range(5)]

    def put_col(ref, values, q, j, rows):
        for r in range(5):
            ref[j, r, q, rows] = values[r]

    def mat(ref, j, rows):
        return [[ref[j, r, c, rows] for c in range(5)] for r in range(5)]

    def products(j, rows):
        inv = mat(inv_ref, j, rows)
        for jac_ref, out_ref in ((low_ref, e_ref), (up_ref, f_ref)):
            for q in range(5):
                product = matvec(inv, col(jac_ref, q, j, rows))
                put_col(out_ref, [OMEGA * x for x in product], q, j, rows)

    def forward(j, carry):
        for rows in halves:
            products(j, rows)
            e = mat(e_ref, j, rows)
            for q in range(5):
                put_col(y_ref, matvec(e, col(y_ref, q, j - 1, rows)), q, j, rows)
        return carry

    for rows in halves:
        products(0, rows)
        for q in range(5):
            put_col(y_ref, col(e_ref, q, 0, rows), q, 0, rows)
    lax.fori_loop(1, planes, forward, 0)
    for rows in halves:
        for q in range(5):
            put_col(mats_ref, col(y_ref, q, last, rows), q, 0, rows)
            put_col(mats_ref, col(y_ref, q, last, rows), q, 1, rows)
            put_col(mats_ref, col(f_ref, q, last, rows), q, 2, rows)

    def backward(step, carry):
        j = planes - 2 - step
        for rows in halves:
            f = mat(f_ref, j, rows)
            for q in range(5):
                turned = matvec(f, col(mats_ref, q, 1, rows))
                put_col(mats_ref, add(col(y_ref, q, j, rows), turned), q, 1, rows)
                put_col(mats_ref, matvec(f, col(mats_ref, q, 2, rows)), q, 2, rows)
        return carry

    lax.fori_loop(0, planes - 1, backward, 0)
    for copy in scalars:
        copy.wait()
    zone = lax.axis_index("zone")
    row = iota(0)
    live_ref[...] = jnp.where(row < depth_ref[zone], 1.0, 0.0)
    for w in range(pick_ref.shape[1]):
        rows = row < depth_ref[w]
        pick_ref[0, w] = jnp.where(rows & (east_ref[w] == zone), 1.0, 0.0)
        pick_ref[1, w] = jnp.where(rows & (east_ref[zone] == w), 1.0, 0.0)


def by_place(mine_refs, other_refs, run):
    odd = lax.axis_index("ja") % 2

    @pl.when(odd == 0)
    def _():
        run(*mine_refs, *other_refs)

    @pl.when(odd == 1)
    def _():
        run(*other_refs, *mine_refs)


def beta_kernel(mine_ref, other_ref, half_ref):
    odd = lax.axis_index("ja") % 2
    for side in range(2):
        lo, hi = (mine_ref, other_ref) if side == 0 else (other_ref, mine_ref)
        rows = pl.ds(8 * side, 8)

        @pl.when(odd == side)
        def _():
            d_hi = [[hi[1, r, c, rows] for c in range(5)] for r in range(5)]
            n_lo = [[lo[2, r, c, rows] for c in range(5)] for r in range(5)]
            for q in range(5):
                m_col = [lo[0, r, q, rows] for r in range(5)]
                d_col = [lo[1, r, q, rows] for r in range(5)]
                out = add(d_col, matvec(n_lo, matvec(d_hi, m_col)))
                for r in range(5):
                    half_ref[r, q] = out[r]


def sweeps(s_ref, e_ref, f_ref, y_ref, ends_ref, last):
    planes = s_ref.shape[0]
    value = cell(s_ref, 0)
    put(y_ref, value, 0)
    for j in range(1, planes):
        value = add(cell(s_ref, j), matvec(block(e_ref, j), value))
        put(y_ref, value, j)
    put(ends_ref, [x + z * (1.0 / OMEGA) for x, z in zip(value, last)], 0)
    for j in range(planes - 2, -1, -1):
        value = add(cell(y_ref, j), matvec(block(f_ref, j), value))
    put(ends_ref, value, 1)


def local_kernel(
    live_ref, pick_ref, tiles_ref, cur_ref, above_ref, force_ref, diag_ref, inv_ref,
    e_ref, f_ref,
    s_ref, ends_ref, y_ref,
):
    planes = cur_ref.shape[0]
    ghosts = ghosts_of(pick_ref, tiles_ref)
    before, here = None, masked(live_ref, cell(cur_ref, 0))
    for j in range(planes):
        after = cell(cur_ref, j + 1) if j < planes - 1 else has_above(cell(above_ref))
        after = masked(live_ref, after)
        own = matvec(block(diag_ref, j), here)
        res = []
        for v in range(5):
            sides = neighbours(here[v]) + ghost_at(ghosts, j, v)
            res.append(force_ref[j, v] - own[v] + COUPLE * sides)
        linked = matvec(block(f_ref, j), after)
        if before is not None:
            linked = add(linked, matvec(block(e_ref, j), before))
        linked = [x * (1.0 / OMEGA) for x in linked]
        put(s_ref, add(matvec(block(inv_ref, j), masked(live_ref, res)), linked), j)
        before, here = here, after
    sweeps(s_ref, e_ref, f_ref, y_ref, ends_ref, masked(live_ref, cell(cur_ref, planes - 1)))


def second_kernel(
    half_ref, live_ref, pick_ref, tiles_ref, cur_ref, above_ref, force_ref, diag_ref, low_ref, up_ref,
    inv_ref, e_ref, f_ref,
    res_ref, s_ref, ends_ref, low0_ref, y_ref,
):
    del half_ref
    planes = cur_ref.shape[0]
    ghosts = ghosts_of(pick_ref, tiles_ref)
    for r in range(5):
        put(low0_ref, cell(low_ref, 0, r), r)
    for j in range(planes):
        here = cell(cur_ref, j)
        applied = matvec(block(diag_ref, j), here)
        if j > 0:
            lower = matvec(block(low_ref, j), cell(cur_ref, j - 1))
            applied = [x - z for x, z in zip(applied, lower)]
        above = cell(cur_ref, j + 1) if j < planes - 1 else cell(above_ref)
        upper = matvec(block(up_ref, j), above)
        res = []
        for v in range(5):
            sides = neighbours(here[v]) + ghost_at(ghosts, j, v)
            all_of = applied[v] - upper[v] - COUPLE * sides
            res.append(force_ref[j, v] - all_of)
        res = masked(live_ref, res)
        put(res_ref, res, j)
        put(s_ref, matvec(block(inv_ref, j), res), j)
    last = cell(cur_ref, planes - 1)
    sweeps(s_ref, e_ref, f_ref, y_ref, ends_ref, last)
    put(ends_ref, last, 2)


def write_kernel(res_ref, res_hbm, sem):
    copy = pltpu.make_async_copy(res_ref, res_hbm, sem)
    copy.start()
    copy.wait()


def mid_kernel(ends_ref, ends_other_ref, mats_ref, mats_other_ref, out_ref):
    def run(ends_lo, mats_lo, ends_hi, mats_hi):
        c_lo = cell(ends_lo, 0)

        @pl.when(lax.axis_index("ja") < 2)
        def _():
            put(out_ref, add(cell(ends_hi, 0), matvec(block(mats_hi, 0), c_lo)), 0)

        @pl.when(lax.axis_index("ja") >= 2)
        def _():
            turned = add(cell(ends_hi, 1), matvec(block(mats_hi, 1), c_lo))
            put(out_ref, add(cell(ends_lo, 1), matvec(block(mats_lo, 2), turned)), 0)

        if out_ref.shape[0] > 1:
            put(out_ref, cell(ends_hi, 2), 1)

    by_place([ends_ref, mats_ref], [ends_other_ref, mats_other_ref], run)


def raise_kernel(pair_ref, pair_other_ref, half_ref, raised_ref):
    odd = lax.axis_index("ja") % 2
    for side in range(2):
        rows = pl.ds(8 * side, 8)

        @pl.when(odd == side)
        def _():
            inflow = [pair_ref[0, v, rows] for v in range(5)]
            alpha = [pair_other_ref[0, v, rows] for v in range(5)]
            put(raised_ref, add(alpha, matvec(block(half_ref), inflow)))


def join(mine_ref, other_ref, *at):
    mine, other = mine_ref[at], other_ref[at]
    odd = lax.axis_index("ja") % 2 == 1
    return jnp.concatenate([jnp.where(odd, other, mine), jnp.where(odd, mine, other)], axis=0)


def inflows(
    ends_ref, ends_other_ref, mats_ref, mats_other_ref, pair_ref, pair_other_ref, far, inflow_ref
):
    ja = lax.axis_index("ja")
    zeros = [jnp.zeros((16, 128), jnp.float32)] * 5

    @pl.when(ja == 0)
    def _():
        put(inflow_ref, zeros, 0)
        b = add(cell(ends_other_ref, 1), matvec(block(mats_other_ref, 1), cell(ends_ref, 0)))
        b = add(b, matvec(block(mats_other_ref, 2), far()))
        put(inflow_ref, b, 1)

    @pl.when(ja == 1)
    def _():
        put(inflow_ref, cell(ends_other_ref, 0), 0)
        put(inflow_ref, far(), 1)

    @pl.when(ja == 2)
    def _():
        a = cell(pair_other_ref, 0)
        put(inflow_ref, a, 0)
        a = add(cell(ends_ref, 0), matvec(block(mats_ref, 0), a))
        b = add(cell(ends_other_ref, 1), matvec(block(mats_other_ref, 1), a))
        put(inflow_ref, b, 1)

    @pl.when(ja == 3)
    def _():
        a = add(cell(ends_other_ref, 0), matvec(block(mats_other_ref, 0), cell(pair_other_ref, 0)))
        put(inflow_ref, a, 0)
        put(inflow_ref, zeros, 1)


def final_kernel(
    live_ref, cur_ref, above_ref, s_ref, e_ref, f_ref,
    ends_ref, ends_other_ref, mats_ref, mats_other_ref, pair_ref, pair_other_ref,
    raised_ref, raised_other_ref,
    new_ref, above_new_ref, tile_ref, y_ref, inflow_ref,
):
    planes = cur_ref.shape[0]
    inflows(
        ends_ref, ends_other_ref, mats_ref, mats_other_ref, pair_ref, pair_other_ref,
        lambda: [join(raised_ref, raised_other_ref, v) for v in range(5)], inflow_ref,
    )
    value = cell(inflow_ref, 0)
    for j in range(planes):
        value = add(cell(s_ref, j), matvec(block(e_ref, j), value))
        put(y_ref, value, j)
    value = cell(inflow_ref, 1)
    put(above_new_ref, add(masked(live_ref, has_above(cell(above_ref))), value))
    for j in range(planes - 1, -1, -1):
        value = add(cell(y_ref, j), matvec(block(f_ref, j), value))
        put(new_ref, add(masked(live_ref, cell(cur_ref, j)), value), j)
    pack_faces(lambda j, v: new_ref[j, v], planes, tile_ref)


def last_kernel(
    live_ref, low0_ref, cur_ref, res_ref, s_ref, e_ref, f_ref,
    ends_ref, ends_other_ref, mats_ref, mats_other_ref, pair_ref, pair_other_ref,
    half_ref, half_other_ref, res_in_hbm,
    new_hbm, res_hbm, y_ref, inflow_ref, new_ref, res0_ref, sems,
):
    del res_in_hbm
    planes = cur_ref.shape[0]
    ja = lax.axis_index("ja")
    before = [
        jnp.where(ja == 0, 0.0, jnp.where(ja == 2, pair_other_ref[1, v], ends_other_ref[2, v]))
        for v in range(5)
    ]
    put(res0_ref, add(cell(res_ref, 0), masked(live_ref, matvec(block(low0_ref), before))))
    copies = [pltpu.make_async_copy(res0_ref, res_hbm.at[0], sems.at[planes])]
    copies[0].start()

    def far():
        beta = [[join(half_ref, half_other_ref, r, c) for c in range(5)] for r in range(5)]
        return add(cell(pair_other_ref, 0), matvec(beta, cell(pair_ref, 0)))

    inflows(
        ends_ref, ends_other_ref, mats_ref, mats_other_ref, pair_ref, pair_other_ref,
        far, inflow_ref,
    )
    value = cell(inflow_ref, 0)
    for j in range(planes):
        value = add(cell(s_ref, j), matvec(block(e_ref, j), value))
        put(y_ref, value, j)
    value = cell(inflow_ref, 1)
    for j in range(planes - 1, -1, -1):
        value = add(cell(y_ref, j), matvec(block(f_ref, j), value))
        put(new_ref, add(cell(cur_ref, j), value), j)
        copies.append(pltpu.make_async_copy(new_ref.at[j], new_hbm.at[j], sems.at[j]))
        copies[-1].start()
    for copy in copies:
        copy.wait()


def per_device(
    flow_state, forcing, diag_block, lower_jac, upper_jac, block_inv, east_zone, zone_depth
):
    zones, parts = lax.axis_size("zone"), lax.axis_size("ja")
    assert parts == 4 and ITERS == 2
    current, force, diag, low, up, inv = (
        x[0] for x in (flow_state, forcing, diag_block, lower_jac, upper_jac, block_inv)
    )
    state = current.shape
    planes, plane, blocks, tiles = state[0], state[1:], diag.shape, (zones, *state[2:])
    matrix = blocks[1:]
    work = [buffer(*state)]

    def swap(x, bit):
        return lax.ppermute(x, "ja", [(p, p ^ bit) for p in range(parts)])

    def faces(x):
        return lax.all_to_all(x, "zone", 0, 0, tiled=True)

    tile = call(pack_kernel, [tiles], flops=2 * 10**10)(current)[0]
    got = faces(tile)
    first = call(first_kernel, [plane], flops=10**5)(got, current)[0]
    above = lax.ppermute(first, "ja", [((p + 1) % parts, p) for p in range(parts)])
    e, f, mats, live, pick = call(
        matrix_kernel,
        [blocks, blocks, (3, *matrix), state[2:], (2, *tiles)],
        [buffer(*blocks)]
        + [pltpu.SMEM((zones,), jnp.int32)] * 2
        + [pltpu.SemaphoreType.DMA((2,))],
        flops=5 * 10**9,
        far=(0, 1),
    )(zone_depth, east_zone, got, inv, low, up)
    mats_other = swap(mats, 1)
    s, ends = call(local_kernel, [state, (2, *plane)], work, flops=2 * 10**10)(
        live, pick, got, current, above, force, diag, inv, e, f
    )
    ends_other = swap(ends, 1)
    half = call(beta_kernel, [(*matrix[:2], 8, matrix[3])], flops=10**5)(mats, mats_other)[0]
    half = swap(half, 2)
    pair = call(mid_kernel, [(1, *plane)], flops=10**5)(ends, ends_other, mats, mats_other)[0]
    pair_other = swap(pair, 2)
    raised = call(raise_kernel, [(plane[0], 8, plane[2])], flops=10**5)(pair, pair_other, half)[0]
    raised_other = swap(raised, 1)
    half_other = swap(half, 1)
    flows = [buffer(2, *plane)]
    current, above, tile = call(final_kernel, [state, plane, tiles], work + flows)(
        live, current, above, s, e, f,
        ends, ends_other, mats, mats_other, pair, pair_other, raised, raised_other,
    )

    got = faces(tile)
    residual, s, ends, low0 = call(
        second_kernel, [state, state, (3, *plane), matrix], work
    )(
        half_other, live, pick, got, current, above, force, diag, low, up, inv, e, f
    )
    ends_other = swap(ends, 1)
    pair = call(mid_kernel, [(2, *plane)])(ends, ends_other, mats, mats_other)[0]
    pair_other = swap(pair, 2)
    written = call(write_kernel, [state], [pltpu.SemaphoreType.DMA], out_specs=[HBM])(residual)[0]
    current, residual = call(
        last_kernel,
        [state, state],
        work + flows + work + [buffer(*plane), pltpu.SemaphoreType.DMA((planes + 1,))],
        out_specs=[HBM, HBM],
        alias={15: 1},
    )(
        live, low0, current, residual, s, e, f,
        ends, ends_other, mats, mats_other, pair, pair_other, half, half_other, written,
    )
    return (current[None], residual[None])


def solution(mesh):
    state = P("zone", "ja", None, None, None)
    blocks = P("zone", "ja", None, None, None, None)
    return jax.shard_map(
        per_device,
        mesh=mesh,
        in_specs=(state, state, blocks, blocks, blocks, blocks, P(), P()),
        out_specs=(state, state),
        check_vma=False,
    )
```

```python
import jax
import jax.numpy as jnp
from jax import lax
from jax.experimental import pallas as pl
from jax.experimental.pallas import tpu as pltpu
from jax.sharding import PartitionSpec as P

ITERS = 2
OMEGA = 1.2
COUPLE = 0.25

VMEM = pl.BlockSpec(memory_space=pltpu.VMEM)
ANY = pl.BlockSpec(memory_space=pl.ANY)
HBM = pl.BlockSpec(memory_space=pltpu.HBM)


def call(kernel, shapes, scratch=(), flops=10**9, far=(), out_specs=None, alias=None):
    alias = alias or {}

    def run(*arrays):
        arrays = [
            pltpu.with_memory_space_constraint(a, pltpu.HBM) if i in far else a
            for i, a in enumerate(arrays)
        ]
        return pl.pallas_call(
            kernel,
            out_shape=[jax.ShapeDtypeStruct(s, jnp.float32) for s in shapes],
            in_specs=[
                HBM if i in far else ANY if i in alias else VMEM for i in range(len(arrays))
            ],
            out_specs=out_specs or [VMEM] * len(shapes),
            scratch_shapes=list(scratch),
            input_output_aliases=alias,
            compiler_params=pltpu.CompilerParams(vmem_limit_bytes=8 * 2**20),
            cost_estimate=pl.CostEstimate(flops=flops, bytes_accessed=flops // 10**3, transcendentals=0),
        )(*arrays)

    return run


def buffer(*shape):
    return pltpu.VMEM(shape, jnp.float32)


def iota(dim):
    return lax.broadcasted_iota(jnp.int32, (16, 128), dim)


def matvec(matrix, vector):
    n = len(vector)
    out = []
    for r in range(n):
        acc = matrix[r][0] * vector[0]
        for c in range(1, n):
            acc = acc + matrix[r][c] * vector[c]
        out.append(acc)
    return out


def block(ref, *lead):
    return [[ref[(*lead, r, c)] for c in range(5)] for r in range(5)]


def cell(ref, *lead):
    return [ref[(*lead, v)] for v in range(5)]


def put(ref, values, *lead):
    for v, value in enumerate(values):
        ref[(*lead, v)] = value


def add(a, b):
    return [x + y for x, y in zip(a, b)]


def pack_faces(load, planes, tile_ref):
    lane = iota(1)
    tile = jnp.zeros((16, 128), jnp.float32)
    for j in range(planes):
        for v in range(5):
            q = 2 * (j * 5 + v)
            here = (lane == q) | (lane == (q - 1) % 128)
            x = load(j, v)
            tile = jnp.where(here, pltpu.roll(x, q, 1) if q else x, tile)
    tile_ref[0] = tile


def masked(live_ref, values):
    live = live_ref[...] > 0.0
    return [jnp.where(live, x, 0.0) for x in values]


def has_above(values):
    inner = lax.axis_index("ja") < lax.axis_size("ja") - 1
    return [jnp.where(inner, x, 0.0) for x in values]


def pack_kernel(flow_ref, tile_ref, first_ref):
    put(first_ref, cell(flow_ref, 0))
    pack_faces(lambda j, v: flow_ref[j, v], flow_ref.shape[0], tile_ref)


def merge_kernel(own_ref, got_ref, after_ref, out_ref):
    del after_ref
    count = own_ref.shape[0]
    for w in range(count):
        out_ref[w] = own_ref[w]
        out_ref[count + w] = got_ref[w]


def neighbours(x):
    lane, row = iota(1), iota(0)
    total = jnp.where(lane == 0, 0.0, pltpu.roll(x, 1, 1))
    total = total + jnp.where(lane == 127, 0.0, pltpu.roll(x, 127, 1))
    total = total + jnp.where(row == 0, 0.0, pltpu.roll(x, 1, 0))
    return total + jnp.where(row == 15, 0.0, pltpu.roll(x, 15, 0))


def ghosts_of(pick_ref, own_ref, got_ref):
    low = high = jnp.zeros((16, 128), jnp.float32)
    count = own_ref.shape[0]
    for w in range(2 * count):
        tile = own_ref[w] if w < count else got_ref[w - count]
        low = jnp.where(pick_ref[0, w] > 0.0, tile, low)
        high = jnp.where(pick_ref[1, w] > 0.0, tile, high)
    return jnp.where(iota(1) % 2 == 0, pltpu.roll(low, 1, 1), pltpu.roll(high, 127, 1))


def ghost_at(ghosts, j, v):
    lane = iota(1)
    q = 2 * (j * 5 + v)
    turned = pltpu.roll(ghosts, 128 - q, 1) if q else ghosts
    return jnp.where((lane == 0) | (lane == 127), turned, 0.0)


HALVES = [pl.ds(0, 8), pl.ds(8, 8)]


def col(ref, q, j, rows):
    return [ref[j, r, q, rows] for r in range(5)]


def put_col(ref, values, q, j, rows):
    for r in range(5):
        ref[j, r, q, rows] = values[r]


def mat(ref, j, rows):
    return [[ref[j, r, c, rows] for c in range(5)] for r in range(5)]


def product_kernel(
    depth_hbm, east_hbm, tile_ref, inv_ref, low_ref, up_ref,
    e_ref, f_ref, live_ref, pick_ref,
    depth_ref, east_ref, sems,
):
    del tile_ref
    scalars = [
        pltpu.make_async_copy(depth_hbm, depth_ref, sems.at[0]),
        pltpu.make_async_copy(east_hbm, east_ref, sems.at[1]),
    ]
    for copy in scalars:
        copy.start()

    def products(j, carry):
        for rows in HALVES:
            inv = mat(inv_ref, j, rows)
            for jac_ref, out_ref in ((low_ref, e_ref), (up_ref, f_ref)):
                for q in range(5):
                    product = matvec(inv, col(jac_ref, q, j, rows))
                    put_col(out_ref, [OMEGA * x for x in product], q, j, rows)
        return carry

    lax.fori_loop(0, inv_ref.shape[0], products, 0)
    for copy in scalars:
        copy.wait()
    zone = lax.axis_index("zone")
    row = iota(0)
    live_ref[...] = jnp.where(row < depth_ref[zone], 1.0, 0.0)
    for i in range(pick_ref.shape[1]):
        w = zone ^ i
        rows = row < depth_ref[w]
        pick_ref[0, i] = jnp.where(rows & (east_ref[w] == zone), 1.0, 0.0)
        pick_ref[1, i] = jnp.where(rows & (east_ref[zone] == w), 1.0, 0.0)


def matrix_kernel(tiles_ref, e_ref, f_ref, mats_ref, y_ref):
    del tiles_ref
    last = e_ref.shape[0] - 1
    for rows in HALVES:
        for q in range(5):
            put_col(y_ref, col(e_ref, q, 0, rows), q, 0, rows)

    def forward(j, carry):
        for rows in HALVES:
            e = mat(e_ref, j, rows)
            for q in range(5):
                put_col(y_ref, matvec(e, col(y_ref, q, j - 1, rows)), q, j, rows)
        return carry

    lax.fori_loop(1, last + 1, forward, 0)
    for rows in HALVES:
        for q in range(5):
            put_col(mats_ref, col(y_ref, q, last, rows), q, 0, rows)
            put_col(mats_ref, col(y_ref, q, last, rows), q, 1, rows)
            put_col(mats_ref, col(f_ref, q, last, rows), q, 2, rows)

    def backward(step, carry):
        j = last - 1 - step
        for rows in HALVES:
            f = mat(f_ref, j, rows)
            for q in range(5):
                turned = matvec(f, col(mats_ref, q, 1, rows))
                put_col(mats_ref, add(col(y_ref, q, j, rows), turned), q, 1, rows)
                put_col(mats_ref, matvec(f, col(mats_ref, q, 2, rows)), q, 2, rows)
        return carry

    lax.fori_loop(0, last, backward, 0)


def by_place(mine_refs, other_refs, run):
    odd = lax.axis_index("ja") % 2

    @pl.when(odd == 0)
    def _():
        run(*mine_refs, *other_refs)

    @pl.when(odd == 1)
    def _():
        run(*other_refs, *mine_refs)


def beta_kernel(mine_ref, other_ref, half_ref):
    odd = lax.axis_index("ja") % 2
    for side in range(2):
        lo, hi = (mine_ref, other_ref) if side == 0 else (other_ref, mine_ref)
        rows = pl.ds(8 * side, 8)

        @pl.when(odd == side)
        def _():
            d_hi = [[hi[1, r, c, rows] for c in range(5)] for r in range(5)]
            n_lo = [[lo[2, r, c, rows] for c in range(5)] for r in range(5)]
            for q in range(5):
                m_col = [lo[0, r, q, rows] for r in range(5)]
                d_col = [lo[1, r, q, rows] for r in range(5)]
                out = add(d_col, matvec(n_lo, matvec(d_hi, m_col)))
                for r in range(5):
                    half_ref[r, q] = out[r]


def sweeps(s_ref, e_ref, f_ref, y_ref, ends_ref, last):
    planes = s_ref.shape[0]
    value = cell(s_ref, 0)
    put(y_ref, value, 0)
    for j in range(1, planes):
        value = add(cell(s_ref, j), matvec(block(e_ref, j), value))
        put(y_ref, value, j)
    put(ends_ref, [x + z * (1.0 / OMEGA) for x, z in zip(value, last)], 0)
    for j in range(planes - 2, -1, -1):
        value = add(cell(y_ref, j), matvec(block(f_ref, j), value))
    put(ends_ref, value, 1)


def source_kernel(
    tiles_ref, live_ref, cur_ref, force_ref, diag_ref, inv_ref, e_ref, f_ref, s_ref
):
    del tiles_ref
    planes = cur_ref.shape[0]
    before, here = None, masked(live_ref, cell(cur_ref, 0))
    for j in range(planes):
        own = matvec(block(diag_ref, j), here)
        res = [force_ref[j, v] - own[v] + COUPLE * neighbours(here[v]) for v in range(5)]
        out = matvec(block(inv_ref, j), masked(live_ref, res))
        if j > 0:
            linked = matvec(block(e_ref, j), before)
            out = add(out, [x * (1.0 / OMEGA) for x in linked])
        if j < planes - 1:
            after = masked(live_ref, cell(cur_ref, j + 1))
            linked = matvec(block(f_ref, j), after)
            out = add(out, [x * (1.0 / OMEGA) for x in linked])
            before, here = here, after
        put(s_ref, out, j)


def add_ghosts(live_ref, ghosts, s0_ref, inv_ref, s_ref, res0_ref=None, res_ref=None):
    ghosts = jnp.where(live_ref[...] > 0.0, COUPLE * ghosts, 0.0)
    for j in range(s_ref.shape[0]):
        extra = [ghost_at(ghosts, j, v) for v in range(5)]
        if res_ref is not None:
            put(res_ref, add(cell(res0_ref, j), extra), j)
        put(s_ref, add(cell(s0_ref, j), matvec(block(inv_ref, j), extra)), j)


def local_kernel(
    half_ref, live_ref, pick_ref, own_ref, got_ref, cur_ref, above_ref, s0_ref,
    inv_ref, e_ref, f_ref,
    s_ref, ends_ref, y_ref,
):
    del half_ref
    last = cur_ref.shape[0] - 1
    add_ghosts(live_ref, ghosts_of(pick_ref, own_ref, got_ref), s0_ref, inv_ref, s_ref)
    above = masked(live_ref, has_above(cell(above_ref)))
    linked = matvec(block(f_ref, last), above)
    put(s_ref, add(cell(s_ref, last), [x * (1.0 / OMEGA) for x in linked]), last)
    sweeps(s_ref, e_ref, f_ref, y_ref, ends_ref, masked(live_ref, cell(cur_ref, last)))


def residual_kernel(
    live_ref, cur_ref, above_ref, force_ref, diag_ref, low_ref, up_ref, inv_ref,
    res_ref, s_ref, low0_ref,
):
    planes = cur_ref.shape[0]
    for r in range(5):
        put(low0_ref, cell(low_ref, 0, r), r)
    for j in range(planes):
        here = cell(cur_ref, j)
        applied = matvec(block(diag_ref, j), here)
        if j > 0:
            lower = matvec(block(low_ref, j), cell(cur_ref, j - 1))
            applied = [x - z for x, z in zip(applied, lower)]
        above = cell(cur_ref, j + 1) if j < planes - 1 else cell(above_ref)
        upper = matvec(block(up_ref, j), above)
        res = []
        for v in range(5):
            all_of = applied[v] - upper[v] - COUPLE * neighbours(here[v])
            res.append(force_ref[j, v] - all_of)
        res = masked(live_ref, res)
        put(res_ref, res, j)
        put(s_ref, matvec(block(inv_ref, j), res), j)


def second_kernel(
    half_ref, live_ref, pick_ref, own_ref, got_ref, cur_ref, res0_ref, s0_ref,
    inv_ref, e_ref, f_ref,
    res_ref, s_ref, ends_ref, y_ref,
):
    del half_ref
    ghosts = ghosts_of(pick_ref, own_ref, got_ref)
    add_ghosts(live_ref, ghosts, s0_ref, inv_ref, s_ref, res0_ref, res_ref)
    last = cell(cur_ref, cur_ref.shape[0] - 1)
    sweeps(s_ref, e_ref, f_ref, y_ref, ends_ref, last)
    put(ends_ref, last, 2)


def write_kernel(res_ref, res_hbm, sem):
    copy = pltpu.make_async_copy(res_ref, res_hbm, sem)
    copy.start()
    copy.wait()


def mid_kernel(ends_ref, ends_other_ref, mats_ref, mats_other_ref, out_ref):
    def run(ends_lo, mats_lo, ends_hi, mats_hi):
        c_lo = cell(ends_lo, 0)

        @pl.when(lax.axis_index("ja") < 2)
        def _():
            put(out_ref, add(cell(ends_hi, 0), matvec(block(mats_hi, 0), c_lo)), 0)

        @pl.when(lax.axis_index("ja") >= 2)
        def _():
            turned = add(cell(ends_hi, 1), matvec(block(mats_hi, 1), c_lo))
            put(out_ref, add(cell(ends_lo, 1), matvec(block(mats_lo, 2), turned)), 0)

        if out_ref.shape[0] > 1:
            put(out_ref, cell(ends_hi, 2), 1)

    by_place([ends_ref, mats_ref], [ends_other_ref, mats_other_ref], run)


def raise_kernel(pair_ref, pair_other_ref, half_ref, raised_ref):
    odd = lax.axis_index("ja") % 2
    for side in range(2):
        rows = pl.ds(8 * side, 8)

        @pl.when(odd == side)
        def _():
            inflow = [pair_ref[0, v, rows] for v in range(5)]
            alpha = [pair_other_ref[0, v, rows] for v in range(5)]
            put(raised_ref, add(alpha, matvec(block(half_ref), inflow)))


def join(mine_ref, other_ref, *at):
    mine, other = mine_ref[at], other_ref[at]
    odd = lax.axis_index("ja") % 2 == 1
    return jnp.concatenate([jnp.where(odd, other, mine), jnp.where(odd, mine, other)], axis=0)


def inflows(
    ends_ref, ends_other_ref, mats_ref, mats_other_ref, pair_ref, pair_other_ref, far, inflow_ref
):
    ja = lax.axis_index("ja")
    zeros = [jnp.zeros((16, 128), jnp.float32)] * 5

    @pl.when(ja == 0)
    def _():
        put(inflow_ref, zeros, 0)
        b = add(cell(ends_other_ref, 1), matvec(block(mats_other_ref, 1), cell(ends_ref, 0)))
        b = add(b, matvec(block(mats_other_ref, 2), far()))
        put(inflow_ref, b, 1)

    @pl.when(ja == 1)
    def _():
        put(inflow_ref, cell(ends_other_ref, 0), 0)
        put(inflow_ref, far(), 1)

    @pl.when(ja == 2)
    def _():
        a = cell(pair_other_ref, 0)
        put(inflow_ref, a, 0)
        a = add(cell(ends_ref, 0), matvec(block(mats_ref, 0), a))
        b = add(cell(ends_other_ref, 1), matvec(block(mats_other_ref, 1), a))
        put(inflow_ref, b, 1)

    @pl.when(ja == 3)
    def _():
        a = add(cell(ends_other_ref, 0), matvec(block(mats_other_ref, 0), cell(pair_other_ref, 0)))
        put(inflow_ref, a, 0)
        put(inflow_ref, zeros, 1)


def final_kernel(
    live_ref, cur_ref, above_ref, s_ref, e_ref, f_ref,
    ends_ref, ends_other_ref, mats_ref, mats_other_ref, pair_ref, pair_other_ref,
    raised_ref, raised_other_ref,
    new_ref, above_new_ref, tile_ref, y_ref, inflow_ref,
):
    planes = cur_ref.shape[0]
    inflows(
        ends_ref, ends_other_ref, mats_ref, mats_other_ref, pair_ref, pair_other_ref,
        lambda: [join(raised_ref, raised_other_ref, v) for v in range(5)], inflow_ref,
    )
    value = cell(inflow_ref, 0)
    for j in range(planes):
        value = add(cell(s_ref, j), matvec(block(e_ref, j), value))
        put(y_ref, value, j)
    value = cell(inflow_ref, 1)
    put(above_new_ref, add(masked(live_ref, has_above(cell(above_ref))), value))
    for j in range(planes - 1, -1, -1):
        value = add(cell(y_ref, j), matvec(block(f_ref, j), value))
        put(new_ref, add(masked(live_ref, cell(cur_ref, j)), value), j)
    pack_faces(lambda j, v: new_ref[j, v], planes, tile_ref)


def last_kernel(
    live_ref, low0_ref, cur_ref, res_ref, s_ref, e_ref, f_ref,
    ends_ref, ends_other_ref, mats_ref, mats_other_ref, pair_ref, pair_other_ref,
    half_ref, half_other_ref, res_in_hbm,
    new_hbm, res_hbm, y_ref, inflow_ref, new_ref, res0_ref, sems,
):
    del res_in_hbm
    planes = cur_ref.shape[0]
    ja = lax.axis_index("ja")
    before = [
        jnp.where(ja == 0, 0.0, jnp.where(ja == 2, pair_other_ref[1, v], ends_other_ref[2, v]))
        for v in range(5)
    ]
    put(res0_ref, add(cell(res_ref, 0), masked(live_ref, matvec(block(low0_ref), before))))
    copies = [pltpu.make_async_copy(res0_ref, res_hbm.at[0], sems.at[planes])]
    copies[0].start()

    def far():
        beta = [[join(half_ref, half_other_ref, r, c) for c in range(5)] for r in range(5)]
        return add(cell(pair_other_ref, 0), matvec(beta, cell(pair_ref, 0)))

    inflows(
        ends_ref, ends_other_ref, mats_ref, mats_other_ref, pair_ref, pair_other_ref,
        far, inflow_ref,
    )
    value = cell(inflow_ref, 0)
    for j in range(planes):
        value = add(cell(s_ref, j), matvec(block(e_ref, j), value))
        put(y_ref, value, j)
    value = cell(inflow_ref, 1)
    for j in range(planes - 1, -1, -1):
        value = add(cell(y_ref, j), matvec(block(f_ref, j), value))
        put(new_ref, add(cell(cur_ref, j), value), j)
        copies.append(pltpu.make_async_copy(new_ref.at[j], new_hbm.at[j], sems.at[j]))
        copies[-1].start()
    for copy in copies:
        copy.wait()


def per_device(
    flow_state, forcing, diag_block, lower_jac, upper_jac, block_inv, east_zone, zone_depth
):
    zones, parts = lax.axis_size("zone"), lax.axis_size("ja")
    assert parts == 4 and ITERS == 2 and zones > 4 and zones & (zones - 1) == 0
    current, force, diag, low, up, inv = (
        x[0] for x in (flow_state, forcing, diag_block, lower_jac, upper_jac, block_inv)
    )
    state = current.shape
    planes, plane, blocks = state[0], state[1:], diag.shape
    matrix = blocks[1:]
    work = [buffer(*state)]

    def swap(x, bit):
        return lax.ppermute(x, "ja", [(p, p ^ bit) for p in range(parts)])

    def doubled(tiles, works):
        stride = 1
        while True:
            pairs = [(z, z ^ stride) for z in range(zones)]
            got = lax.ppermute(tiles, "zone", pairs)
            stride *= 2
            if stride == zones:
                return tiles, got
            after = works.pop(0)(tiles) if works else tiles
            both = [(stride, *tiles.shape[1:])]
            tiles = call(merge_kernel, both, flops=10**5)(tiles, got, after)[0]

    small = {}

    def block_products(tiles):
        small["products"] = call(
            product_kernel,
            [blocks, blocks, state[2:], (2, zones, *state[2:])],
            [pltpu.SMEM((zones,), jnp.int32)] * 2 + [pltpu.SemaphoreType.DMA((2,))],
            flops=2 * 10**9,
            far=(0, 1),
        )(zone_depth, east_zone, tiles, inv, low, up)
        return small["products"][0]

    def matrices(tiles):
        e, f = small["products"][:2]
        small["mats"] = call(
            matrix_kernel, [(3, *matrix)], [buffer(*blocks)], flops=2 * 10**9
        )(tiles, e, f)[0]
        return small["mats"]

    tile, first = call(pack_kernel, [(1, *state[2:]), plane], flops=10**10)(current)
    above = lax.ppermute(first, "ja", [((p + 1) % parts, p) for p in range(parts)])
    tiles, got = doubled(tile, [block_products, matrices])
    e, f, live, pick = small["products"]
    mats = small["mats"]
    mats_other = swap(mats, 1)
    s0 = call(source_kernel, [state])(tiles, live, current, force, diag, inv, e, f)[0]
    half = call(beta_kernel, [(*matrix[:2], 8, matrix[3])], flops=10**5)(mats, mats_other)[0]
    s, ends = call(local_kernel, [state, (2, *plane)], work)(
        half, live, pick, tiles, got, current, above, s0, inv, e, f
    )
    ends_other = swap(ends, 1)
    half = swap(half, 2)
    pair = call(mid_kernel, [(1, *plane)], flops=10**5)(ends, ends_other, mats, mats_other)[0]
    pair_other = swap(pair, 2)
    raised = call(raise_kernel, [(plane[0], 8, plane[2])], flops=10**5)(pair, pair_other, half)[0]
    raised_other = swap(raised, 1)
    half_other = swap(half, 1)
    flows = [buffer(2, *plane)]
    current, above, tile = call(final_kernel, [state, plane, tile.shape], work + flows)(
        live, current, above, s, e, f,
        ends, ends_other, mats, mats_other, pair, pair_other, raised, raised_other,
    )

    residual, s0, low0 = call(residual_kernel, [state, state, matrix])(
        live, current, above, force, diag, low, up, inv
    )
    tiles, got = doubled(tile, [])
    residual, s, ends = call(second_kernel, [state, state, (3, *plane)], work)(
        half_other, live, pick, tiles, got, current, residual, s0, inv, e, f
    )
    ends_other = swap(ends, 1)
    pair = call(mid_kernel, [(2, *plane)])(ends, ends_other, mats, mats_other)[0]
    pair_other = swap(pair, 2)
    written = call(write_kernel, [state], [pltpu.SemaphoreType.DMA], out_specs=[HBM])(residual)[0]
    current, residual = call(
        last_kernel,
        [state, state],
        work + flows + work + [buffer(*plane), pltpu.SemaphoreType.DMA((planes + 1,))],
        out_specs=[HBM, HBM],
        alias={15: 1},
    )(
        live, low0, current, residual, s, e, f,
        ends, ends_other, mats, mats_other, pair, pair_other, half, half_other, written,
    )
    return (current[None], residual[None])


def solution(mesh):
    state = P("zone", "ja", None, None, None)
    blocks = P("zone", "ja", None, None, None, None)
    return jax.shard_map(
        per_device,
        mesh=mesh,
        in_specs=(state, state, blocks, blocks, blocks, blocks, P(), P()),
        out_specs=(state, state),
        check_vma=False,
    )
```

```python
import jax
import jax.numpy as jnp
from jax import lax
from jax.experimental import pallas as pl
from jax.experimental.pallas import tpu as pltpu
from jax.sharding import PartitionSpec as P

ITERS = 2
OMEGA = 1.2
COUPLE = 0.25

VMEM = pl.BlockSpec(memory_space=pltpu.VMEM)
ANY = pl.BlockSpec(memory_space=pl.ANY)
HBM = pl.BlockSpec(memory_space=pltpu.HBM)


def call(kernel, shapes, scratch=(), flops=10**9, far=(), out_specs=None, alias=None):
    alias = alias or {}

    def run(*arrays):
        arrays = [
            pltpu.with_memory_space_constraint(a, pltpu.HBM) if i in far else a
            for i, a in enumerate(arrays)
        ]
        return pl.pallas_call(
            kernel,
            out_shape=[jax.ShapeDtypeStruct(s, jnp.float32) for s in shapes],
            in_specs=[
                HBM if i in far else ANY if i in alias else VMEM for i in range(len(arrays))
            ],
            out_specs=out_specs or [VMEM] * len(shapes),
            scratch_shapes=list(scratch),
            input_output_aliases=alias,
            compiler_params=pltpu.CompilerParams(vmem_limit_bytes=8 * 2**20),
            cost_estimate=pl.CostEstimate(flops=flops, bytes_accessed=flops // 10**3, transcendentals=0),
        )(*arrays)

    return run


def buffer(*shape):
    return pltpu.VMEM(shape, jnp.float32)


def iota(dim):
    return lax.broadcasted_iota(jnp.int32, (16, 128), dim)


def matvec(matrix, vector):
    n = len(vector)
    out = []
    for r in range(n):
        acc = matrix[r][0] * vector[0]
        for c in range(1, n):
            acc = acc + matrix[r][c] * vector[c]
        out.append(acc)
    return out


def block(ref, *lead):
    return [[ref[(*lead, r, c)] for c in range(5)] for r in range(5)]


def cell(ref, *lead):
    return [ref[(*lead, v)] for v in range(5)]


def put(ref, values, *lead):
    for v, value in enumerate(values):
        ref[(*lead, v)] = value


def add(a, b):
    return [x + y for x, y in zip(a, b)]


def pack_faces(load, planes, tile_ref):
    lane = iota(1)
    tile = jnp.zeros((16, 128), jnp.float32)
    for j in range(planes):
        for v in range(5):
            q = 2 * (j * 5 + v)
            here = (lane == q) | (lane == (q - 1) % 128)
            x = load(j, v)
            tile = jnp.where(here, pltpu.roll(x, q, 1) if q else x, tile)
    for w in range(tile_ref.shape[0]):
        tile_ref[w] = tile


def masked(live_ref, values):
    live = live_ref[...] > 0.0
    return [jnp.where(live, x, 0.0) for x in values]


def has_above(values):
    inner = lax.axis_index("ja") < lax.axis_size("ja") - 1
    return [jnp.where(inner, x, 0.0) for x in values]


def pack_kernel(flow_hbm, tile_ref, first_ref, flow_ref, sem):
    copy = pltpu.make_async_copy(flow_hbm, flow_ref, sem)
    copy.start()
    copy.wait()
    put(first_ref, cell(flow_ref, 0))
    pack_faces(lambda j, v: flow_ref[j, v], flow_ref.shape[0], tile_ref)


def merge_kernel(own_ref, got_ref, *refs):
    out_ref = refs[-1]
    count = own_ref.shape[0]
    for w in range(count):
        out_ref[w] = own_ref[w]
        out_ref[count + w] = got_ref[w]


def relay_kernel(own_ref, got_ref, mats_ref, mats_out_ref, out_ref):
    merge_kernel(own_ref, got_ref, out_ref)
    for i in range(3):
        for r in range(5):
            put(mats_out_ref, cell(mats_ref, i, r), i, r)


def neighbours(x):
    lane, row = iota(1), iota(0)
    total = jnp.where(lane == 0, 0.0, pltpu.roll(x, 1, 1))
    total = total + jnp.where(lane == 127, 0.0, pltpu.roll(x, 127, 1))
    total = total + jnp.where(row == 0, 0.0, pltpu.roll(x, 1, 0))
    return total + jnp.where(row == 15, 0.0, pltpu.roll(x, 15, 0))


def ghosts_of(pick_ref, tile_at):
    low = high = jnp.zeros((16, 128), jnp.float32)
    for i in range(pick_ref.shape[1]):
        low = jnp.where(pick_ref[0, i] > 0.0, tile_at(i), low)
        high = jnp.where(pick_ref[1, i] > 0.0, tile_at(i), high)
    return jnp.where(iota(1) % 2 == 0, pltpu.roll(low, 1, 1), pltpu.roll(high, 127, 1))


def ghost_at(ghosts, j, v):
    lane = iota(1)
    q = 2 * (j * 5 + v)
    turned = pltpu.roll(ghosts, 128 - q, 1) if q else ghosts
    return jnp.where((lane == 0) | (lane == 127), turned, 0.0)


HALVES = [pl.ds(0, 8), pl.ds(8, 8)]


def col(ref, q, j, rows):
    return [ref[j, r, q, rows] for r in range(5)]


def put_col(ref, values, q, j, rows):
    for r in range(5):
        ref[j, r, q, rows] = values[r]


def mat(ref, j, rows):
    return [[ref[j, r, c, rows] for c in range(5)] for r in range(5)]


def matrix_kernel(
    depth_hbm, east_hbm, tile_ref, inv_ref, low_ref, up_ref,
    e_ref, f_ref, mats_ref, live_ref, pick_ref,
    y_ref, depth_ref, east_ref, sems,
):
    del tile_ref
    last = inv_ref.shape[0] - 1
    scalars = [
        pltpu.make_async_copy(depth_hbm, depth_ref, sems.at[0]),
        pltpu.make_async_copy(east_hbm, east_ref, sems.at[1]),
    ]
    for copy in scalars:
        copy.start()

    def products(j, rows):
        inv = mat(inv_ref, j, rows)
        for jac_ref, out_ref in ((low_ref, e_ref), (up_ref, f_ref)):
            for q in range(5):
                product = matvec(inv, col(jac_ref, q, j, rows))
                put_col(out_ref, [OMEGA * x for x in product], q, j, rows)

    def forward(j, carry):
        for rows in HALVES:
            products(j, rows)
            e = mat(e_ref, j, rows)
            for q in range(5):
                put_col(y_ref, matvec(e, col(y_ref, q, j - 1, rows)), q, j, rows)
        return carry

    def backward(step, carry):
        j = last - 1 - step
        for rows in HALVES:
            f = mat(f_ref, j, rows)
            for q in range(5):
                turned = matvec(f, col(mats_ref, q, 1, rows))
                put_col(mats_ref, add(col(y_ref, q, j, rows), turned), q, 1, rows)
                put_col(mats_ref, matvec(f, col(mats_ref, q, 2, rows)), q, 2, rows)
        return carry

    for rows in HALVES:
        products(0, rows)
        for q in range(5):
            put_col(y_ref, col(e_ref, q, 0, rows), q, 0, rows)
    lax.fori_loop(1, last + 1, forward, 0)
    for rows in HALVES:
        for q in range(5):
            put_col(mats_ref, col(y_ref, q, last, rows), q, 0, rows)
            put_col(mats_ref, col(y_ref, q, last, rows), q, 1, rows)
            put_col(mats_ref, col(f_ref, q, last, rows), q, 2, rows)
    lax.fori_loop(0, last, backward, 0)
    for copy in scalars:
        copy.wait()
    zone = lax.axis_index("zone")
    row = iota(0)
    live_ref[...] = jnp.where(row < depth_ref[zone], 1.0, 0.0)
    for i in range(pick_ref.shape[1]):
        w = zone ^ i
        rows = row < depth_ref[w]
        pick_ref[0, i] = jnp.where(rows & (east_ref[w] == zone), 1.0, 0.0)
        pick_ref[1, i] = jnp.where(rows & (east_ref[zone] == w), 1.0, 0.0)


def by_place(mine_refs, other_refs, run):
    odd = lax.axis_index("ja") % 2

    @pl.when(odd == 0)
    def _():
        run(*mine_refs, *other_refs)

    @pl.when(odd == 1)
    def _():
        run(*other_refs, *mine_refs)


def beta_kernel(mine_ref, other_ref, half_ref):
    odd = lax.axis_index("ja") % 2
    for side in range(2):
        lo, hi = (mine_ref, other_ref) if side == 0 else (other_ref, mine_ref)
        rows = pl.ds(8 * side, 8)

        @pl.when(odd == side)
        def _():
            d_hi = [[hi[1, r, c, rows] for c in range(5)] for r in range(5)]
            n_lo = [[lo[2, r, c, rows] for c in range(5)] for r in range(5)]
            for q in range(5):
                m_col = [lo[0, r, q, rows] for r in range(5)]
                d_col = [lo[1, r, q, rows] for r in range(5)]
                out = add(d_col, matvec(n_lo, matvec(d_hi, m_col)))
                for r in range(5):
                    half_ref[r, q] = out[r]


def sweeps(s_ref, e_ref, f_ref, y_ref, ends_ref, last):
    planes = s_ref.shape[0]
    value = cell(s_ref, 0)
    put(y_ref, value, 0)
    for j in range(1, planes):
        value = add(cell(s_ref, j), matvec(block(e_ref, j), value))
        put(y_ref, value, j)
    put(ends_ref, [x + z * (1.0 / OMEGA) for x, z in zip(value, last)], 0)
    for j in range(planes - 2, -1, -1):
        value = add(cell(y_ref, j), matvec(block(f_ref, j), value))
    put(ends_ref, value, 1)


def source_kernel(
    tiles_ref, live_ref, cur_ref, force_ref, diag_ref, inv_ref, e_ref, f_ref, s_ref
):
    del tiles_ref
    planes = cur_ref.shape[0]
    before, here = None, masked(live_ref, cell(cur_ref, 0))
    for j in range(planes):
        own = matvec(block(diag_ref, j), here)
        res = [force_ref[j, v] - own[v] + COUPLE * neighbours(here[v]) for v in range(5)]
        out = matvec(block(inv_ref, j), masked(live_ref, res))
        if j > 0:
            linked = matvec(block(e_ref, j), before)
            out = add(out, [x * (1.0 / OMEGA) for x in linked])
        if j < planes - 1:
            after = masked(live_ref, cell(cur_ref, j + 1))
            linked = matvec(block(f_ref, j), after)
            out = add(out, [x * (1.0 / OMEGA) for x in linked])
            before, here = here, after
        put(s_ref, out, j)


def local_kernel(
    half_ref, live_ref, pick_ref, own_ref, got_ref, cur_ref, above_ref, s0_ref,
    inv_ref, e_ref, f_ref,
    s_ref, ends_ref, half_out_ref, y_ref,
):
    for r in range(5):
        put(half_out_ref, cell(half_ref, r), r)
    last = cur_ref.shape[0] - 1
    count = own_ref.shape[0]
    ghosts = ghosts_of(pick_ref, lambda i: own_ref[i] if i < count else got_ref[i - count])
    ghosts = jnp.where(live_ref[...] > 0.0, COUPLE * ghosts, 0.0)
    for j in range(last + 1):
        extra = [ghost_at(ghosts, j, v) for v in range(5)]
        put(s_ref, add(cell(s0_ref, j), matvec(block(inv_ref, j), extra)), j)
    above = masked(live_ref, has_above(cell(above_ref)))
    linked = matvec(block(f_ref, last), above)
    put(s_ref, add(cell(s_ref, last), [x * (1.0 / OMEGA) for x in linked]), last)
    sweeps(s_ref, e_ref, f_ref, y_ref, ends_ref, masked(live_ref, cell(cur_ref, last)))


def second_kernel(
    live_ref, pick_ref, tiles_ref, cur_ref, above_ref, force_ref, diag_ref, low_ref, up_ref,
    inv_ref, e_ref, f_ref,
    res_ref, s_ref, ends_ref, low0_ref, y_ref,
):
    planes = cur_ref.shape[0]
    zone = lax.axis_index("zone")
    ghosts = ghosts_of(pick_ref, lambda i: tiles_ref[zone ^ i])
    for r in range(5):
        put(low0_ref, cell(low_ref, 0, r), r)
    for j in range(planes):
        here = cell(cur_ref, j)
        applied = matvec(block(diag_ref, j), here)
        if j > 0:
            lower = matvec(block(low_ref, j), cell(cur_ref, j - 1))
            applied = [x - z for x, z in zip(applied, lower)]
        above = cell(cur_ref, j + 1) if j < planes - 1 else cell(above_ref)
        upper = matvec(block(up_ref, j), above)
        res = []
        for v in range(5):
            sides = neighbours(here[v]) + ghost_at(ghosts, j, v)
            all_of = applied[v] - upper[v] - COUPLE * sides
            res.append(force_ref[j, v] - all_of)
        res = masked(live_ref, res)
        put(res_ref, res, j)
        put(s_ref, matvec(block(inv_ref, j), res), j)
    last = cell(cur_ref, planes - 1)
    sweeps(s_ref, e_ref, f_ref, y_ref, ends_ref, last)
    put(ends_ref, last, 2)


def write_kernel(res_ref, res_hbm, sem):
    copy = pltpu.make_async_copy(res_ref, res_hbm, sem)
    copy.start()
    copy.wait()


def mid_kernel(ends_ref, ends_other_ref, mats_ref, mats_other_ref, out_ref):
    def run(ends_lo, mats_lo, ends_hi, mats_hi):
        c_lo = cell(ends_lo, 0)

        @pl.when(lax.axis_index("ja") < 2)
        def _():
            put(out_ref, add(cell(ends_hi, 0), matvec(block(mats_hi, 0), c_lo)), 0)

        @pl.when(lax.axis_index("ja") >= 2)
        def _():
            turned = add(cell(ends_hi, 1), matvec(block(mats_hi, 1), c_lo))
            put(out_ref, add(cell(ends_lo, 1), matvec(block(mats_lo, 2), turned)), 0)

        if out_ref.shape[0] > 1:
            put(out_ref, cell(ends_hi, 2), 1)

    by_place([ends_ref, mats_ref], [ends_other_ref, mats_other_ref], run)


def join(mine_ref, other_ref, *at):
    mine, other = mine_ref[at], other_ref[at]
    odd = lax.axis_index("ja") % 2 == 1
    return jnp.concatenate([jnp.where(odd, other, mine), jnp.where(odd, mine, other)], axis=0)


def inflows(
    ends_ref, ends_other_ref, mats_ref, mats_other_ref, pair_ref, pair_other_ref,
    half_ref, half_other_ref, inflow_ref,
):
    ja = lax.axis_index("ja")
    zeros = [jnp.zeros((16, 128), jnp.float32)] * 5

    def far():
        beta = [[join(half_ref, half_other_ref, r, c) for c in range(5)] for r in range(5)]
        return add(cell(pair_other_ref, 0), matvec(beta, cell(pair_ref, 0)))

    @pl.when(ja == 0)
    def _():
        put(inflow_ref, zeros, 0)
        b = add(cell(ends_other_ref, 1), matvec(block(mats_other_ref, 1), cell(ends_ref, 0)))
        b = add(b, matvec(block(mats_other_ref, 2), far()))
        put(inflow_ref, b, 1)

    @pl.when(ja == 1)
    def _():
        put(inflow_ref, cell(ends_other_ref, 0), 0)
        put(inflow_ref, far(), 1)

    @pl.when(ja == 2)
    def _():
        a = cell(pair_other_ref, 0)
        put(inflow_ref, a, 0)
        a = add(cell(ends_ref, 0), matvec(block(mats_ref, 0), a))
        b = add(cell(ends_other_ref, 1), matvec(block(mats_other_ref, 1), a))
        put(inflow_ref, b, 1)

    @pl.when(ja == 3)
    def _():
        a = add(cell(ends_other_ref, 0), matvec(block(mats_other_ref, 0), cell(pair_other_ref, 0)))
        put(inflow_ref, a, 0)
        put(inflow_ref, zeros, 1)


def final_kernel(
    live_ref, cur_ref, above_ref, s_ref, e_ref, f_ref,
    ends_ref, ends_other_ref, mats_ref, mats_other_ref, pair_ref, pair_other_ref,
    half_ref, half_other_ref,
    new_ref, above_new_ref, tile_ref, y_ref, inflow_ref,
):
    planes = cur_ref.shape[0]
    inflows(
        ends_ref, ends_other_ref, mats_ref, mats_other_ref, pair_ref, pair_other_ref,
        half_ref, half_other_ref, inflow_ref,
    )
    value = cell(inflow_ref, 0)
    for j in range(planes):
        value = add(cell(s_ref, j), matvec(block(e_ref, j), value))
        put(y_ref, value, j)
    value = cell(inflow_ref, 1)
    put(above_new_ref, add(masked(live_ref, has_above(cell(above_ref))), value))
    for j in range(planes - 1, -1, -1):
        value = add(cell(y_ref, j), matvec(block(f_ref, j), value))
        put(new_ref, add(masked(live_ref, cell(cur_ref, j)), value), j)
    pack_faces(lambda j, v: new_ref[j, v], planes, tile_ref)


def last_kernel(
    live_ref, low0_ref, cur_ref, res_ref, s_ref, e_ref, f_ref,
    ends_ref, ends_other_ref, mats_ref, mats_other_ref, pair_ref, pair_other_ref,
    half_ref, half_other_ref, res_in_hbm,
    new_hbm, res_hbm, y_ref, inflow_ref, new_ref, res0_ref, sems,
):
    del res_in_hbm
    planes = cur_ref.shape[0]
    ja = lax.axis_index("ja")
    before = [
        jnp.where(ja == 0, 0.0, jnp.where(ja == 2, pair_other_ref[1, v], ends_other_ref[2, v]))
        for v in range(5)
    ]
    put(res0_ref, add(cell(res_ref, 0), masked(live_ref, matvec(block(low0_ref), before))))
    copies = [pltpu.make_async_copy(res0_ref, res_hbm.at[0], sems.at[planes])]
    copies[0].start()
    inflows(
        ends_ref, ends_other_ref, mats_ref, mats_other_ref, pair_ref, pair_other_ref,
        half_ref, half_other_ref, inflow_ref,
    )
    value = cell(inflow_ref, 0)
    for j in range(planes):
        value = add(cell(s_ref, j), matvec(block(e_ref, j), value))
        put(y_ref, value, j)
    value = cell(inflow_ref, 1)
    for j in range(planes - 1, -1, -1):
        value = add(cell(y_ref, j), matvec(block(f_ref, j), value))
        put(new_ref, add(cell(cur_ref, j), value), j)
        copies.append(pltpu.make_async_copy(new_ref.at[j], new_hbm.at[j], sems.at[j]))
        copies[-1].start()
    for copy in copies:
        copy.wait()


def per_device(
    flow_state, forcing, diag_block, lower_jac, upper_jac, block_inv, east_zone, zone_depth
):
    zones, parts = lax.axis_size("zone"), lax.axis_size("ja")
    assert parts == 4 and ITERS == 2 and zones > 4 and zones & (zones - 1) == 0
    current, force, diag, low, up, inv = (
        x[0] for x in (flow_state, forcing, diag_block, lower_jac, upper_jac, block_inv)
    )
    state = current.shape
    planes, plane, blocks = state[0], state[1:], diag.shape
    matrix = blocks[1:]
    work = [buffer(*state)]

    def swap(x, bit):
        return lax.ppermute(x, "ja", [(p, p ^ bit) for p in range(parts)])

    tile, first = call(
        pack_kernel,
        [(1, *state[2:]), plane],
        work + [pltpu.SemaphoreType.DMA],
        flops=10**10,
        far=(0,),
    )(current)
    above = lax.ppermute(first, "ja", [((p + 1) % parts, p) for p in range(parts)])
    e, f, mats, live, pick = call(
        matrix_kernel,
        [blocks, blocks, (3, *matrix), state[2:], (2, zones, *state[2:])],
        [buffer(*blocks)]
        + [pltpu.SMEM((zones,), jnp.int32)] * 2
        + [pltpu.SemaphoreType.DMA((2,))],
        flops=5 * 10**9,
        far=(0, 1),
    )(zone_depth, east_zone, tile, inv, low, up)
    tiles, stride = tile, 1
    while True:
        got = lax.ppermute(tiles, "zone", [(z, z ^ stride) for z in range(zones)])
        stride *= 2
        if stride == zones:
            break
        both = (stride, *state[2:])
        if stride == 2:
            mats, tiles = call(relay_kernel, [mats.shape, both], flops=10**5)(tiles, got, mats)
            mats_other = swap(mats, 1)
            half = call(beta_kernel, [(*matrix[:2], 8, matrix[3])], flops=10**5)(mats, mats_other)[0]
        else:
            tiles = call(merge_kernel, [both], flops=10**5)(tiles, got, half)[0]
    half = swap(half, 2)
    s0 = call(source_kernel, [state])(tiles, live, current, force, diag, inv, e, f)[0]
    s, ends, half = call(local_kernel, [state, (2, *plane), half.shape], work)(
        half, live, pick, tiles, got, current, above, s0, inv, e, f
    )
    ends_other = swap(ends, 1)
    half_other = swap(half, 1)
    pair = call(mid_kernel, [(1, *plane)], flops=10**5)(ends, ends_other, mats, mats_other)[0]
    pair_other = swap(pair, 2)
    flows = [buffer(2, *plane)]
    current, above, tile = call(
        final_kernel, [state, plane, (zones, *state[2:])], work + flows
    )(
        live, current, above, s, e, f,
        ends, ends_other, mats, mats_other, pair, pair_other, half, half_other,
    )

    got = lax.all_to_all(tile, "zone", 0, 0, tiled=True)
    residual, s, ends, low0 = call(second_kernel, [state, state, (3, *plane), matrix], work)(
        live, pick, got, current, above, force, diag, low, up, inv, e, f
    )
    ends_other = swap(ends, 1)
    pair = call(mid_kernel, [(2, *plane)])(ends, ends_other, mats, mats_other)[0]
    pair_other = swap(pair, 2)
    written = call(write_kernel, [state], [pltpu.SemaphoreType.DMA], out_specs=[HBM])(residual)[0]
    current, residual = call(
        last_kernel,
        [state, state],
        work + flows + work + [buffer(*plane), pltpu.SemaphoreType.DMA((planes + 1,))],
        out_specs=[HBM, HBM],
        alias={15: 1},
    )(
        live, low0, current, residual, s, e, f,
        ends, ends_other, mats, mats_other, pair, pair_other, half, half_other, written,
    )
    return (current[None], residual[None])


def solution(mesh):
    state = P("zone", "ja", None, None, None)
    blocks = P("zone", "ja", None, None, None, None)
    return jax.shard_map(
        per_device,
        mesh=mesh,
        in_specs=(state, state, blocks, blocks, blocks, blocks, P(), P()),
        out_specs=(state, state),
        check_vma=False,
    )
```

```python
import jax
import jax.numpy as jnp
from jax import lax
from jax.experimental import pallas as pl
from jax.experimental.pallas import tpu as pltpu
from jax.sharding import PartitionSpec as P

ITERS = 2
OMEGA = 1.2
COUPLE = 0.25

VMEM = pl.BlockSpec(memory_space=pltpu.VMEM)
ANY = pl.BlockSpec(memory_space=pl.ANY)
HBM = pl.BlockSpec(memory_space=pltpu.HBM)


def call(kernel, shapes, scratch=(), flops=10**9, far=(), out_specs=None, alias=None):
    alias = alias or {}

    def run(*arrays):
        arrays = [
            pltpu.with_memory_space_constraint(a, pltpu.HBM) if i in far else a
            for i, a in enumerate(arrays)
        ]
        return pl.pallas_call(
            kernel,
            out_shape=[jax.ShapeDtypeStruct(s, jnp.float32) for s in shapes],
            in_specs=[
                HBM if i in far else ANY if i in alias else VMEM for i in range(len(arrays))
            ],
            out_specs=out_specs or [VMEM] * len(shapes),
            scratch_shapes=list(scratch),
            input_output_aliases=alias,
            compiler_params=pltpu.CompilerParams(vmem_limit_bytes=8 * 2**20),
            cost_estimate=pl.CostEstimate(flops=flops, bytes_accessed=flops // 10**3, transcendentals=0),
        )(*arrays)

    return run


def buffer(*shape):
    return pltpu.VMEM(shape, jnp.float32)


def iota(dim):
    return lax.broadcasted_iota(jnp.int32, (16, 128), dim)


def matvec(matrix, vector):
    n = len(vector)
    out = []
    for r in range(n):
        acc = matrix[r][0] * vector[0]
        for c in range(1, n):
            acc = acc + matrix[r][c] * vector[c]
        out.append(acc)
    return out


def block(ref, *lead):
    return [[ref[(*lead, r, c)] for c in range(5)] for r in range(5)]


def matrix_of(ref, i):
    return [cell(ref, 5 * i + r) for r in range(5)]


def cell(ref, *lead):
    return [ref[(*lead, v)] for v in range(5)]


def put(ref, values, *lead):
    for v, value in enumerate(values):
        ref[(*lead, v)] = value


def add(a, b):
    return [x + y for x, y in zip(a, b)]


def pack_faces(load, planes, tile_ref):
    lane = iota(1)
    tile = jnp.zeros((16, 128), jnp.float32)
    for j in range(planes):
        for v in range(5):
            q = 2 * (j * 5 + v)
            here = (lane == q) | (lane == (q - 1) % 128)
            x = load(j, v)
            tile = jnp.where(here, pltpu.roll(x, q, 1) if q else x, tile)
    for w in range(tile_ref.shape[0]):
        tile_ref[w] = tile


def masked(live_ref, values):
    live = live_ref[...] > 0.0
    return [jnp.where(live, x, 0.0) for x in values]


def pack_kernel(flow_hbm, tile_ref, first_ref, flow_ref, sem):
    copy = pltpu.make_async_copy(flow_hbm, flow_ref, sem)
    copy.start()
    copy.wait()
    put(first_ref, cell(flow_ref, 0))
    pack_faces(lambda j, v: flow_ref[j, v], flow_ref.shape[0], tile_ref)


def merge_kernel(own_ref, got_ref, *refs):
    out_ref = refs[-1]
    count = own_ref.shape[0]
    for w in range(count):
        out_ref[w] = own_ref[w]
        out_ref[count + w] = got_ref[w]


def relay_kernel(own_ref, got_ref, mats_ref, first_ref, mats_out_ref, out_ref):
    merge_kernel(own_ref, got_ref, out_ref)
    for i in range(15):
        put(mats_out_ref, cell(mats_ref, i), i)
    put(mats_out_ref, cell(first_ref), 15)


def neighbours(x):
    lane, row = iota(1), iota(0)
    total = jnp.where(lane == 0, 0.0, pltpu.roll(x, 1, 1))
    total = total + jnp.where(lane == 127, 0.0, pltpu.roll(x, 127, 1))
    total = total + jnp.where(row == 0, 0.0, pltpu.roll(x, 1, 0))
    return total + jnp.where(row == 15, 0.0, pltpu.roll(x, 15, 0))


def ghosts_of(pick_ref, tile_at):
    low = high = jnp.zeros((16, 128), jnp.float32)
    for i in range(pick_ref.shape[1]):
        low = jnp.where(pick_ref[0, i] > 0.0, tile_at(i), low)
        high = jnp.where(pick_ref[1, i] > 0.0, tile_at(i), high)
    return jnp.where(iota(1) % 2 == 0, pltpu.roll(low, 1, 1), pltpu.roll(high, 127, 1))


def ghost_at(ghosts, j, v):
    lane = iota(1)
    q = 2 * (j * 5 + v)
    turned = pltpu.roll(ghosts, 128 - q, 1) if q else ghosts
    return jnp.where((lane == 0) | (lane == 127), turned, 0.0)


HALVES = [pl.ds(0, 8), pl.ds(8, 8)]


def col(ref, q, j, rows):
    return [ref[j, r, q, rows] for r in range(5)]


def put_col(ref, values, q, j, rows):
    for r in range(5):
        ref[j, r, q, rows] = values[r]


def put_mat_col(ref, values, q, i, rows):
    for r in range(5):
        ref[5 * i + r, q, rows] = values[r]


def mat_col(ref, q, i, rows):
    return [ref[5 * i + r, q, rows] for r in range(5)]


def mat(ref, j, rows):
    return [[ref[j, r, c, rows] for c in range(5)] for r in range(5)]


def matrix_kernel(
    depth_hbm, east_hbm, tile_ref, inv_ref, low_ref, up_ref,
    e_ref, f_ref, mats_ref, live_ref, pick_ref,
    y_ref, depth_ref, east_ref, sems,
):
    del tile_ref
    last = inv_ref.shape[0] - 1
    scalars = [
        pltpu.make_async_copy(depth_hbm, depth_ref, sems.at[0]),
        pltpu.make_async_copy(east_hbm, east_ref, sems.at[1]),
    ]
    for copy in scalars:
        copy.start()

    def products(j, rows):
        inv = mat(inv_ref, j, rows)
        for jac_ref, out_ref in ((low_ref, e_ref), (up_ref, f_ref)):
            for q in range(5):
                product = matvec(inv, col(jac_ref, q, j, rows))
                put_col(out_ref, [OMEGA * x for x in product], q, j, rows)

    def forward(j, carry):
        for rows in HALVES:
            products(j, rows)
            e = mat(e_ref, j, rows)
            for q in range(5):
                put_col(y_ref, matvec(e, col(y_ref, q, j - 1, rows)), q, j, rows)
        return carry

    def backward(step, carry):
        j = last - 1 - step
        for rows in HALVES:
            f = mat(f_ref, j, rows)
            for q in range(5):
                turned = matvec(f, mat_col(mats_ref, q, 1, rows))
                put_mat_col(mats_ref, add(col(y_ref, q, j, rows), turned), q, 1, rows)
                put_mat_col(mats_ref, matvec(f, mat_col(mats_ref, q, 2, rows)), q, 2, rows)
        return carry

    for rows in HALVES:
        products(0, rows)
        for q in range(5):
            put_col(y_ref, col(e_ref, q, 0, rows), q, 0, rows)
    lax.fori_loop(1, last + 1, forward, 0)
    for rows in HALVES:
        for q in range(5):
            put_mat_col(mats_ref, col(y_ref, q, last, rows), q, 0, rows)
            put_mat_col(mats_ref, col(y_ref, q, last, rows), q, 1, rows)
            put_mat_col(mats_ref, col(f_ref, q, last, rows), q, 2, rows)
    lax.fori_loop(0, last, backward, 0)
    for copy in scalars:
        copy.wait()
    zone = lax.axis_index("zone")
    row = iota(0)
    live_ref[...] = jnp.where(row < depth_ref[zone], 1.0, 0.0)
    for i in range(pick_ref.shape[1]):
        w = zone ^ i
        rows = row < depth_ref[w]
        pick_ref[0, i] = jnp.where(rows & (east_ref[w] == zone), 1.0, 0.0)
        pick_ref[1, i] = jnp.where(rows & (east_ref[zone] == w), 1.0, 0.0)


def by_place(mine_refs, other_refs, run):
    odd = lax.axis_index("ja") % 2

    @pl.when(odd == 0)
    def _():
        run(*mine_refs, *other_refs)

    @pl.when(odd == 1)
    def _():
        run(*other_refs, *mine_refs)


def beta_kernel(mine_ref, other_ref, half_ref):
    for side in range(2):
        put(half_ref, [mine_ref[15, v, HALVES[side]] for v in range(5)], 5 + side)
    odd = lax.axis_index("ja") % 2
    for side in range(2):
        lo, hi = (mine_ref, other_ref) if side == 0 else (other_ref, mine_ref)
        rows = HALVES[side]

        @pl.when(odd == side)
        def _():
            d_hi = [[hi[5 + r, c, rows] for c in range(5)] for r in range(5)]
            n_lo = [[lo[10 + r, c, rows] for c in range(5)] for r in range(5)]
            for q in range(5):
                out = matvec(n_lo, matvec(d_hi, mat_col(lo, q, 0, rows)))
                out = add(mat_col(lo, q, 1, rows), out)
                for r in range(5):
                    half_ref[r, q] = out[r]


def sweeps(s_ref, e_ref, f_ref, y_ref, ends_ref, last):
    planes = s_ref.shape[0]
    value = cell(s_ref, 0)
    put(y_ref, value, 0)
    for j in range(1, planes):
        value = add(cell(s_ref, j), matvec(block(e_ref, j), value))
        put(y_ref, value, j)
    put(ends_ref, [x + z * (1.0 / OMEGA) for x, z in zip(value, last)], 0)
    for j in range(planes - 2, -1, -1):
        value = add(cell(y_ref, j), matvec(block(f_ref, j), value))
    put(ends_ref, value, 1)


def source_kernel(
    tiles_ref, live_ref, cur_ref, force_ref, diag_ref, inv_ref, e_ref, f_ref, s_ref
):
    del tiles_ref
    planes = cur_ref.shape[0]
    before, here = None, masked(live_ref, cell(cur_ref, 0))
    for j in range(planes):
        own = matvec(block(diag_ref, j), here)
        res = [force_ref[j, v] - own[v] + COUPLE * neighbours(here[v]) for v in range(5)]
        out = matvec(block(inv_ref, j), masked(live_ref, res))
        if j > 0:
            linked = matvec(block(e_ref, j), before)
            out = add(out, [x * (1.0 / OMEGA) for x in linked])
        if j < planes - 1:
            after = masked(live_ref, cell(cur_ref, j + 1))
            linked = matvec(block(f_ref, j), after)
            out = add(out, [x * (1.0 / OMEGA) for x in linked])
            before, here = here, after
        put(s_ref, out, j)


def local_kernel(
    half_ref, mats_other_ref, live_ref, pick_ref, own_ref, got_ref, cur_ref, s0_ref,
    inv_ref, e_ref, f_ref,
    s_ref, ends_ref, above_ref, half_out_ref, y_ref,
):
    for r in range(5):
        put(half_out_ref, cell(half_ref, r), r)
    last = cur_ref.shape[0] - 1
    count = own_ref.shape[0]
    ghosts = ghosts_of(pick_ref, lambda i: own_ref[i] if i < count else got_ref[i - count])
    ghosts = jnp.where(live_ref[...] > 0.0, COUPLE * ghosts, 0.0)
    for j in range(last + 1):
        extra = [ghost_at(ghosts, j, v) for v in range(5)]
        put(s_ref, add(cell(s0_ref, j), matvec(block(inv_ref, j), extra)), j)
    ja = lax.axis_index("ja")
    above = []
    for v in range(5):
        beyond = jnp.concatenate([half_ref[5, v], half_ref[6, v]], axis=0)
        beyond = jnp.where(ja == 1, beyond, 0.0)
        above.append(jnp.where(ja % 2 == 0, mats_other_ref[15, v], beyond))
    above = masked(live_ref, above)
    put(above_ref, above)
    linked = matvec(block(f_ref, last), above)
    put(s_ref, add(cell(s_ref, last), [x * (1.0 / OMEGA) for x in linked]), last)
    sweeps(s_ref, e_ref, f_ref, y_ref, ends_ref, masked(live_ref, cell(cur_ref, last)))


def second_kernel(
    live_ref, pick_ref, tiles_ref, cur_ref, above_ref, force_ref, diag_ref, low_ref, up_ref,
    inv_ref, e_ref, f_ref,
    res_ref, s_ref, ends_ref, low0_ref, y_ref,
):
    planes = cur_ref.shape[0]
    zone = lax.axis_index("zone")
    ghosts = ghosts_of(pick_ref, lambda i: tiles_ref[zone ^ i])
    for r in range(5):
        put(low0_ref, cell(low_ref, 0, r), r)
    for j in range(planes):
        here = cell(cur_ref, j)
        applied = matvec(block(diag_ref, j), here)
        if j > 0:
            lower = matvec(block(low_ref, j), cell(cur_ref, j - 1))
            applied = [x - z for x, z in zip(applied, lower)]
        above = cell(cur_ref, j + 1) if j < planes - 1 else cell(above_ref)
        upper = matvec(block(up_ref, j), above)
        res = []
        for v in range(5):
            sides = neighbours(here[v]) + ghost_at(ghosts, j, v)
            all_of = applied[v] - upper[v] - COUPLE * sides
            res.append(force_ref[j, v] - all_of)
        res = masked(live_ref, res)
        put(res_ref, res, j)
        put(s_ref, matvec(block(inv_ref, j), res), j)
    last = cell(cur_ref, planes - 1)
    sweeps(s_ref, e_ref, f_ref, y_ref, ends_ref, last)
    put(ends_ref, last, 2)


def write_kernel(res_ref, res_hbm, sem):
    copy = pltpu.make_async_copy(res_ref, res_hbm, sem)
    copy.start()
    copy.wait()


def mid_kernel(ends_ref, ends_other_ref, mats_ref, mats_other_ref, out_ref):
    def run(ends_lo, mats_lo, ends_hi, mats_hi):
        c_lo = cell(ends_lo, 0)

        @pl.when(lax.axis_index("ja") < 2)
        def _():
            put(out_ref, add(cell(ends_hi, 0), matvec(matrix_of(mats_hi, 0), c_lo)), 0)

        @pl.when(lax.axis_index("ja") >= 2)
        def _():
            turned = add(cell(ends_hi, 1), matvec(matrix_of(mats_hi, 1), c_lo))
            put(out_ref, add(cell(ends_lo, 1), matvec(matrix_of(mats_lo, 2), turned)), 0)

        if out_ref.shape[0] > 1:
            put(out_ref, cell(ends_hi, 2), 1)

    by_place([ends_ref, mats_ref], [ends_other_ref, mats_other_ref], run)


def join(mine_ref, other_ref, *at):
    mine, other = mine_ref[at], other_ref[at]
    odd = lax.axis_index("ja") % 2 == 1
    return jnp.concatenate([jnp.where(odd, mine, other), jnp.where(odd, other, mine)], axis=0)


def inflows(
    ends_ref, ends_other_ref, mats_ref, mats_other_ref, pair_ref, pair_other_ref,
    half_ref, half_other_ref, inflow_ref,
):
    ja = lax.axis_index("ja")
    zeros = [jnp.zeros((16, 128), jnp.float32)] * 5

    def far():
        beta = [[join(half_ref, half_other_ref, r, c) for c in range(5)] for r in range(5)]
        return add(cell(pair_other_ref, 0), matvec(beta, cell(pair_ref, 0)))

    @pl.when(ja == 0)
    def _():
        put(inflow_ref, zeros, 0)
        b = add(cell(ends_other_ref, 1), matvec(matrix_of(mats_other_ref, 1), cell(ends_ref, 0)))
        b = add(b, matvec(matrix_of(mats_other_ref, 2), far()))
        put(inflow_ref, b, 1)

    @pl.when(ja == 1)
    def _():
        put(inflow_ref, cell(ends_other_ref, 0), 0)
        put(inflow_ref, far(), 1)

    @pl.when(ja == 2)
    def _():
        a = cell(pair_other_ref, 0)
        put(inflow_ref, a, 0)
        a = add(cell(ends_ref, 0), matvec(matrix_of(mats_ref, 0), a))
        b = add(cell(ends_other_ref, 1), matvec(matrix_of(mats_other_ref, 1), a))
        put(inflow_ref, b, 1)

    @pl.when(ja == 3)
    def _():
        a = add(cell(ends_other_ref, 0), matvec(matrix_of(mats_other_ref, 0), cell(pair_other_ref, 0)))
        put(inflow_ref, a, 0)
        put(inflow_ref, zeros, 1)


def final_kernel(
    live_ref, cur_ref, above_ref, s_ref, e_ref, f_ref,
    ends_ref, ends_other_ref, mats_ref, mats_other_ref, pair_ref, pair_other_ref,
    half_ref, half_other_ref,
    new_ref, above_new_ref, tile_ref, y_ref, inflow_ref,
):
    planes = cur_ref.shape[0]
    inflows(
        ends_ref, ends_other_ref, mats_ref, mats_other_ref, pair_ref, pair_other_ref,
        half_ref, half_other_ref, inflow_ref,
    )
    value = cell(inflow_ref, 0)
    for j in range(planes):
        value = add(cell(s_ref, j), matvec(block(e_ref, j), value))
        put(y_ref, value, j)
    value = cell(inflow_ref, 1)
    put(above_new_ref, add(cell(above_ref), value))
    for j in range(planes - 1, -1, -1):
        value = add(cell(y_ref, j), matvec(block(f_ref, j), value))
        put(new_ref, add(masked(live_ref, cell(cur_ref, j)), value), j)
    pack_faces(lambda j, v: new_ref[j, v], planes, tile_ref)


def last_kernel(
    live_ref, low0_ref, cur_ref, res_ref, s_ref, e_ref, f_ref,
    ends_ref, ends_other_ref, mats_ref, mats_other_ref, pair_ref, pair_other_ref,
    half_ref, half_other_ref, res_in_hbm,
    new_hbm, res_hbm, y_ref, inflow_ref, new_ref, res0_ref, sems,
):
    del res_in_hbm
    planes = cur_ref.shape[0]
    ja = lax.axis_index("ja")
    before = [
        jnp.where(ja == 0, 0.0, jnp.where(ja == 2, pair_other_ref[1, v], ends_other_ref[2, v]))
        for v in range(5)
    ]
    put(res0_ref, add(cell(res_ref, 0), masked(live_ref, matvec(block(low0_ref), before))))
    copies = [pltpu.make_async_copy(res0_ref, res_hbm.at[0], sems.at[planes])]
    copies[0].start()
    inflows(
        ends_ref, ends_other_ref, mats_ref, mats_other_ref, pair_ref, pair_other_ref,
        half_ref, half_other_ref, inflow_ref,
    )
    value = cell(inflow_ref, 0)
    for j in range(planes):
        value = add(cell(s_ref, j), matvec(block(e_ref, j), value))
        put(y_ref, value, j)
    value = cell(inflow_ref, 1)
    for j in range(planes - 1, -1, -1):
        value = add(cell(y_ref, j), matvec(block(f_ref, j), value))
        put(new_ref, add(cell(cur_ref, j), value), j)
        copies.append(pltpu.make_async_copy(new_ref.at[j], new_hbm.at[j], sems.at[j]))
        copies[-1].start()
    for copy in copies:
        copy.wait()


def per_device(
    flow_state, forcing, diag_block, lower_jac, upper_jac, block_inv, east_zone, zone_depth
):
    zones, parts = lax.axis_size("zone"), lax.axis_size("ja")
    assert parts == 4 and ITERS == 2 and zones > 4 and zones & (zones - 1) == 0
    current, force, diag, low, up, inv = (
        x[0] for x in (flow_state, forcing, diag_block, lower_jac, upper_jac, block_inv)
    )
    state = current.shape
    planes, plane, blocks = state[0], state[1:], diag.shape
    matrix = blocks[1:]
    work = [buffer(*state)]

    def swap(x, bit):
        return lax.ppermute(x, "ja", [(p, p ^ bit) for p in range(parts)])

    tile, first = call(
        pack_kernel,
        [(1, *state[2:]), plane],
        work + [pltpu.SemaphoreType.DMA],
        flops=10**10,
        far=(0,),
    )(current)
    e, f, mats, live, pick = call(
        matrix_kernel,
        [blocks, blocks, (15, *plane), state[2:], (2, zones, *state[2:])],
        [buffer(*blocks)]
        + [pltpu.SMEM((zones,), jnp.int32)] * 2
        + [pltpu.SemaphoreType.DMA((2,))],
        flops=5 * 10**9,
        far=(0, 1),
    )(zone_depth, east_zone, tile, inv, low, up)
    tiles, stride = tile, 1
    while True:
        got = lax.ppermute(tiles, "zone", [(z, z ^ stride) for z in range(zones)])
        stride *= 2
        if stride == zones:
            break
        both = (stride, *state[2:])
        if stride == 2:
            mats, tiles = call(relay_kernel, [(16, *plane), both], flops=10**5)(
                tiles, got, mats, first
            )
            mats_other = swap(mats, 1)
            half = call(beta_kernel, [(7, plane[0], 8, plane[2])], flops=10**5)(mats, mats_other)[0]
        else:
            tiles = call(merge_kernel, [both], flops=10**5)(tiles, got, half)[0]
    half = swap(half, 3)
    s0 = call(source_kernel, [state], flops=2 * 10**9)(tiles, live, current, force, diag, inv, e, f)[0]
    s, ends, above, half = call(
        local_kernel, [state, (2, *plane), plane, (5, *half.shape[1:])], work
    )(
        half, mats_other, live, pick, tiles, got, current, s0, inv, e, f
    )
    ends_other = swap(ends, 1)
    half_other = swap(half, 1)
    pair = call(mid_kernel, [(1, *plane)], flops=10**5)(ends, ends_other, mats, mats_other)[0]
    pair_other = swap(pair, 3)
    flows = [buffer(2, *plane)]
    current, above, tile = call(
        final_kernel, [state, plane, (zones, *state[2:])], work + flows
    )(
        live, current, above, s, e, f,
        ends, ends_other, mats, mats_other, pair, pair_other, half, half_other,
    )

    got = lax.all_to_all(tile, "zone", 0, 0, tiled=True)
    residual, s, ends, low0 = call(second_kernel, [state, state, (3, *plane), matrix], work)(
        live, pick, got, current, above, force, diag, low, up, inv, e, f
    )
    ends_other = swap(ends, 1)
    pair = call(mid_kernel, [(2, *plane)])(ends, ends_other, mats, mats_other)[0]
    pair_other = swap(pair, 3)
    written = call(write_kernel, [state], [pltpu.SemaphoreType.DMA], out_specs=[HBM])(residual)[0]
    current, residual = call(
        last_kernel,
        [state, state],
        work + flows + work + [buffer(*plane), pltpu.SemaphoreType.DMA((planes + 1,))],
        out_specs=[HBM, HBM],
        alias={15: 1},
    )(
        live, low0, current, residual, s, e, f,
        ends, ends_other, mats, mats_other, pair, pair_other, half, half_other, written,
    )
    return (current[None], residual[None])


def solution(mesh):
    state = P("zone", "ja", None, None, None)
    blocks = P("zone", "ja", None, None, None, None)
    return jax.shard_map(
        per_device,
        mesh=mesh,
        in_specs=(state, state, blocks, blocks, blocks, blocks, P(), P()),
        out_specs=(state, state),
        check_vma=False,
    )
```

```python
import jax
import jax.numpy as jnp
from jax import lax
from jax.experimental import pallas as pl
from jax.experimental.pallas import tpu as pltpu
from jax.sharding import PartitionSpec as P

ITERS = 2
OMEGA = 1.2
COUPLE = 0.25

VMEM = pl.BlockSpec(memory_space=pltpu.VMEM)
ANY = pl.BlockSpec(memory_space=pl.ANY)
HBM = pl.BlockSpec(memory_space=pltpu.HBM)


def call(kernel, shapes, scratch=(), flops=10**9, far=(), out_specs=None, alias=None):
    alias = alias or {}

    def run(*arrays):
        arrays = [
            pltpu.with_memory_space_constraint(a, pltpu.HBM) if i in far else a
            for i, a in enumerate(arrays)
        ]
        return pl.pallas_call(
            kernel,
            out_shape=[jax.ShapeDtypeStruct(s, jnp.float32) for s in shapes],
            in_specs=[
                HBM if i in far else ANY if i in alias else VMEM for i in range(len(arrays))
            ],
            out_specs=out_specs or [VMEM] * len(shapes),
            scratch_shapes=list(scratch),
            input_output_aliases=alias,
            compiler_params=pltpu.CompilerParams(vmem_limit_bytes=8 * 2**20),
            cost_estimate=pl.CostEstimate(flops=flops, bytes_accessed=flops // 10**3, transcendentals=0),
        )(*arrays)

    return run


def buffer(*shape):
    return pltpu.VMEM(shape, jnp.float32)


def iota(dim):
    return lax.broadcasted_iota(jnp.int32, (16, 128), dim)


def matvec(matrix, vector):
    n = len(vector)
    out = []
    for r in range(n):
        acc = matrix[r][0] * vector[0]
        for c in range(1, n):
            acc = acc + matrix[r][c] * vector[c]
        out.append(acc)
    return out


def block(ref, *lead):
    return [[ref[(*lead, r, c)] for c in range(5)] for r in range(5)]


def matrix_of(ref, i):
    return [cell(ref, 5 * i + r) for r in range(5)]


def cell(ref, *lead):
    return [ref[(*lead, v)] for v in range(5)]


def put(ref, values, *lead):
    for v, value in enumerate(values):
        ref[(*lead, v)] = value


def add(a, b):
    return [x + y for x, y in zip(a, b)]


def pack_faces(load, planes, tile_ref):
    lane = iota(1)
    tile = jnp.zeros((16, 128), jnp.float32)
    for j in range(planes):
        for v in range(5):
            q = 2 * (j * 5 + v)
            here = (lane == q) | (lane == (q - 1) % 128)
            x = load(j, v)
            tile = jnp.where(here, pltpu.roll(x, q, 1) if q else x, tile)
    for w in range(tile_ref.shape[0]):
        tile_ref[w] = tile


def masked(live_ref, values):
    live = live_ref[...] > 0.0
    return [jnp.where(live, x, 0.0) for x in values]


def pack_kernel(flow_hbm, tile_ref, first_ref, last_ref, flow_ref, sem):
    copy = pltpu.make_async_copy(flow_hbm, flow_ref, sem)
    copy.start()
    copy.wait()
    put(first_ref, cell(flow_ref, 0))
    put(last_ref, cell(flow_ref, flow_ref.shape[0] - 1))
    pack_faces(lambda j, v: flow_ref[j, v], flow_ref.shape[0], tile_ref)


def merge_kernel(own_ref, got_ref, *refs):
    out_ref = refs[-1]
    count = own_ref.shape[0]
    for w in range(count):
        out_ref[w] = own_ref[w]
        out_ref[count + w] = got_ref[w]


def relay_kernel(own_ref, got_ref, mats_ref, first_ref, mats_out_ref, out_ref):
    merge_kernel(own_ref, got_ref, out_ref)
    for i in range(20):
        put(mats_out_ref, cell(mats_ref, i), i)
    put(mats_out_ref, cell(first_ref), 20)


def neighbours(x):
    lane, row = iota(1), iota(0)
    total = jnp.where(lane == 0, 0.0, pltpu.roll(x, 1, 1))
    total = total + jnp.where(lane == 127, 0.0, pltpu.roll(x, 127, 1))
    total = total + jnp.where(row == 0, 0.0, pltpu.roll(x, 1, 0))
    return total + jnp.where(row == 15, 0.0, pltpu.roll(x, 15, 0))


def offset_of(place, zones):
    offset, stride = 0, zones // 2
    while stride:
        offset, place, stride = offset + stride * (place % 2), place // 2, stride // 2
    return offset


def ghosts_of(pick_ref, tile_at):
    low = high = jnp.zeros((16, 128), jnp.float32)
    for i in range(pick_ref.shape[1]):
        low = jnp.where(pick_ref[0, i] > 0.0, tile_at(i), low)
        high = jnp.where(pick_ref[1, i] > 0.0, tile_at(i), high)
    return jnp.where(iota(1) % 2 == 0, pltpu.roll(low, 1, 1), pltpu.roll(high, 127, 1))


def ghost_at(ghosts, j, v):
    lane = iota(1)
    q = 2 * (j * 5 + v)
    turned = pltpu.roll(ghosts, 128 - q, 1) if q else ghosts
    return jnp.where((lane == 0) | (lane == 127), turned, 0.0)


HALVES = [pl.ds(0, 8), pl.ds(8, 8)]


def col(ref, q, j, rows):
    return [ref[j, r, q, rows] for r in range(5)]


def put_col(ref, values, q, j, rows):
    for r in range(5):
        ref[j, r, q, rows] = values[r]


def put_mat_col(ref, values, q, i, rows):
    for r in range(5):
        ref[5 * i + r, q, rows] = values[r]


def mat_col(ref, q, i, rows):
    return [ref[5 * i + r, q, rows] for r in range(5)]


def mat(ref, j, rows):
    return [[ref[j, r, c, rows] for c in range(5)] for r in range(5)]


def matrix_kernel(
    depth_hbm, east_hbm, tile_ref, inv_ref, low_ref, up_ref,
    e_ref, f_ref, mats_ref, live_ref, pick_ref,
    y_ref, depth_ref, east_ref, sems,
):
    del tile_ref
    last = inv_ref.shape[0] - 1
    scalars = [
        pltpu.make_async_copy(depth_hbm, depth_ref, sems.at[0]),
        pltpu.make_async_copy(east_hbm, east_ref, sems.at[1]),
    ]
    for copy in scalars:
        copy.start()

    def products(j, rows):
        inv = mat(inv_ref, j, rows)
        for jac_ref, out_ref in ((low_ref, e_ref), (up_ref, f_ref)):
            for q in range(5):
                product = matvec(inv, col(jac_ref, q, j, rows))
                put_col(out_ref, [OMEGA * x for x in product], q, j, rows)

    def forward(j, carry):
        for rows in HALVES:
            products(j, rows)
            e = mat(e_ref, j, rows)
            for q in range(5):
                put_col(y_ref, matvec(e, col(y_ref, q, j - 1, rows)), q, j, rows)
        return carry

    def backward(step, carry):
        j = last - 1 - step
        for rows in HALVES:
            f = mat(f_ref, j, rows)
            for q in range(5):
                turned = matvec(f, mat_col(mats_ref, q, 1, rows))
                put_mat_col(mats_ref, add(col(y_ref, q, j, rows), turned), q, 1, rows)
                put_mat_col(mats_ref, matvec(f, mat_col(mats_ref, q, 2, rows)), q, 2, rows)
        return carry

    for rows in HALVES:
        products(0, rows)
        for q in range(5):
            put_col(y_ref, col(e_ref, q, 0, rows), q, 0, rows)
    lax.fori_loop(1, last + 1, forward, 0)
    for rows in HALVES:
        for q in range(5):
            put_mat_col(mats_ref, col(y_ref, q, last, rows), q, 0, rows)
            put_mat_col(mats_ref, col(y_ref, q, last, rows), q, 1, rows)
            put_mat_col(mats_ref, col(f_ref, q, last, rows), q, 2, rows)
            put_mat_col(mats_ref, col(f_ref, q, last, rows), q, 3, rows)
    lax.fori_loop(0, last, backward, 0)
    for copy in scalars:
        copy.wait()
    zone = lax.axis_index("zone")
    row = iota(0)
    live_ref[...] = jnp.where(row < depth_ref[zone], 1.0, 0.0)
    for i in range(pick_ref.shape[1]):
        w = zone ^ offset_of(i, pick_ref.shape[1])
        rows = row < depth_ref[w]
        pick_ref[0, i] = jnp.where(rows & (east_ref[w] == zone), 1.0, 0.0)
        pick_ref[1, i] = jnp.where(rows & (east_ref[zone] == w), 1.0, 0.0)


def by_place(mine_refs, other_refs, run):
    odd = lax.axis_index("ja") % 2

    @pl.when(odd == 0)
    def _():
        run(*mine_refs, *other_refs)

    @pl.when(odd == 1)
    def _():
        run(*other_refs, *mine_refs)


def half_kernel(mine_ref, other_ref, last_ref, half_ref):
    ja = lax.axis_index("ja")
    low_pair = ja < 2
    for side in range(2):
        edge = [jnp.where(low_pair, last_ref[v], mine_ref[20, v]) for v in range(5)]
        put(half_ref, [x[8 * side : 8 * side + 8] for x in edge], 5 + side)
    for side in range(2):
        lo, hi = (mine_ref, other_ref) if side == 0 else (other_ref, mine_ref)
        rows = HALVES[side]

        @pl.when((ja % 2 == side) & low_pair)
        def _():
            for r in range(5):
                put(half_ref, [hi[15 + r, c, rows] for c in range(5)], r)

        @pl.when((ja % 2 == side) & (ja >= 2))
        def _():
            d_hi = [[hi[5 + r, c, rows] for c in range(5)] for r in range(5)]
            n_lo = [[lo[10 + r, c, rows] for c in range(5)] for r in range(5)]
            for q in range(5):
                out = matvec(n_lo, matvec(d_hi, mat_col(lo, q, 0, rows)))
                out = add(mat_col(lo, q, 1, rows), out)
                for r in range(5):
                    half_ref[r, q] = out[r]


def sweeps(s_ref, e_ref, f_ref, y_ref, ends_ref, last):
    planes = s_ref.shape[0]
    value = cell(s_ref, 0)
    put(y_ref, value, 0)
    for j in range(1, planes):
        value = add(cell(s_ref, j), matvec(block(e_ref, j), value))
        put(y_ref, value, j)
    put(ends_ref, [x + z * (1.0 / OMEGA) for x, z in zip(value, last)], 0)
    for j in range(planes - 2, -1, -1):
        value = add(cell(y_ref, j), matvec(block(f_ref, j), value))
    put(ends_ref, value, 1)


def source_kernel(
    tiles_ref, live_ref, cur_ref, force_ref, diag_ref, inv_ref, e_ref, f_ref, s_ref
):
    del tiles_ref
    planes = cur_ref.shape[0]
    before, here = None, masked(live_ref, cell(cur_ref, 0))
    for j in range(planes):
        own = matvec(block(diag_ref, j), here)
        res = [force_ref[j, v] - own[v] + COUPLE * neighbours(here[v]) for v in range(5)]
        out = matvec(block(inv_ref, j), masked(live_ref, res))
        if j > 0:
            linked = matvec(block(e_ref, j), before)
            out = add(out, [x * (1.0 / OMEGA) for x in linked])
        if j < planes - 1:
            after = masked(live_ref, cell(cur_ref, j + 1))
            linked = matvec(block(f_ref, j), after)
            out = add(out, [x * (1.0 / OMEGA) for x in linked])
            before, here = here, after
        put(s_ref, out, j)


def local_kernel(
    half_ref, mats_other_ref, live_ref, pick_ref, own_ref, got_ref, cur_ref, s0_ref,
    inv_ref, e_ref, f_ref,
    s_ref, ends_ref, above_ref, beyond_ref, half_out_ref, y_ref,
):
    for r in range(5):
        put(half_out_ref, cell(half_ref, r), r)
    last = cur_ref.shape[0] - 1
    count = own_ref.shape[0]
    ghosts = ghosts_of(pick_ref, lambda i: own_ref[i] if i < count else got_ref[i - count])
    ghosts = jnp.where(live_ref[...] > 0.0, COUPLE * ghosts, 0.0)
    for j in range(last + 1):
        extra = [ghost_at(ghosts, j, v) for v in range(5)]
        put(s_ref, add(cell(s0_ref, j), matvec(block(inv_ref, j), extra)), j)
    beyond = [jnp.concatenate([half_ref[5, v], half_ref[6, v]], axis=0) for v in range(5)]
    beyond = masked(live_ref, beyond)
    put(beyond_ref, beyond)
    ja = lax.axis_index("ja")
    above = masked(live_ref, cell(mats_other_ref, 20))
    above = [
        jnp.where(ja % 2 == 0, x, jnp.where(ja == 1, z, 0.0)) for x, z in zip(above, beyond)
    ]
    put(above_ref, above)
    linked = matvec(block(f_ref, last), above)
    put(s_ref, add(cell(s_ref, last), [x * (1.0 / OMEGA) for x in linked]), last)
    sweeps(s_ref, e_ref, f_ref, y_ref, ends_ref, masked(live_ref, cell(cur_ref, last)))


def second_kernel(
    live_ref, pick_ref, tiles_ref, cur_ref, above_ref, force_ref, diag_ref, low_ref, up_ref,
    inv_ref, e_ref, f_ref,
    res_ref, s_ref, ends_ref, low0_ref, y_ref,
):
    planes = cur_ref.shape[0]
    zone = lax.axis_index("zone")
    ghosts = ghosts_of(pick_ref, lambda i: tiles_ref[zone ^ offset_of(i, tiles_ref.shape[0])])
    for r in range(5):
        put(low0_ref, cell(low_ref, 0, r), r)
    for j in range(planes):
        here = cell(cur_ref, j)
        applied = matvec(block(diag_ref, j), here)
        if j > 0:
            lower = matvec(block(low_ref, j), cell(cur_ref, j - 1))
            applied = [x - z for x, z in zip(applied, lower)]
        above = cell(cur_ref, j + 1) if j < planes - 1 else cell(above_ref)
        upper = matvec(block(up_ref, j), above)
        res = []
        for v in range(5):
            sides = neighbours(here[v]) + ghost_at(ghosts, j, v)
            all_of = applied[v] - upper[v] - COUPLE * sides
            res.append(force_ref[j, v] - all_of)
        res = masked(live_ref, res)
        put(res_ref, res, j)
        put(s_ref, matvec(block(inv_ref, j), res), j)
    last = cell(cur_ref, planes - 1)
    sweeps(s_ref, e_ref, f_ref, y_ref, ends_ref, last)
    put(ends_ref, last, 2)


def write_kernel(res_ref, res_hbm, sem):
    copy = pltpu.make_async_copy(res_ref, res_hbm, sem)
    copy.start()
    copy.wait()


def mid_kernel(ends_ref, ends_other_ref, mats_ref, mats_other_ref, out_ref):
    def run(ends_lo, mats_lo, ends_hi, mats_hi):
        c_lo = cell(ends_lo, 0)

        @pl.when(lax.axis_index("ja") < 2)
        def _():
            put(out_ref, add(cell(ends_hi, 0), matvec(matrix_of(mats_hi, 0), c_lo)), 0)

        @pl.when(lax.axis_index("ja") >= 2)
        def _():
            turned = add(cell(ends_hi, 1), matvec(matrix_of(mats_hi, 1), c_lo))
            put(out_ref, add(cell(ends_lo, 1), matvec(matrix_of(mats_lo, 2), turned)), 0)


    by_place([ends_ref, mats_ref], [ends_other_ref, mats_other_ref], run)


def join(mine_ref, other_ref, *at):
    mine, other = mine_ref[at], other_ref[at]
    odd = lax.axis_index("ja") % 2 == 1
    return jnp.concatenate([jnp.where(odd, mine, other), jnp.where(odd, other, mine)], axis=0)


def inflows(
    ends_ref, ends_other_ref, mats_ref, mats_other_ref, pair_ref, pair_other_ref,
    half_ref, half_other_ref, inflow_ref,
):
    ja = lax.axis_index("ja")
    zeros = [jnp.zeros((16, 128), jnp.float32)] * 5

    def far():
        beta = [[join(half_ref, half_other_ref, r, c) for c in range(5)] for r in range(5)]
        return add(cell(pair_other_ref, 0), matvec(beta, cell(pair_ref, 0)))

    @pl.when(ja == 0)
    def _():
        put(inflow_ref, zeros, 0)
        b = add(cell(ends_other_ref, 1), matvec(matrix_of(mats_other_ref, 1), cell(ends_ref, 0)))
        b = add(b, matvec(matrix_of(mats_other_ref, 2), far()))
        put(inflow_ref, b, 1)

    @pl.when(ja == 1)
    def _():
        put(inflow_ref, cell(ends_other_ref, 0), 0)
        put(inflow_ref, far(), 1)

    @pl.when(ja == 2)
    def _():
        a = cell(pair_other_ref, 0)
        put(inflow_ref, a, 0)
        a = add(cell(ends_ref, 0), matvec(matrix_of(mats_ref, 0), a))
        b = add(cell(ends_other_ref, 1), matvec(matrix_of(mats_other_ref, 1), a))
        put(inflow_ref, b, 1)

    @pl.when(ja == 3)
    def _():
        a = add(cell(ends_other_ref, 0), matvec(matrix_of(mats_other_ref, 0), cell(pair_other_ref, 0)))
        put(inflow_ref, a, 0)
        put(inflow_ref, zeros, 1)


def final_kernel(
    live_ref, cur_ref, above_ref, beyond_ref, s_ref, e_ref, f_ref,
    ends_ref, ends_other_ref, mats_ref, mats_other_ref, pair_ref, pair_other_ref,
    half_ref, half_other_ref,
    new_ref, above_new_ref, below_new_ref, tile_ref, y_ref, inflow_ref,
):
    planes = cur_ref.shape[0]
    inflows(
        ends_ref, ends_other_ref, mats_ref, mats_other_ref, pair_ref, pair_other_ref,
        half_ref, half_other_ref, inflow_ref,
    )
    value = cell(inflow_ref, 0)
    for j in range(planes):
        value = add(cell(s_ref, j), matvec(block(e_ref, j), value))
        put(y_ref, value, j)
    value = cell(inflow_ref, 1)
    put(above_new_ref, add(cell(above_ref), value))
    for j in range(planes - 1, -1, -1):
        value = add(cell(y_ref, j), matvec(block(f_ref, j), value))
        put(new_ref, add(masked(live_ref, cell(cur_ref, j)), value), j)
    coupling = [[join(half_ref, half_other_ref, r, c) for c in range(5)] for r in range(5)]
    raised = add(cell(inflow_ref, 0), matvec(coupling, value))
    kept = [x * (1.0 - 1.0 / OMEGA) for x in cell(beyond_ref)]
    put(below_new_ref, add(raised, kept))
    pack_faces(lambda j, v: new_ref[j, v], planes, tile_ref)


def last_kernel(
    live_ref, low0_ref, below_ref, cur_ref, res_ref, s_ref, e_ref, f_ref,
    ends_ref, ends_other_ref, mats_ref, mats_other_ref, pair_ref, pair_other_ref,
    half_ref, half_other_ref, res_in_hbm,
    new_hbm, res_hbm, y_ref, inflow_ref, new_ref, res0_ref, sems,
):
    del res_in_hbm
    planes = cur_ref.shape[0]
    ja = lax.axis_index("ja")
    before = [
        jnp.where(ja == 0, 0.0, jnp.where(ja == 2, below_ref[v], ends_other_ref[2, v]))
        for v in range(5)
    ]
    put(res0_ref, add(cell(res_ref, 0), masked(live_ref, matvec(block(low0_ref), before))))
    copies = [pltpu.make_async_copy(res0_ref, res_hbm.at[0], sems.at[planes])]
    copies[0].start()
    inflows(
        ends_ref, ends_other_ref, mats_ref, mats_other_ref, pair_ref, pair_other_ref,
        half_ref, half_other_ref, inflow_ref,
    )
    value = cell(inflow_ref, 0)
    for j in range(planes):
        value = add(cell(s_ref, j), matvec(block(e_ref, j), value))
        put(y_ref, value, j)
    value = cell(inflow_ref, 1)
    for j in range(planes - 1, -1, -1):
        value = add(cell(y_ref, j), matvec(block(f_ref, j), value))
        put(new_ref, add(cell(cur_ref, j), value), j)
        copies.append(pltpu.make_async_copy(new_ref.at[j], new_hbm.at[j], sems.at[j]))
        copies[-1].start()
    for copy in copies:
        copy.wait()


def per_device(
    flow_state, forcing, diag_block, lower_jac, upper_jac, block_inv, east_zone, zone_depth
):
    zones, parts = lax.axis_size("zone"), lax.axis_size("ja")
    assert parts == 4 and ITERS == 2 and zones > 4 and zones & (zones - 1) == 0
    current, force, diag, low, up, inv = (
        x[0] for x in (flow_state, forcing, diag_block, lower_jac, upper_jac, block_inv)
    )
    state = current.shape
    planes, plane, blocks = state[0], state[1:], diag.shape
    matrix = blocks[1:]
    work = [buffer(*state)]

    def swap(x, bit):
        return lax.ppermute(x, "ja", [(p, p ^ bit) for p in range(parts)])

    tile, first, final = call(
        pack_kernel,
        [(1, *state[2:]), plane, plane],
        work + [pltpu.SemaphoreType.DMA],
        flops=10**10,
        far=(0,),
    )(current)
    e, f, mats, live, pick = call(
        matrix_kernel,
        [blocks, blocks, (20, *plane), state[2:], (2, zones, *state[2:])],
        [buffer(*blocks)]
        + [pltpu.SMEM((zones,), jnp.int32)] * 2
        + [pltpu.SemaphoreType.DMA((2,))],
        flops=5 * 10**9,
        far=(0, 1),
    )(zone_depth, east_zone, tile, inv, low, up)
    tiles, stride = tile, zones // 2
    while True:
        got = lax.ppermute(tiles, "zone", [(z, z ^ stride) for z in range(zones)])
        if stride == 1:
            break
        both = (2 * tiles.shape[0], *state[2:])
        if stride == zones // 2:
            mats, tiles = call(relay_kernel, [(21, *plane), both], flops=10**5)(
                tiles, got, mats, first
            )
            mats_other = swap(mats, 1)
            half = call(half_kernel, [(7, plane[0], 8, plane[2])], flops=10**5)(
                mats, mats_other, final
            )[0]
        else:
            tiles = call(merge_kernel, [both], flops=10**5)(tiles, got, half)[0]
        stride //= 2
    half = swap(half, 3)
    s0 = call(source_kernel, [state], flops=2 * 10**9)(tiles, live, current, force, diag, inv, e, f)[0]
    s, ends, above, beyond, half = call(
        local_kernel, [state, (2, *plane), plane, plane, (5, *half.shape[1:])], work
    )(
        half, mats_other, live, pick, tiles, got, current, s0, inv, e, f
    )
    ends_other = swap(ends, 1)
    half_other = swap(half, 1)
    pair = call(mid_kernel, [(1, *plane)], flops=10**5)(ends, ends_other, mats, mats_other)[0]
    pair_other = swap(pair, 3)
    flows = [buffer(2, *plane)]
    current, above, below, tile = call(
        final_kernel, [state, plane, plane, (zones, *state[2:])], work + flows
    )(
        live, current, above, beyond, s, e, f,
        ends, ends_other, mats, mats_other, pair, pair_other, half, half_other,
    )

    got = lax.all_to_all(tile, "zone", 0, 0, tiled=True)
    residual, s, ends, low0 = call(second_kernel, [state, state, (3, *plane), matrix], work)(
        live, pick, got, current, above, force, diag, low, up, inv, e, f
    )
    ends_other = swap(ends, 1)
    pair = call(mid_kernel, [(1, *plane)])(ends, ends_other, mats, mats_other)[0]
    pair_other = swap(pair, 3)
    written = call(write_kernel, [state], [pltpu.SemaphoreType.DMA], out_specs=[HBM])(residual)[0]
    current, residual = call(
        last_kernel,
        [state, state],
        work + flows + work + [buffer(*plane), pltpu.SemaphoreType.DMA((planes + 1,))],
        out_specs=[HBM, HBM],
        alias={16: 1},
    )(
        live, low0, below, current, residual, s, e, f,
        ends, ends_other, mats, mats_other, pair, pair_other, half, half_other, written,
    )
    return (current[None], residual[None])


def solution(mesh):
    state = P("zone", "ja", None, None, None)
    blocks = P("zone", "ja", None, None, None, None)
    return jax.shard_map(
        per_device,
        mesh=mesh,
        in_specs=(state, state, blocks, blocks, blocks, blocks, P(), P()),
        out_specs=(state, state),
        check_vma=False,
    )
```

```python
import jax
import jax.numpy as jnp
from jax import lax
from jax.experimental import pallas as pl
from jax.experimental.pallas import tpu as pltpu
from jax.sharding import PartitionSpec as P

ITERS = 2
OMEGA = 1.2
COUPLE = 0.25

VMEM = pl.BlockSpec(memory_space=pltpu.VMEM)
ANY = pl.BlockSpec(memory_space=pl.ANY)
HBM = pl.BlockSpec(memory_space=pltpu.HBM)


def call(kernel, shapes, scratch=(), flops=10**9, far=(), out_specs=None, alias=None):
    alias = alias or {}

    def run(*arrays):
        arrays = [
            pltpu.with_memory_space_constraint(a, pltpu.HBM) if i in far else a
            for i, a in enumerate(arrays)
        ]
        return pl.pallas_call(
            kernel,
            out_shape=[jax.ShapeDtypeStruct(s, jnp.float32) for s in shapes],
            in_specs=[
                HBM if i in far else ANY if i in alias else VMEM for i in range(len(arrays))
            ],
            out_specs=out_specs or [VMEM] * len(shapes),
            scratch_shapes=list(scratch),
            input_output_aliases=alias,
            compiler_params=pltpu.CompilerParams(vmem_limit_bytes=8 * 2**20),
            cost_estimate=pl.CostEstimate(flops=flops, bytes_accessed=flops // 10**3, transcendentals=0),
        )(*arrays)

    return run


def buffer(*shape):
    return pltpu.VMEM(shape, jnp.float32)


def iota(dim):
    return lax.broadcasted_iota(jnp.int32, (16, 128), dim)


def matvec(matrix, vector):
    n = len(vector)
    out = []
    for r in range(n):
        acc = matrix[r][0] * vector[0]
        for c in range(1, n):
            acc = acc + matrix[r][c] * vector[c]
        out.append(acc)
    return out


def block(ref, *lead):
    return [[ref[(*lead, r, c)] for c in range(5)] for r in range(5)]


def matrix_of(ref, i):
    return [cell(ref, 5 * i + r) for r in range(5)]


def cell(ref, *lead):
    return [ref[(*lead, v)] for v in range(5)]


def put(ref, values, *lead):
    for v, value in enumerate(values):
        ref[(*lead, v)] = value


def add(a, b):
    return [x + y for x, y in zip(a, b)]


def pack_faces(load, planes, tile_ref):
    lane = iota(1)
    tile = jnp.zeros((16, 128), jnp.float32)
    for j in range(planes):
        for v in range(5):
            q = 2 * (j * 5 + v)
            here = (lane == q) | (lane == (q - 1) % 128)
            x = load(j, v)
            tile = jnp.where(here, pltpu.roll(x, q, 1) if q else x, tile)
    for w in range(tile_ref.shape[0]):
        tile_ref[w] = tile


def masked(live_ref, values):
    live = live_ref[...] > 0.0
    return [jnp.where(live, x, 0.0) for x in values]


def pack_kernel(flow_hbm, tile_ref, first_ref, last_ref, flow_ref, sem):
    copy = pltpu.make_async_copy(flow_hbm, flow_ref, sem)
    copy.start()
    copy.wait()
    put(first_ref, cell(flow_ref, 0))
    put(last_ref, cell(flow_ref, flow_ref.shape[0] - 1))
    pack_faces(lambda j, v: flow_ref[j, v], flow_ref.shape[0], tile_ref)


def merge_kernel(own_ref, got_ref, *refs):
    out_ref = refs[-1]
    count = own_ref.shape[0]
    for w in range(count):
        out_ref[w] = own_ref[w]
        out_ref[count + w] = got_ref[w]


def relay_kernel(own_ref, got_ref, mats_ref, first_ref, mats_out_ref, out_ref):
    merge_kernel(own_ref, got_ref, out_ref)
    for i in range(20):
        put(mats_out_ref, cell(mats_ref, i), i)
    put(mats_out_ref, cell(first_ref), 20)


def neighbours(x):
    lane, row = iota(1), iota(0)
    total = jnp.where(lane == 0, 0.0, pltpu.roll(x, 1, 1))
    total = total + jnp.where(lane == 127, 0.0, pltpu.roll(x, 127, 1))
    total = total + jnp.where(row == 0, 0.0, pltpu.roll(x, 1, 0))
    return total + jnp.where(row == 15, 0.0, pltpu.roll(x, 15, 0))


def offset_of(place, zones):
    offset, stride = 0, zones // 2
    while stride:
        offset, place, stride = offset + stride * (place % 2), place // 2, stride // 2
    return offset


def ghosts_of(pick_ref, tile_at):
    low = high = jnp.zeros((16, 128), jnp.float32)
    for i in range(pick_ref.shape[1]):
        low = jnp.where(pick_ref[0, i] > 0.0, tile_at(i), low)
        high = jnp.where(pick_ref[1, i] > 0.0, tile_at(i), high)
    return jnp.where(iota(1) % 2 == 0, pltpu.roll(low, 1, 1), pltpu.roll(high, 127, 1))


def ghost_at(ghosts, j, v):
    lane = iota(1)
    q = 2 * (j * 5 + v)
    turned = pltpu.roll(ghosts, 128 - q, 1) if q else ghosts
    return jnp.where((lane == 0) | (lane == 127), turned, 0.0)


HALVES = [pl.ds(0, 8), pl.ds(8, 8)]


def col(ref, q, j, rows):
    return [ref[j, r, q, rows] for r in range(5)]


def put_col(ref, values, q, j, rows):
    for r in range(5):
        ref[j, r, q, rows] = values[r]


def put_mat_col(ref, values, q, i, rows):
    for r in range(5):
        ref[5 * i + r, q, rows] = values[r]


def mat_col(ref, q, i, rows):
    return [ref[5 * i + r, q, rows] for r in range(5)]


def mat(ref, j, rows):
    return [[ref[j, r, c, rows] for c in range(5)] for r in range(5)]


def matrix_kernel(
    depth_hbm, east_hbm, tile_ref, inv_ref, low_ref, up_ref,
    e_ref, f_ref, mats_ref, live_ref, pick_ref,
    y_ref, depth_ref, east_ref, sems,
):
    del tile_ref
    last = inv_ref.shape[0] - 1
    scalars = [
        pltpu.make_async_copy(depth_hbm, depth_ref, sems.at[0]),
        pltpu.make_async_copy(east_hbm, east_ref, sems.at[1]),
    ]
    for copy in scalars:
        copy.start()

    def products(j, rows):
        inv = mat(inv_ref, j, rows)
        for jac_ref, out_ref in ((low_ref, e_ref), (up_ref, f_ref)):
            for q in range(5):
                product = matvec(inv, col(jac_ref, q, j, rows))
                put_col(out_ref, [OMEGA * x for x in product], q, j, rows)

    def forward(j, carry):
        for rows in HALVES:
            products(j, rows)
            e = mat(e_ref, j, rows)
            for q in range(5):
                put_col(y_ref, matvec(e, col(y_ref, q, j - 1, rows)), q, j, rows)
        return carry

    def backward(step, carry):
        j = last - 1 - step
        for rows in HALVES:
            f = mat(f_ref, j, rows)
            for q in range(5):
                turned = matvec(f, mat_col(mats_ref, q, 1, rows))
                put_mat_col(mats_ref, add(col(y_ref, q, j, rows), turned), q, 1, rows)
                put_mat_col(mats_ref, matvec(f, mat_col(mats_ref, q, 2, rows)), q, 2, rows)
        return carry

    for rows in HALVES:
        products(0, rows)
        for q in range(5):
            put_col(y_ref, col(e_ref, q, 0, rows), q, 0, rows)
    lax.fori_loop(1, last + 1, forward, 0)
    for rows in HALVES:
        for q in range(5):
            put_mat_col(mats_ref, col(y_ref, q, last, rows), q, 0, rows)
            put_mat_col(mats_ref, col(y_ref, q, last, rows), q, 1, rows)
            put_mat_col(mats_ref, col(f_ref, q, last, rows), q, 2, rows)
            put_mat_col(mats_ref, col(f_ref, q, last, rows), q, 3, rows)
    lax.fori_loop(0, last, backward, 0)
    for copy in scalars:
        copy.wait()
    zone = lax.axis_index("zone")
    row = iota(0)
    live_ref[...] = jnp.where(row < depth_ref[zone], 1.0, 0.0)
    for i in range(pick_ref.shape[1]):
        w = zone ^ offset_of(i, pick_ref.shape[1])
        rows = row < depth_ref[w]
        pick_ref[0, i] = jnp.where(rows & (east_ref[w] == zone), 1.0, 0.0)
        pick_ref[1, i] = jnp.where(rows & (east_ref[zone] == w), 1.0, 0.0)


def by_place(mine_refs, other_refs, run):
    odd = lax.axis_index("ja") % 2

    @pl.when(odd == 0)
    def _():
        run(*mine_refs, *other_refs)

    @pl.when(odd == 1)
    def _():
        run(*other_refs, *mine_refs)


def half_kernel(mine_ref, other_ref, last_ref, half_ref):
    ja = lax.axis_index("ja")
    low_pair = ja < 2
    for side in range(2):
        first = [jnp.where(ja == 3, other_ref[20, v], mine_ref[20, v]) for v in range(5)]
        edge = [jnp.where(low_pair, last_ref[v], first[v]) for v in range(5)]
        put(half_ref, [x[8 * side : 8 * side + 8] for x in edge], 5 + side)
    for side in range(2):
        lo, hi = (mine_ref, other_ref) if side == 0 else (other_ref, mine_ref)
        rows = HALVES[side]

        @pl.when((ja % 2 == side) & low_pair)
        def _():
            for r in range(5):
                put(half_ref, [hi[15 + r, c, rows] for c in range(5)], r)

        @pl.when((ja % 2 == side) & (ja >= 2))
        def _():
            d_hi = [[hi[5 + r, c, rows] for c in range(5)] for r in range(5)]
            n_lo = [[lo[10 + r, c, rows] for c in range(5)] for r in range(5)]
            for q in range(5):
                out = matvec(n_lo, matvec(d_hi, mat_col(lo, q, 0, rows)))
                out = add(mat_col(lo, q, 1, rows), out)
                for r in range(5):
                    half_ref[r, q] = out[r]


def sweeps(s_ref, e_ref, f_ref, y_ref, ends_ref, last):
    planes = s_ref.shape[0]
    value = cell(s_ref, 0)
    put(y_ref, value, 0)
    for j in range(1, planes):
        value = add(cell(s_ref, j), matvec(block(e_ref, j), value))
        put(y_ref, value, j)
    put(ends_ref, [x + z * (1.0 / OMEGA) for x, z in zip(value, last)], 0)
    for j in range(planes - 2, -1, -1):
        value = add(cell(y_ref, j), matvec(block(f_ref, j), value))
    put(ends_ref, value, 1)


def source_kernel(
    tiles_ref, live_ref, cur_ref, force_ref, diag_ref, inv_ref, e_ref, f_ref, s_ref
):
    del tiles_ref
    planes = cur_ref.shape[0]
    before, here = None, masked(live_ref, cell(cur_ref, 0))
    for j in range(planes):
        own = matvec(block(diag_ref, j), here)
        res = [force_ref[j, v] - own[v] + COUPLE * neighbours(here[v]) for v in range(5)]
        out = matvec(block(inv_ref, j), masked(live_ref, res))
        if j > 0:
            linked = matvec(block(e_ref, j), before)
            out = add(out, [x * (1.0 / OMEGA) for x in linked])
        if j < planes - 1:
            after = masked(live_ref, cell(cur_ref, j + 1))
            linked = matvec(block(f_ref, j), after)
            out = add(out, [x * (1.0 / OMEGA) for x in linked])
            before, here = here, after
        put(s_ref, out, j)


def local_kernel(
    mats_other_ref, live_ref, pick_ref, own_ref, got_ref, cur_ref, s0_ref,
    inv_ref, e_ref, f_ref,
    s_ref, ends_ref, above_ref, y_ref,
):
    last = cur_ref.shape[0] - 1
    count = own_ref.shape[0]
    ghosts = ghosts_of(pick_ref, lambda i: own_ref[i] if i < count else got_ref[i - count])
    ghosts = jnp.where(live_ref[...] > 0.0, COUPLE * ghosts, 0.0)
    for j in range(last + 1):
        extra = [ghost_at(ghosts, j, v) for v in range(5)]
        put(s_ref, add(cell(s0_ref, j), matvec(block(inv_ref, j), extra)), j)
    even = lax.axis_index("ja") % 2 == 0
    above = [jnp.where(even, x, 0.0) for x in masked(live_ref, cell(mats_other_ref, 20))]
    put(above_ref, above)
    linked = matvec(block(f_ref, last), above)
    put(s_ref, add(cell(s_ref, last), [x * (1.0 / OMEGA) for x in linked]), last)
    sweeps(s_ref, e_ref, f_ref, y_ref, ends_ref, masked(live_ref, cell(cur_ref, last)))


def second_kernel(
    live_ref, pick_ref, tiles_ref, cur_ref, above_ref, force_ref, diag_ref, low_ref, up_ref,
    inv_ref, e_ref, f_ref,
    res_ref, s_ref, ends_ref, low0_ref, y_ref,
):
    planes = cur_ref.shape[0]
    zone = lax.axis_index("zone")
    ghosts = ghosts_of(pick_ref, lambda i: tiles_ref[zone ^ offset_of(i, tiles_ref.shape[0])])
    for r in range(5):
        put(low0_ref, cell(low_ref, 0, r), r)
    for j in range(planes):
        here = cell(cur_ref, j)
        applied = matvec(block(diag_ref, j), here)
        if j > 0:
            lower = matvec(block(low_ref, j), cell(cur_ref, j - 1))
            applied = [x - z for x, z in zip(applied, lower)]
        above = cell(cur_ref, j + 1) if j < planes - 1 else cell(above_ref)
        upper = matvec(block(up_ref, j), above)
        res = []
        for v in range(5):
            sides = neighbours(here[v]) + ghost_at(ghosts, j, v)
            all_of = applied[v] - upper[v] - COUPLE * sides
            res.append(force_ref[j, v] - all_of)
        res = masked(live_ref, res)
        put(res_ref, res, j)
        put(s_ref, matvec(block(inv_ref, j), res), j)
    last = cell(cur_ref, planes - 1)
    sweeps(s_ref, e_ref, f_ref, y_ref, ends_ref, last)
    put(ends_ref, last, 2)


def write_kernel(res_ref, res_hbm, sem):
    copy = pltpu.make_async_copy(res_ref, res_hbm, sem)
    copy.start()
    copy.wait()


def compose(ends_lo, mats_lo, ends_hi, mats_hi, out_ref, first=None):
    c_lo = cell(ends_lo, 0)

    @pl.when(lax.axis_index("ja") < 2)
    def _():
        put(out_ref, add(cell(ends_hi, 0), matvec(matrix_of(mats_hi, 0), c_lo)), 0)

    @pl.when(lax.axis_index("ja") >= 2)
    def _():
        turned = add(cell(ends_hi, 1), matvec(matrix_of(mats_hi, 1), c_lo))
        raised = add(cell(ends_lo, 1), matvec(matrix_of(mats_lo, 2), turned))
        if first is not None:
            raised = add(raised, first(mats_lo))
        put(out_ref, raised, 0)


def mid_kernel(ends_ref, ends_other_ref, mats_ref, mats_other_ref, out_ref):
    def run(ends_lo, mats_lo, ends_hi, mats_hi):
        compose(ends_lo, mats_lo, ends_hi, mats_hi, out_ref)

    by_place([ends_ref, mats_ref], [ends_other_ref, mats_other_ref], run)


def first_mid_kernel(
    live_ref, half_ref, ends_ref, ends_other_ref, mats_ref, mats_other_ref,
    out_ref, beyond_ref, half_out_ref,
):
    def first(mats_lo):
        return [x * (1.0 / OMEGA) for x in masked(live_ref, cell(mats_lo, 20))]

    def run(ends_lo, mats_lo, ends_hi, mats_hi):
        compose(ends_lo, mats_lo, ends_hi, mats_hi, out_ref, first)

    by_place([ends_ref, mats_ref], [ends_other_ref, mats_other_ref], run)
    for r in range(5):
        put(half_out_ref, cell(half_ref, r), r)
    beyond = [jnp.concatenate([half_ref[5, v], half_ref[6, v]], axis=0) for v in range(5)]
    put(beyond_ref, masked(live_ref, beyond))


def join(mine_ref, other_ref, *at):
    mine, other = mine_ref[at], other_ref[at]
    odd = lax.axis_index("ja") % 2 == 1
    return jnp.concatenate([jnp.where(odd, mine, other), jnp.where(odd, other, mine)], axis=0)


def inflows(
    ends_ref, ends_other_ref, mats_ref, mats_other_ref, pair_ref, pair_other_ref,
    half_ref, half_other_ref, inflow_ref, live_ref=None, beyond_ref=None,
):
    ja = lax.axis_index("ja")
    zeros = [jnp.zeros((16, 128), jnp.float32)] * 5

    def joined():
        return [[join(half_ref, half_other_ref, r, c) for c in range(5)] for r in range(5)]

    def passed(value, coupling, first):
        if beyond_ref is None:
            return value
        return add(value, [x * (1.0 / OMEGA) for x in matvec(coupling, first)])

    def far(mats_hi_ref):
        first = None if beyond_ref is None else cell(beyond_ref)
        a = passed(cell(pair_ref, 0), matrix_of(mats_hi_ref, 3), first)
        return add(cell(pair_other_ref, 0), matvec(joined(), a))

    def near(mats_lo_ref):
        first = None if beyond_ref is None else masked(live_ref, cell(mats_lo_ref, 20))
        return passed(cell(pair_other_ref, 0), joined(), first)

    @pl.when(ja == 0)
    def _():
        put(inflow_ref, zeros, 0)
        b = add(cell(ends_other_ref, 1), matvec(matrix_of(mats_other_ref, 1), cell(ends_ref, 0)))
        b = add(b, matvec(matrix_of(mats_other_ref, 2), far(mats_other_ref)))
        put(inflow_ref, b, 1)

    @pl.when(ja == 1)
    def _():
        put(inflow_ref, cell(ends_other_ref, 0), 0)
        put(inflow_ref, far(mats_ref), 1)

    @pl.when(ja == 2)
    def _():
        a = near(mats_ref)
        put(inflow_ref, a, 0)
        a = add(cell(ends_ref, 0), matvec(matrix_of(mats_ref, 0), a))
        b = add(cell(ends_other_ref, 1), matvec(matrix_of(mats_other_ref, 1), a))
        put(inflow_ref, b, 1)

    @pl.when(ja == 3)
    def _():
        a = near(mats_other_ref)
        a = add(cell(ends_other_ref, 0), matvec(matrix_of(mats_other_ref, 0), a))
        put(inflow_ref, a, 0)
        put(inflow_ref, zeros, 1)


def final_kernel(
    live_ref, cur_ref, above_ref, beyond_ref, s_ref, e_ref, f_ref,
    ends_ref, ends_other_ref, mats_ref, mats_other_ref, pair_ref, pair_other_ref,
    half_ref, half_other_ref,
    new_ref, above_new_ref, below_new_ref, tile_ref, y_ref, inflow_ref,
):
    planes = cur_ref.shape[0]
    inflows(
        ends_ref, ends_other_ref, mats_ref, mats_other_ref, pair_ref, pair_other_ref,
        half_ref, half_other_ref, inflow_ref, live_ref, beyond_ref,
    )
    value = cell(inflow_ref, 0)
    for j in range(planes):
        value = add(cell(s_ref, j), matvec(block(e_ref, j), value))
        put(y_ref, value, j)
    value = cell(inflow_ref, 1)
    kept = [x * (1.0 - 1.0 / OMEGA) for x in cell(beyond_ref)]
    inner = lax.axis_index("ja") == 1
    above = add(cell(above_ref), [jnp.where(inner, x, 0.0) for x in kept])
    put(above_new_ref, add(above, value))
    for j in range(planes - 1, -1, -1):
        value = add(cell(y_ref, j), matvec(block(f_ref, j), value))
        put(new_ref, add(masked(live_ref, cell(cur_ref, j)), value), j)
    coupling = [[join(half_ref, half_other_ref, r, c) for c in range(5)] for r in range(5)]
    raised = add(cell(inflow_ref, 0), matvec(coupling, value))
    put(below_new_ref, add(raised, kept))
    pack_faces(lambda j, v: new_ref[j, v], planes, tile_ref)


def last_kernel(
    live_ref, low0_ref, below_ref, cur_ref, res_ref, s_ref, e_ref, f_ref,
    ends_ref, ends_other_ref, mats_ref, mats_other_ref, pair_ref, pair_other_ref,
    half_ref, half_other_ref, res_in_hbm,
    new_hbm, res_hbm, y_ref, inflow_ref, new_ref, res0_ref, sems,
):
    del res_in_hbm
    planes = cur_ref.shape[0]
    ja = lax.axis_index("ja")
    before = [
        jnp.where(ja == 0, 0.0, jnp.where(ja == 2, below_ref[v], ends_other_ref[2, v]))
        for v in range(5)
    ]
    put(res0_ref, add(cell(res_ref, 0), masked(live_ref, matvec(block(low0_ref), before))))
    copies = [pltpu.make_async_copy(res0_ref, res_hbm.at[0], sems.at[planes])]
    copies[0].start()
    inflows(
        ends_ref, ends_other_ref, mats_ref, mats_other_ref, pair_ref, pair_other_ref,
        half_ref, half_other_ref, inflow_ref,
    )
    value = cell(inflow_ref, 0)
    for j in range(planes):
        value = add(cell(s_ref, j), matvec(block(e_ref, j), value))
        put(y_ref, value, j)
    value = cell(inflow_ref, 1)
    for j in range(planes - 1, -1, -1):
        value = add(cell(y_ref, j), matvec(block(f_ref, j), value))
        put(new_ref, add(cell(cur_ref, j), value), j)
        copies.append(pltpu.make_async_copy(new_ref.at[j], new_hbm.at[j], sems.at[j]))
        copies[-1].start()
    for copy in copies:
        copy.wait()


def per_device(
    flow_state, forcing, diag_block, lower_jac, upper_jac, block_inv, east_zone, zone_depth
):
    zones, parts = lax.axis_size("zone"), lax.axis_size("ja")
    assert parts == 4 and ITERS == 2 and zones > 4 and zones & (zones - 1) == 0
    current, force, diag, low, up, inv = (
        x[0] for x in (flow_state, forcing, diag_block, lower_jac, upper_jac, block_inv)
    )
    state = current.shape
    planes, plane, blocks = state[0], state[1:], diag.shape
    matrix = blocks[1:]
    work = [buffer(*state)]

    def swap(x, bit):
        return lax.ppermute(x, "ja", [(p, p ^ bit) for p in range(parts)])

    tile, first, final = call(
        pack_kernel,
        [(1, *state[2:]), plane, plane],
        work + [pltpu.SemaphoreType.DMA],
        flops=10**10,
        far=(0,),
    )(current)
    e, f, mats, live, pick = call(
        matrix_kernel,
        [blocks, blocks, (20, *plane), state[2:], (2, zones, *state[2:])],
        [buffer(*blocks)]
        + [pltpu.SMEM((zones,), jnp.int32)] * 2
        + [pltpu.SemaphoreType.DMA((2,))],
        flops=5 * 10**9,
        far=(0, 1),
    )(zone_depth, east_zone, tile, inv, low, up)
    tiles, stride = tile, zones // 2
    while True:
        got = lax.ppermute(tiles, "zone", [(z, z ^ stride) for z in range(zones)])
        if stride == 1:
            break
        both = (2 * tiles.shape[0], *state[2:])
        if stride == zones // 2:
            mats, tiles = call(relay_kernel, [(21, *plane), both], flops=10**5)(
                tiles, got, mats, first
            )
            mats_other = swap(mats, 1)
            half = call(half_kernel, [(7, plane[0], 8, plane[2])], flops=10**5)(
                mats, mats_other, final
            )[0]
        else:
            tiles = call(merge_kernel, [both], flops=10**5)(tiles, got, half)[0]
        stride //= 2
    half = swap(half, 3)
    s0 = call(source_kernel, [state], flops=2 * 10**9)(tiles, live, current, force, diag, inv, e, f)[0]
    s, ends, above = call(local_kernel, [state, (2, *plane), plane], work)(
        mats_other, live, pick, tiles, got, current, s0, inv, e, f
    )
    ends_other = swap(ends, 1)
    pair, beyond, half = call(
        first_mid_kernel, [(1, *plane), plane, (5, *half.shape[1:])], flops=10**5
    )(live, half, ends, ends_other, mats, mats_other)
    half_other = swap(half, 1)
    pair_other = swap(pair, 3)
    flows = [buffer(2, *plane)]
    current, above, below, tile = call(
        final_kernel, [state, plane, plane, (zones, *state[2:])], work + flows
    )(
        live, current, above, beyond, s, e, f,
        ends, ends_other, mats, mats_other, pair, pair_other, half, half_other,
    )

    got = lax.all_to_all(tile, "zone", 0, 0, tiled=True)
    residual, s, ends, low0 = call(second_kernel, [state, state, (3, *plane), matrix], work)(
        live, pick, got, current, above, force, diag, low, up, inv, e, f
    )
    ends_other = swap(ends, 1)
    pair = call(mid_kernel, [(1, *plane)])(ends, ends_other, mats, mats_other)[0]
    pair_other = swap(pair, 3)
    written = call(write_kernel, [state], [pltpu.SemaphoreType.DMA], out_specs=[HBM])(residual)[0]
    current, residual = call(
        last_kernel,
        [state, state],
        work + flows + work + [buffer(*plane), pltpu.SemaphoreType.DMA((planes + 1,))],
        out_specs=[HBM, HBM],
        alias={16: 1},
    )(
        live, low0, below, current, residual, s, e, f,
        ends, ends_other, mats, mats_other, pair, pair_other, half, half_other, written,
    )
    return (current[None], residual[None])


def solution(mesh):
    state = P("zone", "ja", None, None, None)
    blocks = P("zone", "ja", None, None, None, None)
    return jax.shard_map(
        per_device,
        mesh=mesh,
        in_specs=(state, state, blocks, blocks, blocks, blocks, P(), P()),
        out_specs=(state, state),
        check_vma=False,
    )
```

```python
import jax
import jax.numpy as jnp
from jax import lax
from jax.experimental import pallas as pl
from jax.experimental.pallas import tpu as pltpu
from jax.sharding import PartitionSpec as P

ITERS = 2
OMEGA = 1.2
COUPLE = 0.25

VMEM = pl.BlockSpec(memory_space=pltpu.VMEM)
ANY = pl.BlockSpec(memory_space=pl.ANY)
HBM = pl.BlockSpec(memory_space=pltpu.HBM)


def call(kernel, shapes, scratch=(), flops=10**9, far=(), out_specs=None, alias=None):
    alias = alias or {}

    def run(*arrays):
        arrays = [
            pltpu.with_memory_space_constraint(a, pltpu.HBM) if i in far else a
            for i, a in enumerate(arrays)
        ]
        return pl.pallas_call(
            kernel,
            out_shape=[jax.ShapeDtypeStruct(s, jnp.float32) for s in shapes],
            in_specs=[
                HBM if i in far else ANY if i in alias else VMEM for i in range(len(arrays))
            ],
            out_specs=out_specs or [VMEM] * len(shapes),
            scratch_shapes=list(scratch),
            input_output_aliases=alias,
            compiler_params=pltpu.CompilerParams(vmem_limit_bytes=8 * 2**20),
            cost_estimate=pl.CostEstimate(flops=flops, bytes_accessed=flops // 10**3, transcendentals=0),
        )(*arrays)

    return run


def buffer(*shape):
    return pltpu.VMEM(shape, jnp.float32)


def iota(dim):
    return lax.broadcasted_iota(jnp.int32, (16, 128), dim)


def matvec(matrix, vector):
    n = len(vector)
    out = []
    for r in range(n):
        acc = matrix[r][0] * vector[0]
        for c in range(1, n):
            acc = acc + matrix[r][c] * vector[c]
        out.append(acc)
    return out


def block(ref, *lead):
    return [[ref[(*lead, r, c)] for c in range(5)] for r in range(5)]


def matrix_of(ref, i):
    return [cell(ref, 5 * i + r) for r in range(5)]


def cell(ref, *lead):
    return [ref[(*lead, v)] for v in range(5)]


def put(ref, values, *lead):
    for v, value in enumerate(values):
        ref[(*lead, v)] = value


def add(a, b):
    return [x + y for x, y in zip(a, b)]


def pack_faces(load, planes, tile_ref):
    lane = iota(1)
    tile = jnp.zeros((16, 128), jnp.float32)
    for j in range(planes):
        for v in range(5):
            q = 2 * (j * 5 + v)
            here = (lane == q) | (lane == (q - 1) % 128)
            x = load(j, v)
            tile = jnp.where(here, pltpu.roll(x, q, 1) if q else x, tile)
    for w in range(tile_ref.shape[0]):
        tile_ref[w] = tile


def masked(live_ref, values):
    live = live_ref[...] > 0.0
    return [jnp.where(live, x, 0.0) for x in values]


def pack_kernel(flow_hbm, tile_ref, first_ref, last_ref, flow_ref, sem):
    copy = pltpu.make_async_copy(flow_hbm, flow_ref, sem)
    copy.start()
    copy.wait()
    put(first_ref, cell(flow_ref, 0))
    put(last_ref, cell(flow_ref, flow_ref.shape[0] - 1))
    pack_faces(lambda j, v: flow_ref[j, v], flow_ref.shape[0], tile_ref)


def merge_kernel(own_ref, got_ref, *refs):
    out_ref = refs[-1]
    count = own_ref.shape[0]
    for w in range(count):
        out_ref[w] = own_ref[w]
        out_ref[count + w] = got_ref[w]


def select_kernel(own_ref, got_ref, after_ref, pick_ref, partner_ref, mine_ref, theirs_ref):
    del after_ref
    count = own_ref.shape[0]

    def tile_at(i):
        return own_ref[i] if i < count else got_ref[i - count]

    mine_ref[...] = ghosts_of(pick_ref, tile_at, 2 * count)
    theirs_ref[...] = ghosts_of(partner_ref, tile_at, 2 * count)


def relay_kernel(own_ref, got_ref, mats_ref, first_ref, mats_out_ref, out_ref):
    merge_kernel(own_ref, got_ref, out_ref)
    for i in range(20):
        put(mats_out_ref, cell(mats_ref, i), i)
    put(mats_out_ref, cell(first_ref), 20)


def neighbours(x):
    lane, row = iota(1), iota(0)
    total = jnp.where(lane == 0, 0.0, pltpu.roll(x, 1, 1))
    total = total + jnp.where(lane == 127, 0.0, pltpu.roll(x, 127, 1))
    total = total + jnp.where(row == 0, 0.0, pltpu.roll(x, 1, 0))
    return total + jnp.where(row == 15, 0.0, pltpu.roll(x, 15, 0))


def offset_of(place, zones):
    offset, stride = 0, zones // 2
    while stride:
        offset, place, stride = offset + stride * (place % 2), place // 2, stride // 2
    return offset


def ghosts_of(pick_ref, tile_at, count):
    low = high = jnp.zeros((16, 128), jnp.float32)
    for i in range(count):
        low = jnp.where(pick_ref[0, i] > 0.0, tile_at(i), low)
        high = jnp.where(pick_ref[1, i] > 0.0, tile_at(i), high)
    return jnp.where(iota(1) % 2 == 0, pltpu.roll(low, 1, 1), pltpu.roll(high, 127, 1))


def ghost_at(ghosts, j, v):
    lane = iota(1)
    q = 2 * (j * 5 + v)
    turned = pltpu.roll(ghosts, 128 - q, 1) if q else ghosts
    return jnp.where((lane == 0) | (lane == 127), turned, 0.0)


HALVES = [pl.ds(0, 8), pl.ds(8, 8)]


def col(ref, q, j, rows):
    return [ref[j, r, q, rows] for r in range(5)]


def put_col(ref, values, q, j, rows):
    for r in range(5):
        ref[j, r, q, rows] = values[r]


def put_mat_col(ref, values, q, i, rows):
    for r in range(5):
        ref[5 * i + r, q, rows] = values[r]


def mat_col(ref, q, i, rows):
    return [ref[5 * i + r, q, rows] for r in range(5)]


def mat(ref, j, rows):
    return [[ref[j, r, c, rows] for c in range(5)] for r in range(5)]


def matrix_kernel(
    depth_hbm, east_hbm, tile_ref, inv_ref, low_ref, up_ref,
    e_ref, f_ref, mats_ref, live_ref, pick_ref, partner_ref,
    y_ref, depth_ref, east_ref, sems,
):
    del tile_ref
    last = inv_ref.shape[0] - 1
    scalars = [
        pltpu.make_async_copy(depth_hbm, depth_ref, sems.at[0]),
        pltpu.make_async_copy(east_hbm, east_ref, sems.at[1]),
    ]
    for copy in scalars:
        copy.start()

    def products(j, rows):
        inv = mat(inv_ref, j, rows)
        for jac_ref, out_ref in ((low_ref, e_ref), (up_ref, f_ref)):
            for q in range(5):
                product = matvec(inv, col(jac_ref, q, j, rows))
                put_col(out_ref, [OMEGA * x for x in product], q, j, rows)

    def forward(j, carry):
        for rows in HALVES:
            products(j, rows)
            e = mat(e_ref, j, rows)
            for q in range(5):
                put_col(y_ref, matvec(e, col(y_ref, q, j - 1, rows)), q, j, rows)
        return carry

    def backward(step, carry):
        j = last - 1 - step
        for rows in HALVES:
            f = mat(f_ref, j, rows)
            for q in range(5):
                turned = matvec(f, mat_col(mats_ref, q, 1, rows))
                put_mat_col(mats_ref, add(col(y_ref, q, j, rows), turned), q, 1, rows)
                put_mat_col(mats_ref, matvec(f, mat_col(mats_ref, q, 2, rows)), q, 2, rows)
        return carry

    for rows in HALVES:
        products(0, rows)
        for q in range(5):
            put_col(y_ref, col(e_ref, q, 0, rows), q, 0, rows)
    lax.fori_loop(1, last + 1, forward, 0)
    for rows in HALVES:
        for q in range(5):
            put_mat_col(mats_ref, col(y_ref, q, last, rows), q, 0, rows)
            put_mat_col(mats_ref, col(y_ref, q, last, rows), q, 1, rows)
            put_mat_col(mats_ref, col(f_ref, q, last, rows), q, 2, rows)
            put_mat_col(mats_ref, col(f_ref, q, last, rows), q, 3, rows)
    lax.fori_loop(0, last, backward, 0)
    for copy in scalars:
        copy.wait()
    zone = lax.axis_index("zone")
    row = iota(0)
    live_ref[...] = jnp.where(row < depth_ref[zone], 1.0, 0.0)
    for i in range(pick_ref.shape[1]):
        w = zone ^ offset_of(i, pick_ref.shape[1])
        rows = row < depth_ref[w]
        pick_ref[0, i] = jnp.where(rows & (east_ref[w] == zone), 1.0, 0.0)
        pick_ref[1, i] = jnp.where(rows & (east_ref[zone] == w), 1.0, 0.0)
        if i < partner_ref.shape[1]:
            partner_ref[0, i] = jnp.where(rows & (east_ref[w] == zone ^ 1), 1.0, 0.0)
            partner_ref[1, i] = jnp.where(rows & (east_ref[zone ^ 1] == w), 1.0, 0.0)


def by_place(mine_refs, other_refs, run):
    odd = lax.axis_index("ja") % 2

    @pl.when(odd == 0)
    def _():
        run(*mine_refs, *other_refs)

    @pl.when(odd == 1)
    def _():
        run(*other_refs, *mine_refs)


def half_kernel(mine_ref, other_ref, last_ref, half_ref):
    ja = lax.axis_index("ja")
    low_pair = ja < 2
    for side in range(2):
        first = [jnp.where(ja == 3, other_ref[20, v], mine_ref[20, v]) for v in range(5)]
        edge = [jnp.where(low_pair, last_ref[v], first[v]) for v in range(5)]
        put(half_ref, [x[8 * side : 8 * side + 8] for x in edge], 5 + side)
    for side in range(2):
        lo, hi = (mine_ref, other_ref) if side == 0 else (other_ref, mine_ref)
        rows = HALVES[side]

        @pl.when((ja % 2 == side) & low_pair)
        def _():
            for r in range(5):
                put(half_ref, [hi[15 + r, c, rows] for c in range(5)], r)

        @pl.when((ja % 2 == side) & (ja >= 2))
        def _():
            d_hi = [[hi[5 + r, c, rows] for c in range(5)] for r in range(5)]
            n_lo = [[lo[10 + r, c, rows] for c in range(5)] for r in range(5)]
            for q in range(5):
                out = matvec(n_lo, matvec(d_hi, mat_col(lo, q, 0, rows)))
                out = add(mat_col(lo, q, 1, rows), out)
                for r in range(5):
                    half_ref[r, q] = out[r]


def sweeps(s_ref, e_ref, f_ref, y_ref, ends_ref, last):
    planes = s_ref.shape[0]
    value = cell(s_ref, 0)
    put(y_ref, value, 0)
    for j in range(1, planes):
        value = add(cell(s_ref, j), matvec(block(e_ref, j), value))
        put(y_ref, value, j)
    put(ends_ref, [x + z * (1.0 / OMEGA) for x, z in zip(value, last)], 0)
    for j in range(planes - 2, -1, -1):
        value = add(cell(y_ref, j), matvec(block(f_ref, j), value))
    put(ends_ref, value, 1)


def source_kernel(
    tiles_ref, live_ref, cur_ref, force_ref, diag_ref, inv_ref, e_ref, f_ref, s_ref
):
    del tiles_ref
    planes = cur_ref.shape[0]
    before, here = None, masked(live_ref, cell(cur_ref, 0))
    for j in range(planes):
        own = matvec(block(diag_ref, j), here)
        res = [force_ref[j, v] - own[v] + COUPLE * neighbours(here[v]) for v in range(5)]
        out = matvec(block(inv_ref, j), masked(live_ref, res))
        if j > 0:
            linked = matvec(block(e_ref, j), before)
            out = add(out, [x * (1.0 / OMEGA) for x in linked])
        if j < planes - 1:
            after = masked(live_ref, cell(cur_ref, j + 1))
            linked = matvec(block(f_ref, j), after)
            out = add(out, [x * (1.0 / OMEGA) for x in linked])
            before, here = here, after
        put(s_ref, out, j)


def local_kernel(
    mats_other_ref, live_ref, mine_ref, got_ref, cur_ref, s0_ref,
    inv_ref, e_ref, f_ref,
    s_ref, ends_ref, above_ref, y_ref,
):
    last = cur_ref.shape[0] - 1
    ghosts = jnp.where(live_ref[...] > 0.0, COUPLE * (mine_ref[...] + got_ref[...]), 0.0)
    for j in range(last + 1):
        extra = [ghost_at(ghosts, j, v) for v in range(5)]
        put(s_ref, add(cell(s0_ref, j), matvec(block(inv_ref, j), extra)), j)
    even = lax.axis_index("ja") % 2 == 0
    above = [jnp.where(even, x, 0.0) for x in masked(live_ref, cell(mats_other_ref, 20))]
    put(above_ref, above)
    linked = matvec(block(f_ref, last), above)
    put(s_ref, add(cell(s_ref, last), [x * (1.0 / OMEGA) for x in linked]), last)
    sweeps(s_ref, e_ref, f_ref, y_ref, ends_ref, masked(live_ref, cell(cur_ref, last)))


def second_kernel(
    live_ref, pick_ref, tiles_ref, cur_ref, above_ref, force_ref, diag_ref, inv_ref, e_ref, f_ref,
    own_ref, s_ref, ends_ref, y_ref,
):
    planes = cur_ref.shape[0]
    zone, zones = lax.axis_index("zone"), tiles_ref.shape[0]
    ghosts = ghosts_of(pick_ref, lambda i: tiles_ref[zone ^ offset_of(i, zones)], zones)
    value = None
    for j in range(planes):
        here = cell(cur_ref, j)
        applied = matvec(block(diag_ref, j), here)
        res = []
        for v in range(5):
            sides = neighbours(here[v]) + ghost_at(ghosts, j, v)
            res.append(force_ref[j, v] - applied[v] + COUPLE * sides)
        res = masked(live_ref, res)
        put(own_ref, res, j)
        above = cell(cur_ref, j + 1) if j < planes - 1 else cell(above_ref)
        linked = matvec(block(f_ref, j), [x * (1.0 / OMEGA) for x in above])
        s = add(matvec(block(inv_ref, j), res), linked)
        put(s_ref, s, j)
        value = s if j == 0 else add(s, matvec(block(e_ref, j), value))
        put(y_ref, value, j)
        value = add(value, [x * (1.0 / OMEGA) for x in here])
    put(ends_ref, value, 0)
    put(ends_ref, here, 2)
    value = cell(y_ref, planes - 1)
    for j in range(planes - 2, -1, -1):
        value = add(cell(y_ref, j), matvec(block(f_ref, j), value))
    put(ends_ref, value, 1)


def write_kernel(
    live_ref, below_ref, ends_other_ref, cur_ref, above_ref, own_ref, low_ref, up_ref,
    res_hbm, done_ref, res_ref, sems,
):
    planes = cur_ref.shape[0]
    ja = lax.axis_index("ja")
    before = [
        jnp.where(ja == 0, 0.0, jnp.where(ja == 2, below_ref[v], ends_other_ref[2, v]))
        for v in range(5)
    ]
    copies = []
    for j in range(planes):
        lower = matvec(block(low_ref, j), before if j == 0 else cell(cur_ref, j - 1))
        above = cell(cur_ref, j + 1) if j < planes - 1 else cell(above_ref)
        coupled = masked(live_ref, add(lower, matvec(block(up_ref, j), above)))
        put(res_ref, add(cell(own_ref, j), coupled), j)
        copies.append(pltpu.make_async_copy(res_ref.at[j], res_hbm.at[j], sems.at[j]))
        copies[-1].start()
    done_ref[...] = live_ref[...]
    for copy in copies:
        copy.wait()


def compose(ends_lo, mats_lo, ends_hi, mats_hi, out_ref, first=None):
    c_lo = cell(ends_lo, 0)

    @pl.when(lax.axis_index("ja") < 2)
    def _():
        put(out_ref, add(cell(ends_hi, 0), matvec(matrix_of(mats_hi, 0), c_lo)), 0)

    @pl.when(lax.axis_index("ja") >= 2)
    def _():
        turned = add(cell(ends_hi, 1), matvec(matrix_of(mats_hi, 1), c_lo))
        raised = add(cell(ends_lo, 1), matvec(matrix_of(mats_lo, 2), turned))
        if first is not None:
            raised = add(raised, first(mats_lo))
        put(out_ref, raised, 0)


def mid_kernel(ends_ref, ends_other_ref, mats_ref, mats_other_ref, out_ref):
    def run(ends_lo, mats_lo, ends_hi, mats_hi):
        compose(ends_lo, mats_lo, ends_hi, mats_hi, out_ref)

    by_place([ends_ref, mats_ref], [ends_other_ref, mats_other_ref], run)


def first_mid_kernel(
    live_ref, half_ref, ends_ref, ends_other_ref, mats_ref, mats_other_ref,
    out_ref, beyond_ref, half_out_ref,
):
    def first(mats_lo):
        return [x * (1.0 / OMEGA) for x in masked(live_ref, cell(mats_lo, 20))]

    def run(ends_lo, mats_lo, ends_hi, mats_hi):
        compose(ends_lo, mats_lo, ends_hi, mats_hi, out_ref, first)

    by_place([ends_ref, mats_ref], [ends_other_ref, mats_other_ref], run)
    for r in range(5):
        put(half_out_ref, cell(half_ref, r), r)
    beyond = [jnp.concatenate([half_ref[5, v], half_ref[6, v]], axis=0) for v in range(5)]
    put(beyond_ref, masked(live_ref, beyond))


def join(mine_ref, other_ref, *at):
    mine, other = mine_ref[at], other_ref[at]
    odd = lax.axis_index("ja") % 2 == 1
    return jnp.concatenate([jnp.where(odd, mine, other), jnp.where(odd, other, mine)], axis=0)


def inflows(
    ends_ref, ends_other_ref, mats_ref, mats_other_ref, pair_ref, pair_other_ref,
    half_ref, half_other_ref, inflow_ref, live_ref=None, beyond_ref=None,
):
    ja = lax.axis_index("ja")
    zeros = [jnp.zeros((16, 128), jnp.float32)] * 5

    def joined():
        return [[join(half_ref, half_other_ref, r, c) for c in range(5)] for r in range(5)]

    def passed(value, coupling, first):
        if beyond_ref is None:
            return value
        return add(value, [x * (1.0 / OMEGA) for x in matvec(coupling, first)])

    def far(mats_hi_ref):
        first = None if beyond_ref is None else cell(beyond_ref)
        a = passed(cell(pair_ref, 0), matrix_of(mats_hi_ref, 3), first)
        return add(cell(pair_other_ref, 0), matvec(joined(), a))

    def near(mats_lo_ref):
        first = None if beyond_ref is None else masked(live_ref, cell(mats_lo_ref, 20))
        return passed(cell(pair_other_ref, 0), joined(), first)

    @pl.when(ja == 0)
    def _():
        put(inflow_ref, zeros, 0)
        b = add(cell(ends_other_ref, 1), matvec(matrix_of(mats_other_ref, 1), cell(ends_ref, 0)))
        b = add(b, matvec(matrix_of(mats_other_ref, 2), far(mats_other_ref)))
        put(inflow_ref, b, 1)

    @pl.when(ja == 1)
    def _():
        put(inflow_ref, cell(ends_other_ref, 0), 0)
        put(inflow_ref, far(mats_ref), 1)

    @pl.when(ja == 2)
    def _():
        a = near(mats_ref)
        put(inflow_ref, a, 0)
        a = add(cell(ends_ref, 0), matvec(matrix_of(mats_ref, 0), a))
        b = add(cell(ends_other_ref, 1), matvec(matrix_of(mats_other_ref, 1), a))
        put(inflow_ref, b, 1)

    @pl.when(ja == 3)
    def _():
        a = near(mats_other_ref)
        a = add(cell(ends_other_ref, 0), matvec(matrix_of(mats_other_ref, 0), a))
        put(inflow_ref, a, 0)
        put(inflow_ref, zeros, 1)


def final_kernel(
    live_ref, cur_ref, above_ref, beyond_ref, s_ref, e_ref, f_ref,
    ends_ref, ends_other_ref, mats_ref, mats_other_ref, pair_ref, pair_other_ref,
    half_ref, half_other_ref,
    new_ref, above_new_ref, below_new_ref, tile_ref, y_ref, inflow_ref,
):
    planes = cur_ref.shape[0]
    inflows(
        ends_ref, ends_other_ref, mats_ref, mats_other_ref, pair_ref, pair_other_ref,
        half_ref, half_other_ref, inflow_ref, live_ref, beyond_ref,
    )
    value = cell(inflow_ref, 0)
    for j in range(planes):
        value = add(cell(s_ref, j), matvec(block(e_ref, j), value))
        put(y_ref, value, j)
    value = cell(inflow_ref, 1)
    kept = [x * (1.0 - 1.0 / OMEGA) for x in cell(beyond_ref)]
    inner = lax.axis_index("ja") == 1
    above = add(cell(above_ref), [jnp.where(inner, x, 0.0) for x in kept])
    put(above_new_ref, add(above, value))
    for j in range(planes - 1, -1, -1):
        value = add(cell(y_ref, j), matvec(block(f_ref, j), value))
        put(new_ref, add(masked(live_ref, cell(cur_ref, j)), value), j)
    coupling = [[join(half_ref, half_other_ref, r, c) for c in range(5)] for r in range(5)]
    raised = add(cell(inflow_ref, 0), matvec(coupling, value))
    put(below_new_ref, add(raised, kept))
    pack_faces(lambda j, v: new_ref[j, v], planes, tile_ref)


def last_kernel(
    done_ref, cur_ref, s_ref, e_ref, f_ref,
    ends_ref, ends_other_ref, mats_ref, mats_other_ref, pair_ref, pair_other_ref,
    half_ref, half_other_ref,
    new_hbm, y_ref, inflow_ref, new_ref, sems,
):
    del done_ref
    planes = cur_ref.shape[0]
    copies = []
    inflows(
        ends_ref, ends_other_ref, mats_ref, mats_other_ref, pair_ref, pair_other_ref,
        half_ref, half_other_ref, inflow_ref,
    )
    value = cell(inflow_ref, 0)
    for j in range(planes):
        value = add(cell(s_ref, j), matvec(block(e_ref, j), value))
        put(y_ref, value, j)
        value = add(value, [x * (1.0 / OMEGA) for x in cell(cur_ref, j)])
    value = cell(inflow_ref, 1)
    for j in range(planes - 1, -1, -1):
        value = add(cell(y_ref, j), matvec(block(f_ref, j), value))
        put(new_ref, add(cell(cur_ref, j), value), j)
        copies.append(pltpu.make_async_copy(new_ref.at[j], new_hbm.at[j], sems.at[j]))
        copies[-1].start()
    for copy in copies:
        copy.wait()


def per_device(
    flow_state, forcing, diag_block, lower_jac, upper_jac, block_inv, east_zone, zone_depth
):
    zones, parts = lax.axis_size("zone"), lax.axis_size("ja")
    assert parts == 4 and ITERS == 2 and zones > 4 and zones & (zones - 1) == 0
    current, force, diag, low, up, inv = (
        x[0] for x in (flow_state, forcing, diag_block, lower_jac, upper_jac, block_inv)
    )
    state = current.shape
    planes, plane, blocks = state[0], state[1:], diag.shape
    matrix = blocks[1:]
    work = [buffer(*state)]

    def swap(x, bit):
        return lax.ppermute(x, "ja", [(p, p ^ bit) for p in range(parts)])

    tile, first, final = call(
        pack_kernel,
        [(1, *state[2:]), plane, plane],
        work + [pltpu.SemaphoreType.DMA],
        flops=10**10,
        far=(0,),
    )(current)
    e, f, mats, live, pick, partner = call(
        matrix_kernel,
        [
            blocks, blocks, (20, *plane), state[2:],
            (2, zones, *state[2:]), (2, zones // 2, *state[2:]),
        ],
        [buffer(*blocks)]
        + [pltpu.SMEM((zones,), jnp.int32)] * 2
        + [pltpu.SemaphoreType.DMA((2,))],
        flops=5 * 10**9,
        far=(0, 1),
    )(zone_depth, east_zone, tile, inv, low, up)
    tiles, stride = tile, zones // 2
    while stride > 1:
        got = lax.ppermute(tiles, "zone", [(z, z ^ stride) for z in range(zones)])
        both = (2 * tiles.shape[0], *state[2:])
        if stride == zones // 2:
            mats, tiles = call(relay_kernel, [(21, *plane), both], flops=10**5)(
                tiles, got, mats, first
            )
            mats_other = swap(mats, 1)
            half = call(half_kernel, [(7, plane[0], 8, plane[2])], flops=10**5)(
                mats, mats_other, final
            )[0]
        elif stride > 2:
            tiles = call(merge_kernel, [both], flops=10**5)(tiles, got, half)[0]
        else:
            tiles, theirs = call(select_kernel, [state[2:]] * 2, flops=10**5)(
                tiles, got, half, pick, partner
            )
        stride //= 2
    got = lax.ppermute(theirs, "zone", [(z, z ^ 1) for z in range(zones)])
    half = swap(half, 3)
    s0 = call(source_kernel, [state], flops=2 * 10**9)(tiles, live, current, force, diag, inv, e, f)[0]
    s, ends, above = call(local_kernel, [state, (2, *plane), plane], work)(
        mats_other, live, tiles, got, current, s0, inv, e, f
    )
    ends_other = swap(ends, 1)
    pair, beyond, half = call(
        first_mid_kernel, [(1, *plane), plane, (5, *half.shape[1:])], flops=10**5
    )(live, half, ends, ends_other, mats, mats_other)
    half_other = swap(half, 1)
    pair_other = swap(pair, 3)
    flows = [buffer(2, *plane)]
    current, above, below, tile = call(
        final_kernel, [state, plane, plane, (zones, *state[2:])], work + flows
    )(
        live, current, above, beyond, s, e, f,
        ends, ends_other, mats, mats_other, pair, pair_other, half, half_other,
    )

    got = lax.all_to_all(tile, "zone", 0, 0, tiled=True)
    own, s, ends = call(second_kernel, [state, state, (3, *plane)], work)(
        live, pick, got, current, above, force, diag, inv, e, f
    )
    ends_other = swap(ends, 1)
    pair = call(mid_kernel, [(1, *plane)], flops=10**5)(ends, ends_other, mats, mats_other)[0]
    pair_other = swap(pair, 3)
    residual, done = call(
        write_kernel,
        [state, state[2:]],
        work + [pltpu.SemaphoreType.DMA((planes,))],
        out_specs=[HBM, VMEM],
    )(live, below, ends_other, current, above, own, low, up)
    current = call(
        last_kernel,
        [state],
        work + flows + work + [pltpu.SemaphoreType.DMA((planes,))],
        out_specs=[HBM],
    )(
        done, current, s, e, f,
        ends, ends_other, mats, mats_other, pair, pair_other, half, half_other,
    )[0]
    return (current[None], residual[None])


def solution(mesh):
    state = P("zone", "ja", None, None, None)
    blocks = P("zone", "ja", None, None, None, None)
    return jax.shard_map(
        per_device,
        mesh=mesh,
        in_specs=(state, state, blocks, blocks, blocks, blocks, P(), P()),
        out_specs=(state, state),
        check_vma=False,
    )
```

```python
import jax
import jax.numpy as jnp
from jax import lax
from jax.experimental import pallas as pl
from jax.experimental.pallas import tpu as pltpu
from jax.sharding import PartitionSpec as P

ITERS = 2
OMEGA = 1.2
PART = 7
COUPLE = 0.25

VMEM = pl.BlockSpec(memory_space=pltpu.VMEM)
ANY = pl.BlockSpec(memory_space=pl.ANY)
HBM = pl.BlockSpec(memory_space=pltpu.HBM)


def call(kernel, shapes, scratch=(), flops=10**9, far=(), out_specs=None, alias=None):
    alias = alias or {}

    def run(*arrays):
        arrays = [
            pltpu.with_memory_space_constraint(a, pltpu.HBM) if i in far else a
            for i, a in enumerate(arrays)
        ]
        return pl.pallas_call(
            kernel,
            out_shape=[jax.ShapeDtypeStruct(s, jnp.float32) for s in shapes],
            in_specs=[
                HBM if i in far else ANY if i in alias else VMEM for i in range(len(arrays))
            ],
            out_specs=out_specs or [VMEM] * len(shapes),
            scratch_shapes=list(scratch),
            input_output_aliases=alias,
            compiler_params=pltpu.CompilerParams(vmem_limit_bytes=8 * 2**20),
            cost_estimate=pl.CostEstimate(flops=flops, bytes_accessed=flops // 10**3, transcendentals=0),
        )(*arrays)

    return run


def buffer(*shape):
    return pltpu.VMEM(shape, jnp.float32)


def iota(dim):
    return lax.broadcasted_iota(jnp.int32, (16, 128), dim)


def matvec(matrix, vector):
    n = len(vector)
    out = []
    for r in range(n):
        acc = matrix[r][0] * vector[0]
        for c in range(1, n):
            acc = acc + matrix[r][c] * vector[c]
        out.append(acc)
    return out


def block(ref, *lead):
    return [[ref[(*lead, r, c)] for c in range(5)] for r in range(5)]


def matrix_of(ref, i):
    return [cell(ref, 5 * i + r) for r in range(5)]


def cell(ref, *lead):
    return [ref[(*lead, v)] for v in range(5)]


def put(ref, values, *lead):
    for v, value in enumerate(values):
        ref[(*lead, v)] = value


def add(a, b):
    return [x + y for x, y in zip(a, b)]


def pack_faces(load, planes, tile_ref):
    lane = iota(1)
    tile = jnp.zeros((16, 128), jnp.float32)
    for j in range(planes):
        for v in range(5):
            q = 2 * (j * 5 + v)
            here = (lane == q) | (lane == (q - 1) % 128)
            x = load(j, v)
            tile = jnp.where(here, pltpu.roll(x, q, 1) if q else x, tile)
    for w in range(tile_ref.shape[0]):
        tile_ref[w] = tile


def masked(live_ref, values):
    live = live_ref[...] > 0.0
    return [jnp.where(live, x, 0.0) for x in values]


def pack_kernel(flow_hbm, tile_ref, first_ref, last_ref, flow_ref, sems):
    copies = [
        pltpu.make_async_copy(flow_hbm.at[j], flow_ref.at[j], sems.at[j])
        for j in range(flow_ref.shape[0])
    ]
    for copy in copies:
        copy.start()
    for copy in copies:
        copy.wait()
    put(first_ref, cell(flow_ref, 0))
    put(last_ref, cell(flow_ref, flow_ref.shape[0] - 1))
    pack_faces(lambda j, v: flow_ref[j, v], flow_ref.shape[0], tile_ref)


def merge_kernel(own_ref, got_ref, *refs):
    out_ref = refs[-1]
    count = own_ref.shape[0]
    for w in range(count):
        out_ref[w] = own_ref[w]
        out_ref[count + w] = got_ref[w]


def select_kernel(own_ref, got_ref, after_ref, pick_ref, partner_ref, mine_ref, theirs_ref):
    del after_ref
    count = own_ref.shape[0]

    def tile_at(i):
        return own_ref[i] if i < count else got_ref[i - count]

    mine_ref[...] = ghosts_of(pick_ref, tile_at, 2 * count)
    theirs_ref[...] = ghosts_of(partner_ref, tile_at, 2 * count)


def relay_kernel(own_ref, got_ref, mats_ref, first_ref, mats_out_ref, out_ref):
    merge_kernel(own_ref, got_ref, out_ref)
    for i in range(20):
        put(mats_out_ref, cell(mats_ref, i), i)
    put(mats_out_ref, cell(first_ref), 20)


def neighbours(x):
    lane, row = iota(1), iota(0)
    total = jnp.where(lane == 0, 0.0, pltpu.roll(x, 1, 1))
    total = total + jnp.where(lane == 127, 0.0, pltpu.roll(x, 127, 1))
    total = total + jnp.where(row == 0, 0.0, pltpu.roll(x, 1, 0))
    return total + jnp.where(row == 15, 0.0, pltpu.roll(x, 15, 0))


def offset_of(place, zones):
    offset, stride = 0, zones // 2
    while stride:
        offset, place, stride = offset + stride * (place % 2), place // 2, stride // 2
    return offset


def ghosts_of(pick_ref, tile_at, count):
    low = high = jnp.zeros((16, 128), jnp.float32)
    for i in range(count):
        low = jnp.where(pick_ref[0, i] > 0.0, tile_at(i), low)
        high = jnp.where(pick_ref[1, i] > 0.0, tile_at(i), high)
    return jnp.where(iota(1) % 2 == 0, pltpu.roll(low, 1, 1), pltpu.roll(high, 127, 1))


def ghost_at(ghosts, j, v):
    lane = iota(1)
    q = 2 * (j * 5 + v)
    turned = pltpu.roll(ghosts, 128 - q, 1) if q else ghosts
    return jnp.where((lane == 0) | (lane == 127), turned, 0.0)


HALVES = [pl.ds(0, 8), pl.ds(8, 8)]


def col(ref, q, j, rows):
    return [ref[j, r, q, rows] for r in range(5)]


def put_col(ref, values, q, j, rows):
    for r in range(5):
        ref[j, r, q, rows] = values[r]


def put_mat_col(ref, values, q, i, rows):
    for r in range(5):
        ref[5 * i + r, q, rows] = values[r]


def mat_col(ref, q, i, rows):
    return [ref[5 * i + r, q, rows] for r in range(5)]


def mat(ref, j, rows):
    return [[ref[j, r, c, rows] for c in range(5)] for r in range(5)]


def matrix_kernel(
    depth_hbm, east_hbm, tile_ref, inv_ref, low_ref, up_ref,
    e_ref, f_ref, mats_ref, live_ref, pick_ref, partner_ref,
    y_ref, depth_ref, east_ref, sems,
):
    del tile_ref
    last = inv_ref.shape[0] - 1
    scalars = [
        pltpu.make_async_copy(depth_hbm, depth_ref, sems.at[0]),
        pltpu.make_async_copy(east_hbm, east_ref, sems.at[1]),
    ]
    for copy in scalars:
        copy.start()

    def products(j, rows):
        inv = mat(inv_ref, j, rows)
        for jac_ref, out_ref in ((low_ref, e_ref), (up_ref, f_ref)):
            for q in range(5):
                product = matvec(inv, col(jac_ref, q, j, rows))
                put_col(out_ref, [OMEGA * x for x in product], q, j, rows)

    def forward(j, carry):
        for rows in HALVES:
            products(j, rows)
            e = mat(e_ref, j, rows)
            for q in range(5):
                put_col(y_ref, matvec(e, col(y_ref, q, j - 1, rows)), q, j, rows)
        return carry

    def backward(step, carry):
        j = last - 1 - step
        for rows in HALVES:
            f = mat(f_ref, j, rows)
            for q in range(5):
                turned = matvec(f, mat_col(mats_ref, q, 1, rows))
                put_mat_col(mats_ref, add(col(y_ref, q, j, rows), turned), q, 1, rows)
                put_mat_col(mats_ref, matvec(f, mat_col(mats_ref, q, 2, rows)), q, 2, rows)
        return carry

    for rows in HALVES:
        products(0, rows)
        for q in range(5):
            put_col(y_ref, col(e_ref, q, 0, rows), q, 0, rows)
    lax.fori_loop(1, last + 1, forward, 0)
    for rows in HALVES:
        for q in range(5):
            put_mat_col(mats_ref, col(y_ref, q, last, rows), q, 0, rows)
            put_mat_col(mats_ref, col(y_ref, q, last, rows), q, 1, rows)
            put_mat_col(mats_ref, col(f_ref, q, last, rows), q, 2, rows)
            put_mat_col(mats_ref, col(f_ref, q, last, rows), q, 3, rows)
    lax.fori_loop(0, last, backward, 0)
    for copy in scalars:
        copy.wait()
    zone = lax.axis_index("zone")
    row = iota(0)
    live_ref[...] = jnp.where(row < depth_ref[zone], 1.0, 0.0)
    for i in range(pick_ref.shape[1]):
        w = zone ^ offset_of(i, pick_ref.shape[1])
        rows = row < depth_ref[w]
        pick_ref[0, i] = jnp.where(rows & (east_ref[w] == zone), 1.0, 0.0)
        pick_ref[1, i] = jnp.where(rows & (east_ref[zone] == w), 1.0, 0.0)
        if i < partner_ref.shape[1]:
            partner_ref[0, i] = jnp.where(rows & (east_ref[w] == zone ^ 1), 1.0, 0.0)
            partner_ref[1, i] = jnp.where(rows & (east_ref[zone ^ 1] == w), 1.0, 0.0)


def by_place(mine_refs, other_refs, run):
    odd = lax.axis_index("ja") % 2

    @pl.when(odd == 0)
    def _():
        run(*mine_refs, *other_refs)

    @pl.when(odd == 1)
    def _():
        run(*other_refs, *mine_refs)


def half_kernel(mine_ref, other_ref, last_ref, half_ref):
    ja = lax.axis_index("ja")
    low_pair = ja < 2
    for side in range(2):
        first = [jnp.where(ja == 3, other_ref[20, v], mine_ref[20, v]) for v in range(5)]
        edge = [jnp.where(low_pair, last_ref[v], first[v]) for v in range(5)]
        put(half_ref, [x[8 * side : 8 * side + 8] for x in edge], 5 + side)
    for side in range(2):
        lo, hi = (mine_ref, other_ref) if side == 0 else (other_ref, mine_ref)
        rows = HALVES[side]

        @pl.when((ja % 2 == side) & low_pair)
        def _():
            for r in range(5):
                put(half_ref, [hi[15 + r, c, rows] for c in range(5)], r)

        @pl.when((ja % 2 == side) & (ja >= 2))
        def _():
            d_hi = [[hi[5 + r, c, rows] for c in range(5)] for r in range(5)]
            n_lo = [[lo[10 + r, c, rows] for c in range(5)] for r in range(5)]
            for q in range(5):
                out = matvec(n_lo, matvec(d_hi, mat_col(lo, q, 0, rows)))
                out = add(mat_col(lo, q, 1, rows), out)
                for r in range(5):
                    half_ref[r, q] = out[r]


def sweeps(s_ref, e_ref, f_ref, y_ref, ends_ref, last):
    planes = s_ref.shape[0]
    value = cell(s_ref, 0)
    put(y_ref, value, 0)
    for j in range(1, planes):
        value = add(cell(s_ref, j), matvec(block(e_ref, j), value))
        put(y_ref, value, j)
    put(ends_ref, [x + z * (1.0 / OMEGA) for x, z in zip(value, last)], 0)
    for j in range(planes - 2, -1, -1):
        value = add(cell(y_ref, j), matvec(block(f_ref, j), value))
    put(ends_ref, value, 1)


def source_kernel(
    tiles_ref, live_ref, cur_ref, force_ref, diag_ref, inv_ref, e_ref, f_ref, s_ref
):
    del tiles_ref
    planes = cur_ref.shape[0]
    before, here = None, masked(live_ref, cell(cur_ref, 0))
    for j in range(planes):
        own = matvec(block(diag_ref, j), here)
        res = [force_ref[j, v] - own[v] + COUPLE * neighbours(here[v]) for v in range(5)]
        out = matvec(block(inv_ref, j), masked(live_ref, res))
        if j > 0:
            linked = matvec(block(e_ref, j), before)
            out = add(out, [x * (1.0 / OMEGA) for x in linked])
        if j < planes - 1:
            after = masked(live_ref, cell(cur_ref, j + 1))
            linked = matvec(block(f_ref, j), after)
            out = add(out, [x * (1.0 / OMEGA) for x in linked])
            before, here = here, after
        put(s_ref, out, j)


def local_kernel(
    mats_other_ref, live_ref, mine_ref, got_ref, cur_ref, s0_ref,
    inv_ref, e_ref, f_ref,
    s_ref, ends_ref, above_ref, y_ref,
):
    last = cur_ref.shape[0] - 1
    ghosts = jnp.where(live_ref[...] > 0.0, COUPLE * (mine_ref[...] + got_ref[...]), 0.0)
    for j in range(last + 1):
        extra = [ghost_at(ghosts, j, v) for v in range(5)]
        put(s_ref, add(cell(s0_ref, j), matvec(block(inv_ref, j), extra)), j)
    even = lax.axis_index("ja") % 2 == 0
    above = [jnp.where(even, x, 0.0) for x in masked(live_ref, cell(mats_other_ref, 20))]
    put(above_ref, above)
    linked = matvec(block(f_ref, last), above)
    put(s_ref, add(cell(s_ref, last), [x * (1.0 / OMEGA) for x in linked]), last)
    sweeps(s_ref, e_ref, f_ref, y_ref, ends_ref, masked(live_ref, cell(cur_ref, last)))


def second_kernel(
    live_ref, pick_ref, tiles_ref, cur_ref, above_ref, force_ref, diag_ref, inv_ref, e_ref, f_ref,
    own_ref, s_ref, ends_ref, y_ref,
):
    planes = cur_ref.shape[0]
    zone, zones = lax.axis_index("zone"), tiles_ref.shape[0]
    ghosts = ghosts_of(pick_ref, lambda i: tiles_ref[zone ^ offset_of(i, zones)], zones)
    value = None
    for j in range(planes):
        here = cell(cur_ref, j)
        applied = matvec(block(diag_ref, j), here)
        res = []
        for v in range(5):
            sides = neighbours(here[v]) + ghost_at(ghosts, j, v)
            res.append(force_ref[j, v] - applied[v] + COUPLE * sides)
        res = masked(live_ref, res)
        put(own_ref, res, j)
        above = cell(cur_ref, j + 1) if j < planes - 1 else cell(above_ref)
        linked = matvec(block(f_ref, j), [x * (1.0 / OMEGA) for x in above])
        s = add(matvec(block(inv_ref, j), res), linked)
        put(s_ref, s, j)
        value = s if j == 0 else add(s, matvec(block(e_ref, j), value))
        put(y_ref, value, j)
        value = add(value, [x * (1.0 / OMEGA) for x in here])
    put(ends_ref, value, 0)
    put(ends_ref, here, 2)
    value = cell(y_ref, planes - 1)
    for j in range(planes - 2, -1, -1):
        value = add(cell(y_ref, j), matvec(block(f_ref, j), value))
    put(ends_ref, value, 1)


def write_kernel(
    live_ref, below_ref, ends_other_ref, cur_ref, above_ref, own_ref, low_ref, up_ref,
    res_hbm, done_ref, res_ref, sems,
):
    planes = cur_ref.shape[0]
    ja = lax.axis_index("ja")
    before = [
        jnp.where(ja == 0, 0.0, jnp.where(ja == 2, below_ref[v], ends_other_ref[2, v]))
        for v in range(5)
    ]
    copies = []
    for j in range(planes):
        lower = matvec(block(low_ref, j), before if j == 0 else cell(cur_ref, j - 1))
        above = cell(cur_ref, j + 1) if j < planes - 1 else cell(above_ref)
        coupled = masked(live_ref, add(lower, matvec(block(up_ref, j), above)))
        put(res_ref, add(cell(own_ref, j), coupled), j)
        copies.append(pltpu.make_async_copy(res_ref.at[j], res_hbm.at[j], sems.at[j]))
        copies[-1].start()
    done_ref[...] = live_ref[...]
    for copy in copies:
        copy.wait()


def compose(ends_lo, mats_lo, ends_hi, mats_hi, out_ref, first=None):
    c_lo = cell(ends_lo, 0)

    @pl.when(lax.axis_index("ja") < 2)
    def _():
        put(out_ref, add(cell(ends_hi, 0), matvec(matrix_of(mats_hi, 0), c_lo)), 0)

    @pl.when(lax.axis_index("ja") >= 2)
    def _():
        turned = add(cell(ends_hi, 1), matvec(matrix_of(mats_hi, 1), c_lo))
        raised = add(cell(ends_lo, 1), matvec(matrix_of(mats_lo, 2), turned))
        if first is not None:
            raised = add(raised, first(mats_lo))
        put(out_ref, raised, 0)


def mid_kernel(ends_ref, ends_other_ref, mats_ref, mats_other_ref, out_ref):
    def run(ends_lo, mats_lo, ends_hi, mats_hi):
        compose(ends_lo, mats_lo, ends_hi, mats_hi, out_ref)

    by_place([ends_ref, mats_ref], [ends_other_ref, mats_other_ref], run)


def first_mid_kernel(
    live_ref, half_ref, ends_ref, ends_other_ref, mats_ref, mats_other_ref,
    out_ref, beyond_ref, half_out_ref, *part_refs,
):
    def first(mats_lo):
        return [x * (1.0 / OMEGA) for x in masked(live_ref, cell(mats_lo, 20))]

    def run(ends_lo, mats_lo, ends_hi, mats_hi):
        compose(ends_lo, mats_lo, ends_hi, mats_hi, out_ref, first)

    by_place([ends_ref, mats_ref], [ends_other_ref, mats_other_ref], run)
    for r in range(5):
        put(half_out_ref, cell(half_ref, r), r)
        for c in range(5):
            part, place = divmod(5 * r + c, PART)
            part_refs[part][place] = half_ref[r, c]
    beyond = [jnp.concatenate([half_ref[5, v], half_ref[6, v]], axis=0) for v in range(5)]
    put(beyond_ref, masked(live_ref, beyond))


def join(mine_ref, other_refs, r, c):
    part, place = divmod(5 * r + c, PART)
    mine, other = mine_ref[r, c], other_refs[part][place]
    odd = lax.axis_index("ja") % 2 == 1
    return jnp.concatenate([jnp.where(odd, mine, other), jnp.where(odd, other, mine)], axis=0)


def inflows(
    ends_ref, ends_other_ref, mats_ref, mats_other_ref, pair_ref, pair_other_ref,
    half_ref, half_other_refs, inflow_ref, live_ref=None, beyond_ref=None,
):
    ja = lax.axis_index("ja")
    zeros = [jnp.zeros((16, 128), jnp.float32)] * 5

    def joined():
        return [[join(half_ref, half_other_refs, r, c) for c in range(5)] for r in range(5)]

    def passed(value, coupling, first):
        if beyond_ref is None:
            return value
        return add(value, [x * (1.0 / OMEGA) for x in matvec(coupling, first)])

    def far(mats_hi_ref):
        first = None if beyond_ref is None else cell(beyond_ref)
        a = passed(cell(pair_ref, 0), matrix_of(mats_hi_ref, 3), first)
        return add(cell(pair_other_ref, 0), matvec(joined(), a))

    def near(mats_lo_ref):
        first = None if beyond_ref is None else masked(live_ref, cell(mats_lo_ref, 20))
        return passed(cell(pair_other_ref, 0), joined(), first)

    @pl.when(ja == 0)
    def _():
        put(inflow_ref, zeros, 0)
        b = add(cell(ends_other_ref, 1), matvec(matrix_of(mats_other_ref, 1), cell(ends_ref, 0)))
        b = add(b, matvec(matrix_of(mats_other_ref, 2), far(mats_other_ref)))
        put(inflow_ref, b, 1)

    @pl.when(ja == 1)
    def _():
        put(inflow_ref, cell(ends_other_ref, 0), 0)
        put(inflow_ref, far(mats_ref), 1)

    @pl.when(ja == 2)
    def _():
        a = near(mats_ref)
        put(inflow_ref, a, 0)
        a = add(cell(ends_ref, 0), matvec(matrix_of(mats_ref, 0), a))
        b = add(cell(ends_other_ref, 1), matvec(matrix_of(mats_other_ref, 1), a))
        put(inflow_ref, b, 1)

    @pl.when(ja == 3)
    def _():
        a = near(mats_other_ref)
        a = add(cell(ends_other_ref, 0), matvec(matrix_of(mats_other_ref, 0), a))
        put(inflow_ref, a, 0)
        put(inflow_ref, zeros, 1)


def final_kernel(
    live_ref, cur_ref, above_ref, beyond_ref, s_ref, e_ref, f_ref,
    ends_ref, ends_other_ref, mats_ref, mats_other_ref, pair_ref, pair_other_ref,
    half_ref, *rest,
):
    half_other_refs = rest[:4]
    new_ref, above_new_ref, below_new_ref, tile_ref, y_ref, inflow_ref = rest[4:]
    planes = cur_ref.shape[0]
    inflows(
        ends_ref, ends_other_ref, mats_ref, mats_other_ref, pair_ref, pair_other_ref,
        half_ref, half_other_refs, inflow_ref, live_ref, beyond_ref,
    )
    value = cell(inflow_ref, 0)
    for j in range(planes):
        value = add(cell(s_ref, j), matvec(block(e_ref, j), value))
        put(y_ref, value, j)
    value = cell(inflow_ref, 1)
    kept = [x * (1.0 - 1.0 / OMEGA) for x in cell(beyond_ref)]
    inner = lax.axis_index("ja") == 1
    above = add(cell(above_ref), [jnp.where(inner, x, 0.0) for x in kept])
    put(above_new_ref, add(above, value))
    for j in range(planes - 1, -1, -1):
        value = add(cell(y_ref, j), matvec(block(f_ref, j), value))
        put(new_ref, add(masked(live_ref, cell(cur_ref, j)), value), j)
    coupling = [[join(half_ref, half_other_refs, r, c) for c in range(5)] for r in range(5)]
    raised = add(cell(inflow_ref, 0), matvec(coupling, value))
    put(below_new_ref, add(raised, kept))
    pack_faces(lambda j, v: new_ref[j, v], planes, tile_ref)


def last_kernel(
    done_ref, cur_ref, s_ref, e_ref, f_ref,
    ends_ref, ends_other_ref, mats_ref, mats_other_ref, pair_ref, pair_other_ref,
    half_ref, *rest,
):
    half_other_refs = rest[:4]
    new_hbm, y_ref, inflow_ref, new_ref, sems = rest[4:]
    del done_ref
    planes = cur_ref.shape[0]
    copies = []
    inflows(
        ends_ref, ends_other_ref, mats_ref, mats_other_ref, pair_ref, pair_other_ref,
        half_ref, half_other_refs, inflow_ref,
    )
    value = cell(inflow_ref, 0)
    for j in range(planes):
        value = add(cell(s_ref, j), matvec(block(e_ref, j), value))
        put(y_ref, value, j)
        value = add(value, [x * (1.0 / OMEGA) for x in cell(cur_ref, j)])
    value = cell(inflow_ref, 1)
    for j in range(planes - 1, -1, -1):
        value = add(cell(y_ref, j), matvec(block(f_ref, j), value))
        put(new_ref, add(cell(cur_ref, j), value), j)
        copies.append(pltpu.make_async_copy(new_ref.at[j], new_hbm.at[j], sems.at[j]))
        copies[-1].start()
    for copy in copies:
        copy.wait()


def per_device(
    flow_state, forcing, diag_block, lower_jac, upper_jac, block_inv, east_zone, zone_depth
):
    zones, parts = lax.axis_size("zone"), lax.axis_size("ja")
    assert parts == 4 and ITERS == 2 and zones > 4 and zones & (zones - 1) == 0
    current, force, diag, low, up, inv = (
        x[0] for x in (flow_state, forcing, diag_block, lower_jac, upper_jac, block_inv)
    )
    state = current.shape
    planes, plane, blocks = state[0], state[1:], diag.shape
    matrix = blocks[1:]
    work = [buffer(*state)]

    def swap(x, bit):
        return lax.ppermute(x, "ja", [(p, p ^ bit) for p in range(parts)])

    tile, first, final = call(
        pack_kernel,
        [(1, *state[2:]), plane, plane],
        work + [pltpu.SemaphoreType.DMA((planes,))],
        flops=10**10,
        far=(0,),
    )(current)
    e, f, mats, live, pick, partner = call(
        matrix_kernel,
        [
            blocks, blocks, (20, *plane), state[2:],
            (2, zones, *state[2:]), (2, zones // 2, *state[2:]),
        ],
        [buffer(*blocks)]
        + [pltpu.SMEM((zones,), jnp.int32)] * 2
        + [pltpu.SemaphoreType.DMA((2,))],
        flops=5 * 10**9,
        far=(0, 1),
    )(zone_depth, east_zone, tile, inv, low, up)
    tiles, stride = tile, zones // 2
    while stride > 1:
        got = lax.ppermute(tiles, "zone", [(z, z ^ stride) for z in range(zones)])
        both = (2 * tiles.shape[0], *state[2:])
        if stride == zones // 2:
            mats, tiles = call(relay_kernel, [(21, *plane), both], flops=10**5)(
                tiles, got, mats, first
            )
            mats_other = swap(mats, 1)
            half = call(half_kernel, [(7, plane[0], 8, plane[2])], flops=10**5)(
                mats, mats_other, final
            )[0]
        elif stride > 2:
            tiles = call(merge_kernel, [both], flops=10**5)(tiles, got, half)[0]
        else:
            tiles, theirs = call(select_kernel, [state[2:]] * 2, flops=10**5)(
                tiles, got, half, pick, partner
            )
        stride //= 2
    got = lax.ppermute(theirs, "zone", [(z, z ^ 1) for z in range(zones)])
    half = swap(half, 3)
    s0 = call(source_kernel, [state], flops=2 * 10**9)(tiles, live, current, force, diag, inv, e, f)[0]
    s, ends, above = call(local_kernel, [state, (2, *plane), plane], work)(
        mats_other, live, tiles, got, current, s0, inv, e, f
    )
    ends_other = swap(ends, 1)
    parts_of = [(min(PART, 25 - i), *half.shape[2:]) for i in range(0, 25, PART)]
    pair, beyond, half, *sent = call(
        first_mid_kernel, [(1, *plane), plane, (5, *half.shape[1:])] + parts_of, flops=10**5
    )(live, half, ends, ends_other, mats, mats_other)
    half_other = [swap(x, 1) for x in sent]
    pair_other = swap(pair, 3)
    flows = [buffer(2, *plane)]
    current, above, below, tile = call(
        final_kernel, [state, plane, plane, (zones, *state[2:])], work + flows
    )(
        live, current, above, beyond, s, e, f,
        ends, ends_other, mats, mats_other, pair, pair_other, half, *half_other,
    )

    got = lax.all_to_all(tile, "zone", 0, 0, tiled=True)
    own, s, ends = call(second_kernel, [state, state, (3, *plane)], work)(
        live, pick, got, current, above, force, diag, inv, e, f
    )
    ends_other = swap(ends, 1)
    pair = call(mid_kernel, [(1, *plane)], flops=10**5)(ends, ends_other, mats, mats_other)[0]
    pair_other = swap(pair, 3)
    residual, done = call(
        write_kernel,
        [state, state[2:]],
        work + [pltpu.SemaphoreType.DMA((planes,))],
        out_specs=[HBM, VMEM],
    )(live, below, ends_other, current, above, own, low, up)
    current = call(
        last_kernel,
        [state],
        work + flows + work + [pltpu.SemaphoreType.DMA((planes,))],
        out_specs=[HBM],
    )(
        done, current, s, e, f,
        ends, ends_other, mats, mats_other, pair, pair_other, half, *half_other,
    )[0]
    return (current[None], residual[None])


def solution(mesh):
    state = P("zone", "ja", None, None, None)
    blocks = P("zone", "ja", None, None, None, None)
    return jax.shard_map(
        per_device,
        mesh=mesh,
        in_specs=(state, state, blocks, blocks, blocks, blocks, P(), P()),
        out_specs=(state, state),
        check_vma=False,
    )
```

```python
import jax
import jax.numpy as jnp
from jax import lax
from jax.experimental import pallas as pl
from jax.experimental.pallas import tpu as pltpu
from jax.sharding import PartitionSpec as P

ITERS = 2
OMEGA = 1.2
PART = 7
COUPLE = 0.25

VMEM = pl.BlockSpec(memory_space=pltpu.VMEM)
ANY = pl.BlockSpec(memory_space=pl.ANY)
HBM = pl.BlockSpec(memory_space=pltpu.HBM)


def call(kernel, shapes, scratch=(), flops=10**9, far=(), out_specs=None, alias=None):
    alias = alias or {}

    def run(*arrays):
        arrays = [
            pltpu.with_memory_space_constraint(a, pltpu.HBM) if i in far else a
            for i, a in enumerate(arrays)
        ]
        return pl.pallas_call(
            kernel,
            out_shape=[jax.ShapeDtypeStruct(s, jnp.float32) for s in shapes],
            in_specs=[
                HBM if i in far else ANY if i in alias else VMEM for i in range(len(arrays))
            ],
            out_specs=out_specs or [VMEM] * len(shapes),
            scratch_shapes=list(scratch),
            input_output_aliases=alias,
            compiler_params=pltpu.CompilerParams(vmem_limit_bytes=8 * 2**20),
            cost_estimate=pl.CostEstimate(flops=flops, bytes_accessed=flops // 10**3, transcendentals=0),
        )(*arrays)

    return run


def buffer(*shape):
    return pltpu.VMEM(shape, jnp.float32)


def iota(dim):
    return lax.broadcasted_iota(jnp.int32, (16, 128), dim)


def matvec(matrix, vector, base=None):
    out = []
    for r, row in enumerate(matrix):
        terms = [m * x for m, x in zip(row, vector)]
        if base is not None:
            terms.insert(0, base[r])
        while len(terms) > 1:
            pairs = [x + z for x, z in zip(terms[::2], terms[1::2])]
            terms = pairs + terms[2 * len(pairs) :]
        out.append(terms[0])
    return out


def block(ref, *lead):
    return [[ref[(*lead, r, c)] for c in range(5)] for r in range(5)]


def matrix_of(ref, i):
    return [cell(ref, 5 * i + r) for r in range(5)]


def cell(ref, *lead):
    return [ref[(*lead, v)] for v in range(5)]


def put(ref, values, *lead):
    for v, value in enumerate(values):
        ref[(*lead, v)] = value


def add(a, b):
    return [x + y for x, y in zip(a, b)]


def pack_faces(load, planes, tile_ref):
    lane = iota(1)
    tile = jnp.zeros((16, 128), jnp.float32)
    for j in range(planes):
        for v in range(5):
            q = 2 * (j * 5 + v)
            here = (lane == q) | (lane == (q - 1) % 128)
            x = load(j, v)
            tile = jnp.where(here, pltpu.roll(x, q, 1) if q else x, tile)
    for w in range(tile_ref.shape[0]):
        tile_ref[w] = tile


def masked(live_ref, values):
    live = live_ref[...] > 0.0
    return [jnp.where(live, x, 0.0) for x in values]


def pack_kernel(flow_hbm, tile_ref, first_ref, last_ref, flow_ref, sems):
    copies = [
        pltpu.make_async_copy(flow_hbm.at[j], flow_ref.at[j], sems.at[j])
        for j in range(flow_ref.shape[0])
    ]
    for copy in copies:
        copy.start()
    for copy in copies:
        copy.wait()
    put(first_ref, cell(flow_ref, 0))
    put(last_ref, cell(flow_ref, flow_ref.shape[0] - 1))
    pack_faces(lambda j, v: flow_ref[j, v], flow_ref.shape[0], tile_ref)


def merge_kernel(own_ref, got_ref, *refs):
    out_ref = refs[-1]
    count = own_ref.shape[0]
    for w in range(count):
        out_ref[w] = own_ref[w]
        out_ref[count + w] = got_ref[w]


def select_kernel(own_ref, got_ref, after_ref, pick_ref, partner_ref, mine_ref, theirs_ref):
    del after_ref
    count = own_ref.shape[0]

    def tile_at(i):
        return own_ref[i] if i < count else got_ref[i - count]

    mine_ref[...] = ghosts_of(pick_ref, tile_at, 2 * count)
    theirs_ref[...] = ghosts_of(partner_ref, tile_at, 2 * count)


def relay_kernel(own_ref, got_ref, mats_ref, first_ref, mats_out_ref, out_ref):
    merge_kernel(own_ref, got_ref, out_ref)
    for i in range(20):
        put(mats_out_ref, cell(mats_ref, i), i)
    put(mats_out_ref, cell(first_ref), 20)


def neighbours(x):
    lane, row = iota(1), iota(0)
    total = jnp.where(lane == 0, 0.0, pltpu.roll(x, 1, 1))
    total = total + jnp.where(lane == 127, 0.0, pltpu.roll(x, 127, 1))
    total = total + jnp.where(row == 0, 0.0, pltpu.roll(x, 1, 0))
    return total + jnp.where(row == 15, 0.0, pltpu.roll(x, 15, 0))


def offset_of(place, zones):
    offset, stride = 0, zones // 2
    while stride:
        offset, place, stride = offset + stride * (place % 2), place // 2, stride // 2
    return offset


def ghosts_of(pick_ref, tile_at, count):
    low = high = jnp.zeros((16, 128), jnp.float32)
    for i in range(count):
        low = jnp.where(pick_ref[0, i] > 0.0, tile_at(i), low)
        high = jnp.where(pick_ref[1, i] > 0.0, tile_at(i), high)
    return jnp.where(iota(1) % 2 == 0, pltpu.roll(low, 1, 1), pltpu.roll(high, 127, 1))


def ghost_at(ghosts, j, v):
    lane = iota(1)
    q = 2 * (j * 5 + v)
    turned = pltpu.roll(ghosts, 128 - q, 1) if q else ghosts
    return jnp.where((lane == 0) | (lane == 127), turned, 0.0)


HALVES = [pl.ds(0, 8), pl.ds(8, 8)]


def col(ref, q, j, rows):
    return [ref[j, r, q, rows] for r in range(5)]


def put_col(ref, values, q, j, rows):
    for r in range(5):
        ref[j, r, q, rows] = values[r]


def put_mat_col(ref, values, q, i, rows):
    for r in range(5):
        ref[5 * i + r, q, rows] = values[r]


def mat_col(ref, q, i, rows):
    return [ref[5 * i + r, q, rows] for r in range(5)]


def mat(ref, j, rows):
    return [[ref[j, r, c, rows] for c in range(5)] for r in range(5)]


def matrix_kernel(
    depth_hbm, east_hbm, tile_ref, inv_ref, low_ref, up_ref,
    e_ref, f_ref, mats_ref, live_ref, pick_ref, partner_ref,
    y_ref, depth_ref, east_ref, sems,
):
    del tile_ref
    last = inv_ref.shape[0] - 1
    scalars = [
        pltpu.make_async_copy(depth_hbm, depth_ref, sems.at[0]),
        pltpu.make_async_copy(east_hbm, east_ref, sems.at[1]),
    ]
    for copy in scalars:
        copy.start()

    def products(j, rows):
        inv = mat(inv_ref, j, rows)
        for jac_ref, out_ref in ((low_ref, e_ref), (up_ref, f_ref)):
            for q in range(5):
                product = matvec(inv, col(jac_ref, q, j, rows))
                put_col(out_ref, [OMEGA * x for x in product], q, j, rows)

    def forward(j, carry):
        for rows in HALVES:
            products(j, rows)
            e = mat(e_ref, j, rows)
            for q in range(5):
                put_col(y_ref, matvec(e, col(y_ref, q, j - 1, rows)), q, j, rows)
        return carry

    def backward(step, carry):
        j = last - 1 - step
        for rows in HALVES:
            f = mat(f_ref, j, rows)
            for q in range(5):
                turned = matvec(f, mat_col(mats_ref, q, 1, rows))
                put_mat_col(mats_ref, add(col(y_ref, q, j, rows), turned), q, 1, rows)
                put_mat_col(mats_ref, matvec(f, mat_col(mats_ref, q, 2, rows)), q, 2, rows)
        return carry

    for rows in HALVES:
        products(0, rows)
        for q in range(5):
            put_col(y_ref, col(e_ref, q, 0, rows), q, 0, rows)
    lax.fori_loop(1, last + 1, forward, 0)
    for rows in HALVES:
        for q in range(5):
            put_mat_col(mats_ref, col(y_ref, q, last, rows), q, 0, rows)
            put_mat_col(mats_ref, col(y_ref, q, last, rows), q, 1, rows)
            put_mat_col(mats_ref, col(f_ref, q, last, rows), q, 2, rows)
            put_mat_col(mats_ref, col(f_ref, q, last, rows), q, 3, rows)
    lax.fori_loop(0, last, backward, 0)
    for copy in scalars:
        copy.wait()
    zone = lax.axis_index("zone")
    row = iota(0)
    live_ref[...] = jnp.where(row < depth_ref[zone], 1.0, 0.0)
    for i in range(pick_ref.shape[1]):
        w = zone ^ offset_of(i, pick_ref.shape[1])
        rows = row < depth_ref[w]
        pick_ref[0, i] = jnp.where(rows & (east_ref[w] == zone), 1.0, 0.0)
        pick_ref[1, i] = jnp.where(rows & (east_ref[zone] == w), 1.0, 0.0)
        if i < partner_ref.shape[1]:
            partner_ref[0, i] = jnp.where(rows & (east_ref[w] == zone ^ 1), 1.0, 0.0)
            partner_ref[1, i] = jnp.where(rows & (east_ref[zone ^ 1] == w), 1.0, 0.0)


def by_place(mine_refs, other_refs, run):
    odd = lax.axis_index("ja") % 2

    @pl.when(odd == 0)
    def _():
        run(*mine_refs, *other_refs)

    @pl.when(odd == 1)
    def _():
        run(*other_refs, *mine_refs)


def half_kernel(mine_ref, other_ref, last_ref, half_ref):
    ja = lax.axis_index("ja")
    low_pair = ja < 2
    for side in range(2):
        first = [jnp.where(ja == 3, other_ref[20, v], mine_ref[20, v]) for v in range(5)]
        edge = [jnp.where(low_pair, last_ref[v], first[v]) for v in range(5)]
        put(half_ref, [x[8 * side : 8 * side + 8] for x in edge], 5 + side)
    for side in range(2):
        lo, hi = (mine_ref, other_ref) if side == 0 else (other_ref, mine_ref)
        rows = HALVES[side]

        @pl.when((ja % 2 == side) & low_pair)
        def _():
            for r in range(5):
                put(half_ref, [hi[15 + r, c, rows] for c in range(5)], r)

        @pl.when((ja % 2 == side) & (ja >= 2))
        def _():
            d_hi = [[hi[5 + r, c, rows] for c in range(5)] for r in range(5)]
            n_lo = [[lo[10 + r, c, rows] for c in range(5)] for r in range(5)]
            for q in range(5):
                out = matvec(n_lo, matvec(d_hi, mat_col(lo, q, 0, rows)))
                out = add(mat_col(lo, q, 1, rows), out)
                for r in range(5):
                    half_ref[r, q] = out[r]


def sweeps(s_ref, e_ref, f_ref, y_ref, ends_ref, last):
    planes = s_ref.shape[0]
    value = cell(s_ref, 0)
    put(y_ref, value, 0)
    for j in range(1, planes):
        value = matvec(block(e_ref, j), value, cell(s_ref, j))
        put(y_ref, value, j)
    put(ends_ref, [x + z * (1.0 / OMEGA) for x, z in zip(value, last)], 0)
    for j in range(planes - 2, -1, -1):
        value = matvec(block(f_ref, j), value, cell(y_ref, j))
    put(ends_ref, value, 1)


def source_kernel(
    tiles_ref, live_ref, cur_ref, force_ref, diag_ref, inv_ref, e_ref, f_ref, s_ref
):
    del tiles_ref
    planes = cur_ref.shape[0]
    before, here = None, masked(live_ref, cell(cur_ref, 0))
    for j in range(planes):
        own = matvec(block(diag_ref, j), here)
        res = [force_ref[j, v] - own[v] + COUPLE * neighbours(here[v]) for v in range(5)]
        out = matvec(block(inv_ref, j), masked(live_ref, res))
        if j > 0:
            linked = matvec(block(e_ref, j), before)
            out = add(out, [x * (1.0 / OMEGA) for x in linked])
        if j < planes - 1:
            after = masked(live_ref, cell(cur_ref, j + 1))
            linked = matvec(block(f_ref, j), after)
            out = add(out, [x * (1.0 / OMEGA) for x in linked])
            before, here = here, after
        put(s_ref, out, j)


def local_kernel(
    mats_other_ref, live_ref, mine_ref, got_ref, cur_ref, s0_ref,
    inv_ref, e_ref, f_ref,
    s_ref, ends_ref, above_ref, y_ref,
):
    last = cur_ref.shape[0] - 1
    ghosts = jnp.where(live_ref[...] > 0.0, COUPLE * (mine_ref[...] + got_ref[...]), 0.0)
    for j in range(last + 1):
        extra = [ghost_at(ghosts, j, v) for v in range(5)]
        put(s_ref, matvec(block(inv_ref, j), extra, cell(s0_ref, j)), j)
    even = lax.axis_index("ja") % 2 == 0
    above = [jnp.where(even, x, 0.0) for x in masked(live_ref, cell(mats_other_ref, 20))]
    put(above_ref, above)
    linked = matvec(block(f_ref, last), above)
    put(s_ref, add(cell(s_ref, last), [x * (1.0 / OMEGA) for x in linked]), last)
    sweeps(s_ref, e_ref, f_ref, y_ref, ends_ref, masked(live_ref, cell(cur_ref, last)))


def second_kernel(
    live_ref, pick_ref, tiles_ref, cur_ref, above_ref, force_ref, diag_ref, inv_ref, e_ref, f_ref,
    own_ref, s_ref, ends_ref, y_ref,
):
    planes = cur_ref.shape[0]
    zone, zones = lax.axis_index("zone"), tiles_ref.shape[0]
    ghosts = ghosts_of(pick_ref, lambda i: tiles_ref[zone ^ offset_of(i, zones)], zones)
    value = None
    for j in range(planes):
        here = cell(cur_ref, j)
        applied = matvec(block(diag_ref, j), here)
        res = []
        for v in range(5):
            sides = neighbours(here[v]) + ghost_at(ghosts, j, v)
            res.append(force_ref[j, v] - applied[v] + COUPLE * sides)
        res = masked(live_ref, res)
        put(own_ref, res, j)
        above = cell(cur_ref, j + 1) if j < planes - 1 else cell(above_ref)
        linked = matvec(block(f_ref, j), [x * (1.0 / OMEGA) for x in above])
        s = add(matvec(block(inv_ref, j), res), linked)
        put(s_ref, s, j)
        value = s if j == 0 else matvec(block(e_ref, j), value, s)
        put(y_ref, value, j)
        value = add(value, [x * (1.0 / OMEGA) for x in here])
    put(ends_ref, value, 0)
    put(ends_ref, here, 2)
    value = cell(y_ref, planes - 1)
    for j in range(planes - 2, -1, -1):
        value = matvec(block(f_ref, j), value, cell(y_ref, j))
    put(ends_ref, value, 1)


def write_kernel(
    live_ref, below_ref, ends_other_ref, cur_ref, above_ref, own_ref, low_ref, up_ref,
    res_hbm, done_ref, res_ref, sems,
):
    planes = cur_ref.shape[0]
    ja = lax.axis_index("ja")
    before = [
        jnp.where(ja == 0, 0.0, jnp.where(ja == 2, below_ref[v], ends_other_ref[2, v]))
        for v in range(5)
    ]
    copies = []
    for j in range(planes):
        lower = matvec(block(low_ref, j), before if j == 0 else cell(cur_ref, j - 1))
        above = cell(cur_ref, j + 1) if j < planes - 1 else cell(above_ref)
        coupled = masked(live_ref, add(lower, matvec(block(up_ref, j), above)))
        put(res_ref, add(cell(own_ref, j), coupled), j)
        copies.append(pltpu.make_async_copy(res_ref.at[j], res_hbm.at[j], sems.at[j]))
        copies[-1].start()
    done_ref[...] = live_ref[...]
    for copy in copies:
        copy.wait()


def compose(ends_lo, mats_lo, ends_hi, mats_hi, out_ref, first=None):
    c_lo = cell(ends_lo, 0)

    @pl.when(lax.axis_index("ja") < 2)
    def _():
        put(out_ref, matvec(matrix_of(mats_hi, 0), c_lo, cell(ends_hi, 0)), 0)

    @pl.when(lax.axis_index("ja") >= 2)
    def _():
        turned = matvec(matrix_of(mats_hi, 1), c_lo, cell(ends_hi, 1))
        raised = matvec(matrix_of(mats_lo, 2), turned, cell(ends_lo, 1))
        if first is not None:
            raised = add(raised, first(mats_lo))
        put(out_ref, raised, 0)


def mid_kernel(ends_ref, ends_other_ref, mats_ref, mats_other_ref, out_ref):
    def run(ends_lo, mats_lo, ends_hi, mats_hi):
        compose(ends_lo, mats_lo, ends_hi, mats_hi, out_ref)

    by_place([ends_ref, mats_ref], [ends_other_ref, mats_other_ref], run)


def first_mid_kernel(
    live_ref, half_ref, ends_ref, ends_other_ref, mats_ref, mats_other_ref,
    out_ref, beyond_ref, half_out_ref, *part_refs,
):
    def first(mats_lo):
        return [x * (1.0 / OMEGA) for x in masked(live_ref, cell(mats_lo, 20))]

    def run(ends_lo, mats_lo, ends_hi, mats_hi):
        compose(ends_lo, mats_lo, ends_hi, mats_hi, out_ref, first)

    by_place([ends_ref, mats_ref], [ends_other_ref, mats_other_ref], run)
    for r in range(5):
        put(half_out_ref, cell(half_ref, r), r)
        for c in range(5):
            part, place = divmod(5 * r + c, PART)
            part_refs[part][place] = half_ref[r, c]
    beyond = [jnp.concatenate([half_ref[5, v], half_ref[6, v]], axis=0) for v in range(5)]
    put(beyond_ref, masked(live_ref, beyond))


def join(mine_ref, other_refs, r, c):
    part, place = divmod(5 * r + c, PART)
    mine, other = mine_ref[r, c], other_refs[part][place]
    odd = lax.axis_index("ja") % 2 == 1
    return jnp.concatenate([jnp.where(odd, mine, other), jnp.where(odd, other, mine)], axis=0)


def inflows(
    ends_ref, ends_other_ref, mats_ref, mats_other_ref, pair_ref, pair_other_ref,
    half_ref, half_other_refs, inflow_ref, live_ref=None, beyond_ref=None,
):
    ja = lax.axis_index("ja")
    zeros = [jnp.zeros((16, 128), jnp.float32)] * 5

    def joined():
        return [[join(half_ref, half_other_refs, r, c) for c in range(5)] for r in range(5)]

    def passed(value, coupling, first):
        if beyond_ref is None:
            return value
        return add(value, [x * (1.0 / OMEGA) for x in matvec(coupling, first)])

    def far(mats_hi_ref):
        first = None if beyond_ref is None else cell(beyond_ref)
        a = passed(cell(pair_ref, 0), matrix_of(mats_hi_ref, 3), first)
        return add(cell(pair_other_ref, 0), matvec(joined(), a))

    def near(mats_lo_ref):
        first = None if beyond_ref is None else masked(live_ref, cell(mats_lo_ref, 20))
        return passed(cell(pair_other_ref, 0), joined(), first)

    @pl.when(ja == 0)
    def _():
        put(inflow_ref, zeros, 0)
        b = matvec(matrix_of(mats_other_ref, 1), cell(ends_ref, 0), cell(ends_other_ref, 1))
        b = matvec(matrix_of(mats_other_ref, 2), far(mats_other_ref), b)
        put(inflow_ref, b, 1)

    @pl.when(ja == 1)
    def _():
        put(inflow_ref, cell(ends_other_ref, 0), 0)
        put(inflow_ref, far(mats_ref), 1)

    @pl.when(ja == 2)
    def _():
        a = near(mats_ref)
        put(inflow_ref, a, 0)
        a = matvec(matrix_of(mats_ref, 0), a, cell(ends_ref, 0))
        b = matvec(matrix_of(mats_other_ref, 1), a, cell(ends_other_ref, 1))
        put(inflow_ref, b, 1)

    @pl.when(ja == 3)
    def _():
        a = near(mats_other_ref)
        a = matvec(matrix_of(mats_other_ref, 0), a, cell(ends_other_ref, 0))
        put(inflow_ref, a, 0)
        put(inflow_ref, zeros, 1)


def final_kernel(
    live_ref, cur_ref, above_ref, beyond_ref, s_ref, e_ref, f_ref,
    ends_ref, ends_other_ref, mats_ref, mats_other_ref, pair_ref, pair_other_ref,
    half_ref, *rest,
):
    half_other_refs = rest[:4]
    new_ref, above_new_ref, below_new_ref, tile_ref, y_ref, inflow_ref = rest[4:]
    planes = cur_ref.shape[0]
    inflows(
        ends_ref, ends_other_ref, mats_ref, mats_other_ref, pair_ref, pair_other_ref,
        half_ref, half_other_refs, inflow_ref, live_ref, beyond_ref,
    )
    value = cell(inflow_ref, 0)
    for j in range(planes):
        value = matvec(block(e_ref, j), value, cell(s_ref, j))
        put(y_ref, value, j)
    value = cell(inflow_ref, 1)
    kept = [x * (1.0 - 1.0 / OMEGA) for x in cell(beyond_ref)]
    inner = lax.axis_index("ja") == 1
    above = add(cell(above_ref), [jnp.where(inner, x, 0.0) for x in kept])
    put(above_new_ref, add(above, value))
    for j in range(planes - 1, -1, -1):
        value = matvec(block(f_ref, j), value, cell(y_ref, j))
        put(new_ref, add(masked(live_ref, cell(cur_ref, j)), value), j)
    coupling = [[join(half_ref, half_other_refs, r, c) for c in range(5)] for r in range(5)]
    raised = add(cell(inflow_ref, 0), matvec(coupling, value))
    put(below_new_ref, add(raised, kept))
    pack_faces(lambda j, v: new_ref[j, v], planes, tile_ref)


def last_kernel(
    done_ref, cur_ref, s_ref, e_ref, f_ref,
    ends_ref, ends_other_ref, mats_ref, mats_other_ref, pair_ref, pair_other_ref,
    half_ref, *rest,
):
    half_other_refs = rest[:4]
    new_hbm, y_ref, inflow_ref, new_ref, sems = rest[4:]
    del done_ref
    planes = cur_ref.shape[0]
    copies = []
    inflows(
        ends_ref, ends_other_ref, mats_ref, mats_other_ref, pair_ref, pair_other_ref,
        half_ref, half_other_refs, inflow_ref,
    )
    value = cell(inflow_ref, 0)
    for j in range(planes):
        value = matvec(block(e_ref, j), value, cell(s_ref, j))
        put(y_ref, value, j)
        value = add(value, [x * (1.0 / OMEGA) for x in cell(cur_ref, j)])
    value = cell(inflow_ref, 1)
    for j in range(planes - 1, -1, -1):
        value = matvec(block(f_ref, j), value, cell(y_ref, j))
        put(new_ref, add(cell(cur_ref, j), value), j)
        copies.append(pltpu.make_async_copy(new_ref.at[j], new_hbm.at[j], sems.at[j]))
        copies[-1].start()
    for copy in copies:
        copy.wait()


def per_device(
    flow_state, forcing, diag_block, lower_jac, upper_jac, block_inv, east_zone, zone_depth
):
    zones, parts = lax.axis_size("zone"), lax.axis_size("ja")
    assert parts == 4 and ITERS == 2 and zones > 4 and zones & (zones - 1) == 0
    current, force, diag, low, up, inv = (
        x[0] for x in (flow_state, forcing, diag_block, lower_jac, upper_jac, block_inv)
    )
    state = current.shape
    planes, plane, blocks = state[0], state[1:], diag.shape
    matrix = blocks[1:]
    work = [buffer(*state)]

    def swap(x, bit):
        return lax.ppermute(x, "ja", [(p, p ^ bit) for p in range(parts)])

    tile, first, final = call(
        pack_kernel,
        [(1, *state[2:]), plane, plane],
        work + [pltpu.SemaphoreType.DMA((planes,))],
        flops=10**10,
        far=(0,),
    )(current)
    e, f, mats, live, pick, partner = call(
        matrix_kernel,
        [
            blocks, blocks, (20, *plane), state[2:],
            (2, zones, *state[2:]), (2, zones // 2, *state[2:]),
        ],
        [buffer(*blocks)]
        + [pltpu.SMEM((zones,), jnp.int32)] * 2
        + [pltpu.SemaphoreType.DMA((2,))],
        flops=5 * 10**9,
        far=(0, 1),
    )(zone_depth, east_zone, tile, inv, low, up)
    tiles, stride = tile, zones // 2
    while stride > 1:
        got = lax.ppermute(tiles, "zone", [(z, z ^ stride) for z in range(zones)])
        both = (2 * tiles.shape[0], *state[2:])
        if stride == zones // 2:
            mats, tiles = call(relay_kernel, [(21, *plane), both], flops=10**5)(
                tiles, got, mats, first
            )
            mats_other = swap(mats, 1)
            half = call(half_kernel, [(7, plane[0], 8, plane[2])], flops=10**5)(
                mats, mats_other, final
            )[0]
        elif stride > 2:
            tiles = call(merge_kernel, [both], flops=10**5)(tiles, got, half)[0]
        else:
            tiles, theirs = call(select_kernel, [state[2:]] * 2, flops=10**5)(
                tiles, got, half, pick, partner
            )
        stride //= 2
    got = lax.ppermute(theirs, "zone", [(z, z ^ 1) for z in range(zones)])
    half = swap(half, 3)
    s0 = call(source_kernel, [state], flops=2 * 10**9)(tiles, live, current, force, diag, inv, e, f)[0]
    s, ends, above = call(local_kernel, [state, (2, *plane), plane], work)(
        mats_other, live, tiles, got, current, s0, inv, e, f
    )
    ends_other = swap(ends, 1)
    parts_of = [(min(PART, 25 - i), *half.shape[2:]) for i in range(0, 25, PART)]
    pair, beyond, half, *sent = call(
        first_mid_kernel, [(1, *plane), plane, (5, *half.shape[1:])] + parts_of, flops=10**5
    )(live, half, ends, ends_other, mats, mats_other)
    half_other = [swap(x, 1) for x in sent]
    pair_other = swap(pair, 3)
    flows = [buffer(2, *plane)]
    current, above, below, tile = call(
        final_kernel, [state, plane, plane, (zones, *state[2:])], work + flows
    )(
        live, current, above, beyond, s, e, f,
        ends, ends_other, mats, mats_other, pair, pair_other, half, *half_other,
    )

    got = lax.all_to_all(tile, "zone", 0, 0, tiled=True)
    own, s, ends = call(second_kernel, [state, state, (3, *plane)], work)(
        live, pick, got, current, above, force, diag, inv, e, f
    )
    ends_other = swap(ends, 1)
    pair = call(mid_kernel, [(1, *plane)], flops=10**5)(ends, ends_other, mats, mats_other)[0]
    pair_other = swap(pair, 3)
    residual, done = call(
        write_kernel,
        [state, state[2:]],
        work + [pltpu.SemaphoreType.DMA((planes,))],
        out_specs=[HBM, VMEM],
    )(live, below, ends_other, current, above, own, low, up)
    current = call(
        last_kernel,
        [state],
        work + flows + work + [pltpu.SemaphoreType.DMA((planes,))],
        out_specs=[HBM],
    )(
        done, current, s, e, f,
        ends, ends_other, mats, mats_other, pair, pair_other, half, *half_other,
    )[0]
    return (current[None], residual[None])


def solution(mesh):
    state = P("zone", "ja", None, None, None)
    blocks = P("zone", "ja", None, None, None, None)
    return jax.shard_map(
        per_device,
        mesh=mesh,
        in_specs=(state, state, blocks, blocks, blocks, blocks, P(), P()),
        out_specs=(state, state),
        check_vma=False,
    )
```

```python
import jax
import jax.numpy as jnp
from jax import lax
from jax.experimental import pallas as pl
from jax.experimental.pallas import tpu as pltpu
from jax.sharding import PartitionSpec as P

ITERS = 2
OMEGA = 1.2
PART = 7
COUPLE = 0.25

VMEM = pl.BlockSpec(memory_space=pltpu.VMEM)
ANY = pl.BlockSpec(memory_space=pl.ANY)
HBM = pl.BlockSpec(memory_space=pltpu.HBM)


def call(kernel, shapes, scratch=(), flops=10**9, far=(), out_specs=None, alias=None):
    alias = alias or {}

    def run(*arrays):
        arrays = [
            pltpu.with_memory_space_constraint(a, pltpu.HBM) if i in far else a
            for i, a in enumerate(arrays)
        ]
        return pl.pallas_call(
            kernel,
            out_shape=[jax.ShapeDtypeStruct(s, jnp.float32) for s in shapes],
            in_specs=[
                HBM if i in far else ANY if i in alias else VMEM for i in range(len(arrays))
            ],
            out_specs=out_specs or [VMEM] * len(shapes),
            scratch_shapes=list(scratch),
            input_output_aliases=alias,
            compiler_params=pltpu.CompilerParams(vmem_limit_bytes=8 * 2**20),
            cost_estimate=pl.CostEstimate(flops=flops, bytes_accessed=flops // 10**3, transcendentals=0),
        )(*arrays)

    return run


def buffer(*shape):
    return pltpu.VMEM(shape, jnp.float32)


def iota(dim):
    return lax.broadcasted_iota(jnp.int32, (16, 128), dim)


def matvec(matrix, vector, base=None):
    out = []
    for r, row in enumerate(matrix):
        terms = [m * x for m, x in zip(row, vector)]
        if base is not None:
            terms.insert(0, base[r])
        while len(terms) > 1:
            pairs = [x + z for x, z in zip(terms[::2], terms[1::2])]
            terms = pairs + terms[2 * len(pairs) :]
        out.append(terms[0])
    return out


def block(ref, *lead):
    return [[ref[(*lead, r, c)] for c in range(5)] for r in range(5)]


def matrix_of(ref, i):
    return [cell(ref, 5 * i + r) for r in range(5)]


def cell(ref, *lead):
    return [ref[(*lead, v)] for v in range(5)]


def put(ref, values, *lead):
    for v, value in enumerate(values):
        ref[(*lead, v)] = value


def add(a, b):
    return [x + y for x, y in zip(a, b)]


def pack_faces(load, planes, tile_ref):
    lane = iota(1)
    tile = jnp.zeros((16, 128), jnp.float32)
    for j in range(planes):
        for v in range(5):
            q = 2 * (j * 5 + v)
            here = (lane == q) | (lane == (q - 1) % 128)
            x = load(j, v)
            tile = jnp.where(here, pltpu.roll(x, q, 1) if q else x, tile)
    for w in range(tile_ref.shape[0]):
        tile_ref[w] = tile


def masked(live_ref, values):
    live = live_ref[...] > 0.0
    return [jnp.where(live, x, 0.0) for x in values]


def pack_kernel(flow_hbm, tile_ref, first_ref, last_ref, flow_ref, sems):
    copies = [
        pltpu.make_async_copy(flow_hbm.at[j], flow_ref.at[j], sems.at[j])
        for j in range(flow_ref.shape[0])
    ]
    for copy in copies:
        copy.start()
    for copy in copies:
        copy.wait()
    put(first_ref, cell(flow_ref, 0))
    put(last_ref, cell(flow_ref, flow_ref.shape[0] - 1))
    pack_faces(lambda j, v: flow_ref[j, v], flow_ref.shape[0], tile_ref)


def merge_kernel(own_ref, got_ref, *refs):
    out_ref = refs[-1]
    count = own_ref.shape[0]
    for w in range(count):
        out_ref[w] = own_ref[w]
        out_ref[count + w] = got_ref[w]


def select_kernel(tiles_ref, pick_ref, partner_ref, mine_ref, theirs_ref):
    def tile_at(i):
        return tiles_ref[i]

    mine_ref[...] = ghosts_of(pick_ref, tile_at, tiles_ref.shape[0])
    theirs_ref[...] = ghosts_of(partner_ref, tile_at, tiles_ref.shape[0])


def relay_kernel(
    own_ref, half_ref, quarter_ref, both_ref, mats_ref, first_ref, mats_out_ref, out_ref
):
    for i, ref in enumerate((own_ref, half_ref, quarter_ref, both_ref)):
        out_ref[i] = ref[0]
    for i in range(20):
        put(mats_out_ref, cell(mats_ref, i), i)
    put(mats_out_ref, cell(first_ref), 20)


def neighbours(x):
    lane, row = iota(1), iota(0)
    total = jnp.where(lane == 0, 0.0, pltpu.roll(x, 1, 1))
    total = total + jnp.where(lane == 127, 0.0, pltpu.roll(x, 127, 1))
    total = total + jnp.where(row == 0, 0.0, pltpu.roll(x, 1, 0))
    return total + jnp.where(row == 15, 0.0, pltpu.roll(x, 15, 0))


def offset_of(place, zones):
    offset, stride = 0, zones // 2
    while stride:
        offset, place, stride = offset + stride * (place % 2), place // 2, stride // 2
    return offset


def ghosts_of(pick_ref, tile_at, count):
    low = high = jnp.zeros((16, 128), jnp.float32)
    for i in range(count):
        low = jnp.where(pick_ref[0, i] > 0.0, tile_at(i), low)
        high = jnp.where(pick_ref[1, i] > 0.0, tile_at(i), high)
    return jnp.where(iota(1) % 2 == 0, pltpu.roll(low, 1, 1), pltpu.roll(high, 127, 1))


def ghost_at(ghosts, j, v):
    lane = iota(1)
    q = 2 * (j * 5 + v)
    turned = pltpu.roll(ghosts, 128 - q, 1) if q else ghosts
    return jnp.where((lane == 0) | (lane == 127), turned, 0.0)


HALVES = [pl.ds(0, 8), pl.ds(8, 8)]


def col(ref, q, j, rows):
    return [ref[j, r, q, rows] for r in range(5)]


def put_col(ref, values, q, j, rows):
    for r in range(5):
        ref[j, r, q, rows] = values[r]


def put_mat_col(ref, values, q, i, rows):
    for r in range(5):
        ref[5 * i + r, q, rows] = values[r]


def mat_col(ref, q, i, rows):
    return [ref[5 * i + r, q, rows] for r in range(5)]


def mat(ref, j, rows):
    return [[ref[j, r, c, rows] for c in range(5)] for r in range(5)]


def matrix_kernel(
    depth_hbm, east_hbm, tile_ref, inv_ref, low_ref, up_ref,
    e_ref, f_ref, mats_ref, live_ref, pick_ref, partner_ref,
    y_ref, depth_ref, east_ref, sems,
):
    del tile_ref
    last = inv_ref.shape[0] - 1
    scalars = [
        pltpu.make_async_copy(depth_hbm, depth_ref, sems.at[0]),
        pltpu.make_async_copy(east_hbm, east_ref, sems.at[1]),
    ]
    for copy in scalars:
        copy.start()

    def products(j, rows):
        inv = mat(inv_ref, j, rows)
        for jac_ref, out_ref in ((low_ref, e_ref), (up_ref, f_ref)):
            for q in range(5):
                product = matvec(inv, col(jac_ref, q, j, rows))
                put_col(out_ref, [OMEGA * x for x in product], q, j, rows)

    def forward(j, carry):
        for rows in HALVES:
            products(j, rows)
            e = mat(e_ref, j, rows)
            for q in range(5):
                put_col(y_ref, matvec(e, col(y_ref, q, j - 1, rows)), q, j, rows)
        return carry

    def backward(step, carry):
        j = last - 1 - step
        for rows in HALVES:
            f = mat(f_ref, j, rows)
            for q in range(5):
                turned = matvec(f, mat_col(mats_ref, q, 1, rows))
                put_mat_col(mats_ref, add(col(y_ref, q, j, rows), turned), q, 1, rows)
                put_mat_col(mats_ref, matvec(f, mat_col(mats_ref, q, 2, rows)), q, 2, rows)
        return carry

    for rows in HALVES:
        products(0, rows)
        for q in range(5):
            put_col(y_ref, col(e_ref, q, 0, rows), q, 0, rows)
    lax.fori_loop(1, last + 1, forward, 0)
    for rows in HALVES:
        for q in range(5):
            put_mat_col(mats_ref, col(y_ref, q, last, rows), q, 0, rows)
            put_mat_col(mats_ref, col(y_ref, q, last, rows), q, 1, rows)
            put_mat_col(mats_ref, col(f_ref, q, last, rows), q, 2, rows)
            put_mat_col(mats_ref, col(f_ref, q, last, rows), q, 3, rows)
    lax.fori_loop(0, last, backward, 0)
    for copy in scalars:
        copy.wait()
    zone = lax.axis_index("zone")
    row = iota(0)
    live_ref[...] = jnp.where(row < depth_ref[zone], 1.0, 0.0)
    for i in range(pick_ref.shape[1]):
        w = zone ^ offset_of(i, pick_ref.shape[1])
        rows = row < depth_ref[w]
        pick_ref[0, i] = jnp.where(rows & (east_ref[w] == zone), 1.0, 0.0)
        pick_ref[1, i] = jnp.where(rows & (east_ref[zone] == w), 1.0, 0.0)
        if i < partner_ref.shape[1]:
            partner_ref[0, i] = jnp.where(rows & (east_ref[w] == zone ^ 1), 1.0, 0.0)
            partner_ref[1, i] = jnp.where(rows & (east_ref[zone ^ 1] == w), 1.0, 0.0)


def by_place(mine_refs, other_refs, run):
    odd = lax.axis_index("ja") % 2

    @pl.when(odd == 0)
    def _():
        run(*mine_refs, *other_refs)

    @pl.when(odd == 1)
    def _():
        run(*other_refs, *mine_refs)


def half_kernel(mine_ref, other_ref, last_ref, half_ref):
    ja = lax.axis_index("ja")
    low_pair = ja < 2
    for side in range(2):
        first = [jnp.where(ja == 3, other_ref[20, v], mine_ref[20, v]) for v in range(5)]
        edge = [jnp.where(low_pair, last_ref[v], first[v]) for v in range(5)]
        put(half_ref, [x[8 * side : 8 * side + 8] for x in edge], 5 + side)
    for side in range(2):
        lo, hi = (mine_ref, other_ref) if side == 0 else (other_ref, mine_ref)
        rows = HALVES[side]

        @pl.when((ja % 2 == side) & low_pair)
        def _():
            for r in range(5):
                put(half_ref, [hi[15 + r, c, rows] for c in range(5)], r)

        @pl.when((ja % 2 == side) & (ja >= 2))
        def _():
            d_hi = [[hi[5 + r, c, rows] for c in range(5)] for r in range(5)]
            n_lo = [[lo[10 + r, c, rows] for c in range(5)] for r in range(5)]
            for q in range(5):
                out = matvec(n_lo, matvec(d_hi, mat_col(lo, q, 0, rows)))
                out = add(mat_col(lo, q, 1, rows), out)
                for r in range(5):
                    half_ref[r, q] = out[r]


def sweeps(s_ref, e_ref, f_ref, y_ref, ends_ref, last):
    planes = s_ref.shape[0]
    value = cell(s_ref, 0)
    put(y_ref, value, 0)
    for j in range(1, planes):
        value = matvec(block(e_ref, j), value, cell(s_ref, j))
        put(y_ref, value, j)
    put(ends_ref, [x + z * (1.0 / OMEGA) for x, z in zip(value, last)], 0)
    for j in range(planes - 2, -1, -1):
        value = matvec(block(f_ref, j), value, cell(y_ref, j))
    put(ends_ref, value, 1)


def source_kernel(
    tiles_ref, live_ref, cur_ref, force_ref, diag_ref, inv_ref, e_ref, f_ref, s_ref
):
    del tiles_ref
    planes = cur_ref.shape[0]
    before, here = None, masked(live_ref, cell(cur_ref, 0))
    for j in range(planes):
        own = matvec(block(diag_ref, j), here)
        res = [force_ref[j, v] - own[v] + COUPLE * neighbours(here[v]) for v in range(5)]
        out = matvec(block(inv_ref, j), masked(live_ref, res))
        if j > 0:
            linked = matvec(block(e_ref, j), before)
            out = add(out, [x * (1.0 / OMEGA) for x in linked])
        if j < planes - 1:
            after = masked(live_ref, cell(cur_ref, j + 1))
            linked = matvec(block(f_ref, j), after)
            out = add(out, [x * (1.0 / OMEGA) for x in linked])
            before, here = here, after
        put(s_ref, out, j)


def local_kernel(
    half_ref, mats_other_ref, live_ref, mine_ref, got_ref, cur_ref, s0_ref,
    inv_ref, e_ref, f_ref,
    s_ref, ends_ref, above_ref, y_ref,
):
    del half_ref
    last = cur_ref.shape[0] - 1
    ghosts = jnp.where(live_ref[...] > 0.0, COUPLE * (mine_ref[...] + got_ref[...]), 0.0)
    for j in range(last + 1):
        extra = [ghost_at(ghosts, j, v) for v in range(5)]
        put(s_ref, matvec(block(inv_ref, j), extra, cell(s0_ref, j)), j)
    even = lax.axis_index("ja") % 2 == 0
    above = [jnp.where(even, x, 0.0) for x in masked(live_ref, cell(mats_other_ref, 20))]
    put(above_ref, above)
    linked = matvec(block(f_ref, last), above)
    put(s_ref, add(cell(s_ref, last), [x * (1.0 / OMEGA) for x in linked]), last)
    sweeps(s_ref, e_ref, f_ref, y_ref, ends_ref, masked(live_ref, cell(cur_ref, last)))


def second_kernel(
    live_ref, pick_ref, tiles_ref, cur_ref, above_ref, force_ref, diag_ref, inv_ref, e_ref, f_ref,
    own_ref, s_ref, ends_ref, y_ref,
):
    planes = cur_ref.shape[0]
    zone, zones = lax.axis_index("zone"), tiles_ref.shape[0]
    ghosts = ghosts_of(pick_ref, lambda i: tiles_ref[zone ^ offset_of(i, zones)], zones)
    value = None
    for j in range(planes):
        here = cell(cur_ref, j)
        applied = matvec(block(diag_ref, j), here)
        res = []
        for v in range(5):
            sides = neighbours(here[v]) + ghost_at(ghosts, j, v)
            res.append(force_ref[j, v] - applied[v] + COUPLE * sides)
        res = masked(live_ref, res)
        put(own_ref, res, j)
        above = cell(cur_ref, j + 1) if j < planes - 1 else cell(above_ref)
        linked = matvec(block(f_ref, j), [x * (1.0 / OMEGA) for x in above])
        s = add(matvec(block(inv_ref, j), res), linked)
        put(s_ref, s, j)
        value = s if j == 0 else matvec(block(e_ref, j), value, s)
        put(y_ref, value, j)
        value = add(value, [x * (1.0 / OMEGA) for x in here])
    put(ends_ref, value, 0)
    put(ends_ref, here, 2)
    value = cell(y_ref, planes - 1)
    for j in range(planes - 2, -1, -1):
        value = matvec(block(f_ref, j), value, cell(y_ref, j))
    put(ends_ref, value, 1)


def write_kernel(
    live_ref, below_ref, ends_other_ref, cur_ref, above_ref, own_ref, low_ref, up_ref,
    res_hbm, done_ref, res_ref, sems,
):
    planes = cur_ref.shape[0]
    ja = lax.axis_index("ja")
    before = [
        jnp.where(ja == 0, 0.0, jnp.where(ja == 2, below_ref[v], ends_other_ref[2, v]))
        for v in range(5)
    ]
    copies = []
    for j in range(planes):
        lower = matvec(block(low_ref, j), before if j == 0 else cell(cur_ref, j - 1))
        above = cell(cur_ref, j + 1) if j < planes - 1 else cell(above_ref)
        coupled = masked(live_ref, add(lower, matvec(block(up_ref, j), above)))
        put(res_ref, add(cell(own_ref, j), coupled), j)
        copies.append(pltpu.make_async_copy(res_ref.at[j], res_hbm.at[j], sems.at[j]))
        copies[-1].start()
    done_ref[...] = live_ref[...]
    for copy in copies:
        copy.wait()


def compose(ends_lo, mats_lo, ends_hi, mats_hi, out_ref, first=None):
    c_lo = cell(ends_lo, 0)

    @pl.when(lax.axis_index("ja") < 2)
    def _():
        put(out_ref, matvec(matrix_of(mats_hi, 0), c_lo, cell(ends_hi, 0)), 0)

    @pl.when(lax.axis_index("ja") >= 2)
    def _():
        turned = matvec(matrix_of(mats_hi, 1), c_lo, cell(ends_hi, 1))
        raised = matvec(matrix_of(mats_lo, 2), turned, cell(ends_lo, 1))
        if first is not None:
            raised = add(raised, first(mats_lo))
        put(out_ref, raised, 0)


def mid_kernel(ends_ref, ends_other_ref, mats_ref, mats_other_ref, out_ref):
    def run(ends_lo, mats_lo, ends_hi, mats_hi):
        compose(ends_lo, mats_lo, ends_hi, mats_hi, out_ref)

    by_place([ends_ref, mats_ref], [ends_other_ref, mats_other_ref], run)


def first_mid_kernel(live_ref, ends_ref, ends_other_ref, mats_ref, mats_other_ref, out_ref):
    def first(mats_lo):
        return [x * (1.0 / OMEGA) for x in masked(live_ref, cell(mats_lo, 20))]

    def run(ends_lo, mats_lo, ends_hi, mats_hi):
        compose(ends_lo, mats_lo, ends_hi, mats_hi, out_ref, first)

    by_place([ends_ref, mats_ref], [ends_other_ref, mats_other_ref], run)


def parts_kernel(live_ref, half_ref, pair_ref, beyond_ref, half_out_ref, *part_refs):
    del pair_ref
    for r in range(5):
        put(half_out_ref, cell(half_ref, r), r)
        for c in range(5):
            part, place = divmod(5 * r + c, PART)
            part_refs[part][place] = half_ref[r, c]
    beyond = [jnp.concatenate([half_ref[5, v], half_ref[6, v]], axis=0) for v in range(5)]
    put(beyond_ref, masked(live_ref, beyond))


def join(mine_ref, other_refs, r, c):
    part, place = divmod(5 * r + c, PART)
    mine, other = mine_ref[r, c], other_refs[part][place]
    odd = lax.axis_index("ja") % 2 == 1
    return jnp.concatenate([jnp.where(odd, mine, other), jnp.where(odd, other, mine)], axis=0)


def inflows(
    ends_ref, ends_other_ref, mats_ref, mats_other_ref, pair_ref, pair_other_ref,
    half_ref, half_other_refs, inflow_ref, live_ref=None, beyond_ref=None,
):
    ja = lax.axis_index("ja")
    zeros = [jnp.zeros((16, 128), jnp.float32)] * 5

    def joined():
        return [[join(half_ref, half_other_refs, r, c) for c in range(5)] for r in range(5)]

    def passed(value, coupling, first):
        if beyond_ref is None:
            return value
        return add(value, [x * (1.0 / OMEGA) for x in matvec(coupling, first)])

    def far(mats_hi_ref):
        first = None if beyond_ref is None else cell(beyond_ref)
        a = passed(cell(pair_ref, 0), matrix_of(mats_hi_ref, 3), first)
        return add(cell(pair_other_ref, 0), matvec(joined(), a))

    def near(mats_lo_ref):
        first = None if beyond_ref is None else masked(live_ref, cell(mats_lo_ref, 20))
        return passed(cell(pair_other_ref, 0), joined(), first)

    @pl.when(ja == 0)
    def _():
        put(inflow_ref, zeros, 0)
        b = matvec(matrix_of(mats_other_ref, 1), cell(ends_ref, 0), cell(ends_other_ref, 1))
        b = matvec(matrix_of(mats_other_ref, 2), far(mats_other_ref), b)
        put(inflow_ref, b, 1)

    @pl.when(ja == 1)
    def _():
        put(inflow_ref, cell(ends_other_ref, 0), 0)
        put(inflow_ref, far(mats_ref), 1)

    @pl.when(ja == 2)
    def _():
        a = near(mats_ref)
        put(inflow_ref, a, 0)
        a = matvec(matrix_of(mats_ref, 0), a, cell(ends_ref, 0))
        b = matvec(matrix_of(mats_other_ref, 1), a, cell(ends_other_ref, 1))
        put(inflow_ref, b, 1)

    @pl.when(ja == 3)
    def _():
        a = near(mats_other_ref)
        a = matvec(matrix_of(mats_other_ref, 0), a, cell(ends_other_ref, 0))
        put(inflow_ref, a, 0)
        put(inflow_ref, zeros, 1)


def final_kernel(
    live_ref, cur_ref, above_ref, beyond_ref, s_ref, e_ref, f_ref,
    ends_ref, ends_other_ref, mats_ref, mats_other_ref, pair_ref, pair_other_ref,
    half_ref, *rest,
):
    half_other_refs = rest[:4]
    new_ref, above_new_ref, below_new_ref, tile_ref, y_ref, inflow_ref = rest[4:]
    planes = cur_ref.shape[0]
    inflows(
        ends_ref, ends_other_ref, mats_ref, mats_other_ref, pair_ref, pair_other_ref,
        half_ref, half_other_refs, inflow_ref, live_ref, beyond_ref,
    )
    value = cell(inflow_ref, 0)
    for j in range(planes):
        value = matvec(block(e_ref, j), value, cell(s_ref, j))
        put(y_ref, value, j)
    value = cell(inflow_ref, 1)
    kept = [x * (1.0 - 1.0 / OMEGA) for x in cell(beyond_ref)]
    inner = lax.axis_index("ja") == 1
    above = add(cell(above_ref), [jnp.where(inner, x, 0.0) for x in kept])
    put(above_new_ref, add(above, value))
    for j in range(planes - 1, -1, -1):
        value = matvec(block(f_ref, j), value, cell(y_ref, j))
        put(new_ref, add(masked(live_ref, cell(cur_ref, j)), value), j)
    coupling = [[join(half_ref, half_other_refs, r, c) for c in range(5)] for r in range(5)]
    raised = add(cell(inflow_ref, 0), matvec(coupling, value))
    put(below_new_ref, add(raised, kept))
    pack_faces(lambda j, v: new_ref[j, v], planes, tile_ref)


def last_kernel(
    done_ref, cur_ref, s_ref, e_ref, f_ref,
    ends_ref, ends_other_ref, mats_ref, mats_other_ref, pair_ref, pair_other_ref,
    half_ref, *rest,
):
    half_other_refs = rest[:4]
    new_hbm, y_ref, inflow_ref, new_ref, sems = rest[4:]
    del done_ref
    planes = cur_ref.shape[0]
    copies = []
    inflows(
        ends_ref, ends_other_ref, mats_ref, mats_other_ref, pair_ref, pair_other_ref,
        half_ref, half_other_refs, inflow_ref,
    )
    value = cell(inflow_ref, 0)
    for j in range(planes):
        value = matvec(block(e_ref, j), value, cell(s_ref, j))
        put(y_ref, value, j)
        value = add(value, [x * (1.0 / OMEGA) for x in cell(cur_ref, j)])
    value = cell(inflow_ref, 1)
    for j in range(planes - 1, -1, -1):
        value = matvec(block(f_ref, j), value, cell(y_ref, j))
        put(new_ref, add(cell(cur_ref, j), value), j)
        copies.append(pltpu.make_async_copy(new_ref.at[j], new_hbm.at[j], sems.at[j]))
        copies[-1].start()
    for copy in copies:
        copy.wait()


def per_device(
    flow_state, forcing, diag_block, lower_jac, upper_jac, block_inv, east_zone, zone_depth
):
    zones, parts = lax.axis_size("zone"), lax.axis_size("ja")
    assert parts == 4 and ITERS == 2 and zones > 4 and zones & (zones - 1) == 0
    current, force, diag, low, up, inv = (
        x[0] for x in (flow_state, forcing, diag_block, lower_jac, upper_jac, block_inv)
    )
    state = current.shape
    planes, plane, blocks = state[0], state[1:], diag.shape
    matrix = blocks[1:]
    work = [buffer(*state)]

    def swap(x, bit):
        return lax.ppermute(x, "ja", [(p, p ^ bit) for p in range(parts)])

    tile, first, final = call(
        pack_kernel,
        [(1, *state[2:]), plane, plane],
        work + [pltpu.SemaphoreType.DMA((planes,))],
        flops=10**10,
        far=(0,),
    )(current)
    e, f, mats, live, pick, partner = call(
        matrix_kernel,
        [
            blocks, blocks, (20, *plane), state[2:],
            (2, zones, *state[2:]), (2, zones // 2, *state[2:]),
        ],
        [buffer(*blocks)]
        + [pltpu.SMEM((zones,), jnp.int32)] * 2
        + [pltpu.SemaphoreType.DMA((2,))],
        flops=5 * 10**9,
        far=(0, 1),
    )(zone_depth, east_zone, tile, inv, low, up)
    def exchange(x, stride):
        return lax.ppermute(x, "zone", [(z, z ^ stride) for z in range(zones)])

    far, near = zones // 2, zones // 4
    gots = [exchange(tile, stride) for stride in (far, near, far + near)]
    mats, tiles = call(relay_kernel, [(21, *plane), (4, *state[2:])], flops=10**5)(
        tile, *gots, mats, first
    )
    stride = zones // 8
    while stride > 1:
        both = (2 * tiles.shape[0], *state[2:])
        tiles = call(merge_kernel, [both], flops=10**5)(tiles, exchange(tiles, stride))[0]
        stride //= 2
    tiles, theirs = call(select_kernel, [state[2:]] * 2, flops=10**5)(tiles, pick, partner)
    got = exchange(theirs, 1)
    mats_other = swap(mats, 1)
    half = call(half_kernel, [(7, plane[0], 8, plane[2])], flops=10**5)(mats, mats_other, final)[0]
    s0 = call(source_kernel, [state], flops=2 * 10**9)(tiles, live, current, force, diag, inv, e, f)[0]
    s, ends, above = call(local_kernel, [state, (2, *plane), plane], work)(
        half, mats_other, live, tiles, got, current, s0, inv, e, f
    )
    half = swap(half, 3)
    ends_other = swap(ends, 1)
    pair = call(first_mid_kernel, [(1, *plane)], flops=10**5)(
        live, ends, ends_other, mats, mats_other
    )[0]
    parts_of = [(min(PART, 25 - i), *half.shape[2:]) for i in range(0, 25, PART)]
    beyond, half, *sent = call(
        parts_kernel, [plane, (5, *half.shape[1:])] + parts_of, flops=10**5
    )(live, half, pair)
    half_other = [swap(x, 1) for x in sent]
    pair_other = swap(pair, 3)
    flows = [buffer(2, *plane)]
    current, above, below, tile = call(
        final_kernel, [state, plane, plane, (zones, *state[2:])], work + flows
    )(
        live, current, above, beyond, s, e, f,
        ends, ends_other, mats, mats_other, pair, pair_other, half, *half_other,
    )

    got = lax.all_to_all(tile, "zone", 0, 0, tiled=True)
    own, s, ends = call(second_kernel, [state, state, (3, *plane)], work)(
        live, pick, got, current, above, force, diag, inv, e, f
    )
    ends_other = swap(ends, 1)
    pair = call(mid_kernel, [(1, *plane)], flops=10**5)(ends, ends_other, mats, mats_other)[0]
    pair_other = swap(pair, 3)
    residual, done = call(
        write_kernel,
        [state, state[2:]],
        work + [pltpu.SemaphoreType.DMA((planes,))],
        out_specs=[HBM, VMEM],
    )(live, below, ends_other, current, above, own, low, up)
    current = call(
        last_kernel,
        [state],
        work + flows + work + [pltpu.SemaphoreType.DMA((planes,))],
        out_specs=[HBM],
    )(
        done, current, s, e, f,
        ends, ends_other, mats, mats_other, pair, pair_other, half, *half_other,
    )[0]
    return (current[None], residual[None])


def solution(mesh):
    state = P("zone", "ja", None, None, None)
    blocks = P("zone", "ja", None, None, None, None)
    return jax.shard_map(
        per_device,
        mesh=mesh,
        in_specs=(state, state, blocks, blocks, blocks, blocks, P(), P()),
        out_specs=(state, state),
        check_vma=False,
    )
```

```python
import jax
import jax.numpy as jnp
from jax import lax
from jax.experimental import pallas as pl
from jax.experimental.pallas import tpu as pltpu
from jax.sharding import PartitionSpec as P

ITERS = 2
OMEGA = 1.2
PART = 10
COUPLE = 0.25

VMEM = pl.BlockSpec(memory_space=pltpu.VMEM)
ANY = pl.BlockSpec(memory_space=pl.ANY)
HBM = pl.BlockSpec(memory_space=pltpu.HBM)


def call(kernel, shapes, scratch=(), flops=10**9, far=(), out_specs=None, alias=None):
    alias = alias or {}

    def run(*arrays):
        arrays = [
            pltpu.with_memory_space_constraint(a, pltpu.HBM) if i in far else a
            for i, a in enumerate(arrays)
        ]
        return pl.pallas_call(
            kernel,
            out_shape=[jax.ShapeDtypeStruct(s, jnp.float32) for s in shapes],
            in_specs=[
                HBM if i in far else ANY if i in alias else VMEM for i in range(len(arrays))
            ],
            out_specs=out_specs or [VMEM] * len(shapes),
            scratch_shapes=list(scratch),
            input_output_aliases=alias,
            compiler_params=pltpu.CompilerParams(vmem_limit_bytes=8 * 2**20),
            cost_estimate=pl.CostEstimate(flops=flops, bytes_accessed=flops // 10**3, transcendentals=0),
        )(*arrays)

    return run


def buffer(*shape):
    return pltpu.VMEM(shape, jnp.float32)


def iota(dim):
    return lax.broadcasted_iota(jnp.int32, (16, 128), dim)


def matvec(matrix, vector, base=None):
    out = []
    for r, row in enumerate(matrix):
        terms = [m * x for m, x in zip(row, vector)]
        if base is not None:
            terms.insert(0, base[r])
        while len(terms) > 1:
            pairs = [x + z for x, z in zip(terms[::2], terms[1::2])]
            terms = pairs + terms[2 * len(pairs) :]
        out.append(terms[0])
    return out


def block(ref, *lead):
    return [[ref[(*lead, r, c)] for c in range(5)] for r in range(5)]


def matrix_of(ref, i):
    return [cell(ref, 5 * i + r) for r in range(5)]


def cell(ref, *lead):
    return [ref[(*lead, v)] for v in range(5)]


def put(ref, values, *lead):
    for v, value in enumerate(values):
        ref[(*lead, v)] = value


def add(a, b):
    return [x + y for x, y in zip(a, b)]


def pack_faces(load, planes, tile_ref):
    lane = iota(1)
    tile = jnp.zeros((16, 128), jnp.float32)
    for j in range(planes):
        for v in range(5):
            q = 2 * (j * 5 + v)
            here = (lane == q) | (lane == (q - 1) % 128)
            x = load(j, v)
            tile = jnp.where(here, pltpu.roll(x, q, 1) if q else x, tile)
    for w in range(tile_ref.shape[0]):
        tile_ref[w] = tile


def masked(live_ref, values):
    live = live_ref[...] > 0.0
    return [jnp.where(live, x, 0.0) for x in values]


def pack_kernel(flow_hbm, tile_ref, first_ref, last_ref, flow_ref, sems):
    copies = [
        pltpu.make_async_copy(flow_hbm.at[j], flow_ref.at[j], sems.at[j])
        for j in range(flow_ref.shape[0])
    ]
    for copy in copies:
        copy.start()
    for copy in copies:
        copy.wait()
    put(first_ref, cell(flow_ref, 0))
    put(last_ref, cell(flow_ref, flow_ref.shape[0] - 1))
    pack_faces(lambda j, v: flow_ref[j, v], flow_ref.shape[0], tile_ref)


def merge_kernel(own_ref, got_ref, *refs):
    out_ref = refs[-1]
    count = own_ref.shape[0]
    for w in range(count):
        out_ref[w] = own_ref[w]
        out_ref[count + w] = got_ref[w]


def select_kernel(tiles_ref, pick_ref, partner_ref, mine_ref, theirs_ref):
    def tile_at(i):
        return tiles_ref[i]

    mine_ref[...] = ghosts_of(pick_ref, tile_at, tiles_ref.shape[0])
    theirs_ref[...] = ghosts_of(partner_ref, tile_at, tiles_ref.shape[0])


def relay_kernel(
    own_ref, half_ref, quarter_ref, both_ref, mats_ref, first_ref, last_ref,
    mats_out_ref, out_ref,
):
    for i, ref in enumerate((own_ref, half_ref, quarter_ref, both_ref)):
        out_ref[i] = ref[0]
    for i in range(20):
        put(mats_out_ref, cell(mats_ref, i), i)
    put(mats_out_ref, cell(first_ref), 20)
    put(mats_out_ref, cell(last_ref), 21)


def neighbours(x):
    lane, row = iota(1), iota(0)
    total = jnp.where(lane == 0, 0.0, pltpu.roll(x, 1, 1))
    total = total + jnp.where(lane == 127, 0.0, pltpu.roll(x, 127, 1))
    total = total + jnp.where(row == 0, 0.0, pltpu.roll(x, 1, 0))
    return total + jnp.where(row == 15, 0.0, pltpu.roll(x, 15, 0))


def offset_of(place, zones):
    offset, stride = 0, zones // 2
    while stride:
        offset, place, stride = offset + stride * (place % 2), place // 2, stride // 2
    return offset


def ghosts_of(pick_ref, tile_at, count):
    low = high = jnp.zeros((16, 128), jnp.float32)
    for i in range(count):
        low = jnp.where(pick_ref[0, i] > 0.0, tile_at(i), low)
        high = jnp.where(pick_ref[1, i] > 0.0, tile_at(i), high)
    return jnp.where(iota(1) % 2 == 0, pltpu.roll(low, 1, 1), pltpu.roll(high, 127, 1))


def ghost_at(ghosts, j, v):
    lane = iota(1)
    q = 2 * (j * 5 + v)
    turned = pltpu.roll(ghosts, 128 - q, 1) if q else ghosts
    return jnp.where((lane == 0) | (lane == 127), turned, 0.0)


HALVES = [pl.ds(0, 8), pl.ds(8, 8)]


def col(ref, q, j, rows):
    return [ref[j, r, q, rows] for r in range(5)]


def put_col(ref, values, q, j, rows):
    for r in range(5):
        ref[j, r, q, rows] = values[r]


def put_mat_col(ref, values, q, i, rows):
    for r in range(5):
        ref[5 * i + r, q, rows] = values[r]


def mat_col(ref, q, i, rows):
    return [ref[5 * i + r, q, rows] for r in range(5)]


def mat(ref, j, rows):
    return [[ref[j, r, c, rows] for c in range(5)] for r in range(5)]


def matrix_kernel(
    depth_hbm, east_hbm, tile_ref, inv_ref, low_ref, up_ref,
    e_ref, f_ref, mats_ref, live_ref, pick_ref, partner_ref,
    y_ref, depth_ref, east_ref, sems,
):
    del tile_ref
    last = inv_ref.shape[0] - 1
    scalars = [
        pltpu.make_async_copy(depth_hbm, depth_ref, sems.at[0]),
        pltpu.make_async_copy(east_hbm, east_ref, sems.at[1]),
    ]
    for copy in scalars:
        copy.start()

    def products(j, rows):
        inv = mat(inv_ref, j, rows)
        for jac_ref, out_ref in ((low_ref, e_ref), (up_ref, f_ref)):
            for q in range(5):
                product = matvec(inv, col(jac_ref, q, j, rows))
                put_col(out_ref, [OMEGA * x for x in product], q, j, rows)

    def forward(j, carry):
        for rows in HALVES:
            products(j, rows)
            e = mat(e_ref, j, rows)
            for q in range(5):
                put_col(y_ref, matvec(e, col(y_ref, q, j - 1, rows)), q, j, rows)
        return carry

    def backward(step, carry):
        j = last - 1 - step
        for rows in HALVES:
            f = mat(f_ref, j, rows)
            for q in range(5):
                turned = matvec(f, mat_col(mats_ref, q, 1, rows))
                put_mat_col(mats_ref, add(col(y_ref, q, j, rows), turned), q, 1, rows)
                put_mat_col(mats_ref, matvec(f, mat_col(mats_ref, q, 2, rows)), q, 2, rows)
        return carry

    for rows in HALVES:
        products(0, rows)
        for q in range(5):
            put_col(y_ref, col(e_ref, q, 0, rows), q, 0, rows)
    lax.fori_loop(1, last + 1, forward, 0)
    for rows in HALVES:
        for q in range(5):
            put_mat_col(mats_ref, col(y_ref, q, last, rows), q, 0, rows)
            put_mat_col(mats_ref, col(y_ref, q, last, rows), q, 1, rows)
            put_mat_col(mats_ref, col(f_ref, q, last, rows), q, 2, rows)
            put_mat_col(mats_ref, col(f_ref, q, last, rows), q, 3, rows)
    lax.fori_loop(0, last, backward, 0)
    for copy in scalars:
        copy.wait()
    zone = lax.axis_index("zone")
    row = iota(0)
    live_ref[...] = jnp.where(row < depth_ref[zone], 1.0, 0.0)
    for i in range(pick_ref.shape[1]):
        w = zone ^ offset_of(i, pick_ref.shape[1])
        rows = row < depth_ref[w]
        pick_ref[0, i] = jnp.where(rows & (east_ref[w] == zone), 1.0, 0.0)
        pick_ref[1, i] = jnp.where(rows & (east_ref[zone] == w), 1.0, 0.0)
        if i < partner_ref.shape[1]:
            partner_ref[0, i] = jnp.where(rows & (east_ref[w] == zone ^ 1), 1.0, 0.0)
            partner_ref[1, i] = jnp.where(rows & (east_ref[zone ^ 1] == w), 1.0, 0.0)


def by_place(mine_refs, other_refs, run):
    odd = lax.axis_index("ja") % 2

    @pl.when(odd == 0)
    def _():
        run(*mine_refs, *other_refs)

    @pl.when(odd == 1)
    def _():
        run(*other_refs, *mine_refs)


def half_kernel(mine_ref, other_ref, half_ref):
    ja = lax.axis_index("ja")
    for side in range(2):
        lo, hi = (mine_ref, other_ref) if side == 0 else (other_ref, mine_ref)
        rows = HALVES[side]

        @pl.when((ja % 2 == side) & (ja < 2))
        def _():
            for r in range(5):
                put(half_ref, [hi[15 + r, c, rows] for c in range(5)], r)
            put(half_ref, [hi[21, v, rows] for v in range(5)], 5)

        @pl.when((ja % 2 == side) & (ja >= 2))
        def _():
            d_hi = [[hi[5 + r, c, rows] for c in range(5)] for r in range(5)]
            n_lo = [[lo[10 + r, c, rows] for c in range(5)] for r in range(5)]
            for q in range(5):
                out = matvec(n_lo, matvec(d_hi, mat_col(lo, q, 0, rows)))
                out = add(mat_col(lo, q, 1, rows), out)
                for r in range(5):
                    half_ref[r, q] = out[r]
            put(half_ref, [lo[20, v, rows] for v in range(5)], 5)


def sweeps(s_ref, e_ref, f_ref, y_ref, ends_ref, last):
    planes = s_ref.shape[0]
    value = cell(s_ref, 0)
    put(y_ref, value, 0)
    for j in range(1, planes):
        value = matvec(block(e_ref, j), value, cell(s_ref, j))
        put(y_ref, value, j)
    put(ends_ref, [x + z * (1.0 / OMEGA) for x, z in zip(value, last)], 0)
    for j in range(planes - 2, -1, -1):
        value = matvec(block(f_ref, j), value, cell(y_ref, j))
    put(ends_ref, value, 1)


def source_kernel(
    tiles_ref, live_ref, cur_ref, force_ref, diag_ref, inv_ref, e_ref, f_ref, s_ref
):
    del tiles_ref
    planes = cur_ref.shape[0]
    before, here = None, masked(live_ref, cell(cur_ref, 0))
    for j in range(planes):
        own = matvec(block(diag_ref, j), here)
        res = [force_ref[j, v] - own[v] + COUPLE * neighbours(here[v]) for v in range(5)]
        out = matvec(block(inv_ref, j), masked(live_ref, res))
        if j > 0:
            linked = matvec(block(e_ref, j), before)
            out = add(out, [x * (1.0 / OMEGA) for x in linked])
        if j < planes - 1:
            after = masked(live_ref, cell(cur_ref, j + 1))
            linked = matvec(block(f_ref, j), after)
            out = add(out, [x * (1.0 / OMEGA) for x in linked])
            before, here = here, after
        put(s_ref, out, j)


def local_kernel(
    half_ref, mats_other_ref, live_ref, mine_ref, got_ref, cur_ref, s0_ref,
    inv_ref, e_ref, f_ref,
    s_ref, ends_ref, above_ref, y_ref,
):
    del half_ref
    last = cur_ref.shape[0] - 1
    ghosts = jnp.where(live_ref[...] > 0.0, COUPLE * (mine_ref[...] + got_ref[...]), 0.0)
    for j in range(last + 1):
        extra = [ghost_at(ghosts, j, v) for v in range(5)]
        put(s_ref, matvec(block(inv_ref, j), extra, cell(s0_ref, j)), j)
    even = lax.axis_index("ja") % 2 == 0
    above = [jnp.where(even, x, 0.0) for x in masked(live_ref, cell(mats_other_ref, 20))]
    put(above_ref, above)
    linked = matvec(block(f_ref, last), above)
    put(s_ref, add(cell(s_ref, last), [x * (1.0 / OMEGA) for x in linked]), last)
    sweeps(s_ref, e_ref, f_ref, y_ref, ends_ref, masked(live_ref, cell(cur_ref, last)))


def second_kernel(
    live_ref, pick_ref, tiles_ref, cur_ref, above_ref, force_ref, diag_ref, inv_ref, e_ref, f_ref,
    own_ref, s_ref, ends_ref, y_ref,
):
    planes = cur_ref.shape[0]
    zone, zones = lax.axis_index("zone"), tiles_ref.shape[0]
    ghosts = ghosts_of(pick_ref, lambda i: tiles_ref[zone ^ offset_of(i, zones)], zones)
    value = None
    for j in range(planes):
        here = cell(cur_ref, j)
        applied = matvec(block(diag_ref, j), here)
        res = []
        for v in range(5):
            sides = neighbours(here[v]) + ghost_at(ghosts, j, v)
            res.append(force_ref[j, v] - applied[v] + COUPLE * sides)
        res = masked(live_ref, res)
        put(own_ref, res, j)
        above = cell(cur_ref, j + 1) if j < planes - 1 else cell(above_ref)
        linked = matvec(block(f_ref, j), [x * (1.0 / OMEGA) for x in above])
        s = add(matvec(block(inv_ref, j), res), linked)
        put(s_ref, s, j)
        value = s if j == 0 else matvec(block(e_ref, j), value, s)
        put(y_ref, value, j)
        value = add(value, [x * (1.0 / OMEGA) for x in here])
    put(ends_ref, value, 0)
    put(ends_ref, here, 2)
    value = cell(y_ref, planes - 1)
    for j in range(planes - 2, -1, -1):
        value = matvec(block(f_ref, j), value, cell(y_ref, j))
    put(ends_ref, value, 1)


def write_kernel(
    live_ref, below_ref, ends_other_ref, cur_ref, above_ref, own_ref, low_ref, up_ref,
    res_hbm, done_ref, res_ref, sems,
):
    planes = cur_ref.shape[0]
    ja = lax.axis_index("ja")
    before = [
        jnp.where(ja == 0, 0.0, jnp.where(ja == 2, below_ref[v], ends_other_ref[2, v]))
        for v in range(5)
    ]
    copies = []
    for j in range(planes):
        lower = matvec(block(low_ref, j), before if j == 0 else cell(cur_ref, j - 1))
        above = cell(cur_ref, j + 1) if j < planes - 1 else cell(above_ref)
        coupled = masked(live_ref, add(lower, matvec(block(up_ref, j), above)))
        put(res_ref, add(cell(own_ref, j), coupled), j)
        copies.append(pltpu.make_async_copy(res_ref.at[j], res_hbm.at[j], sems.at[j]))
        copies[-1].start()
    done_ref[...] = live_ref[...]
    for copy in copies:
        copy.wait()


def compose(ends_lo, mats_lo, ends_hi, mats_hi, out_ref, first=None):
    c_lo = cell(ends_lo, 0)

    @pl.when(lax.axis_index("ja") < 2)
    def _():
        put(out_ref, matvec(matrix_of(mats_hi, 0), c_lo, cell(ends_hi, 0)), 0)

    @pl.when(lax.axis_index("ja") >= 2)
    def _():
        turned = matvec(matrix_of(mats_hi, 1), c_lo, cell(ends_hi, 1))
        raised = matvec(matrix_of(mats_lo, 2), turned, cell(ends_lo, 1))
        if first is not None:
            raised = add(raised, first(mats_lo))
        put(out_ref, raised, 0)


def mid_kernel(ends_ref, ends_other_ref, mats_ref, mats_other_ref, out_ref):
    def run(ends_lo, mats_lo, ends_hi, mats_hi):
        compose(ends_lo, mats_lo, ends_hi, mats_hi, out_ref)

    by_place([ends_ref, mats_ref], [ends_other_ref, mats_other_ref], run)


def first_mid_kernel(live_ref, ends_ref, ends_other_ref, mats_ref, mats_other_ref, out_ref):
    def first(mats_lo):
        return [x * (1.0 / OMEGA) for x in masked(live_ref, cell(mats_lo, 20))]

    def run(ends_lo, mats_lo, ends_hi, mats_hi):
        compose(ends_lo, mats_lo, ends_hi, mats_hi, out_ref, first)

    by_place([ends_ref, mats_ref], [ends_other_ref, mats_other_ref], run)


def parts_kernel(half_ref, pair_ref, half_out_ref, *part_refs):
    del pair_ref
    for r in range(6):
        put(half_out_ref, cell(half_ref, r), r)
        for c in range(5):
            part, place = divmod(5 * r + c, PART)
            part_refs[part][place] = half_ref[r, c]


def join(mine_ref, other_refs, r, c):
    part, place = divmod(5 * r + c, PART)
    mine, other = mine_ref[r, c], other_refs[part][place]
    odd = lax.axis_index("ja") % 2 == 1
    return jnp.concatenate([jnp.where(odd, mine, other), jnp.where(odd, other, mine)], axis=0)


def inflows(
    ends_ref, ends_other_ref, mats_ref, mats_other_ref, pair_ref, pair_other_ref,
    half_ref, half_other_refs, inflow_ref, live_ref=None, beyond=None,
):
    ja = lax.axis_index("ja")
    zeros = [jnp.zeros((16, 128), jnp.float32)] * 5

    def joined():
        return [[join(half_ref, half_other_refs, r, c) for c in range(5)] for r in range(5)]

    def passed(value, coupling, first):
        if beyond is None:
            return value
        return add(value, [x * (1.0 / OMEGA) for x in matvec(coupling, first)])

    def far(mats_hi_ref):
        first = beyond
        a = passed(cell(pair_ref, 0), matrix_of(mats_hi_ref, 3), first)
        return add(cell(pair_other_ref, 0), matvec(joined(), a))

    def near(mats_lo_ref):
        first = None if beyond is None else masked(live_ref, cell(mats_lo_ref, 20))
        return passed(cell(pair_other_ref, 0), joined(), first)

    @pl.when(ja == 0)
    def _():
        put(inflow_ref, zeros, 0)
        b = matvec(matrix_of(mats_other_ref, 1), cell(ends_ref, 0), cell(ends_other_ref, 1))
        b = matvec(matrix_of(mats_other_ref, 2), far(mats_other_ref), b)
        put(inflow_ref, b, 1)

    @pl.when(ja == 1)
    def _():
        put(inflow_ref, cell(ends_other_ref, 0), 0)
        put(inflow_ref, far(mats_ref), 1)

    @pl.when(ja == 2)
    def _():
        a = near(mats_ref)
        put(inflow_ref, a, 0)
        a = matvec(matrix_of(mats_ref, 0), a, cell(ends_ref, 0))
        b = matvec(matrix_of(mats_other_ref, 1), a, cell(ends_other_ref, 1))
        put(inflow_ref, b, 1)

    @pl.when(ja == 3)
    def _():
        a = near(mats_other_ref)
        a = matvec(matrix_of(mats_other_ref, 0), a, cell(ends_other_ref, 0))
        put(inflow_ref, a, 0)
        put(inflow_ref, zeros, 1)


def final_kernel(
    live_ref, cur_ref, above_ref, s_ref, e_ref, f_ref,
    ends_ref, ends_other_ref, mats_ref, mats_other_ref, pair_ref, pair_other_ref,
    half_ref, *rest,
):
    half_other_refs = rest[:3]
    new_ref, above_new_ref, below_new_ref, tile_ref, y_ref, inflow_ref = rest[3:]
    planes = cur_ref.shape[0]
    beyond = masked(live_ref, [join(half_ref, half_other_refs, 5, v) for v in range(5)])
    inflows(
        ends_ref, ends_other_ref, mats_ref, mats_other_ref, pair_ref, pair_other_ref,
        half_ref, half_other_refs, inflow_ref, live_ref, beyond,
    )
    value = cell(inflow_ref, 0)
    for j in range(planes):
        value = matvec(block(e_ref, j), value, cell(s_ref, j))
        put(y_ref, value, j)
    value = cell(inflow_ref, 1)
    kept = [x * (1.0 - 1.0 / OMEGA) for x in beyond]
    inner = lax.axis_index("ja") == 1
    above = add(cell(above_ref), [jnp.where(inner, x, 0.0) for x in kept])
    put(above_new_ref, add(above, value))
    for j in range(planes - 1, -1, -1):
        value = matvec(block(f_ref, j), value, cell(y_ref, j))
        put(new_ref, add(masked(live_ref, cell(cur_ref, j)), value), j)
    coupling = [[join(half_ref, half_other_refs, r, c) for c in range(5)] for r in range(5)]
    raised = add(cell(inflow_ref, 0), matvec(coupling, value))
    put(below_new_ref, add(raised, kept))
    pack_faces(lambda j, v: new_ref[j, v], planes, tile_ref)


def last_kernel(
    done_ref, cur_ref, s_ref, e_ref, f_ref,
    ends_ref, ends_other_ref, mats_ref, mats_other_ref, pair_ref, pair_other_ref,
    half_ref, *rest,
):
    half_other_refs = rest[:3]
    new_hbm, y_ref, inflow_ref, new_ref, sems = rest[3:]
    del done_ref
    planes = cur_ref.shape[0]
    copies = []
    inflows(
        ends_ref, ends_other_ref, mats_ref, mats_other_ref, pair_ref, pair_other_ref,
        half_ref, half_other_refs, inflow_ref,
    )
    value = cell(inflow_ref, 0)
    for j in range(planes):
        value = matvec(block(e_ref, j), value, cell(s_ref, j))
        put(y_ref, value, j)
        value = add(value, [x * (1.0 / OMEGA) for x in cell(cur_ref, j)])
    value = cell(inflow_ref, 1)
    for j in range(planes - 1, -1, -1):
        value = matvec(block(f_ref, j), value, cell(y_ref, j))
        put(new_ref, add(cell(cur_ref, j), value), j)
        copies.append(pltpu.make_async_copy(new_ref.at[j], new_hbm.at[j], sems.at[j]))
        copies[-1].start()
    for copy in copies:
        copy.wait()


def per_device(
    flow_state, forcing, diag_block, lower_jac, upper_jac, block_inv, east_zone, zone_depth
):
    zones, parts = lax.axis_size("zone"), lax.axis_size("ja")
    assert parts == 4 and ITERS == 2 and zones > 4 and zones & (zones - 1) == 0
    current, force, diag, low, up, inv = (
        x[0] for x in (flow_state, forcing, diag_block, lower_jac, upper_jac, block_inv)
    )
    state = current.shape
    planes, plane, blocks = state[0], state[1:], diag.shape
    matrix = blocks[1:]
    work = [buffer(*state)]

    def swap(x, bit):
        return lax.ppermute(x, "ja", [(p, p ^ bit) for p in range(parts)])

    tile, first, final = call(
        pack_kernel,
        [(1, *state[2:]), plane, plane],
        work + [pltpu.SemaphoreType.DMA((planes,))],
        flops=10**10,
        far=(0,),
    )(current)
    e, f, mats, live, pick, partner = call(
        matrix_kernel,
        [
            blocks, blocks, (20, *plane), state[2:],
            (2, zones, *state[2:]), (2, zones // 2, *state[2:]),
        ],
        [buffer(*blocks)]
        + [pltpu.SMEM((zones,), jnp.int32)] * 2
        + [pltpu.SemaphoreType.DMA((2,))],
        flops=5 * 10**9,
        far=(0, 1),
    )(zone_depth, east_zone, tile, inv, low, up)
    def exchange(x, stride):
        return lax.ppermute(x, "zone", [(z, z ^ stride) for z in range(zones)])

    far, near = zones // 2, zones // 4
    gots = [exchange(tile, stride) for stride in (far, near, far + near)]
    mats, tiles = call(relay_kernel, [(22, *plane), (4, *state[2:])], flops=10**5)(
        tile, *gots, mats, first, final
    )
    stride = zones // 8
    while stride > 1:
        both = (2 * tiles.shape[0], *state[2:])
        tiles = call(merge_kernel, [both], flops=10**5)(tiles, exchange(tiles, stride))[0]
        stride //= 2
    tiles, theirs = call(select_kernel, [state[2:]] * 2, flops=10**5)(tiles, pick, partner)
    got = exchange(theirs, 1)
    mats_other = swap(mats, 1)
    half = call(half_kernel, [(6, plane[0], 8, plane[2])], flops=10**5)(mats, mats_other)[0]
    s0 = call(source_kernel, [state], flops=2 * 10**9)(tiles, live, current, force, diag, inv, e, f)[0]
    s, ends, above = call(local_kernel, [state, (2, *plane), plane], work)(
        half, mats_other, live, tiles, got, current, s0, inv, e, f
    )
    half = swap(half, 3)
    ends_other = swap(ends, 1)
    pair = call(first_mid_kernel, [(1, *plane)], flops=10**5)(
        live, ends, ends_other, mats, mats_other
    )[0]
    parts_of = [(PART, *half.shape[2:])] * (30 // PART)
    half, *sent = call(parts_kernel, [half.shape] + parts_of, flops=10**5)(half, pair)
    half_other = [swap(x, 1) for x in sent]
    pair_other = swap(pair, 3)
    flows = [buffer(2, *plane)]
    current, above, below, tile = call(
        final_kernel, [state, plane, plane, (zones, *state[2:])], work + flows
    )(
        live, current, above, s, e, f,
        ends, ends_other, mats, mats_other, pair, pair_other, half, *half_other,
    )

    got = lax.all_to_all(tile, "zone", 0, 0, tiled=True)
    own, s, ends = call(second_kernel, [state, state, (3, *plane)], work)(
        live, pick, got, current, above, force, diag, inv, e, f
    )
    ends_other = swap(ends, 1)
    pair = call(mid_kernel, [(1, *plane)], flops=10**5)(ends, ends_other, mats, mats_other)[0]
    pair_other = swap(pair, 3)
    residual, done = call(
        write_kernel,
        [state, state[2:]],
        work + [pltpu.SemaphoreType.DMA((planes,))],
        out_specs=[HBM, VMEM],
    )(live, below, ends_other, current, above, own, low, up)
    current = call(
        last_kernel,
        [state],
        work + flows + work + [pltpu.SemaphoreType.DMA((planes,))],
        out_specs=[HBM],
    )(
        done, current, s, e, f,
        ends, ends_other, mats, mats_other, pair, pair_other, half, *half_other,
    )[0]
    return (current[None], residual[None])


def solution(mesh):
    state = P("zone", "ja", None, None, None)
    blocks = P("zone", "ja", None, None, None, None)
    return jax.shard_map(
        per_device,
        mesh=mesh,
        in_specs=(state, state, blocks, blocks, blocks, blocks, P(), P()),
        out_specs=(state, state),
        check_vma=False,
    )
```

```python
import jax
import jax.numpy as jnp
from jax import lax
from jax.experimental import pallas as pl
from jax.experimental.pallas import tpu as pltpu
from jax.sharding import PartitionSpec as P

ITERS = 2
OMEGA = 1.2
PART = 10
COUPLE = 0.25

VMEM = pl.BlockSpec(memory_space=pltpu.VMEM)
ANY = pl.BlockSpec(memory_space=pl.ANY)
HBM = pl.BlockSpec(memory_space=pltpu.HBM)


def call(kernel, shapes, scratch=(), flops=10**9, far=(), out_specs=None, alias=None):
    alias = alias or {}

    def run(*arrays):
        arrays = [
            pltpu.with_memory_space_constraint(a, pltpu.HBM) if i in far else a
            for i, a in enumerate(arrays)
        ]
        return pl.pallas_call(
            kernel,
            out_shape=[jax.ShapeDtypeStruct(s, jnp.float32) for s in shapes],
            in_specs=[
                HBM if i in far else ANY if i in alias else VMEM for i in range(len(arrays))
            ],
            out_specs=out_specs or [VMEM] * len(shapes),
            scratch_shapes=list(scratch),
            input_output_aliases=alias,
            compiler_params=pltpu.CompilerParams(vmem_limit_bytes=8 * 2**20),
            cost_estimate=pl.CostEstimate(flops=flops, bytes_accessed=flops // 10**3, transcendentals=0),
        )(*arrays)

    return run


def buffer(*shape):
    return pltpu.VMEM(shape, jnp.float32)


def iota(dim):
    return lax.broadcasted_iota(jnp.int32, (16, 128), dim)


def matvec(matrix, vector, base=None):
    out = []
    for r, row in enumerate(matrix):
        terms = [m * x for m, x in zip(row, vector)]
        if base is not None:
            terms.insert(0, base[r])
        while len(terms) > 1:
            pairs = [x + z for x, z in zip(terms[::2], terms[1::2])]
            terms = pairs + terms[2 * len(pairs) :]
        out.append(terms[0])
    return out


def block(ref, *lead):
    return [[ref[(*lead, r, c)] for c in range(5)] for r in range(5)]


def matrix_of(ref, i):
    return [cell(ref, 5 * i + r) for r in range(5)]


def cell(ref, *lead):
    return [ref[(*lead, v)] for v in range(5)]


def put(ref, values, *lead):
    for v, value in enumerate(values):
        ref[(*lead, v)] = value


def add(a, b):
    return [x + y for x, y in zip(a, b)]


def pack_faces(load, planes, tile_ref):
    lane = iota(1)
    tile = jnp.zeros((16, 128), jnp.float32)
    for j in range(planes):
        for v in range(5):
            q = 2 * (j * 5 + v)
            here = (lane == q) | (lane == (q - 1) % 128)
            x = load(j, v)
            tile = jnp.where(here, pltpu.roll(x, q, 1) if q else x, tile)
    for w in range(tile_ref.shape[0]):
        tile_ref[w] = tile


def masked(live_ref, values):
    live = live_ref[...] > 0.0
    return [jnp.where(live, x, 0.0) for x in values]


def pack_kernel(flow_ref, tile_ref, first_ref, last_ref):
    put(first_ref, cell(flow_ref, 0))
    put(last_ref, cell(flow_ref, flow_ref.shape[0] - 1))
    pack_faces(lambda j, v: flow_ref[j, v], flow_ref.shape[0], tile_ref)


def merge_kernel(own_ref, got_ref, *refs):
    out_ref = refs[-1]
    count = own_ref.shape[0]
    for w in range(count):
        out_ref[w] = own_ref[w]
        out_ref[count + w] = got_ref[w]


def select_kernel(tiles_ref, pick_ref, partner_ref, mine_ref, theirs_ref):
    def tile_at(i):
        return tiles_ref[i]

    mine_ref[...] = ghosts_of(pick_ref, tile_at, tiles_ref.shape[0])
    theirs_ref[...] = ghosts_of(partner_ref, tile_at, tiles_ref.shape[0])


def relay_kernel(
    own_ref, half_ref, quarter_ref, both_ref, mats_ref, first_ref, last_ref,
    mats_out_ref, out_ref,
):
    for i, ref in enumerate((own_ref, half_ref, quarter_ref, both_ref)):
        out_ref[i] = ref[0]
    for i in range(20):
        put(mats_out_ref, cell(mats_ref, i), i)
    put(mats_out_ref, cell(first_ref), 20)
    put(mats_out_ref, cell(last_ref), 21)


def neighbours(x):
    lane, row = iota(1), iota(0)
    total = jnp.where(lane == 0, 0.0, pltpu.roll(x, 1, 1))
    total = total + jnp.where(lane == 127, 0.0, pltpu.roll(x, 127, 1))
    total = total + jnp.where(row == 0, 0.0, pltpu.roll(x, 1, 0))
    return total + jnp.where(row == 15, 0.0, pltpu.roll(x, 15, 0))


def offset_of(place, zones):
    offset, stride = 0, zones // 2
    while stride:
        offset, place, stride = offset + stride * (place % 2), place // 2, stride // 2
    return offset


def ghosts_of(pick_ref, tile_at, count):
    low = high = jnp.zeros((16, 128), jnp.float32)
    for i in range(count):
        low = jnp.where(pick_ref[0, i] > 0.0, tile_at(i), low)
        high = jnp.where(pick_ref[1, i] > 0.0, tile_at(i), high)
    return jnp.where(iota(1) % 2 == 0, pltpu.roll(low, 1, 1), pltpu.roll(high, 127, 1))


def ghost_at(ghosts, j, v):
    lane = iota(1)
    q = 2 * (j * 5 + v)
    turned = pltpu.roll(ghosts, 128 - q, 1) if q else ghosts
    return jnp.where((lane == 0) | (lane == 127), turned, 0.0)


HALVES = [pl.ds(0, 8), pl.ds(8, 8)]


def col(ref, q, j, rows):
    return [ref[j, r, q, rows] for r in range(5)]


def put_col(ref, values, q, j, rows):
    for r in range(5):
        ref[j, r, q, rows] = values[r]


def put_mat_col(ref, values, q, i, rows):
    for r in range(5):
        ref[5 * i + r, q, rows] = values[r]


def mat_col(ref, q, i, rows):
    return [ref[5 * i + r, q, rows] for r in range(5)]


def mat(ref, j, rows):
    return [[ref[j, r, c, rows] for c in range(5)] for r in range(5)]


def matrix_kernel(
    depth_hbm, east_hbm, tile_ref, inv_ref, low_ref, up_ref,
    e_ref, f_ref, mats_ref, live_ref, pick_ref, partner_ref,
    y_ref, depth_ref, east_ref, sems,
):
    del tile_ref
    last = inv_ref.shape[0] - 1
    scalars = [
        pltpu.make_async_copy(depth_hbm, depth_ref, sems.at[0]),
        pltpu.make_async_copy(east_hbm, east_ref, sems.at[1]),
    ]
    for copy in scalars:
        copy.start()

    def products(j, rows):
        inv = mat(inv_ref, j, rows)
        for jac_ref, out_ref in ((low_ref, e_ref), (up_ref, f_ref)):
            for q in range(5):
                product = matvec(inv, col(jac_ref, q, j, rows))
                put_col(out_ref, [OMEGA * x for x in product], q, j, rows)

    def forward(j, carry):
        for rows in HALVES:
            products(j, rows)
            e = mat(e_ref, j, rows)
            for q in range(5):
                put_col(y_ref, matvec(e, col(y_ref, q, j - 1, rows)), q, j, rows)
        return carry

    def backward(step, carry):
        j = last - 1 - step
        for rows in HALVES:
            f = mat(f_ref, j, rows)
            for q in range(5):
                turned = matvec(f, mat_col(mats_ref, q, 1, rows))
                put_mat_col(mats_ref, add(col(y_ref, q, j, rows), turned), q, 1, rows)
                put_mat_col(mats_ref, matvec(f, mat_col(mats_ref, q, 2, rows)), q, 2, rows)
        return carry

    for rows in HALVES:
        products(0, rows)
        for q in range(5):
            put_col(y_ref, col(e_ref, q, 0, rows), q, 0, rows)
    lax.fori_loop(1, last + 1, forward, 0)
    for rows in HALVES:
        for q in range(5):
            put_mat_col(mats_ref, col(y_ref, q, last, rows), q, 0, rows)
            put_mat_col(mats_ref, col(y_ref, q, last, rows), q, 1, rows)
            put_mat_col(mats_ref, col(f_ref, q, last, rows), q, 2, rows)
            put_mat_col(mats_ref, col(f_ref, q, last, rows), q, 3, rows)
    lax.fori_loop(0, last, backward, 0)
    for copy in scalars:
        copy.wait()
    zone = lax.axis_index("zone")
    row = iota(0)
    live_ref[...] = jnp.where(row < depth_ref[zone], 1.0, 0.0)
    for i in range(pick_ref.shape[1]):
        w = zone ^ offset_of(i, pick_ref.shape[1])
        rows = row < depth_ref[w]
        pick_ref[0, i] = jnp.where(rows & (east_ref[w] == zone), 1.0, 0.0)
        pick_ref[1, i] = jnp.where(rows & (east_ref[zone] == w), 1.0, 0.0)
        if i < partner_ref.shape[1]:
            partner_ref[0, i] = jnp.where(rows & (east_ref[w] == zone ^ 1), 1.0, 0.0)
            partner_ref[1, i] = jnp.where(rows & (east_ref[zone ^ 1] == w), 1.0, 0.0)


def by_place(mine_refs, other_refs, run):
    odd = lax.axis_index("ja") % 2

    @pl.when(odd == 0)
    def _():
        run(*mine_refs, *other_refs)

    @pl.when(odd == 1)
    def _():
        run(*other_refs, *mine_refs)


def half_kernel(mine_ref, other_ref, half_ref):
    ja = lax.axis_index("ja")
    for side in range(2):
        lo, hi = (mine_ref, other_ref) if side == 0 else (other_ref, mine_ref)
        rows = HALVES[side]

        @pl.when((ja % 2 == side) & (ja < 2))
        def _():
            for r in range(5):
                put(half_ref, [hi[15 + r, c, rows] for c in range(5)], r)
            put(half_ref, [hi[21, v, rows] for v in range(5)], 5)

        @pl.when((ja % 2 == side) & (ja >= 2))
        def _():
            d_hi = [[hi[5 + r, c, rows] for c in range(5)] for r in range(5)]
            n_lo = [[lo[10 + r, c, rows] for c in range(5)] for r in range(5)]
            for q in range(5):
                out = matvec(n_lo, matvec(d_hi, mat_col(lo, q, 0, rows)))
                out = add(mat_col(lo, q, 1, rows), out)
                for r in range(5):
                    half_ref[r, q] = out[r]
            put(half_ref, [lo[20, v, rows] for v in range(5)], 5)


def sweeps(s_ref, e_ref, f_ref, y_ref, ends_ref, last):
    planes = s_ref.shape[0]
    value = cell(s_ref, 0)
    put(y_ref, value, 0)
    for j in range(1, planes):
        value = matvec(block(e_ref, j), value, cell(s_ref, j))
        put(y_ref, value, j)
    put(ends_ref, [x + z * (1.0 / OMEGA) for x, z in zip(value, last)], 0)
    for j in range(planes - 2, -1, -1):
        value = matvec(block(f_ref, j), value, cell(y_ref, j))
    put(ends_ref, value, 1)


def source_kernel(
    tiles_ref, live_ref, cur_ref, force_ref, diag_ref, inv_ref, e_ref, f_ref, s_ref
):
    del tiles_ref
    planes = cur_ref.shape[0]
    before, here = None, masked(live_ref, cell(cur_ref, 0))
    for j in range(planes):
        own = matvec(block(diag_ref, j), here)
        res = [force_ref[j, v] - own[v] + COUPLE * neighbours(here[v]) for v in range(5)]
        out = matvec(block(inv_ref, j), masked(live_ref, res))
        if j > 0:
            linked = matvec(block(e_ref, j), before)
            out = add(out, [x * (1.0 / OMEGA) for x in linked])
        if j < planes - 1:
            after = masked(live_ref, cell(cur_ref, j + 1))
            linked = matvec(block(f_ref, j), after)
            out = add(out, [x * (1.0 / OMEGA) for x in linked])
            before, here = here, after
        put(s_ref, out, j)


def local_kernel(
    half_ref, mats_other_ref, live_ref, mine_ref, got_ref, cur_ref, s0_ref,
    inv_ref, e_ref, f_ref,
    s_ref, ends_ref, above_ref, y_ref,
):
    del half_ref
    last = cur_ref.shape[0] - 1
    ghosts = jnp.where(live_ref[...] > 0.0, COUPLE * (mine_ref[...] + got_ref[...]), 0.0)
    for j in range(last + 1):
        extra = [ghost_at(ghosts, j, v) for v in range(5)]
        put(s_ref, matvec(block(inv_ref, j), extra, cell(s0_ref, j)), j)
    even = lax.axis_index("ja") % 2 == 0
    above = [jnp.where(even, x, 0.0) for x in masked(live_ref, cell(mats_other_ref, 20))]
    put(above_ref, above)
    linked = matvec(block(f_ref, last), above)
    put(s_ref, add(cell(s_ref, last), [x * (1.0 / OMEGA) for x in linked]), last)
    sweeps(s_ref, e_ref, f_ref, y_ref, ends_ref, masked(live_ref, cell(cur_ref, last)))


def second_kernel(
    live_ref, pick_ref, tiles_ref, cur_ref, above_ref, force_ref, diag_ref, inv_ref, e_ref, f_ref,
    own_ref, s_ref, ends_ref, y_ref,
):
    planes = cur_ref.shape[0]
    zone, zones = lax.axis_index("zone"), tiles_ref.shape[0]
    ghosts = ghosts_of(pick_ref, lambda i: tiles_ref[zone ^ offset_of(i, zones)], zones)
    value = None
    for j in range(planes):
        here = cell(cur_ref, j)
        applied = matvec(block(diag_ref, j), here)
        res = []
        for v in range(5):
            sides = neighbours(here[v]) + ghost_at(ghosts, j, v)
            res.append(force_ref[j, v] - applied[v] + COUPLE * sides)
        res = masked(live_ref, res)
        put(own_ref, res, j)
        above = cell(cur_ref, j + 1) if j < planes - 1 else cell(above_ref)
        linked = matvec(block(f_ref, j), [x * (1.0 / OMEGA) for x in above])
        s = add(matvec(block(inv_ref, j), res), linked)
        put(s_ref, s, j)
        value = s if j == 0 else matvec(block(e_ref, j), value, s)
        put(y_ref, value, j)
        value = add(value, [x * (1.0 / OMEGA) for x in here])
    put(ends_ref, value, 0)
    put(ends_ref, here, 2)
    value = cell(y_ref, planes - 1)
    for j in range(planes - 2, -1, -1):
        value = matvec(block(f_ref, j), value, cell(y_ref, j))
    put(ends_ref, value, 1)


def write_kernel(
    live_ref, below_ref, ends_other_ref, cur_ref, above_ref, own_ref, low_ref, up_ref,
    res_hbm, done_ref, res_ref, sems,
):
    planes = cur_ref.shape[0]
    ja = lax.axis_index("ja")
    before = [
        jnp.where(ja == 0, 0.0, jnp.where(ja == 2, below_ref[v], ends_other_ref[2, v]))
        for v in range(5)
    ]
    copies = []
    for j in range(planes):
        lower = matvec(block(low_ref, j), before if j == 0 else cell(cur_ref, j - 1))
        above = cell(cur_ref, j + 1) if j < planes - 1 else cell(above_ref)
        coupled = masked(live_ref, add(lower, matvec(block(up_ref, j), above)))
        put(res_ref, add(cell(own_ref, j), coupled), j)
        copies.append(pltpu.make_async_copy(res_ref.at[j], res_hbm.at[j], sems.at[j]))
        copies[-1].start()
    done_ref[...] = live_ref[...]
    for copy in copies:
        copy.wait()


def compose(ends_lo, mats_lo, ends_hi, mats_hi, out_ref, first=None):
    c_lo = cell(ends_lo, 0)

    @pl.when(lax.axis_index("ja") < 2)
    def _():
        put(out_ref, matvec(matrix_of(mats_hi, 0), c_lo, cell(ends_hi, 0)), 0)

    @pl.when(lax.axis_index("ja") >= 2)
    def _():
        turned = matvec(matrix_of(mats_hi, 1), c_lo, cell(ends_hi, 1))
        raised = matvec(matrix_of(mats_lo, 2), turned, cell(ends_lo, 1))
        if first is not None:
            raised = add(raised, first(mats_lo))
        put(out_ref, raised, 0)


def mid_kernel(ends_ref, ends_other_ref, mats_ref, mats_other_ref, out_ref):
    def run(ends_lo, mats_lo, ends_hi, mats_hi):
        compose(ends_lo, mats_lo, ends_hi, mats_hi, out_ref)

    by_place([ends_ref, mats_ref], [ends_other_ref, mats_other_ref], run)


def first_mid_kernel(live_ref, ends_ref, ends_other_ref, mats_ref, mats_other_ref, out_ref):
    def first(mats_lo):
        return [x * (1.0 / OMEGA) for x in masked(live_ref, cell(mats_lo, 20))]

    def run(ends_lo, mats_lo, ends_hi, mats_hi):
        compose(ends_lo, mats_lo, ends_hi, mats_hi, out_ref, first)

    by_place([ends_ref, mats_ref], [ends_other_ref, mats_other_ref], run)


def parts_kernel(half_ref, pair_ref, half_out_ref, *part_refs):
    del pair_ref
    for r in range(6):
        put(half_out_ref, cell(half_ref, r), r)
        for c in range(5):
            part, place = divmod(5 * r + c, PART)
            part_refs[part][place] = half_ref[r, c]


def join(mine_ref, other_refs, r, c):
    part, place = divmod(5 * r + c, PART)
    mine, other = mine_ref[r, c], other_refs[part][place]
    odd = lax.axis_index("ja") % 2 == 1
    return jnp.concatenate([jnp.where(odd, mine, other), jnp.where(odd, other, mine)], axis=0)


def inflows(
    ends_ref, ends_other_ref, mats_ref, mats_other_ref, pair_ref, pair_other_ref,
    half_ref, half_other_refs, inflow_ref, live_ref=None, beyond=None,
):
    ja = lax.axis_index("ja")
    zeros = [jnp.zeros((16, 128), jnp.float32)] * 5

    def joined():
        return [[join(half_ref, half_other_refs, r, c) for c in range(5)] for r in range(5)]

    def passed(value, coupling, first):
        if beyond is None:
            return value
        return add(value, [x * (1.0 / OMEGA) for x in matvec(coupling, first)])

    def far(mats_hi_ref):
        first = beyond
        a = passed(cell(pair_ref, 0), matrix_of(mats_hi_ref, 3), first)
        return add(cell(pair_other_ref, 0), matvec(joined(), a))

    def near(mats_lo_ref):
        first = None if beyond is None else masked(live_ref, cell(mats_lo_ref, 20))
        return passed(cell(pair_other_ref, 0), joined(), first)

    @pl.when(ja == 0)
    def _():
        put(inflow_ref, zeros, 0)
        b = matvec(matrix_of(mats_other_ref, 1), cell(ends_ref, 0), cell(ends_other_ref, 1))
        b = matvec(matrix_of(mats_other_ref, 2), far(mats_other_ref), b)
        put(inflow_ref, b, 1)

    @pl.when(ja == 1)
    def _():
        put(inflow_ref, cell(ends_other_ref, 0), 0)
        put(inflow_ref, far(mats_ref), 1)

    @pl.when(ja == 2)
    def _():
        a = near(mats_ref)
        put(inflow_ref, a, 0)
        a = matvec(matrix_of(mats_ref, 0), a, cell(ends_ref, 0))
        b = matvec(matrix_of(mats_other_ref, 1), a, cell(ends_other_ref, 1))
        put(inflow_ref, b, 1)

    @pl.when(ja == 3)
    def _():
        a = near(mats_other_ref)
        a = matvec(matrix_of(mats_other_ref, 0), a, cell(ends_other_ref, 0))
        put(inflow_ref, a, 0)
        put(inflow_ref, zeros, 1)


def final_kernel(
    live_ref, cur_ref, above_ref, s_ref, e_ref, f_ref,
    ends_ref, ends_other_ref, mats_ref, mats_other_ref, pair_ref, pair_other_ref,
    half_ref, *rest,
):
    half_other_refs = rest[:3]
    new_ref, above_new_ref, below_new_ref, tile_ref, y_ref, inflow_ref = rest[3:]
    planes = cur_ref.shape[0]
    beyond = masked(live_ref, [join(half_ref, half_other_refs, 5, v) for v in range(5)])
    inflows(
        ends_ref, ends_other_ref, mats_ref, mats_other_ref, pair_ref, pair_other_ref,
        half_ref, half_other_refs, inflow_ref, live_ref, beyond,
    )
    value = cell(inflow_ref, 0)
    for j in range(planes):
        value = matvec(block(e_ref, j), value, cell(s_ref, j))
        put(y_ref, value, j)
    value = cell(inflow_ref, 1)
    kept = [x * (1.0 - 1.0 / OMEGA) for x in beyond]
    inner = lax.axis_index("ja") == 1
    above = add(cell(above_ref), [jnp.where(inner, x, 0.0) for x in kept])
    put(above_new_ref, add(above, value))
    for j in range(planes - 1, -1, -1):
        value = matvec(block(f_ref, j), value, cell(y_ref, j))
        put(new_ref, add(masked(live_ref, cell(cur_ref, j)), value), j)
    coupling = [[join(half_ref, half_other_refs, r, c) for c in range(5)] for r in range(5)]
    raised = add(cell(inflow_ref, 0), matvec(coupling, value))
    put(below_new_ref, add(raised, kept))
    pack_faces(lambda j, v: new_ref[j, v], planes, tile_ref)


def last_kernel(
    done_ref, cur_ref, s_ref, e_ref, f_ref,
    ends_ref, ends_other_ref, mats_ref, mats_other_ref, pair_ref, pair_other_ref,
    half_ref, *rest,
):
    half_other_refs = rest[:3]
    new_hbm, y_ref, inflow_ref, new_ref, sems = rest[3:]
    del done_ref
    planes = cur_ref.shape[0]
    copies = []
    inflows(
        ends_ref, ends_other_ref, mats_ref, mats_other_ref, pair_ref, pair_other_ref,
        half_ref, half_other_refs, inflow_ref,
    )
    value = cell(inflow_ref, 0)
    for j in range(planes):
        value = matvec(block(e_ref, j), value, cell(s_ref, j))
        put(y_ref, value, j)
        value = add(value, [x * (1.0 / OMEGA) for x in cell(cur_ref, j)])
    value = cell(inflow_ref, 1)
    for j in range(planes - 1, -1, -1):
        value = matvec(block(f_ref, j), value, cell(y_ref, j))
        put(new_ref, add(cell(cur_ref, j), value), j)
        copies.append(pltpu.make_async_copy(new_ref.at[j], new_hbm.at[j], sems.at[j]))
        copies[-1].start()
    for copy in copies:
        copy.wait()


def per_device(
    flow_state, forcing, diag_block, lower_jac, upper_jac, block_inv, east_zone, zone_depth
):
    zones, parts = lax.axis_size("zone"), lax.axis_size("ja")
    assert parts == 4 and ITERS == 2 and zones > 4 and zones & (zones - 1) == 0
    current, force, diag, low, up, inv = (
        x[0] for x in (flow_state, forcing, diag_block, lower_jac, upper_jac, block_inv)
    )
    state = current.shape
    planes, plane, blocks = state[0], state[1:], diag.shape
    matrix = blocks[1:]
    work = [buffer(*state)]

    def swap(x, bit):
        return lax.ppermute(x, "ja", [(p, p ^ bit) for p in range(parts)])

    tile, first, final = call(
        pack_kernel, [(1, *state[2:]), plane, plane], flops=10**10
    )(current)
    e, f, mats, live, pick, partner = call(
        matrix_kernel,
        [
            blocks, blocks, (20, *plane), state[2:],
            (2, zones, *state[2:]), (2, zones // 2, *state[2:]),
        ],
        [buffer(*blocks)]
        + [pltpu.SMEM((zones,), jnp.int32)] * 2
        + [pltpu.SemaphoreType.DMA((2,))],
        flops=5 * 10**9,
        far=(0, 1),
    )(zone_depth, east_zone, tile, inv, low, up)
    def exchange(x, stride):
        return lax.ppermute(x, "zone", [(z, z ^ stride) for z in range(zones)])

    far, near = zones // 2, zones // 4
    gots = [exchange(tile, stride) for stride in (far, near, far + near)]
    mats, tiles = call(relay_kernel, [(22, *plane), (4, *state[2:])], flops=10**5)(
        tile, *gots, mats, first, final
    )
    stride = zones // 8
    while stride > 1:
        both = (2 * tiles.shape[0], *state[2:])
        tiles = call(merge_kernel, [both], flops=10**5)(tiles, exchange(tiles, stride))[0]
        stride //= 2
    tiles, theirs = call(select_kernel, [state[2:]] * 2, flops=10**5)(tiles, pick, partner)
    got = exchange(theirs, 1)
    mats_other = swap(mats, 1)
    half = call(half_kernel, [(6, plane[0], 8, plane[2])], flops=10**5)(mats, mats_other)[0]
    s0 = call(source_kernel, [state], flops=2 * 10**9)(tiles, live, current, force, diag, inv, e, f)[0]
    s, ends, above = call(local_kernel, [state, (2, *plane), plane], work)(
        half, mats_other, live, tiles, got, current, s0, inv, e, f
    )
    half = swap(half, 3)
    ends_other = swap(ends, 1)
    pair = call(first_mid_kernel, [(1, *plane)], flops=10**5)(
        live, ends, ends_other, mats, mats_other
    )[0]
    parts_of = [(PART, *half.shape[2:])] * (30 // PART)
    half, *sent = call(parts_kernel, [half.shape] + parts_of, flops=10**5)(half, pair)
    half_other = [swap(x, 1) for x in sent]
    pair_other = swap(pair, 3)
    flows = [buffer(2, *plane)]
    current, above, below, tile = call(
        final_kernel, [state, plane, plane, (zones, *state[2:])], work + flows
    )(
        live, current, above, s, e, f,
        ends, ends_other, mats, mats_other, pair, pair_other, half, *half_other,
    )

    got = lax.all_to_all(tile, "zone", 0, 0, tiled=True)
    own, s, ends = call(second_kernel, [state, state, (3, *plane)], work)(
        live, pick, got, current, above, force, diag, inv, e, f
    )
    ends_other = swap(ends, 1)
    pair = call(mid_kernel, [(1, *plane)], flops=10**5)(ends, ends_other, mats, mats_other)[0]
    pair_other = swap(pair, 3)
    residual, done = call(
        write_kernel,
        [state, state[2:]],
        work + [pltpu.SemaphoreType.DMA((planes,))],
        out_specs=[HBM, VMEM],
    )(live, below, ends_other, current, above, own, low, up)
    current = call(
        last_kernel,
        [state],
        work + flows + work + [pltpu.SemaphoreType.DMA((planes,))],
        out_specs=[HBM],
    )(
        done, current, s, e, f,
        ends, ends_other, mats, mats_other, pair, pair_other, half, *half_other,
    )[0]
    return (current[None], residual[None])


def solution(mesh):
    state = P("zone", "ja", None, None, None)
    blocks = P("zone", "ja", None, None, None, None)
    return jax.shard_map(
        per_device,
        mesh=mesh,
        in_specs=(state, state, blocks, blocks, blocks, blocks, P(), P()),
        out_specs=(state, state),
        check_vma=False,
    )
```
